32 devices in a mesh: parts: 2 (over y), ctx: 4 (over z), ch: 2 (over x), sub: 2 (over core).
Axes of the slice: x: 2, y: 2, z: 4, core: 2. Of those that a mesh axis runs over, the one named last changes fastest.
Arguments:
- x_one: bfloat16 [1024, 8192], P(('parts', 'ctx'), ('ch', 'sub')), parts along dimension 0, may hold values from -6 to 6
- x_two: bfloat16 [1024, 8192], P(('parts', 'ctx'), ('ch', 'sub')), parts along dimension 0, may hold values from -6 to 6
- values: bfloat16 [1024, 8192], P(('parts', 'ctx'), ('ch', 'sub')), parts along dimension 0, may hold values from -6 to 6
- grad_out: bfloat16 [1024, 8192], P(('parts', 'ctx'), ('ch', 'sub')), parts along dimension 0, may hold values from -6 to 6
- first_weight: float32 [32, 64], replicated, may hold values from -3 to 3
- second_weight: float32 [64, 8192], P(None, ('ch', 'sub')), may hold values from -0.75 to 0.75
- skip_bias: float32 [8192], P(('ch', 'sub')), may hold values from 0.5 to 1.5
- decay_rate: float32 [8192], P(('ch', 'sub')), may hold values from 9.765625e-05 to 0.033
Outputs:
- grad_one: bfloat16 [1024, 8192], P(('parts', 'ctx'), ('ch', 'sub')), parts along dimension 0
- grad_two: bfloat16 [1024, 8192], P(('parts', 'ctx'), ('ch', 'sub')), parts along dimension 0
- grad_value: bfloat16 [1024, 8192], P(('parts', 'ctx'), ('ch', 'sub')), parts along dimension 0
- grad_first: float32 [64, 64], P('parts'), parts along dimension 0
- grad_second: float32 [128, 8192], P('parts', ('ch', 'sub')), parts along dimension 0
- grad_bias: float32 [16384], P(('parts', 'ch', 'sub')), parts along dimension 0
The draws below stay inside these ranges and needn't reach their ends.
There are 2 independent parts, one for each index of `parts`. The reference program is written for one: setup_inputs(seed, part) draws one part's arguments, and reference() takes and returns one part's arrays. A program takes and returns all parts, laid end to end along the dimension named above; an argument that names none is the same for every part. Nothing has to cross between parts.
All inputs are finite; a program needn't handle non-finite values.
Results may differ from the reference program's by a relative error of at most 0.004.
Values may be sent and summed in bfloat16 or wider, within the bound.
No kernel may reach another device: no remote copies, remote signals or barrier semaphores. Data moves between devices by JAX's collectives and lax.ppermute only.
A program may use at most 128 MiB of HBM per device.

```python
import math
import jax
import jax.numpy as jnp
from jax import lax

D = 8192
F = 32
FH = 64
SEQ = 512


def block_levels(rng, dims, split, low, largest):
    gain = 1.0
    for dim, shards_of in split:
        steps = jax.random.uniform(jax.random.fold_in(jax.random.fold_in(rng, 6), dim), (shards_of,), jnp.float32, low / len(split), largest / len(split))
        gain = gain * jnp.repeat(jnp.exp(steps), dims[dim] // shards_of).reshape((-1,) + (1,) * (len(dims) - 1 - dim))
    return gain


def scatter_about(own_key, shape, scale, bound, split=(), kind=jnp.bfloat16):
    level = block_levels(own_key, shape, split, -0.22, 0.18) if split else 1.0
    entries = jax.random.normal(own_key, shape, jnp.float32) * scale * level
    return jnp.minimum(jnp.maximum(entries, -bound), bound).astype(kind)


def setup_inputs(seed: int = 0, part: int = 0) -> dict:
    streams_of = jax.random.split(jax.random.key(seed), 9)
    part_keys = jax.random.split(jax.random.fold_in(streams_of[8], part), 9)
    x_one = scatter_about(part_keys[0], (SEQ, D), 1.0, 6.0, ((0, 4), (1, 4)))
    x_two = scatter_about(part_keys[1], (SEQ, D), 1.0, 6.0, ((0, 4), (1, 4)))
    values = scatter_about(part_keys[2], (SEQ, D), 1.0, 6.0, ((0, 4), (1, 4)))
    grad_out = scatter_about(part_keys[3], (SEQ, D), 1.0, 6.0, ((0, 4), (1, 4)))
    first_weight = scatter_about(streams_of[4], (F, FH), (F // 8) ** -0.5, 3.0, (), jnp.float32)
    second_weight = scatter_about(streams_of[5], (FH, D), FH ** -0.5, 0.75, ((1, 4),), jnp.float32)
    skip_bias = jnp.clip(0.5 + 1.0 * jax.random.uniform(streams_of[6], (D,), jnp.float32) ** block_levels(streams_of[6], (D,), ((0, 4),), -0.2, 0.2), 0.5, 1.5)
    decay_rate = jnp.clip(jnp.exp(math.log(0.033) - 5.822809 * jax.random.uniform(streams_of[7], (D,), jnp.float32) ** block_levels(streams_of[7], (D,), ((0, 4),), -0.2, 0.2)), 9.765625145519152e-05, 0.033)
    return dict(x_one=x_one, x_two=x_two, values=values, grad_out=grad_out, first_weight=first_weight, second_weight=second_weight, skip_bias=skip_bias, decay_rate=decay_rate)


band_steps = (1763, 1201, 811, 547, 367, 251, 167, 113, 79, 53, 37, 23, 17, 11, 7, 3)
highest = lax.Precision.HIGHEST


def features(positions):
    multiplier = jnp.array(band_steps, dtype=jnp.int32)
    phase = (positions[:, None] * multiplier[None, :]) % 4096
    angle = phase.astype(jnp.float32) * (2.0 * math.pi / 4096.0)
    return jnp.concatenate([jnp.cos(angle), jnp.sin(angle)], axis=1)


def reference(x_one, x_two, values, grad_out, first_weight, second_weight, skip_bias, decay_rate):
    seq_len, model_width = x_one.shape
    total = 2 * seq_len
    block_width = math.gcd(model_width, 512)
    block_count = model_width // block_width
    positions = jnp.arange(seq_len, dtype=jnp.int32)
    pos_float = positions.astype(jnp.float32)
    feats = features(positions)
    pre_act = jnp.dot(feats, first_weight, precision=highest, preferred_element_type=jnp.float32)
    hidden = jnp.sin(pre_act)

    def blocks_of(array):
        return array.reshape(array.shape[0], block_count, block_width).transpose(1, 0, 2)

    def one_block(pieces):
        first, second, value_in, cotan_in, weight, bias, rate = pieces
        source = first.astype(jnp.float32) * value_in.astype(jnp.float32)
        cotan = cotan_in.astype(jnp.float32) * second.astype(jnp.float32)
        envelope = jnp.exp(-pos_float[:, None] * rate[None, :]) * (float(seq_len) ** -0.5)
        filt = jnp.dot(hidden, weight, precision=highest, preferred_element_type=jnp.float32) * envelope
        source_spec = jnp.fft.rfft(source, n=total, axis=0)
        cotan_spec = jnp.fft.rfft(cotan, n=total, axis=0)
        filter_spec = jnp.fft.rfft(filt, n=total, axis=0)
        conv = jnp.fft.irfft(source_spec * filter_spec, n=total, axis=0)[:seq_len]
        corr = jnp.fft.irfft(cotan_spec * jnp.conj(filter_spec), n=total, axis=0)[:seq_len]
        filt_grad = jnp.fft.irfft(cotan_spec * jnp.conj(source_spec), n=total, axis=0)[:seq_len]
        grad_two = (cotan_in.astype(jnp.float32) * (conv + bias[None, :] * source)).astype(jnp.bfloat16)
        grad_mid = corr + bias[None, :] * cotan
        grad_one = (grad_mid * value_in.astype(jnp.float32)).astype(jnp.bfloat16)
        grad_value = (grad_mid * first.astype(jnp.float32)).astype(jnp.bfloat16)
        grad_bias = jnp.sum(source * cotan, axis=0)
        modulated = filt_grad * envelope
        grad_second = jnp.dot(hidden.T, modulated, precision=highest, preferred_element_type=jnp.float32)
        hidden_grad = jnp.dot(modulated, weight.T, precision=highest, preferred_element_type=jnp.float32)
        return grad_one, grad_two, grad_value, grad_second, grad_bias, hidden_grad

    results = lax.map(one_block, (blocks_of(x_one), blocks_of(x_two), blocks_of(values), blocks_of(grad_out),
                                  blocks_of(second_weight), skip_bias.reshape(block_count, block_width),
                                  decay_rate.reshape(block_count, block_width)))

    def unblock(array):
        return array.transpose(1, 0, 2).reshape(array.shape[1], model_width)

    grad_one = unblock(results[0])
    grad_two = unblock(results[1])
    grad_value = unblock(results[2])
    grad_second = unblock(results[3])
    grad_bias = results[4].reshape(model_width)
    hidden_grad = jnp.sum(results[5], axis=0)
    grad_first = jnp.dot(feats.T, hidden_grad * jnp.cos(pre_act), precision=highest, preferred_element_type=jnp.float32)
    return grad_one, grad_two, grad_value, grad_first, grad_second, grad_bias
```

```python
import functools
import math

import jax
import jax.numpy as jnp
import numpy as np
from jax import lax
from jax.experimental import pallas as pl
from jax.experimental.pallas import tpu as pltpu
from jax.sharding import PartitionSpec as P

band_steps = (1763, 1201, 811, 547, 367, 251, 167, 113, 79, 53, 37, 23, 17, 11, 7, 3)
highest = lax.Precision.HIGHEST
f32 = jnp.float32
bf16 = jnp.bfloat16


def features(positions):
    multiplier = jnp.array(band_steps, dtype=jnp.int32)
    phase = positions[:, None] * multiplier[None, :] % 4096
    angle = phase.astype(jnp.float32) * (2.0 * math.pi / 4096.0)
    return jnp.concatenate([jnp.cos(angle), jnp.sin(angle)], axis=1)


def tables(out_count, in_count, modulus, sign_value):
    row_index = lax.broadcasted_iota(jnp.int32, (out_count, in_count), 0)
    col_index = lax.broadcasted_iota(jnp.int32, (out_count, in_count), 1)
    angle = (row_index * col_index % modulus).astype(jnp.float32) * (2.0 * math.pi / modulus)
    return (jnp.cos(angle), sign_value * jnp.sin(angle))


def twiddle(spec_re, spec_im, freq_count, span, modulus, sign_value):
    freq_index = lax.broadcasted_iota(jnp.int32, (freq_count, span), 0)
    pos_index = lax.broadcasted_iota(jnp.int32, (freq_count, span), 1)
    angle = (freq_index * pos_index % modulus).astype(jnp.float32) * (2.0 * math.pi / modulus)
    factor_re = jnp.cos(angle)[None, None, :, :]
    factor_im = (sign_value * jnp.sin(angle))[None, None, :, :]
    return (spec_re * factor_re - spec_im * factor_im, spec_re * factor_im + spec_im * factor_re)


def contract(kernel, array):
    return jnp.einsum(
        "lj,mckj->mckl", kernel, array, precision=highest, preferred_element_type=jnp.float32
    )


def along_positions(spec_re, spec_im, kernel_re, kernel_im):
    return (
        contract(kernel_re, spec_re) - contract(kernel_im, spec_im),
        contract(kernel_re, spec_im) + contract(kernel_im, spec_re),
    )


def many_shards_body(
    x_one, x_two, values, grad_out, first_weight, second_weight, skip_bias, decay_rate
):
    row_count, chan_count = x_one.shape
    shards = lax.axis_size("ctx")
    rank = lax.axis_index("ctx")
    seq_len = row_count * shards
    total = 2 * seq_len
    narrow = chan_count // shards
    chan_weight = lax.dynamic_slice_in_dim(second_weight, rank * narrow, narrow, 1)
    chan_rate = lax.dynamic_slice_in_dim(decay_rate, rank * narrow, narrow, 0)
    source = x_one.astype(jnp.float32) * values.astype(jnp.float32)
    cotan = grad_out.astype(jnp.float32) * x_two.astype(jnp.float32)
    spread = lax.all_to_all(
        jnp.stack([source.T, cotan.T])[:, :, None, :],
        "ctx",
        split_axis=1,
        concat_axis=2,
        tiled=True,
    )
    far_source = spread[0]
    far_cotan = spread[1]
    positions = jnp.arange(seq_len, dtype=jnp.int32)
    feats = features(positions)
    pre_act = jnp.dot(feats, first_weight, precision=highest, preferred_element_type=jnp.float32)
    hidden = jnp.sin(pre_act)
    envelope = jnp.exp(-chan_rate[:, None] * positions.astype(jnp.float32)[None, :]) * float(
        seq_len
    ) ** (-0.5)
    filt = (
        jnp.einsum(
            "th,hc->ct", hidden, chan_weight, precision=highest, preferred_element_type=jnp.float32
        )
        * envelope
    )
    filt_blocks = filt.reshape(narrow, shards, row_count)
    fields = jnp.stack([far_source, far_cotan])

    def first_section(kernel):
        field_part = jnp.einsum(
            "kn,mcnj->mckj", kernel, fields, precision=highest, preferred_element_type=jnp.float32
        )
        filter_part = jnp.einsum(
            "kn,cnj->ckj",
            kernel,
            filt_blocks,
            precision=highest,
            preferred_element_type=jnp.float32,
        )
        return jnp.concatenate([field_part, filter_part[None]], axis=0)

    first_re, first_im = tables(2 * shards, shards, 2 * shards, -1.0)
    spec_re, spec_im = (first_section(first_re), first_section(first_im))
    spec_re, spec_im = twiddle(spec_re, spec_im, 2 * shards, row_count, total, -1.0)
    fwd_re, fwd_im = tables(row_count, row_count, row_count, -1.0)
    spec_re, spec_im = along_positions(spec_re, spec_im, fwd_re, fwd_im)
    source_re, source_im = (spec_re[0], spec_im[0])
    cotan_re, cotan_im = (spec_re[1], spec_im[1])
    filter_re, filter_im = (spec_re[2], spec_im[2])
    prod_re = jnp.stack(
        [
            source_re * filter_re - source_im * filter_im,
            cotan_re * filter_re + cotan_im * filter_im,
            cotan_re * source_re + cotan_im * source_im,
        ]
    )
    prod_im = jnp.stack(
        [
            source_re * filter_im + source_im * filter_re,
            cotan_im * filter_re - cotan_re * filter_im,
            cotan_im * source_re - cotan_re * source_im,
        ]
    )
    back_re, back_im = tables(row_count, row_count, row_count, 1.0)
    prod_re, prod_im = along_positions(prod_re, prod_im, back_re, back_im)
    prod_re, prod_im = twiddle(prod_re, prod_im, 2 * shards, row_count, total, 1.0)
    last_re, last_im = tables(shards, 2 * shards, 2 * shards, 1.0)
    field_out = jnp.einsum(
        "nk,mckj->mcnj", last_re, prod_re[:2], precision=highest, preferred_element_type=jnp.float32
    ) - jnp.einsum(
        "nk,mckj->mcnj", last_im, prod_im[:2], precision=highest, preferred_element_type=jnp.float32
    )
    field_out = field_out * (1.0 / total)
    filt_grad = jnp.einsum(
        "nk,ckj->cnj", last_re, prod_re[2], precision=highest, preferred_element_type=jnp.float32
    ) - jnp.einsum(
        "nk,ckj->cnj", last_im, prod_im[2], precision=highest, preferred_element_type=jnp.float32
    )
    filt_grad = (filt_grad * (1.0 / total)).reshape(narrow, seq_len)
    modulated = filt_grad * envelope
    weight_part = jnp.einsum(
        "th,ct->hc", hidden, modulated, precision=highest, preferred_element_type=jnp.float32
    )
    hidden_grad = jnp.einsum(
        "ct,hc->th", modulated, chan_weight, precision=highest, preferred_element_type=jnp.float32
    )
    first_part = jnp.dot(
        feats.T,
        hidden_grad * jnp.cos(pre_act),
        precision=highest,
        preferred_element_type=jnp.float32,
    )
    grad_first = lax.psum(first_part, ("ctx", "ch", "sub"))
    returned = lax.all_to_all(
        field_out.astype(jnp.bfloat16), "ctx", split_axis=2, concat_axis=1, tiled=True
    ).astype(field_out.dtype)
    conv_part = returned[0, :, 0, :].T
    corr_part = returned[1, :, 0, :].T
    grad_two = (grad_out.astype(jnp.float32) * (conv_part + skip_bias[None, :] * source)).astype(
        jnp.bfloat16
    )
    grad_mid = corr_part + skip_bias[None, :] * cotan
    grad_one = (grad_mid * values.astype(jnp.float32)).astype(jnp.bfloat16)
    grad_value = (grad_mid * x_one.astype(jnp.float32)).astype(jnp.bfloat16)
    grad_bias = lax.psum(jnp.sum(source * cotan, axis=0), "ctx")
    grad_second = lax.all_gather(weight_part, "ctx", axis=1, tiled=True)
    return (grad_one, grad_two, grad_value, grad_first, grad_second, grad_bias)


def halves(array):
    array = np.asarray(array, np.float32)
    high = array.astype(bf16)
    low = (array - high.astype(np.float32)).astype(bf16)
    return high, low


def block_tables(rows):
    double = 2 * rows
    freq = 2 * np.arange(rows)[:, None] + 1
    place = np.arange(double)[None, :]
    angle = (freq * place % (2 * double)) * (2.0 * np.pi / (2 * double))
    full = np.concatenate([np.cos(angle), -np.sin(angle)], axis=0)
    window = np.concatenate([-full[:, rows:], full[:, :rows]], axis=1)
    front_high, front_low = halves(full[:, :rows])
    return dict(
        front=np.concatenate([front_high, front_low], axis=1),
        window=halves(window),
        back=halves(full[:, :rows].T / rows),
        back_window=halves(window.T / rows),
    )


def feature_table(seq_len):
    phase = np.arange(seq_len)[:, None] * np.array(band_steps)[None, :] % 4096
    angle = phase * (2.0 * np.pi / 4096.0)
    return np.concatenate([np.cos(angle), np.sin(angle)], axis=1).astype(np.float32)


def split(array):
    high = array.astype(bf16)
    return high, (array - high.astype(f32)).astype(bf16)


def dot(left, right):
    return jnp.dot(left, right, preferred_element_type=f32)


def dot_across(left, right):
    return lax.dot_general(left, right, (((1,), (1,)), ((), ())), preferred_element_type=f32)


def decay(rate, first, count, scale):
    place = lax.broadcasted_iota(jnp.int32, (count, rate.shape[1]), 0) + first
    return jnp.exp(-place.astype(f32) * rate) * scale


def products_kernel(rank_ref, one_ref, two_ref, val_ref, out_ref, source_ref, cotan_ref, edge_ref, bias_ref):
    source = one_ref[...].astype(f32) * val_ref[...].astype(f32)
    cotan = out_ref[...].astype(f32) * two_ref[...].astype(f32)
    source_ref[...] = source.astype(bf16)
    cotan_ref[...] = cotan.astype(bf16)
    edge_ref[...] = jnp.where(rank_ref[0] == 0, cotan, source).astype(bf16)
    bias_ref[...] = jnp.sum(source * cotan, axis=0, keepdims=True)


def filter_kernel(rows, shards, hidden_ref, weight_ref, rate_ref, front_ref, win_high_ref, win_low_ref, spec_ref):
    seq_len = rows * shards
    w_high, w_low = split(weight_ref[...])
    stacked = jnp.concatenate([w_high, w_low, w_high], axis=0)
    filt = dot(hidden_ref[...], stacked) * decay(rate_ref[...], 0, seq_len, float(seq_len) ** -0.5)
    f_high, f_low = split(filt)
    first = f_high[:rows]
    spec_ref[0] = dot(front_ref[...], jnp.concatenate([first, first], axis=0)) + dot(
        front_ref[:, :rows], f_low[:rows]
    )
    for lag in range(1, shards):
        span = slice((lag - 1) * rows, (lag + 1) * rows)
        spec_ref[lag] = (
            dot(win_high_ref[...], f_high[span])
            + dot(win_low_ref[...], f_high[span])
            + dot(win_high_ref[...], f_low[span])
        )


def times(a, b):
    return a[0] * b[0] - a[1] * b[1], a[0] * b[1] + a[1] * b[0]


def conj_times(a, b):
    return a[0] * b[0] + a[1] * b[1], a[0] * b[1] - a[1] * b[0]


def plus(a, b):
    return a[0] + b[0], a[1] + b[1]


def main_kernel(
    rows, shards, step_rows, rank_ref, x0_ref, c0_ref, x1_ref, c1_ref, x2_ref, c2_ref, edge_ref, spec_ref,
    weight_ref, rate_ref, front_ref, back_high_ref, back_low_ref, bw_high_ref, bw_low_ref, ht_high_ref, ht_low_ref,
    featt_ref, slope_ref, conv_ref, corr_ref, part_ref, second_ref, first_ref, fields, prod_high, prod_low, hid_acc,
):
    rank = rank_ref[0]
    seq_len = rows * shards
    lower = rank == 1
    second = x2_ref[...] + c2_ref[...]
    blocks = (x0_ref[...], c0_ref[...], x1_ref[...], c1_ref[...], second, edge_ref[...])
    for index, block in enumerate(blocks):
        fields[index] = dot(front_ref[...], jnp.concatenate([block, block], axis=0))
    mask_up = jnp.where(rank == 2, 1.0, 0.0).astype(f32)
    mask_down = jnp.where(rank == 1, 1.0, 0.0).astype(f32)
    side = mask_up - mask_down

    def one_step(step, carry):
        low_rows = pl.ds(pl.multiple_of(step * step_rows, step_rows), step_rows)
        high_rows = pl.ds(pl.multiple_of(rows + step * step_rows, step_rows), step_rows)

        def get(ref, index):
            return ref[index, low_rows, :], ref[index, high_rows, :]

        def put(index, value):
            for part, where in zip(value, (low_rows, high_rows)):
                high, low = split(part)
                prod_high[index, where, :] = high
                prod_low[index, where, :] = low

        x0, c0, x1, c1, far, edge = (get(fields, i) for i in range(6))
        w0, w1, w2, w3 = (get(spec_ref, i) for i in range(4))
        x2 = (far[0] * mask_up, far[1] * mask_up)
        c2 = (far[0] * mask_down, far[1] * mask_down)
        put(0, plus(plus(times(w0, x0), times(w1, x1)), times(w2, x2)))
        put(1, plus(plus(conj_times(w0, c0), conj_times(w1, c1)), conj_times(w2, c2)))
        near = (jnp.where(lower, c1[0], x1[0]), jnp.where(lower, c1[1], x1[1]))
        w2s = (w2[0], w2[1] * side)
        w3s = (w3[0], w3[1] * side)
        put(2, plus(times(w2s, near), times(w3s, far)))
        own_a = (jnp.where(lower, x1[0], edge[0]), jnp.where(lower, x1[1], edge[1]))
        own_b = (jnp.where(lower, edge[0], c1[0]), jnp.where(lower, edge[1], c1[1]))
        put(3, plus(conj_times(x0, c0), conj_times(own_a, own_b)))
        up = conj_times(x0, c1)
        put(4, plus(conj_times(x1, c0), (up[0] * mask_up, up[1] * mask_up)))
        put(5, conj_times(x1, c1))
        put(6, conj_times(x1, c2))
        return carry

    lax.fori_loop(0, rows // step_rows, one_step, 0)

    def back(index):
        return (
            dot(back_high_ref[...], prod_high[index])
            + dot(back_low_ref[...], prod_high[index])
            + dot(back_high_ref[...], prod_low[index])
        )

    def back_window(index):
        return (
            dot(bw_high_ref[...], prod_high[index])
            + dot(bw_low_ref[...], prod_high[index])
            + dot(bw_high_ref[...], prod_low[index])
        )

    part_ref[...] = back(2).astype(bf16)
    conv_ref[...] = back(0)
    corr_ref[...] = back(1)
    wide = [back_window(4 + lag) for lag in range(shards - 1)]
    grads = [back(3) + wide[0][:rows]]
    for lag in range(1, shards):
        tail = wide[lag - 1][rows:]
        grads.append(tail + wide[lag][:rows] if lag < shards - 1 else tail)
    rate = rate_ref[...]
    scale = float(seq_len) ** -0.5
    grads = [g * decay(rate, lag * rows, rows, scale) for lag, g in enumerate(grads)]
    m_high, m_low = split(jnp.concatenate(grads, axis=0))
    second_ref[...] = (
        dot(ht_high_ref[...], m_high) + dot(ht_low_ref[...], m_high) + dot(ht_high_ref[...], m_low)
    )
    w_high, w_low = split(weight_ref[...])
    hid = dot_across(m_high, w_high) + dot_across(m_low, w_high) + dot_across(m_high, w_low)
    block = pl.program_id(0)

    @pl.when(block == 0)
    def _():
        hid_acc[...] = hid

    @pl.when(block > 0)
    def _():
        hid_acc[...] += hid

    @pl.when(block == pl.num_programs(0) - 1)
    def _():
        first_ref[...] = jnp.dot(
            featt_ref[...], hid_acc[...] * slope_ref[...], precision=highest, preferred_element_type=f32
        )


def final_kernel(
    shards, rank_ref, one_ref, two_ref, val_ref, out_ref, skip_ref, conv_ref, corr_ref, part_ref, *rest
):
    grad_one_ref, grad_two_ref, grad_value_ref = rest[-3:]
    rank = rank_ref[0]
    part = part_ref[...].astype(f32)
    zero = jnp.zeros_like(part)
    one = one_ref[...].astype(f32)
    val = val_ref[...].astype(f32)
    out = out_ref[...].astype(f32)
    skip = skip_ref[...]
    conv = conv_ref[...] + jnp.where(rank == shards - 1, part, zero)
    corr = corr_ref[...] + jnp.where(rank == 0, part, zero)
    grad_two_ref[...] = (out * (conv + skip * (one * val))).astype(bf16)
    mid = corr + skip * (out * two_ref[...].astype(f32))
    grad_one_ref[...] = (mid * val).astype(bf16)
    grad_value_ref[...] = (mid * one).astype(bf16)


def few_shards_body(
    x_one, x_two, values, grad_out, first_weight, second_weight, skip_bias, decay_rate, pieces=2
):
    rows, chan_count = x_one.shape
    shards = lax.axis_size("ctx")
    hid_count = second_weight.shape[0]
    feat_count = first_weight.shape[0]
    seq_len = rows * shards
    double = 2 * rows
    narrow = chan_count // pieces
    width = min(256, narrow)
    blocks = narrow // width
    rank = lax.axis_index("ctx")
    rank_cell = rank.astype(jnp.int32).reshape(1)
    table = block_tables(rows)
    skip_row = skip_bias.reshape(1, chan_count)
    rate_row = decay_rate.reshape(1, chan_count)
    smem = pl.BlockSpec(memory_space=pltpu.SMEM)
    params = pltpu.CompilerParams(vmem_limit_bytes=48 * 1024 * 1024)

    def whole(shape):
        return pl.BlockSpec(shape, lambda i: (0,) * len(shape))

    def local(*lead):
        return pl.BlockSpec(lead + (width,), lambda i: (0,) * len(lead) + (i,))

    def strip(count, piece):
        return pl.BlockSpec((count, width), lambda i: (0, piece * blocks + i))

    def shape(*dims, dtype=f32):
        return jax.ShapeDtypeStruct(dims, dtype)

    def products(piece):
        gate = strip(rows, piece)
        return pl.pallas_call(
            products_kernel,
            grid=(blocks,),
            in_specs=[smem, gate, gate, gate, gate],
            out_specs=[local(rows), local(rows), local(rows), local(1)],
            out_shape=[shape(rows, narrow, dtype=bf16)] * 3 + [shape(1, narrow)],
            compiler_params=params,
            cost_estimate=pl.CostEstimate(
                flops=6 * rows * narrow, bytes_accessed=14 * rows * narrow, transcendentals=0
            ),
            name="products",
        )(rank_cell, x_one, x_two, values, grad_out)

    def filters(piece, stacked_hidden):
        return pl.pallas_call(
            functools.partial(filter_kernel, rows, shards),
            grid=(blocks,),
            in_specs=[
                whole((seq_len, 3 * hid_count)),
                strip(hid_count, piece),
                strip(1, piece),
                whole((double, double)),
                whole((double, double)),
                whole((double, double)),
            ],
            out_specs=local(shards, double),
            out_shape=shape(shards, double, narrow),
            compiler_params=params,
            cost_estimate=pl.CostEstimate(
                flops=2 * 14 * double * double * narrow,
                bytes_accessed=4 * shards * double * narrow,
                transcendentals=seq_len * narrow,
            ),
            name="filters",
        )(stacked_hidden, second_weight, rate_row, table["front"], *table["window"])

    def main(piece, fields, spec, ht_high, ht_low, featt, slope):
        return pl.pallas_call(
            functools.partial(main_kernel, rows, shards, 16),
            grid=(blocks,),
            in_specs=[smem]
            + [local(rows)] * 7
            + [
                local(shards, double),
                strip(hid_count, piece),
                strip(1, piece),
                whole((double, double)),
                whole((rows, double)),
                whole((rows, double)),
                whole((double, double)),
                whole((double, double)),
                whole((hid_count, seq_len)),
                whole((hid_count, seq_len)),
                whole((feat_count, seq_len)),
                whole((seq_len, hid_count)),
            ],
            out_specs=[
                local(rows),
                local(rows),
                local(rows),
                local(hid_count),
                whole((feat_count, hid_count)),
            ],
            out_shape=[
                shape(rows, narrow),
                shape(rows, narrow),
                shape(rows, narrow, dtype=bf16),
                shape(hid_count, narrow),
                shape(feat_count, hid_count),
            ],
            scratch_shapes=[
                pltpu.VMEM((6, double, width), f32),
                pltpu.VMEM((7, double, width), bf16),
                pltpu.VMEM((7, double, width), bf16),
                pltpu.VMEM((seq_len, hid_count), f32),
            ],
            compiler_params=params,
            cost_estimate=pl.CostEstimate(
                flops=2 * 25 * double * double * narrow,
                bytes_accessed=6 * shards * double * narrow,
                transcendentals=seq_len * narrow,
            ),
            name="block_products",
        )(
            rank_cell, *fields, spec, second_weight, rate_row, table["front"], *table["back"],
            *table["back_window"], ht_high, ht_low, featt, slope,
        )

    def final(piece, conv, corr, part, before):
        gate = strip(rows, piece)
        held = [pl.BlockSpec(memory_space=pl.ANY)] * len(before)
        return pl.pallas_call(
            functools.partial(final_kernel, shards),
            grid=(blocks,),
            in_specs=[smem, gate, gate, gate, gate, strip(1, piece)] + [local(rows)] * 3 + held,
            out_specs=[gate] * 3,
            out_shape=[shape(rows, chan_count, dtype=bf16)] * 3,
            input_output_aliases={9 + i: i for i in range(len(before))},
            compiler_params=params,
            cost_estimate=pl.CostEstimate(
                flops=10 * rows * narrow, bytes_accessed=24 * rows * narrow, transcendentals=0
            ),
            name="gates",
        )(rank_cell, x_one, x_two, values, grad_out, skip_row, conv, corr, part, *before)

    def move(array, pairs):
        return lax.ppermute(array, "ctx", pairs)

    up = [(i, i + 1) for i in range(shards - 1)]
    down = [(i + 1, i) for i in range(shards - 1)]
    inward = [(0, 1), (shards - 1, shards - 2)]
    outward = [(1, 0), (shards - 2, shards - 1)]
    across = [(1, 2), (2, 1)]

    starts = [products(p) for p in range(pieces)]
    x1 = [move(s[0], up) for s in starts]
    c1 = [move(s[1], down) for s in starts]
    x2 = [move(a, [(1, 2)]) for a in x1]
    c2 = [move(a, [(2, 1)]) for a in c1]
    edge = [move(s[2], inward) for s in starts]

    feats = feature_table(seq_len)
    pre_act = jnp.dot(feats, first_weight, precision=highest, preferred_element_type=f32)
    hidden = jnp.sin(pre_act)
    slope = jnp.cos(pre_act)
    h_high, h_low = split(hidden)
    stacked_hidden = jnp.concatenate([h_high, h_high, h_low], axis=1)
    specs = [filters(p, stacked_hidden) for p in range(pieces)]

    bias = jnp.concatenate([s[3] for s in starts], axis=1)
    bias = bias + move(bias, [(i, i ^ 1) for i in range(shards)])
    bias = bias + move(bias, [(i, i ^ 2) for i in range(shards)])

    inner = (rank == 1) | (rank == 2)
    outs = ()
    seconds = []
    firsts = []
    for p in range(pieces):
        fields = (starts[p][0], starts[p][1], x1[p], c1[p], x2[p], c2[p], edge[p])
        conv, corr, part, second, first = main(
            p, fields, specs[p], h_high.T, h_low.T, jnp.asarray(feats.T), slope
        )
        outs = final(p, conv, corr, move(part, outward), outs)
        total = second + move(second, across)
        seconds.append(jnp.where(inner, total, move(total, outward)))
        firsts.append(first)
    first = sum(firsts)
    group = lax.axis_size(("ch", "sub"))

    def swap(array, bit):
        return lax.ppermute(array, ("ch", "sub"), [(i, i ^ bit) for i in range(group)])

    bit = 1
    while bit < group:
        first = first + swap(first, bit)
        bit *= 2
    total = first + move(first, across)
    grad_first = jnp.where(inner, total, move(total, outward))
    grad_second = jnp.concatenate(seconds, axis=1)
    return (*outs, grad_first, grad_second, bias.reshape(chan_count))


def solution(mesh):
    in_specs = (
        P(("parts", "ctx"), ("ch", "sub")),
        P(("parts", "ctx"), ("ch", "sub")),
        P(("parts", "ctx"), ("ch", "sub")),
        P(("parts", "ctx"), ("ch", "sub")),
        P(),
        P(None, ("ch", "sub")),
        P(("ch", "sub")),
        P(("ch", "sub")),
    )
    out_specs = (
        P(("parts", "ctx"), ("ch", "sub")),
        P(("parts", "ctx"), ("ch", "sub")),
        P(("parts", "ctx"), ("ch", "sub")),
        P("parts", None),
        P("parts", ("ch", "sub")),
        P(("parts", "ch", "sub")),
    )
    body = few_shards_body if mesh.shape["ctx"] == 4 else many_shards_body
    return jax.shard_map(body, mesh=mesh, in_specs=in_specs, out_specs=out_specs, check_vma=False)
```

```python
import functools
import math

import jax
import jax.numpy as jnp
import numpy as np
from jax import lax
from jax.experimental import pallas as pl
from jax.experimental.pallas import tpu as pltpu
from jax.sharding import PartitionSpec as P

band_steps = (1763, 1201, 811, 547, 367, 251, 167, 113, 79, 53, 37, 23, 17, 11, 7, 3)
highest = lax.Precision.HIGHEST
f32 = jnp.float32
bf16 = jnp.bfloat16


def features(positions):
    multiplier = jnp.array(band_steps, dtype=jnp.int32)
    phase = positions[:, None] * multiplier[None, :] % 4096
    angle = phase.astype(jnp.float32) * (2.0 * math.pi / 4096.0)
    return jnp.concatenate([jnp.cos(angle), jnp.sin(angle)], axis=1)


def tables(out_count, in_count, modulus, sign_value):
    row_index = lax.broadcasted_iota(jnp.int32, (out_count, in_count), 0)
    col_index = lax.broadcasted_iota(jnp.int32, (out_count, in_count), 1)
    angle = (row_index * col_index % modulus).astype(jnp.float32) * (2.0 * math.pi / modulus)
    return (jnp.cos(angle), sign_value * jnp.sin(angle))


def twiddle(spec_re, spec_im, freq_count, span, modulus, sign_value):
    freq_index = lax.broadcasted_iota(jnp.int32, (freq_count, span), 0)
    pos_index = lax.broadcasted_iota(jnp.int32, (freq_count, span), 1)
    angle = (freq_index * pos_index % modulus).astype(jnp.float32) * (2.0 * math.pi / modulus)
    factor_re = jnp.cos(angle)[None, None, :, :]
    factor_im = (sign_value * jnp.sin(angle))[None, None, :, :]
    return (spec_re * factor_re - spec_im * factor_im, spec_re * factor_im + spec_im * factor_re)


def contract(kernel, array):
    return jnp.einsum(
        "lj,mckj->mckl", kernel, array, precision=highest, preferred_element_type=jnp.float32
    )


def along_positions(spec_re, spec_im, kernel_re, kernel_im):
    return (
        contract(kernel_re, spec_re) - contract(kernel_im, spec_im),
        contract(kernel_re, spec_im) + contract(kernel_im, spec_re),
    )


def many_shards_body(
    x_one, x_two, values, grad_out, first_weight, second_weight, skip_bias, decay_rate
):
    row_count, chan_count = x_one.shape
    shards = lax.axis_size("ctx")
    rank = lax.axis_index("ctx")
    seq_len = row_count * shards
    total = 2 * seq_len
    narrow = chan_count // shards
    chan_weight = lax.dynamic_slice_in_dim(second_weight, rank * narrow, narrow, 1)
    chan_rate = lax.dynamic_slice_in_dim(decay_rate, rank * narrow, narrow, 0)
    source = x_one.astype(jnp.float32) * values.astype(jnp.float32)
    cotan = grad_out.astype(jnp.float32) * x_two.astype(jnp.float32)
    spread = lax.all_to_all(
        jnp.stack([source.T, cotan.T])[:, :, None, :],
        "ctx",
        split_axis=1,
        concat_axis=2,
        tiled=True,
    )
    far_source = spread[0]
    far_cotan = spread[1]
    positions = jnp.arange(seq_len, dtype=jnp.int32)
    feats = features(positions)
    pre_act = jnp.dot(feats, first_weight, precision=highest, preferred_element_type=jnp.float32)
    hidden = jnp.sin(pre_act)
    envelope = jnp.exp(-chan_rate[:, None] * positions.astype(jnp.float32)[None, :]) * float(
        seq_len
    ) ** (-0.5)
    filt = (
        jnp.einsum(
            "th,hc->ct", hidden, chan_weight, precision=highest, preferred_element_type=jnp.float32
        )
        * envelope
    )
    filt_blocks = filt.reshape(narrow, shards, row_count)
    fields = jnp.stack([far_source, far_cotan])

    def first_section(kernel):
        field_part = jnp.einsum(
            "kn,mcnj->mckj", kernel, fields, precision=highest, preferred_element_type=jnp.float32
        )
        filter_part = jnp.einsum(
            "kn,cnj->ckj",
            kernel,
            filt_blocks,
            precision=highest,
            preferred_element_type=jnp.float32,
        )
        return jnp.concatenate([field_part, filter_part[None]], axis=0)

    first_re, first_im = tables(2 * shards, shards, 2 * shards, -1.0)
    spec_re, spec_im = (first_section(first_re), first_section(first_im))
    spec_re, spec_im = twiddle(spec_re, spec_im, 2 * shards, row_count, total, -1.0)
    fwd_re, fwd_im = tables(row_count, row_count, row_count, -1.0)
    spec_re, spec_im = along_positions(spec_re, spec_im, fwd_re, fwd_im)
    source_re, source_im = (spec_re[0], spec_im[0])
    cotan_re, cotan_im = (spec_re[1], spec_im[1])
    filter_re, filter_im = (spec_re[2], spec_im[2])
    prod_re = jnp.stack(
        [
            source_re * filter_re - source_im * filter_im,
            cotan_re * filter_re + cotan_im * filter_im,
            cotan_re * source_re + cotan_im * source_im,
        ]
    )
    prod_im = jnp.stack(
        [
            source_re * filter_im + source_im * filter_re,
            cotan_im * filter_re - cotan_re * filter_im,
            cotan_im * source_re - cotan_re * source_im,
        ]
    )
    back_re, back_im = tables(row_count, row_count, row_count, 1.0)
    prod_re, prod_im = along_positions(prod_re, prod_im, back_re, back_im)
    prod_re, prod_im = twiddle(prod_re, prod_im, 2 * shards, row_count, total, 1.0)
    last_re, last_im = tables(shards, 2 * shards, 2 * shards, 1.0)
    field_out = jnp.einsum(
        "nk,mckj->mcnj", last_re, prod_re[:2], precision=highest, preferred_element_type=jnp.float32
    ) - jnp.einsum(
        "nk,mckj->mcnj", last_im, prod_im[:2], precision=highest, preferred_element_type=jnp.float32
    )
    field_out = field_out * (1.0 / total)
    filt_grad = jnp.einsum(
        "nk,ckj->cnj", last_re, prod_re[2], precision=highest, preferred_element_type=jnp.float32
    ) - jnp.einsum(
        "nk,ckj->cnj", last_im, prod_im[2], precision=highest, preferred_element_type=jnp.float32
    )
    filt_grad = (filt_grad * (1.0 / total)).reshape(narrow, seq_len)
    modulated = filt_grad * envelope
    weight_part = jnp.einsum(
        "th,ct->hc", hidden, modulated, precision=highest, preferred_element_type=jnp.float32
    )
    hidden_grad = jnp.einsum(
        "ct,hc->th", modulated, chan_weight, precision=highest, preferred_element_type=jnp.float32
    )
    first_part = jnp.dot(
        feats.T,
        hidden_grad * jnp.cos(pre_act),
        precision=highest,
        preferred_element_type=jnp.float32,
    )
    grad_first = lax.psum(first_part, ("ctx", "ch", "sub"))
    returned = lax.all_to_all(
        field_out.astype(jnp.bfloat16), "ctx", split_axis=2, concat_axis=1, tiled=True
    ).astype(field_out.dtype)
    conv_part = returned[0, :, 0, :].T
    corr_part = returned[1, :, 0, :].T
    grad_two = (grad_out.astype(jnp.float32) * (conv_part + skip_bias[None, :] * source)).astype(
        jnp.bfloat16
    )
    grad_mid = corr_part + skip_bias[None, :] * cotan
    grad_one = (grad_mid * values.astype(jnp.float32)).astype(jnp.bfloat16)
    grad_value = (grad_mid * x_one.astype(jnp.float32)).astype(jnp.bfloat16)
    grad_bias = lax.psum(jnp.sum(source * cotan, axis=0), "ctx")
    grad_second = lax.all_gather(weight_part, "ctx", axis=1, tiled=True)
    return (grad_one, grad_two, grad_value, grad_first, grad_second, grad_bias)


STEP = 16
SIDE = 256


def halves(array):
    array = np.asarray(array, np.float32)
    high = array.astype(bf16)
    low = (array - high.astype(np.float32)).astype(bf16)
    return high, low


def block_tables(rows):
    freq = np.concatenate([np.arange(0, rows, 2), np.arange(1, rows, 2)])
    phase = (2 * freq + 1)[:, None] * np.arange(rows)[None, :] % (4 * rows)
    angle = phase * (2.0 * np.pi / (4 * rows))
    forward = np.concatenate([np.cos(angle), -np.sin(angle)], axis=0)
    front = np.ascontiguousarray(np.concatenate(halves(forward), axis=1))
    back = np.ascontiguousarray(np.concatenate(halves(forward.T / rows), axis=0))
    return front, back


def feature_table(seq_len):
    phase = np.arange(seq_len)[:, None] * np.array(band_steps)[None, :] % 4096
    angle = phase * (2.0 * np.pi / 4096.0)
    return np.concatenate([np.cos(angle), np.sin(angle)], axis=1).astype(np.float32)


def split(array):
    high = array.astype(bf16)
    return high, (array - high.astype(f32)).astype(bf16)


def dot(left, right):
    return jnp.dot(left, right, preferred_element_type=f32)


def exact_dot(left, right):
    return jnp.dot(left, right, precision=highest, preferred_element_type=f32)


def dot_across(left, right):
    return lax.dot_general(left, right, (((1,), (1,)), ((), ())), preferred_element_type=f32)


def decay(rate, rows, scale):
    place = lax.broadcasted_iota(jnp.int32, (rows, rate.shape[1]), 0)
    return jnp.exp(-place.astype(f32) * rate) * scale


def times(a, b):
    return a[0] * b[0] - a[1] * b[1], a[0] * b[1] + a[1] * b[0]


def conj_times(a, b):
    return a[0] * b[0] + a[1] * b[1], a[0] * b[1] - a[1] * b[0]


def plus(a, b):
    return a[0] + b[0], a[1] + b[1]


def scaled(a, factor):
    return a[0] * factor, a[1] * factor


def choose(condition, a, b):
    return jnp.where(condition, a[0], b[0]), jnp.where(condition, a[1], b[1])


def turned(a, sign):
    return (a[1], -a[0]) if sign > 0 else (-a[1], a[0])


def forward(front_ref, block):
    return dot(front_ref[...], jnp.concatenate([block, block], axis=0))


def backward(back_ref, high, low=None):
    both = dot(back_ref[...], high)
    rows = both.shape[0] // 2
    out = both[:rows] + both[rows:]
    return out if low is None else out + dot(back_ref[:rows], low)


def row_groups(rows):
    for step in range(rows // STEP):
        sign = 1 if step * STEP < rows // 2 else -1
        yield slice(step * STEP, (step + 1) * STEP), slice(rows + step * STEP, rows + (step + 1) * STEP), sign


def weight_sums(trans, m_high, m_low):
    both = dot(trans, m_high)
    count = both.shape[0] // 2
    return both[:count] + both[count:] + dot(trans[:count], m_low)


def hidden_sums(m_high, m_low, w_high, w_low):
    left = jnp.concatenate([m_high, m_high, m_low], axis=1)
    right = jnp.concatenate([w_high, w_low, w_high], axis=1)
    return dot_across(left, right)


def add_up(ref, value, block):
    @pl.when(block == 0)
    def _():
        ref[...] = value

    @pl.when(block > 0)
    def _():
        ref[...] += value


def products_kernel(one_ref, two_ref, val_ref, out_ref, source_ref, cotan_ref, bias_ref):
    source = one_ref[...].astype(f32) * val_ref[...].astype(f32)
    cotan = out_ref[...].astype(f32) * two_ref[...].astype(f32)
    source_ref[...] = source.astype(bf16)
    cotan_ref[...] = cotan.astype(bf16)
    bias_ref[...] = jnp.sum(source * cotan, axis=0, keepdims=True)


def filters_kernel(
    rows, shards, feats_ref, featt_ref, first_ref, weight_ref, rate_ref, front_ref, back_ref, source_ref, cotan_ref,
    bias_ref, spec_ref, sums_ref, trans_ref, slope_ref, hid_ref, acc_ref,
):
    block = pl.program_id(0)
    last = pl.num_programs(0) - 1
    hid_count, width = weight_ref.shape
    channels = bias_ref.shape[1]
    scale = float(rows * shards) ** -0.5

    @pl.when(block == 0)
    def _():
        pre_act = exact_dot(feats_ref[...], first_ref[...])
        hidden = jnp.sin(pre_act)
        slope = jnp.cos(pre_act)
        slope_ref[...] = slope
        high, low = split(hidden)
        hid_ref[...] = jnp.concatenate([high, high, low], axis=1)
        turned_over = jnp.concatenate([hidden, slope], axis=1).T[:hid_count]
        trans_ref[...] = jnp.concatenate(split(turned_over), axis=0)

    w_high, w_low = split(weight_ref[...])
    stacked = jnp.concatenate([w_high, w_low, w_high], axis=0)
    rate = rate_ref[...]
    env = decay(rate, rows, scale)
    before = None
    for lag in range(shards):
        part = dot(hid_ref[lag * rows : (lag + 1) * rows, :], stacked)
        part = part * (env * jnp.exp(rate * (-float(lag * rows))))
        f_high, f_low = split(part)
        now = forward(front_ref, f_high) + dot(front_ref[:, :rows], f_low)
        for re, im, sign in row_groups(rows):
            here = (now[re], now[im])
            if before is not None:
                here = plus(here, turned((before[re], before[im]), -sign))
            spec_ref[lag, re, :] = here[0]
            spec_ref[lag, im, :] = here[1]
        before = now

    x0 = forward(front_ref, source_ref[...])
    c0 = forward(front_ref, cotan_ref[...])
    pair = conj_times((x0[:rows], x0[rows:]), (c0[:rows], c0[rows:]))
    high, low = split(jnp.concatenate(pair, axis=0))
    m_high, m_low = split(backward(back_ref, high, low) * env)
    sums_ref[:, pl.ds(pl.multiple_of(block * width, width), width)] = weight_sums(
        trans_ref[:, :rows], m_high, m_low
    )
    add_up(acc_ref, hidden_sums(m_high, m_low, w_high, w_low), block)

    @pl.when(block == last)
    def _():
        bias = bias_ref[...]
        lanes = channels // 128
        sums_ref[:, channels:] = jnp.zeros((hid_count, SIDE), f32)
        sums_ref[:lanes, channels : channels + 128] = jnp.concatenate(
            [bias[:, i * 128 : (i + 1) * 128] for i in range(lanes)], axis=0
        )
        first = exact_dot(featt_ref[:, :rows], acc_ref[...] * slope_ref[:rows, :])
        sums_ref[hid_count // 2 :, channels : channels + hid_count] = first


def near_kernel(
    rows, shards, rank_ref, x0_ref, c0_ref, x1_ref, c1_ref, spec_ref, weight_ref, rate_ref, front_ref, back_ref,
    trans_ref, featt_ref, slope_ref, own_ref, conv_ref, corr_ref, ahead_ref, sums_ref, first_ref, fields, fast, high_ref,
    low_ref, acc_ref,
):
    block = pl.program_id(0)
    last = pl.num_programs(0) - 1
    rank = rank_ref[0]
    count = shards - 1
    lower = rank == 1
    upper = jnp.where(rank == 2, 1.0, 0.0).astype(f32)
    below_top = jnp.where(rank == shards - 1, 0.0, 1.0).astype(f32)
    side = jnp.where(rank == 2, 1.0, -1.0).astype(f32)
    for index, ref in enumerate((x0_ref, c0_ref, x1_ref, c1_ref)):
        fields[index] = forward(front_ref, ref[...])
    for re, im, sign in row_groups(rows):
        x0, c0, x1, c1 = ((fields[i, re, :], fields[i, im, :]) for i in range(4))
        w0, w1, w2 = ((spec_ref[i, re, :], spec_ref[i, im, :]) for i in range(3))
        ahead = times((w2[0], w2[1] * side), choose(lower, c1, x1))
        for index, value in enumerate(
            (plus(times(w0, x0), times(w1, x1)), plus(conj_times(w0, c0), conj_times(w1, c1)), ahead)
        ):
            fast[index, re, :] = value[0].astype(bf16)
            fast[index, im, :] = value[1].astype(bf16)
        one = plus(scaled(conj_times(x1, c0), below_top), scaled(conj_times(x0, c1), upper))
        two = conj_times(x1, c1)
        for index, value in enumerate((turned(one, sign), plus(one, turned(two, sign)), two)):
            for part, where in zip(value, (re, im)):
                high_ref[index, where, :], low_ref[index, where, :] = split(part)
    conv_ref[...] = backward(back_ref, fast[0])
    corr_ref[...] = backward(back_ref, fast[1])
    ahead_ref[...] = backward(back_ref, fast[2])
    rate = rate_ref[...]
    env = decay(rate, rows, float(rows * shards) ** -0.5)
    parts = []
    for lag in range(count):
        grad = backward(back_ref, high_ref[lag], low_ref[lag])
        parts.append(split(grad * (env * jnp.exp(rate * (-float(lag * rows))))))
    m_high = jnp.concatenate([p[0] for p in parts], axis=0)
    m_low = jnp.concatenate([p[1] for p in parts], axis=0)
    sums_ref[...] = own_ref[...] + weight_sums(trans_ref[:, : count * rows], m_high, m_low)
    w_high, w_low = split(weight_ref[...])
    add_up(acc_ref, hidden_sums(m_high, m_low, w_high, w_low), block)

    @pl.when(block == last)
    def _():
        first_ref[...] = exact_dot(
            featt_ref[:, : count * rows], acc_ref[...] * slope_ref[: count * rows, :]
        )


def far_kernel(rows, rank_ref, x2_ref, c2_ref, spec_ref, front_ref, back_ref, ahead_ref, part_ref, late_ref):
    side = jnp.where(rank_ref[0] == 2, 1.0, -1.0).astype(f32)
    far = forward(front_ref, x2_ref[...] + c2_ref[...])
    far = (far[:rows], far[rows:])
    w2, w3 = ((spec_ref[i, :rows, :], spec_ref[i, rows:, :] * side) for i in range(2))
    ahead = jnp.concatenate(times(w3, far), axis=0).astype(bf16)
    part_ref[...] = (ahead_ref[...] + backward(back_ref, ahead)).astype(bf16)
    late = jnp.concatenate(times(w2, far), axis=0).astype(bf16)
    late_ref[...] = backward(back_ref, late)


def last_kernel(
    rows, shards, channels, rank_ref, x1_ref, c1_ref, x2_ref, c2_ref, weight_ref, rate_ref, front_ref, back_ref,
    trans_ref, featt_ref, slope_ref, sums_ref, first_ref, own_ref, in_ref, after_ref, pay_ref, total_ref, acc_ref,
):
    del after_ref
    block = pl.program_id(0)
    blocks = pl.num_programs(0)
    hid_count, width = weight_ref.shape
    rank = rank_ref[0]
    lower = rank == 1
    start = pl.multiple_of(block * width, width)
    here = sums_ref[...] + in_ref[:, pl.ds(start, width)]
    mine = (block < blocks // 2) == lower

    @pl.when(block == 0)
    def _():
        acc_ref[...] = jnp.zeros_like(acc_ref)

    @pl.when(mine)
    def _():
        sign = jnp.where(lower, 1.0, -1.0).astype(f32)
        near = forward(front_ref, jnp.where(lower, x1_ref[...], c1_ref[...]))
        far = forward(front_ref, x2_ref[...] + c2_ref[...])
        three = conj_times((near[:rows], near[rows:]), (far[:rows], far[rows:]))
        three = (three[0], three[1] * sign)
        half = rows // 2
        two = jnp.concatenate([three[1][:half], -three[1][half:], -three[0][:half], three[0][half:]], axis=0)
        rate = rate_ref[...]
        env = decay(rate, rows, float(rows * shards) ** -0.5)
        parts = []
        for lag, value in ((shards - 2, two), (shards - 1, jnp.concatenate(three, axis=0))):
            grad = backward(back_ref, *split(value))
            parts.append(split(grad * (env * jnp.exp(rate * (-float(lag * rows))))))
        m_high = jnp.concatenate([p[0] for p in parts], axis=0)
        m_low = jnp.concatenate([p[1] for p in parts], axis=0)
        trans = trans_ref[:, (shards - 2) * rows :]
        pay_ref[:, pl.ds(start, width)] = (here + weight_sums(trans, m_high, m_low)).astype(bf16)
        w_high, w_low = split(weight_ref[...])
        acc_ref[...] += hidden_sums(m_high, m_low, w_high, w_low)

    @pl.when(jnp.logical_not(mine))
    def _():
        pay_ref[:, pl.ds(start, width)] = here.astype(bf16)

    @pl.when(block == blocks - 1)
    def _():
        lanes = channels // 128
        half = hid_count // 2
        pay_ref[:, channels:] = jnp.zeros((hid_count, SIDE), bf16)
        bias = own_ref[:half, :128] + in_ref[:half, channels : channels + 128]
        high, low = split(bias)
        pay_ref[:half, channels : channels + 128] = high
        pay_ref[:half, channels + 128 : channels + SIDE] = low
        first = exact_dot(
            featt_ref[:, (shards - 2) * rows :], acc_ref[...] * slope_ref[(shards - 2) * rows :, :]
        )
        total_ref[...] = (
            first
            + first_ref[...]
            + own_ref[half:, :hid_count]
            + in_ref[half:, channels : channels + hid_count]
        )


def total_kernel(channels, own_ref, come_ref, first_ref, far_first_ref, pay_ref):
    half = own_ref.shape[0] // 2
    hid_count = first_ref.shape[1]
    pay_ref[:, :channels] = (own_ref[:, :channels].astype(f32) + come_ref[:, :channels].astype(f32)).astype(bf16)
    high = own_ref[:half, channels : channels + 128].astype(f32) + come_ref[:half, channels : channels + 128].astype(f32)
    low = own_ref[:half, channels + 128 :].astype(f32) + come_ref[:half, channels + 128 :].astype(f32)
    pay_ref[:, channels:] = jnp.zeros((2 * half, SIDE), bf16)
    high, low = split(high + low)
    pay_ref[:half, channels : channels + 128] = high
    pay_ref[:half, channels + 128 :] = low
    high, low = split(first_ref[...] + far_first_ref[...])
    pay_ref[half:, channels : channels + hid_count] = high
    pay_ref[half:, channels + 128 : channels + 128 + hid_count] = low


def gates_kernel(
    shards, rank_ref, one_ref, two_ref, val_ref, out_ref, skip_ref, conv_ref, corr_ref, late_ref, part_ref,
    grad_one_ref, grad_two_ref, grad_value_ref,
):
    rank = rank_ref[0]

    def mask(wanted):
        return jnp.where(rank == wanted, 1.0, 0.0).astype(f32)

    part = part_ref[...].astype(f32)
    late = late_ref[...]
    one = one_ref[...].astype(f32)
    val = val_ref[...].astype(f32)
    out = out_ref[...].astype(f32)
    skip = skip_ref[...]
    conv = conv_ref[...] + late * mask(2) + part * mask(shards - 1)
    corr = corr_ref[...] + late * mask(1) + part * mask(0)
    grad_two_ref[...] = (out * (conv + skip * (one * val))).astype(bf16)
    mid = corr + skip * (out * two_ref[...].astype(f32))
    grad_one_ref[...] = (mid * val).astype(bf16)
    grad_value_ref[...] = (mid * one).astype(bf16)


def finish_kernel(channels, shards, rank_ref, own_ref, come_ref, second_ref, first_ref, bias_ref):
    rank = rank_ref[0]
    inner = jnp.logical_and(rank > 0, rank < shards - 1)
    hid_count = second_ref.shape[0]
    half = hid_count // 2
    lanes = channels // 128

    def pick(rows, cols):
        return jnp.where(inner, own_ref[rows, cols].astype(f32), come_ref[rows, cols].astype(f32))

    second_ref[...] = pick(slice(None), slice(0, channels))
    top = pick(slice(0, half), slice(channels, channels + SIDE))
    bias = top[:, :128] + top[:, 128:]
    for i in range(lanes):
        bias_ref[:, i * 128 : (i + 1) * 128] = bias[i : i + 1]
    low = pick(slice(half, hid_count), slice(channels, channels + SIDE))
    first_ref[...] = (low[:, :128] + low[:, 128:])[:, :hid_count]


def few_shards_body(
    x_one, x_two, values, grad_out, first_weight, second_weight, skip_bias, decay_rate
):
    rows, channels = x_one.shape
    shards = lax.axis_size("ctx")
    feat_count, hid_count = first_weight.shape
    seq_len = rows * shards
    double = 2 * rows
    width = min(512, channels)
    blocks = channels // width
    rank = lax.axis_index("ctx").astype(jnp.int32).reshape(1)
    front, back = block_tables(rows)
    feats = feature_table(seq_len)
    featt = np.ascontiguousarray(feats.T)
    skip_row = skip_bias.reshape(1, channels)
    rate_row = decay_rate.reshape(1, channels)
    smem = pl.BlockSpec(memory_space=pltpu.SMEM)

    def whole(*dims):
        return pl.BlockSpec(dims, lambda i: (0,) * len(dims))

    def strip(*lead):
        return pl.BlockSpec(lead + (width,), lambda i: (0,) * len(lead) + (i,))

    def shape(*dims, dtype=f32):
        return jax.ShapeDtypeStruct(dims, dtype)

    def call(kernel, name, units, size, **how):
        how.setdefault("grid", (blocks,))
        return pl.pallas_call(
            kernel,
            compiler_params=pltpu.CompilerParams(vmem_limit_bytes=64 * 1024 * 1024),
            cost_estimate=pl.CostEstimate(
                flops=2 * units * double * double * channels, bytes_accessed=size * rows * channels, transcendentals=0
            ),
            name=name,
            **how,
        )

    def move(array, pairs):
        return lax.ppermute(array, "ctx", pairs)

    up = [(i, i + 1) for i in range(shards - 1)]
    down = [(i + 1, i) for i in range(shards - 1)]
    inward = [(0, 1), (shards - 1, shards - 2)]
    outward = [(1, 0), (shards - 2, shards - 1)]
    across = [(1, 2), (2, 1)]
    block_like = strip(rows)
    pay_shape = (hid_count, channels + SIDE)

    x0, c0, bias = call(
        products_kernel, "products", 0, 12,
        in_specs=[block_like] * 4,
        out_specs=[block_like, block_like, strip(1)],
        out_shape=[shape(rows, channels, dtype=bf16)] * 2 + [shape(1, channels)],
    )(x_one, x_two, values, grad_out)
    x1 = move(x0, up)
    c1 = move(c0, down)

    spec, own, trans, slope = call(
        functools.partial(filters_kernel, rows, shards), "filters", 16, 40,
        in_specs=[
            whole(seq_len, feat_count), whole(feat_count, seq_len), whole(feat_count, hid_count), strip(hid_count),
            strip(1), whole(double, double), whole(double, double), block_like, block_like, whole(1, channels),
        ],
        out_specs=[
            strip(shards, double), whole(*pay_shape), whole(2 * hid_count, seq_len), whole(seq_len, hid_count),
        ],
        out_shape=[
            shape(shards, double, channels), shape(*pay_shape), shape(2 * hid_count, seq_len, dtype=bf16),
            shape(seq_len, hid_count),
        ],
        scratch_shapes=[pltpu.VMEM((seq_len, 3 * hid_count), bf16), pltpu.VMEM((rows, hid_count), f32)],
    )(feats, featt, first_weight, second_weight, rate_row, front, back, x0, c0, bias)
    come = move(own, inward)

    x2 = move(x1, [(1, 2)])
    c2 = move(c1, [(2, 1)])
    conv, corr, ahead, sums, first = call(
        functools.partial(near_kernel, rows, shards), "near_blocks", 20, 50,
        in_specs=[smem] + [block_like] * 4 + [
            strip(shards - 1, double), strip(hid_count), strip(1), whole(double, double), whole(double, double),
            whole(2 * hid_count, seq_len), whole(feat_count, seq_len), whole(seq_len, hid_count), strip(hid_count),
        ],
        out_specs=[block_like] * 3 + [strip(hid_count), whole(feat_count, hid_count)],
        out_shape=[shape(rows, channels)] * 3 + [shape(hid_count, channels), shape(feat_count, hid_count)],
        scratch_shapes=[
            pltpu.VMEM((4, double, width), f32),
            pltpu.VMEM((3, double, width), bf16),
            pltpu.VMEM((shards - 1, double, width), bf16),
            pltpu.VMEM((shards - 1, double, width), bf16),
            pltpu.VMEM(((shards - 1) * rows, hid_count), f32),
        ],
    )(rank, x0, c0, x1, c1, spec, second_weight, rate_row, front, back, trans, featt, slope, own)

    part, late = call(
        functools.partial(far_kernel, rows), "far_block", 4, 30,
        in_specs=[smem, block_like, block_like, pl.BlockSpec((2, double, width), lambda i: (1, 0, i)),
                  whole(double, double), whole(double, double), block_like],
        out_specs=[block_like] * 2,
        out_shape=[shape(rows, channels, dtype=bf16), shape(rows, channels)],
    )(rank, x2, c2, spec, front, back, ahead)
    part_come = move(part, outward)

    side_block = (channels // SIDE) if channels % SIDE == 0 else 0
    pay, first = call(
        functools.partial(last_kernel, rows, shards, channels), "last_pair", 5, 10,
        in_specs=[smem] + [block_like] * 4 + [
            strip(hid_count), strip(1), whole(double, double), whole(double, double), whole(2 * hid_count, seq_len),
            whole(feat_count, seq_len), whole(seq_len, hid_count), strip(hid_count), whole(feat_count, hid_count),
            pl.BlockSpec((hid_count, SIDE), lambda i: (0, side_block)), whole(*pay_shape),
            pl.BlockSpec(memory_space=pl.ANY),
        ],
        out_specs=[whole(*pay_shape), whole(feat_count, hid_count)],
        out_shape=[shape(*pay_shape, dtype=bf16), shape(feat_count, hid_count)],
        scratch_shapes=[pltpu.VMEM((2 * rows, hid_count), f32)],
    )(
        rank, x1, c1, x2, c2, second_weight, rate_row, front, back, trans, featt, slope, sums, first, own, come,
        late,
    )
    pay_come = move(pay, across)
    group = lax.axis_size(("ch", "sub"))
    bit = 1
    while bit < group:
        first = first + lax.ppermute(first, ("ch", "sub"), [(i, i ^ bit) for i in range(group)])
        bit *= 2
    first_come = move(first, across)

    vmem = pl.BlockSpec(memory_space=pltpu.VMEM)
    total = call(
        functools.partial(total_kernel, channels), "total", 0, 4,
        grid=(),
        in_specs=[vmem] * 4,
        out_specs=vmem,
        out_shape=shape(*pay_shape, dtype=bf16),
    )(pay, pay_come, first, first_come)
    total_come = move(total, outward)

    grad_one, grad_two, grad_value = call(
        functools.partial(gates_kernel, shards), "gates", 0, 30,
        in_specs=[smem] + [block_like] * 4 + [strip(1)] + [block_like] * 4,
        out_specs=[block_like] * 3,
        out_shape=[shape(rows, channels, dtype=bf16)] * 3,
    )(rank, x_one, x_two, values, grad_out, skip_row, conv, corr, late, part_come)

    grad_second, grad_first, grad_bias = call(
        functools.partial(finish_kernel, channels, shards), "finish", 0, 4,
        grid=(),
        in_specs=[smem, vmem, vmem],
        out_specs=[vmem] * 3,
        out_shape=[shape(hid_count, channels), shape(feat_count, hid_count), shape(1, channels)],
    )(rank, total, total_come)
    return (grad_one, grad_two, grad_value, grad_first, grad_second, grad_bias.reshape(channels))


def solution(mesh):
    in_specs = (
        P(("parts", "ctx"), ("ch", "sub")),
        P(("parts", "ctx"), ("ch", "sub")),
        P(("parts", "ctx"), ("ch", "sub")),
        P(("parts", "ctx"), ("ch", "sub")),
        P(),
        P(None, ("ch", "sub")),
        P(("ch", "sub")),
        P(("ch", "sub")),
    )
    out_specs = (
        P(("parts", "ctx"), ("ch", "sub")),
        P(("parts", "ctx"), ("ch", "sub")),
        P(("parts", "ctx"), ("ch", "sub")),
        P("parts", None),
        P("parts", ("ch", "sub")),
        P(("parts", "ch", "sub")),
    )
    body = few_shards_body if mesh.shape["ctx"] == 4 else many_shards_body
    return jax.shard_map(body, mesh=mesh, in_specs=in_specs, out_specs=out_specs, check_vma=False)
```

```python
import functools
import math

import jax
import jax.numpy as jnp
import numpy as np
from jax import lax
from jax.experimental import pallas as pl
from jax.experimental.pallas import tpu as pltpu
from jax.sharding import PartitionSpec as P

band_steps = (1763, 1201, 811, 547, 367, 251, 167, 113, 79, 53, 37, 23, 17, 11, 7, 3)
highest = lax.Precision.HIGHEST
f32 = jnp.float32
bf16 = jnp.bfloat16


def features(positions):
    multiplier = jnp.array(band_steps, dtype=jnp.int32)
    phase = positions[:, None] * multiplier[None, :] % 4096
    angle = phase.astype(jnp.float32) * (2.0 * math.pi / 4096.0)
    return jnp.concatenate([jnp.cos(angle), jnp.sin(angle)], axis=1)


def tables(out_count, in_count, modulus, sign_value):
    row_index = lax.broadcasted_iota(jnp.int32, (out_count, in_count), 0)
    col_index = lax.broadcasted_iota(jnp.int32, (out_count, in_count), 1)
    angle = (row_index * col_index % modulus).astype(jnp.float32) * (2.0 * math.pi / modulus)
    return (jnp.cos(angle), sign_value * jnp.sin(angle))


def twiddle(spec_re, spec_im, freq_count, span, modulus, sign_value):
    freq_index = lax.broadcasted_iota(jnp.int32, (freq_count, span), 0)
    pos_index = lax.broadcasted_iota(jnp.int32, (freq_count, span), 1)
    angle = (freq_index * pos_index % modulus).astype(jnp.float32) * (2.0 * math.pi / modulus)
    factor_re = jnp.cos(angle)[None, None, :, :]
    factor_im = (sign_value * jnp.sin(angle))[None, None, :, :]
    return (spec_re * factor_re - spec_im * factor_im, spec_re * factor_im + spec_im * factor_re)


def contract(kernel, array):
    return jnp.einsum(
        "lj,mckj->mckl", kernel, array, precision=highest, preferred_element_type=jnp.float32
    )


def along_positions(spec_re, spec_im, kernel_re, kernel_im):
    return (
        contract(kernel_re, spec_re) - contract(kernel_im, spec_im),
        contract(kernel_re, spec_im) + contract(kernel_im, spec_re),
    )


def many_shards_body(
    x_one, x_two, values, grad_out, first_weight, second_weight, skip_bias, decay_rate
):
    row_count, chan_count = x_one.shape
    shards = lax.axis_size("ctx")
    rank = lax.axis_index("ctx")
    seq_len = row_count * shards
    total = 2 * seq_len
    narrow = chan_count // shards
    chan_weight = lax.dynamic_slice_in_dim(second_weight, rank * narrow, narrow, 1)
    chan_rate = lax.dynamic_slice_in_dim(decay_rate, rank * narrow, narrow, 0)
    source = x_one.astype(jnp.float32) * values.astype(jnp.float32)
    cotan = grad_out.astype(jnp.float32) * x_two.astype(jnp.float32)
    spread = lax.all_to_all(
        jnp.stack([source.T, cotan.T])[:, :, None, :],
        "ctx",
        split_axis=1,
        concat_axis=2,
        tiled=True,
    )
    far_source = spread[0]
    far_cotan = spread[1]
    positions = jnp.arange(seq_len, dtype=jnp.int32)
    feats = features(positions)
    pre_act = jnp.dot(feats, first_weight, precision=highest, preferred_element_type=jnp.float32)
    hidden = jnp.sin(pre_act)
    envelope = jnp.exp(-chan_rate[:, None] * positions.astype(jnp.float32)[None, :]) * float(
        seq_len
    ) ** (-0.5)
    filt = (
        jnp.einsum(
            "th,hc->ct", hidden, chan_weight, precision=highest, preferred_element_type=jnp.float32
        )
        * envelope
    )
    filt_blocks = filt.reshape(narrow, shards, row_count)
    fields = jnp.stack([far_source, far_cotan])

    def first_section(kernel):
        field_part = jnp.einsum(
            "kn,mcnj->mckj", kernel, fields, precision=highest, preferred_element_type=jnp.float32
        )
        filter_part = jnp.einsum(
            "kn,cnj->ckj",
            kernel,
            filt_blocks,
            precision=highest,
            preferred_element_type=jnp.float32,
        )
        return jnp.concatenate([field_part, filter_part[None]], axis=0)

    first_re, first_im = tables(2 * shards, shards, 2 * shards, -1.0)
    spec_re, spec_im = (first_section(first_re), first_section(first_im))
    spec_re, spec_im = twiddle(spec_re, spec_im, 2 * shards, row_count, total, -1.0)
    fwd_re, fwd_im = tables(row_count, row_count, row_count, -1.0)
    spec_re, spec_im = along_positions(spec_re, spec_im, fwd_re, fwd_im)
    source_re, source_im = (spec_re[0], spec_im[0])
    cotan_re, cotan_im = (spec_re[1], spec_im[1])
    filter_re, filter_im = (spec_re[2], spec_im[2])
    prod_re = jnp.stack(
        [
            source_re * filter_re - source_im * filter_im,
            cotan_re * filter_re + cotan_im * filter_im,
            cotan_re * source_re + cotan_im * source_im,
        ]
    )
    prod_im = jnp.stack(
        [
            source_re * filter_im + source_im * filter_re,
            cotan_im * filter_re - cotan_re * filter_im,
            cotan_im * source_re - cotan_re * source_im,
        ]
    )
    back_re, back_im = tables(row_count, row_count, row_count, 1.0)
    prod_re, prod_im = along_positions(prod_re, prod_im, back_re, back_im)
    prod_re, prod_im = twiddle(prod_re, prod_im, 2 * shards, row_count, total, 1.0)
    last_re, last_im = tables(shards, 2 * shards, 2 * shards, 1.0)
    field_out = jnp.einsum(
        "nk,mckj->mcnj", last_re, prod_re[:2], precision=highest, preferred_element_type=jnp.float32
    ) - jnp.einsum(
        "nk,mckj->mcnj", last_im, prod_im[:2], precision=highest, preferred_element_type=jnp.float32
    )
    field_out = field_out * (1.0 / total)
    filt_grad = jnp.einsum(
        "nk,ckj->cnj", last_re, prod_re[2], precision=highest, preferred_element_type=jnp.float32
    ) - jnp.einsum(
        "nk,ckj->cnj", last_im, prod_im[2], precision=highest, preferred_element_type=jnp.float32
    )
    filt_grad = (filt_grad * (1.0 / total)).reshape(narrow, seq_len)
    modulated = filt_grad * envelope
    weight_part = jnp.einsum(
        "th,ct->hc", hidden, modulated, precision=highest, preferred_element_type=jnp.float32
    )
    hidden_grad = jnp.einsum(
        "ct,hc->th", modulated, chan_weight, precision=highest, preferred_element_type=jnp.float32
    )
    first_part = jnp.dot(
        feats.T,
        hidden_grad * jnp.cos(pre_act),
        precision=highest,
        preferred_element_type=jnp.float32,
    )
    grad_first = lax.psum(first_part, ("ctx", "ch", "sub"))
    returned = lax.all_to_all(
        field_out.astype(jnp.bfloat16), "ctx", split_axis=2, concat_axis=1, tiled=True
    ).astype(field_out.dtype)
    conv_part = returned[0, :, 0, :].T
    corr_part = returned[1, :, 0, :].T
    grad_two = (grad_out.astype(jnp.float32) * (conv_part + skip_bias[None, :] * source)).astype(
        jnp.bfloat16
    )
    grad_mid = corr_part + skip_bias[None, :] * cotan
    grad_one = (grad_mid * values.astype(jnp.float32)).astype(jnp.bfloat16)
    grad_value = (grad_mid * x_one.astype(jnp.float32)).astype(jnp.bfloat16)
    grad_bias = lax.psum(jnp.sum(source * cotan, axis=0), "ctx")
    grad_second = lax.all_gather(weight_part, "ctx", axis=1, tiled=True)
    return (grad_one, grad_two, grad_value, grad_first, grad_second, grad_bias)


STEP = 16
SIDE = 256


def halves(array):
    array = np.asarray(array, np.float32)
    high = array.astype(bf16)
    low = (array - high.astype(np.float32)).astype(bf16)
    return high, low


def block_tables(rows):
    freq = np.concatenate([np.arange(0, rows, 2), np.arange(1, rows, 2)])
    phase = (2 * freq + 1)[:, None] * np.arange(rows)[None, :] % (4 * rows)
    angle = phase * (2.0 * np.pi / (4 * rows))
    forward = np.concatenate([np.cos(angle), -np.sin(angle)], axis=0)
    front = np.ascontiguousarray(np.concatenate(halves(forward), axis=1))
    back = np.ascontiguousarray(np.concatenate(halves(forward.T / rows), axis=0))
    return front, back


def feature_table(seq_len):
    phase = np.arange(seq_len)[:, None] * np.array(band_steps)[None, :] % 4096
    angle = phase * (2.0 * np.pi / 4096.0)
    return np.concatenate([np.cos(angle), np.sin(angle)], axis=1).astype(np.float32)


def split(array):
    high = array.astype(bf16)
    return high, (array - high.astype(f32)).astype(bf16)


def dot(left, right):
    return jnp.dot(left, right, preferred_element_type=f32)


def exact_dot(left, right):
    return jnp.dot(left, right, precision=highest, preferred_element_type=f32)


def dot_across(left, right):
    return lax.dot_general(left, right, (((1,), (1,)), ((), ())), preferred_element_type=f32)


def decay(rate, rows, scale):
    place = lax.broadcasted_iota(jnp.int32, (rows, rate.shape[1]), 0)
    return jnp.exp(-place.astype(f32) * rate) * scale


def times(a, b):
    return a[0] * b[0] - a[1] * b[1], a[0] * b[1] + a[1] * b[0]


def conj_times(a, b):
    return a[0] * b[0] + a[1] * b[1], a[0] * b[1] - a[1] * b[0]


def plus(a, b):
    return a[0] + b[0], a[1] + b[1]


def scaled(a, factor):
    return a[0] * factor, a[1] * factor


def choose(condition, a, b):
    return jnp.where(condition, a[0], b[0]), jnp.where(condition, a[1], b[1])


def turned(a, sign):
    return (a[1], -a[0]) if sign > 0 else (-a[1], a[0])


def forward(front_ref, block):
    return dot(front_ref[...], jnp.concatenate([block, block], axis=0))


def backward(back_ref, high, low=None):
    both = dot(back_ref[...], high)
    rows = both.shape[0] // 2
    out = both[:rows] + both[rows:]
    return out if low is None else out + dot(back_ref[:rows], low)


def row_groups(rows):
    for step in range(rows // STEP):
        sign = 1 if step * STEP < rows // 2 else -1
        yield slice(step * STEP, (step + 1) * STEP), slice(rows + step * STEP, rows + (step + 1) * STEP), sign


def weight_sums(trans, m_high, m_low):
    both = dot(trans, m_high)
    count = both.shape[0] // 2
    return both[:count] + both[count:] + dot(trans[:count], m_low)


def hidden_sums(m_high, m_low, w_high, w_low):
    left = jnp.concatenate([m_high, m_high, m_low], axis=1)
    right = jnp.concatenate([w_high, w_low, w_high], axis=1)
    return dot_across(left, right)


def add_up(ref, value, block):
    @pl.when(block == 0)
    def _():
        ref[...] = value

    @pl.when(block > 0)
    def _():
        ref[...] += value


def products_kernel(rank_ref, one_ref, two_ref, val_ref, out_ref, source_ref, cotan_ref, far_ref, bias_ref):
    source = one_ref[...].astype(f32) * val_ref[...].astype(f32)
    cotan = out_ref[...].astype(f32) * two_ref[...].astype(f32)
    source_ref[...] = source.astype(bf16)
    cotan_ref[...] = cotan.astype(bf16)
    far_ref[...] = jnp.where(rank_ref[0] == 0, source, cotan).astype(bf16)
    add_up(bias_ref, jnp.sum(source * cotan, axis=0, keepdims=True), pl.program_id(0))


def sin_cos(angle):
    turns = jnp.floor(angle * (2.0 / math.pi) + 0.5)
    rest = ((angle - turns * 1.5703125) - turns * 4.837512969970703e-4) - turns * 7.54978995489188e-8
    square = rest * rest
    sine = rest + rest * square * (
        -1.6666654611e-1 + square * (8.3321608736e-3 + square * -1.9515295891e-4)
    )
    cosine = 1.0 - 0.5 * square + square * square * (
        4.166664568298827e-2 + square * (-1.388731625493765e-3 + square * 2.443315711809948e-5)
    )
    quarter = turns.astype(jnp.int32)
    odd = (quarter & 1) == 1
    sin_sign = jnp.where((quarter & 2) == 2, -1.0, 1.0).astype(f32)
    cos_sign = jnp.where(((quarter + 1) & 2) == 2, -1.0, 1.0).astype(f32)
    return jnp.where(odd, cosine, sine) * sin_sign, jnp.where(odd, sine, cosine) * cos_sign


def filters_kernel(
    rows, shards, feats_ref, featt_ref, first_ref, weight_ref, rate_ref, front_ref, back_ref, source_ref, cotan_ref,
    bias_ref, spec_ref, sums_ref, send_ref, trans_ref, slope_ref, hid_ref, acc_ref,
):
    block = pl.program_id(0)
    last = pl.num_programs(0) - 1
    hid_count, width = weight_ref.shape
    channels = bias_ref.shape[1]
    scale = float(rows * shards) ** -0.5

    @pl.when(block == 0)
    def _():
        pre_act = exact_dot(feats_ref[...], first_ref[...])
        hidden, slope = sin_cos(pre_act)
        slope_ref[...] = slope
        high, low = split(hidden)
        hid_ref[...] = jnp.concatenate([high, high, low], axis=1)
        turned_over = jnp.concatenate([hidden, slope], axis=1).T[:hid_count]
        trans_ref[...] = jnp.concatenate(split(turned_over), axis=0)

    w_high, w_low = split(weight_ref[...])
    stacked = jnp.concatenate([w_high, w_low, w_high], axis=0)
    rate = rate_ref[...]
    env = decay(rate, rows, scale)
    before = None
    for lag in range(shards):
        part = dot(hid_ref[lag * rows : (lag + 1) * rows, :], stacked)
        part = part * (env * jnp.exp(rate * (-float(lag * rows))))
        f_high, f_low = split(part)
        now = forward(front_ref, f_high) + dot(front_ref[:, :rows], f_low)
        for re, im, sign in row_groups(rows):
            here = (now[re], now[im])
            if before is not None:
                here = plus(here, turned((before[re], before[im]), -sign))
            spec_ref[lag, re, :] = here[0].astype(bf16)
            spec_ref[lag, im, :] = here[1].astype(bf16)
        before = now

    x0 = forward(front_ref, source_ref[...])
    c0 = forward(front_ref, cotan_ref[...])
    pair = conj_times((x0[:rows], x0[rows:]), (c0[:rows], c0[rows:]))
    high, low = split(jnp.concatenate(pair, axis=0))
    m_high, m_low = split(backward(back_ref, high, low) * env)
    sums = weight_sums(trans_ref[:, :rows], m_high, m_low)
    sums_ref[...] = sums
    send_ref[:, pl.ds(pl.multiple_of(block * width, width), width)] = sums.astype(bf16)
    add_up(acc_ref, hidden_sums(m_high, m_low, w_high, w_low), block)

    @pl.when(block == last)
    def _():
        first = exact_dot(featt_ref[:, :rows], acc_ref[...] * slope_ref[:rows, :])
        put_side(send_ref, channels, fold(bias_ref[...]), first)


def fold(bias):
    return jnp.concatenate([bias[:, i * 128 : (i + 1) * 128] for i in range(bias.shape[1] // 128)], axis=0)


def put_side(pay_ref, channels, bias, first):
    half = pay_ref.shape[0] // 2
    pay_ref[:, channels:] = jnp.zeros((2 * half, SIDE), bf16)
    for start, bias_part, first_part in zip((0, 128), split(bias), split(first)):
        at = channels + start
        pay_ref[: bias.shape[0], at : at + 128] = bias_part
        pay_ref[half:, at : at + first.shape[1]] = first_part


def get_side(pay, channels, lanes, hid_count):
    half = pay.shape[0] // 2
    side = pay[:, channels : channels + 128].astype(f32) + pay[:, channels + 128 :].astype(f32)
    return side[:lanes], side[half:, :hid_count]


def near_kernel(
    rows, shards, rank_ref, x0_ref, c0_ref, x1_ref, c1_ref, spec_ref, weight_ref, rate_ref, front_ref, back_ref,
    trans_ref, featt_ref, slope_ref, own_ref, conv_ref, corr_ref, ahead_ref, sums_ref, first_ref, fields, fast, high_ref,
    low_ref, acc_ref,
):
    block = pl.program_id(0)
    last = pl.num_programs(0) - 1
    rank = rank_ref[0]
    count = shards - 1
    lower = rank == 1
    upper = jnp.where(rank == 2, 1.0, 0.0).astype(f32)
    below_top = jnp.where(rank == shards - 1, 0.0, 1.0).astype(f32)
    side = jnp.where(rank == 2, 1.0, -1.0).astype(f32)
    for index, ref in enumerate((x0_ref, c0_ref, x1_ref, c1_ref)):
        fields[index] = forward(front_ref, ref[...])
    for re, im, sign in row_groups(rows):
        x0, c0, x1, c1 = ((fields[i, re, :], fields[i, im, :]) for i in range(4))
        w0, w1, w2 = ((spec_ref[i, re, :].astype(f32), spec_ref[i, im, :].astype(f32)) for i in range(3))
        ahead = times((w2[0], w2[1] * side), choose(lower, c1, x1))
        for index, value in enumerate(
            (plus(times(w0, x0), times(w1, x1)), plus(conj_times(w0, c0), conj_times(w1, c1)), ahead)
        ):
            fast[index, re, :] = value[0].astype(bf16)
            fast[index, im, :] = value[1].astype(bf16)
        one = plus(scaled(conj_times(x1, c0), below_top), scaled(conj_times(x0, c1), upper))
        two = conj_times(x1, c1)
        for index, value in enumerate((turned(one, sign), plus(one, turned(two, sign)), two)):
            for part, where in zip(value, (re, im)):
                high_ref[index, where, :], low_ref[index, where, :] = split(part)
    conv_ref[...] = backward(back_ref, fast[0])
    corr_ref[...] = backward(back_ref, fast[1])
    ahead_ref[...] = backward(back_ref, fast[2])
    rate = rate_ref[...]
    env = decay(rate, rows, float(rows * shards) ** -0.5)
    parts = []
    for lag in range(count):
        grad = backward(back_ref, high_ref[lag], low_ref[lag])
        parts.append(split(grad * (env * jnp.exp(rate * (-float(lag * rows))))))
    m_high = jnp.concatenate([p[0] for p in parts], axis=0)
    m_low = jnp.concatenate([p[1] for p in parts], axis=0)
    sums_ref[...] = own_ref[...] + weight_sums(trans_ref[:, : count * rows], m_high, m_low)
    w_high, w_low = split(weight_ref[...])
    add_up(acc_ref, hidden_sums(m_high, m_low, w_high, w_low), block)

    @pl.when(block == last)
    def _():
        first_ref[...] = exact_dot(
            featt_ref[:, : count * rows], acc_ref[...] * slope_ref[: count * rows, :]
        )


def far_kernel(rows, rank_ref, far_ref, spec_ref, front_ref, back_ref, ahead_ref, part_ref, late_ref):
    side = jnp.where(rank_ref[0] == 2, 1.0, -1.0).astype(f32)
    far = forward(front_ref, far_ref[...])
    far = (far[:rows], far[rows:])
    w2, w3 = ((spec_ref[i, :rows, :].astype(f32), spec_ref[i, rows:, :].astype(f32) * side) for i in range(2))
    ahead = jnp.concatenate(times(w3, far), axis=0).astype(bf16)
    part_ref[...] = (ahead_ref[...] + backward(back_ref, ahead)).astype(bf16)
    late = jnp.concatenate(times(w2, far), axis=0).astype(bf16)
    late_ref[...] = backward(back_ref, late)


def last_kernel(
    rows, shards, channels, rank_ref, x1_ref, c1_ref, far_ref, weight_ref, rate_ref, front_ref, back_ref,
    trans_ref, featt_ref, slope_ref, sums_ref, first_ref, own_ref, bias_ref, in_ref, after_ref, pay_ref, total_ref,
    acc_ref,
):
    del after_ref
    block = pl.program_id(0)
    blocks = pl.num_programs(0)
    hid_count, width = weight_ref.shape
    lower = rank_ref[0] == 1
    start = pl.multiple_of(block * width, width)
    here = sums_ref[...] + in_ref[:, pl.ds(start, width)].astype(f32)
    mine = (block < blocks // 2) == lower

    @pl.when(block == 0)
    def _():
        acc_ref[...] = jnp.zeros_like(acc_ref)

    @pl.when(mine)
    def _():
        sign = jnp.where(lower, 1.0, -1.0).astype(f32)
        near = forward(front_ref, jnp.where(lower, x1_ref[...], c1_ref[...]))
        far = forward(front_ref, far_ref[...])
        three = conj_times((near[:rows], near[rows:]), (far[:rows], far[rows:]))
        three = (three[0], three[1] * sign)
        half = rows // 2
        two = jnp.concatenate([three[1][:half], -three[1][half:], -three[0][:half], three[0][half:]], axis=0)
        rate = rate_ref[...]
        env = decay(rate, rows, float(rows * shards) ** -0.5)
        parts = []
        for lag, value in ((shards - 2, two), (shards - 1, jnp.concatenate(three, axis=0))):
            grad = backward(back_ref, *split(value))
            parts.append(split(grad * (env * jnp.exp(rate * (-float(lag * rows))))))
        m_high = jnp.concatenate([p[0] for p in parts], axis=0)
        m_low = jnp.concatenate([p[1] for p in parts], axis=0)
        trans = trans_ref[:, (shards - 2) * rows :]
        pay_ref[:, pl.ds(start, width)] = (here + weight_sums(trans, m_high, m_low)).astype(bf16)
        w_high, w_low = split(weight_ref[...])
        acc_ref[...] += hidden_sums(m_high, m_low, w_high, w_low)

    @pl.when(jnp.logical_not(mine))
    def _():
        pay_ref[:, pl.ds(start, width)] = here.astype(bf16)

    @pl.when(block == blocks - 1)
    def _():
        first = exact_dot(
            featt_ref[:, (shards - 2) * rows :], acc_ref[...] * slope_ref[(shards - 2) * rows :, :]
        )
        lanes = channels // 128
        own_first = get_side(own_ref[...], 0, lanes, hid_count)[1]
        in_bias, in_first = get_side(in_ref[...], channels, lanes, hid_count)
        first = first + first_ref[...] + own_first + in_first
        put_side(pay_ref, channels, fold(bias_ref[...]) + in_bias, first)
        total_ref[...] = first


def total_kernel(channels, own_ref, come_ref, first_ref, far_first_ref, pay_ref):
    hid_count = first_ref.shape[1]
    lanes = channels // 128
    pay_ref[:, :channels] = (own_ref[:, :channels].astype(f32) + come_ref[:, :channels].astype(f32)).astype(bf16)
    bias = get_side(own_ref[...], channels, lanes, hid_count)[0] + get_side(come_ref[...], channels, lanes, hid_count)[0]
    put_side(pay_ref, channels, bias, first_ref[...] + far_first_ref[...])


def gates_kernel(
    shards, rank_ref, one_ref, two_ref, val_ref, out_ref, skip_ref, conv_ref, corr_ref, late_ref, part_ref,
    grad_one_ref, grad_two_ref, grad_value_ref,
):
    rank = rank_ref[0]

    def mask(wanted):
        return jnp.where(rank == wanted, 1.0, 0.0).astype(f32)

    part = part_ref[...].astype(f32)
    late = late_ref[...]
    one = one_ref[...].astype(f32)
    val = val_ref[...].astype(f32)
    out = out_ref[...].astype(f32)
    skip = skip_ref[...]
    conv = conv_ref[...] + late * mask(2) + part * mask(shards - 1)
    corr = corr_ref[...] + late * mask(1) + part * mask(0)
    grad_two_ref[...] = (out * (conv + skip * (one * val))).astype(bf16)
    mid = corr + skip * (out * two_ref[...].astype(f32))
    grad_one_ref[...] = (mid * val).astype(bf16)
    grad_value_ref[...] = (mid * one).astype(bf16)


def finish_kernel(channels, shards, rank_ref, own_ref, come_ref, second_ref, first_ref, bias_ref):
    rank = rank_ref[0]
    inner = jnp.logical_and(rank > 0, rank < shards - 1)
    hid_count = second_ref.shape[0]
    lanes = channels // 128
    picked = jnp.where(inner, own_ref[...], come_ref[...])
    second_ref[...] = picked[:, :channels].astype(f32)
    bias, first = get_side(picked, channels, lanes, hid_count)
    for i in range(lanes):
        bias_ref[:, i * 128 : (i + 1) * 128] = bias[i : i + 1]
    first_ref[...] = first


def few_shards_body(
    x_one, x_two, values, grad_out, first_weight, second_weight, skip_bias, decay_rate
):
    rows, channels = x_one.shape
    shards = lax.axis_size("ctx")
    feat_count, hid_count = first_weight.shape
    seq_len = rows * shards
    double = 2 * rows
    width = min(512, channels)
    blocks = channels // width
    rank = lax.axis_index("ctx").astype(jnp.int32).reshape(1)
    front, back = block_tables(rows)
    feats = feature_table(seq_len)
    featt = np.ascontiguousarray(feats.T)
    skip_row = skip_bias.reshape(1, channels)
    rate_row = decay_rate.reshape(1, channels)
    smem = pl.BlockSpec(memory_space=pltpu.SMEM)

    def whole(*dims):
        return pl.BlockSpec(dims, lambda i: (0,) * len(dims))

    def strip(*lead):
        return pl.BlockSpec(lead + (width,), lambda i: (0,) * len(lead) + (i,))

    def shape(*dims, dtype=f32):
        return jax.ShapeDtypeStruct(dims, dtype)

    def call(kernel, name, units, size, **how):
        how.setdefault("grid", (blocks,))
        return pl.pallas_call(
            kernel,
            compiler_params=pltpu.CompilerParams(vmem_limit_bytes=64 * 1024 * 1024),
            cost_estimate=pl.CostEstimate(
                flops=2 * units * double * double * channels, bytes_accessed=size * rows * channels, transcendentals=0
            ),
            name=name,
            **how,
        )

    def move(array, pairs):
        return lax.ppermute(array, "ctx", pairs)

    up = [(i, i + 1) for i in range(shards - 1)]
    down = [(i + 1, i) for i in range(shards - 1)]
    inward = [(0, 1), (shards - 1, shards - 2)]
    outward = [(1, 0), (shards - 2, shards - 1)]
    across = [(1, 2), (2, 1)]
    block_like = strip(rows)
    pay_shape = (hid_count, channels + SIDE)

    row_step = max(rows // 4, 16)
    gate_rows = pl.BlockSpec((row_step, channels), lambda i: (i, 0))
    x0, c0, edge, bias = call(
        products_kernel, "products", 0, 12,
        grid=(rows // row_step,),
        in_specs=[smem] + [gate_rows] * 4,
        out_specs=[gate_rows] * 3 + [whole(1, channels)],
        out_shape=[shape(rows, channels, dtype=bf16)] * 3 + [shape(1, channels)],
    )(rank, x_one, x_two, values, grad_out)
    x1 = move(x0, up)
    c1 = move(c0, down)
    far = move(edge, [(0, 2), (shards - 1, shards - 3)])

    spec, own, send, trans, slope = call(
        functools.partial(filters_kernel, rows, shards), "filters", 16, 40,
        in_specs=[
            whole(seq_len, feat_count), whole(feat_count, seq_len), whole(feat_count, hid_count), strip(hid_count),
            strip(1), whole(double, double), whole(double, double), block_like, block_like, whole(1, channels),
        ],
        out_specs=[
            strip(shards, double), strip(hid_count), whole(*pay_shape), whole(2 * hid_count, seq_len),
            whole(seq_len, hid_count),
        ],
        out_shape=[
            shape(shards, double, channels, dtype=bf16), shape(hid_count, channels), shape(*pay_shape, dtype=bf16),
            shape(2 * hid_count, seq_len, dtype=bf16), shape(seq_len, hid_count),
        ],
        scratch_shapes=[pltpu.VMEM((seq_len, 3 * hid_count), bf16), pltpu.VMEM((rows, hid_count), f32)],
    )(feats, featt, first_weight, second_weight, rate_row, front, back, x0, c0, bias)
    come = move(send, inward)

    conv, corr, ahead, sums, first = call(
        functools.partial(near_kernel, rows, shards), "near_blocks", 20, 50,
        in_specs=[smem] + [block_like] * 4 + [
            strip(shards - 1, double), strip(hid_count), strip(1), whole(double, double), whole(double, double),
            whole(2 * hid_count, seq_len), whole(feat_count, seq_len), whole(seq_len, hid_count), strip(hid_count),
        ],
        out_specs=[block_like] * 3 + [strip(hid_count), whole(feat_count, hid_count)],
        out_shape=[shape(rows, channels)] * 3 + [shape(hid_count, channels), shape(feat_count, hid_count)],
        scratch_shapes=[
            pltpu.VMEM((4, double, width), f32),
            pltpu.VMEM((3, double, width), bf16),
            pltpu.VMEM((shards - 1, double, width), bf16),
            pltpu.VMEM((shards - 1, double, width), bf16),
            pltpu.VMEM(((shards - 1) * rows, hid_count), f32),
        ],
    )(rank, x0, c0, x1, c1, spec, second_weight, rate_row, front, back, trans, featt, slope, own)

    part, late = call(
        functools.partial(far_kernel, rows), "far_block", 4, 30,
        in_specs=[smem, block_like, pl.BlockSpec((2, double, width), lambda i: (1, 0, i)),
                  whole(double, double), whole(double, double), block_like],
        out_specs=[block_like] * 2,
        out_shape=[shape(rows, channels, dtype=bf16), shape(rows, channels)],
    )(rank, far, spec, front, back, ahead)
    part_come = move(part, outward)

    pay, first = call(
        functools.partial(last_kernel, rows, shards, channels), "last_pair", 0, 1,
        in_specs=[smem] + [block_like] * 3 + [
            strip(hid_count), strip(1), whole(double, double), whole(double, double), whole(2 * hid_count, seq_len),
            whole(feat_count, seq_len), whole(seq_len, hid_count), strip(hid_count), whole(feat_count, hid_count),
            pl.BlockSpec((hid_count, SIDE), lambda i: (0, channels // SIDE)), whole(1, channels), whole(*pay_shape),
            pl.BlockSpec(memory_space=pl.ANY),
        ],
        out_specs=[whole(*pay_shape), whole(feat_count, hid_count)],
        out_shape=[shape(*pay_shape, dtype=bf16), shape(feat_count, hid_count)],
        scratch_shapes=[pltpu.VMEM((2 * rows, hid_count), f32)],
    )(
        rank, x1, c1, far, second_weight, rate_row, front, back, trans, featt, slope, sums, first, send, bias, come,
        late,
    )
    pay_come = move(pay, across)
    group = lax.axis_size(("ch", "sub"))
    bit = 1
    while bit < group:
        first = first + lax.ppermute(first, ("ch", "sub"), [(i, i ^ bit) for i in range(group)])
        bit *= 2
    first_come = move(first, across)

    vmem = pl.BlockSpec(memory_space=pltpu.VMEM)
    total = call(
        functools.partial(total_kernel, channels), "total", 0, 1,
        grid=(),
        in_specs=[vmem] * 4,
        out_specs=vmem,
        out_shape=shape(*pay_shape, dtype=bf16),
    )(pay, pay_come, first, first_come)
    total_come = move(total, outward)

    grad_one, grad_two, grad_value = call(
        functools.partial(gates_kernel, shards), "gates", 0, 1,
        in_specs=[smem] + [block_like] * 4 + [strip(1)] + [block_like] * 4,
        out_specs=[block_like] * 3,
        out_shape=[shape(rows, channels, dtype=bf16)] * 3,
    )(rank, x_one, x_two, values, grad_out, skip_row, conv, corr, late, part_come)

    grad_second, grad_first, grad_bias = call(
        functools.partial(finish_kernel, channels, shards), "finish", 0, 1,
        grid=(),
        in_specs=[smem, vmem, vmem],
        out_specs=[vmem] * 3,
        out_shape=[shape(hid_count, channels), shape(feat_count, hid_count), shape(1, channels)],
    )(rank, total, total_come)
    return (grad_one, grad_two, grad_value, grad_first, grad_second, grad_bias.reshape(channels))


def solution(mesh):
    in_specs = (
        P(("parts", "ctx"), ("ch", "sub")),
        P(("parts", "ctx"), ("ch", "sub")),
        P(("parts", "ctx"), ("ch", "sub")),
        P(("parts", "ctx"), ("ch", "sub")),
        P(),
        P(None, ("ch", "sub")),
        P(("ch", "sub")),
        P(("ch", "sub")),
    )
    out_specs = (
        P(("parts", "ctx"), ("ch", "sub")),
        P(("parts", "ctx"), ("ch", "sub")),
        P(("parts", "ctx"), ("ch", "sub")),
        P("parts", None),
        P("parts", ("ch", "sub")),
        P(("parts", "ch", "sub")),
    )
    body = few_shards_body if mesh.shape["ctx"] == 4 else many_shards_body
    return jax.shard_map(body, mesh=mesh, in_specs=in_specs, out_specs=out_specs, check_vma=False)
```

```python
import functools
import math

import jax
import jax.numpy as jnp
import numpy as np
from jax import lax
from jax.experimental import pallas as pl
from jax.experimental.pallas import tpu as pltpu
from jax.sharding import PartitionSpec as P

band_steps = (1763, 1201, 811, 547, 367, 251, 167, 113, 79, 53, 37, 23, 17, 11, 7, 3)
highest = lax.Precision.HIGHEST
f32 = jnp.float32
bf16 = jnp.bfloat16


def features(positions):
    multiplier = jnp.array(band_steps, dtype=jnp.int32)
    phase = positions[:, None] * multiplier[None, :] % 4096
    angle = phase.astype(jnp.float32) * (2.0 * math.pi / 4096.0)
    return jnp.concatenate([jnp.cos(angle), jnp.sin(angle)], axis=1)


def tables(out_count, in_count, modulus, sign_value):
    row_index = lax.broadcasted_iota(jnp.int32, (out_count, in_count), 0)
    col_index = lax.broadcasted_iota(jnp.int32, (out_count, in_count), 1)
    angle = (row_index * col_index % modulus).astype(jnp.float32) * (2.0 * math.pi / modulus)
    return (jnp.cos(angle), sign_value * jnp.sin(angle))


def twiddle(spec_re, spec_im, freq_count, span, modulus, sign_value):
    freq_index = lax.broadcasted_iota(jnp.int32, (freq_count, span), 0)
    pos_index = lax.broadcasted_iota(jnp.int32, (freq_count, span), 1)
    angle = (freq_index * pos_index % modulus).astype(jnp.float32) * (2.0 * math.pi / modulus)
    factor_re = jnp.cos(angle)[None, None, :, :]
    factor_im = (sign_value * jnp.sin(angle))[None, None, :, :]
    return (spec_re * factor_re - spec_im * factor_im, spec_re * factor_im + spec_im * factor_re)


def contract(kernel, array):
    return jnp.einsum(
        "lj,mckj->mckl", kernel, array, precision=highest, preferred_element_type=jnp.float32
    )


def along_positions(spec_re, spec_im, kernel_re, kernel_im):
    return (
        contract(kernel_re, spec_re) - contract(kernel_im, spec_im),
        contract(kernel_re, spec_im) + contract(kernel_im, spec_re),
    )


def many_shards_body(
    x_one, x_two, values, grad_out, first_weight, second_weight, skip_bias, decay_rate
):
    row_count, chan_count = x_one.shape
    shards = lax.axis_size("ctx")
    rank = lax.axis_index("ctx")
    seq_len = row_count * shards
    total = 2 * seq_len
    narrow = chan_count // shards
    chan_weight = lax.dynamic_slice_in_dim(second_weight, rank * narrow, narrow, 1)
    chan_rate = lax.dynamic_slice_in_dim(decay_rate, rank * narrow, narrow, 0)
    source = x_one.astype(jnp.float32) * values.astype(jnp.float32)
    cotan = grad_out.astype(jnp.float32) * x_two.astype(jnp.float32)
    spread = lax.all_to_all(
        jnp.stack([source.T, cotan.T])[:, :, None, :],
        "ctx",
        split_axis=1,
        concat_axis=2,
        tiled=True,
    )
    far_source = spread[0]
    far_cotan = spread[1]
    positions = jnp.arange(seq_len, dtype=jnp.int32)
    feats = features(positions)
    pre_act = jnp.dot(feats, first_weight, precision=highest, preferred_element_type=jnp.float32)
    hidden = jnp.sin(pre_act)
    envelope = jnp.exp(-chan_rate[:, None] * positions.astype(jnp.float32)[None, :]) * float(
        seq_len
    ) ** (-0.5)
    filt = (
        jnp.einsum(
            "th,hc->ct", hidden, chan_weight, precision=highest, preferred_element_type=jnp.float32
        )
        * envelope
    )
    filt_blocks = filt.reshape(narrow, shards, row_count)
    fields = jnp.stack([far_source, far_cotan])

    def first_section(kernel):
        field_part = jnp.einsum(
            "kn,mcnj->mckj", kernel, fields, precision=highest, preferred_element_type=jnp.float32
        )
        filter_part = jnp.einsum(
            "kn,cnj->ckj",
            kernel,
            filt_blocks,
            precision=highest,
            preferred_element_type=jnp.float32,
        )
        return jnp.concatenate([field_part, filter_part[None]], axis=0)

    first_re, first_im = tables(2 * shards, shards, 2 * shards, -1.0)
    spec_re, spec_im = (first_section(first_re), first_section(first_im))
    spec_re, spec_im = twiddle(spec_re, spec_im, 2 * shards, row_count, total, -1.0)
    fwd_re, fwd_im = tables(row_count, row_count, row_count, -1.0)
    spec_re, spec_im = along_positions(spec_re, spec_im, fwd_re, fwd_im)
    source_re, source_im = (spec_re[0], spec_im[0])
    cotan_re, cotan_im = (spec_re[1], spec_im[1])
    filter_re, filter_im = (spec_re[2], spec_im[2])
    prod_re = jnp.stack(
        [
            source_re * filter_re - source_im * filter_im,
            cotan_re * filter_re + cotan_im * filter_im,
            cotan_re * source_re + cotan_im * source_im,
        ]
    )
    prod_im = jnp.stack(
        [
            source_re * filter_im + source_im * filter_re,
            cotan_im * filter_re - cotan_re * filter_im,
            cotan_im * source_re - cotan_re * source_im,
        ]
    )
    back_re, back_im = tables(row_count, row_count, row_count, 1.0)
    prod_re, prod_im = along_positions(prod_re, prod_im, back_re, back_im)
    prod_re, prod_im = twiddle(prod_re, prod_im, 2 * shards, row_count, total, 1.0)
    last_re, last_im = tables(shards, 2 * shards, 2 * shards, 1.0)
    field_out = jnp.einsum(
        "nk,mckj->mcnj", last_re, prod_re[:2], precision=highest, preferred_element_type=jnp.float32
    ) - jnp.einsum(
        "nk,mckj->mcnj", last_im, prod_im[:2], precision=highest, preferred_element_type=jnp.float32
    )
    field_out = field_out * (1.0 / total)
    filt_grad = jnp.einsum(
        "nk,ckj->cnj", last_re, prod_re[2], precision=highest, preferred_element_type=jnp.float32
    ) - jnp.einsum(
        "nk,ckj->cnj", last_im, prod_im[2], precision=highest, preferred_element_type=jnp.float32
    )
    filt_grad = (filt_grad * (1.0 / total)).reshape(narrow, seq_len)
    modulated = filt_grad * envelope
    weight_part = jnp.einsum(
        "th,ct->hc", hidden, modulated, precision=highest, preferred_element_type=jnp.float32
    )
    hidden_grad = jnp.einsum(
        "ct,hc->th", modulated, chan_weight, precision=highest, preferred_element_type=jnp.float32
    )
    first_part = jnp.dot(
        feats.T,
        hidden_grad * jnp.cos(pre_act),
        precision=highest,
        preferred_element_type=jnp.float32,
    )
    grad_first = lax.psum(first_part, ("ctx", "ch", "sub"))
    returned = lax.all_to_all(
        field_out.astype(jnp.bfloat16), "ctx", split_axis=2, concat_axis=1, tiled=True
    ).astype(field_out.dtype)
    conv_part = returned[0, :, 0, :].T
    corr_part = returned[1, :, 0, :].T
    grad_two = (grad_out.astype(jnp.float32) * (conv_part + skip_bias[None, :] * source)).astype(
        jnp.bfloat16
    )
    grad_mid = corr_part + skip_bias[None, :] * cotan
    grad_one = (grad_mid * values.astype(jnp.float32)).astype(jnp.bfloat16)
    grad_value = (grad_mid * x_one.astype(jnp.float32)).astype(jnp.bfloat16)
    grad_bias = lax.psum(jnp.sum(source * cotan, axis=0), "ctx")
    grad_second = lax.all_gather(weight_part, "ctx", axis=1, tiled=True)
    return (grad_one, grad_two, grad_value, grad_first, grad_second, grad_bias)


STEP = 16
SIDE = 256


def halves(array):
    array = np.asarray(array, np.float32)
    high = array.astype(bf16)
    low = (array - high.astype(np.float32)).astype(bf16)
    return high, low


def block_tables(rows):
    freq = np.concatenate([np.arange(0, rows, 2), np.arange(1, rows, 2)])
    phase = (2 * freq + 1)[:, None] * np.arange(rows)[None, :] % (4 * rows)
    angle = phase * (2.0 * np.pi / (4 * rows))
    forward = np.concatenate([np.cos(angle), -np.sin(angle)], axis=0)
    front = np.ascontiguousarray(np.concatenate(halves(forward), axis=1))
    back = np.ascontiguousarray(np.concatenate(halves(forward.T / rows), axis=0))
    return front, back


def feature_table(seq_len):
    phase = np.arange(seq_len)[:, None] * np.array(band_steps)[None, :] % 4096
    angle = phase * (2.0 * np.pi / 4096.0)
    return np.concatenate([np.cos(angle), np.sin(angle)], axis=1).astype(np.float32)


def split(array):
    high = array.astype(bf16)
    return high, (array - high.astype(f32)).astype(bf16)


def dot(left, right):
    return jnp.dot(left, right, preferred_element_type=f32)


def exact_dot(left, right):
    return jnp.dot(left, right, precision=highest, preferred_element_type=f32)


def dot_across(left, right):
    return lax.dot_general(left, right, (((1,), (1,)), ((), ())), preferred_element_type=f32)


def decay(rate, rows, scale):
    place = lax.broadcasted_iota(jnp.int32, (rows, rate.shape[1]), 0)
    return jnp.exp(-place.astype(f32) * rate) * scale


def times(a, b):
    return a[0] * b[0] - a[1] * b[1], a[0] * b[1] + a[1] * b[0]


def conj_times(a, b):
    return a[0] * b[0] + a[1] * b[1], a[0] * b[1] - a[1] * b[0]


def plus(a, b):
    return a[0] + b[0], a[1] + b[1]


def scaled(a, factor):
    return a[0] * factor, a[1] * factor


def choose(condition, a, b):
    return jnp.where(condition, a[0], b[0]), jnp.where(condition, a[1], b[1])


def turned(a, sign):
    return (a[1], -a[0]) if sign > 0 else (-a[1], a[0])


def forward(front_ref, block):
    return dot(front_ref[...], jnp.concatenate([block, block], axis=0))


def backward(back_ref, high, low=None):
    both = dot(back_ref[...], high)
    rows = both.shape[0] // 2
    out = both[:rows] + both[rows:]
    return out if low is None else out + dot(back_ref[:rows], low)


def row_groups(rows):
    for step in range(rows // STEP):
        sign = 1 if step * STEP < rows // 2 else -1
        yield slice(step * STEP, (step + 1) * STEP), slice(rows + step * STEP, rows + (step + 1) * STEP), sign


def weight_sums(trans, m_high, m_low):
    both = dot(trans, m_high)
    count = both.shape[0] // 2
    return both[:count] + both[count:] + dot(trans[:count], m_low)


def hidden_sums(m_high, m_low, w_high, w_low):
    left = jnp.concatenate([m_high, m_high, m_low], axis=1)
    right = jnp.concatenate([w_high, w_low, w_high], axis=1)
    return dot_across(left, right)


def looped(kernel, kinds, blocks, width):
    def over_strips(*refs):
        def step(block, carry):
            cols = pl.ds(pl.multiple_of(block * width, width), width)
            views = [
                ref if kind is None else ref.at[(*kind, cols)]
                for ref, kind in zip(refs, kinds + (None,) * (len(refs) - len(kinds)))
            ]
            kernel(block, blocks, *views)
            return carry

        lax.fori_loop(0, blocks, step, 0)

    return over_strips


ROWS = (slice(None),)
CUBE = (slice(None), slice(None))


def products_kernel(one_ref, two_ref, val_ref, out_ref, source_ref, cotan_ref, bias_ref):
    source = one_ref[...].astype(f32) * val_ref[...].astype(f32)
    cotan = out_ref[...].astype(f32) * two_ref[...].astype(f32)
    source_ref[...] = source.astype(bf16)
    cotan_ref[...] = cotan.astype(bf16)
    part = jnp.sum(source * cotan, axis=0, keepdims=True)

    @pl.when(pl.program_id(0) == 0)
    def _():
        bias_ref[...] = part

    @pl.when(pl.program_id(0) > 0)
    def _():
        bias_ref[...] += part


def sin_cos(angle):
    turns = jnp.floor(angle * (2.0 / math.pi) + 0.5)
    rest = ((angle - turns * 1.5703125) - turns * 4.837512969970703e-4) - turns * 7.54978995489188e-8
    square = rest * rest
    sine = rest + rest * square * (
        -1.6666654611e-1 + square * (8.3321608736e-3 + square * -1.9515295891e-4)
    )
    cosine = 1.0 - 0.5 * square + square * square * (
        4.166664568298827e-2 + square * (-1.388731625493765e-3 + square * 2.443315711809948e-5)
    )
    quarter = turns.astype(jnp.int32)
    odd = (quarter & 1) == 1
    sin_sign = jnp.where((quarter & 2) == 2, -1.0, 1.0).astype(f32)
    cos_sign = jnp.where(((quarter + 1) & 2) == 2, -1.0, 1.0).astype(f32)
    return jnp.where(odd, cosine, sine) * sin_sign, jnp.where(odd, sine, cosine) * cos_sign


def filters_kernel(
    rows, shards, block, blocks, rank_ref, feats_ref, first_ref, weight_ref, rate_ref, front_ref, source_ref, cotan_ref,
    spec_ref, trans_ref, slope_ref, edge_ref, hid_ref,
):
    hid_count = first_ref.shape[1]
    scale = float(rows * shards) ** -0.5

    @pl.when(block == 0)
    def _():
        pre_act = exact_dot(feats_ref[...], first_ref[...])
        hidden, slope = sin_cos(pre_act)
        slope_ref[...] = slope
        high, low = split(hidden)
        hid_ref[...] = jnp.concatenate([high, high, low], axis=1)
        turned_over = jnp.concatenate([hidden, slope], axis=1).T[:hid_count]
        trans_ref[...] = jnp.concatenate(split(turned_over), axis=0)

    edge_ref[...] = jnp.where(rank_ref[0] == 0, source_ref[...], cotan_ref[...])
    w_high, w_low = split(weight_ref[...])
    stacked = jnp.concatenate([w_high, w_low, w_high], axis=0)
    rate = rate_ref[...]
    env = decay(rate, rows, scale)
    before = None
    for lag in range(shards):
        part = dot(hid_ref[lag * rows : (lag + 1) * rows, :], stacked)
        part = part * (env * jnp.exp(rate * (-float(lag * rows))))
        f_high, f_low = split(part)
        now = forward(front_ref, f_high) + dot(front_ref[:, :rows], f_low)
        for re, im, sign in row_groups(rows):
            here = (now[re], now[im])
            if before is not None:
                here = plus(here, turned((before[re], before[im]), -sign))
            spec_ref[lag, re, :] = here[0].astype(bf16)
            spec_ref[lag, im, :] = here[1].astype(bf16)
        before = now


def own_kernel(
    rows, shards, channels, block, blocks, source_ref, cotan_ref, weight_ref, rate_ref, front_ref, back_ref, trans_ref,
    slope_ref, featt_ref, bias_ref, sums_ref, send_ref, acc_ref,
):
    width = weight_ref.shape[1]

    @pl.when(block == 0)
    def _():
        acc_ref[...] = jnp.zeros_like(acc_ref)

    x0 = forward(front_ref, source_ref[...])
    c0 = forward(front_ref, cotan_ref[...])
    pair = conj_times((x0[:rows], x0[rows:]), (c0[:rows], c0[rows:]))
    high, low = split(jnp.concatenate(pair, axis=0))
    env = decay(rate_ref[...], rows, float(rows * shards) ** -0.5)
    m_high, m_low = split(backward(back_ref, high, low) * env)
    sums = weight_sums(trans_ref[:, :rows], m_high, m_low)
    sums_ref[...] = sums
    send_ref[:, pl.ds(pl.multiple_of(block * width, width), width)] = sums.astype(bf16)
    acc_ref[...] += hidden_sums(m_high, m_low, *split(weight_ref[...]))

    @pl.when(block == blocks - 1)
    def _():
        first = exact_dot(featt_ref[:, :rows], acc_ref[...] * slope_ref[:rows, :])
        put_side(send_ref, channels, fold(bias_ref[...]), first)


def fold(bias):
    return jnp.concatenate([bias[:, i * 128 : (i + 1) * 128] for i in range(bias.shape[1] // 128)], axis=0)


def put_side(pay_ref, channels, bias, first=None):
    half = pay_ref.shape[0] // 2
    pay_ref[:, channels:] = jnp.zeros((2 * half, SIDE), bf16)
    for start, part in zip((0, 128), split(bias)):
        pay_ref[: bias.shape[0], channels + start : channels + start + 128] = part
    if first is not None:
        for start, part in zip((0, 128), split(first)):
            pay_ref[half:, channels + start : channels + start + first.shape[1]] = part


def get_side(pay, channels, lanes, hid_count):
    half = pay.shape[0] // 2
    side = pay[:, channels : channels + 128].astype(f32) + pay[:, channels + 128 :].astype(f32)
    return side[:lanes], side[half:, :hid_count]


def near_kernel(
    rows, shards, block, blocks, rank_ref, x0_ref, c0_ref, x1_ref, c1_ref, spec_ref, weight_ref, rate_ref, front_ref, back_ref,
    trans_ref, featt_ref, slope_ref, own_ref, conv_ref, corr_ref, ahead_ref, sums_ref, first_ref, fields, fast, high_ref,
    low_ref, acc_ref,
):
    rank = rank_ref[0]
    count = shards - 1

    @pl.when(block == 0)
    def _():
        acc_ref[...] = jnp.zeros_like(acc_ref)

    lower = rank == 1
    upper = jnp.where(rank == 2, 1.0, 0.0).astype(f32)
    below_top = jnp.where(rank == shards - 1, 0.0, 1.0).astype(f32)
    side = jnp.where(rank == 2, 1.0, -1.0).astype(f32)
    for index, ref in enumerate((x0_ref, c0_ref, x1_ref, c1_ref)):
        fields[index] = forward(front_ref, ref[...])
    for re, im, sign in row_groups(rows):
        x0, c0, x1, c1 = ((fields[i, re, :], fields[i, im, :]) for i in range(4))
        w0, w1, w2 = ((spec_ref[i, re, :].astype(f32), spec_ref[i, im, :].astype(f32)) for i in range(3))
        ahead = times((w2[0], w2[1] * side), choose(lower, c1, x1))
        for index, value in enumerate(
            (plus(times(w0, x0), times(w1, x1)), plus(conj_times(w0, c0), conj_times(w1, c1)), ahead)
        ):
            fast[index, re, :] = value[0].astype(bf16)
            fast[index, im, :] = value[1].astype(bf16)
        one = plus(scaled(conj_times(x1, c0), below_top), scaled(conj_times(x0, c1), upper))
        two = conj_times(x1, c1)
        for index, value in enumerate((turned(one, sign), plus(one, turned(two, sign)), two)):
            for part, where in zip(value, (re, im)):
                high_ref[index, where, :], low_ref[index, where, :] = split(part)
    conv_ref[...] = backward(back_ref, fast[0])
    corr_ref[...] = backward(back_ref, fast[1])
    ahead_ref[...] = backward(back_ref, fast[2])
    rate = rate_ref[...]
    env = decay(rate, rows, float(rows * shards) ** -0.5)
    parts = []
    for lag in range(count):
        grad = backward(back_ref, high_ref[lag], low_ref[lag])
        parts.append(split(grad * (env * jnp.exp(rate * (-float(lag * rows))))))
    m_high = jnp.concatenate([p[0] for p in parts], axis=0)
    m_low = jnp.concatenate([p[1] for p in parts], axis=0)
    sums_ref[...] = own_ref[...] + weight_sums(trans_ref[:, : count * rows], m_high, m_low)
    w_high, w_low = split(weight_ref[...])
    acc_ref[...] += hidden_sums(m_high, m_low, w_high, w_low)

    @pl.when(block == blocks - 1)
    def _():
        first_ref[...] = exact_dot(
            featt_ref[:, : count * rows], acc_ref[...] * slope_ref[: count * rows, :]
        )


def far_kernel(rows, block, blocks, rank_ref, far_ref, spec_ref, front_ref, back_ref, ahead_ref, part_ref, late_ref):
    side = jnp.where(rank_ref[0] == 2, 1.0, -1.0).astype(f32)
    far = forward(front_ref, far_ref[...])
    far = (far[:rows], far[rows:])
    w2, w3 = ((spec_ref[i, :rows, :].astype(f32), spec_ref[i, rows:, :].astype(f32) * side) for i in range(2))
    ahead = jnp.concatenate(times(w3, far), axis=0).astype(bf16)
    part_ref[...] = (ahead_ref[...] + backward(back_ref, ahead)).astype(bf16)
    late = jnp.concatenate(times(w2, far), axis=0).astype(bf16)
    late_ref[...] = backward(back_ref, late)


def last_kernel(
    rows, shards, channels, block, blocks, rank_ref, x1_ref, c1_ref, far_ref, weight_ref, rate_ref, front_ref, back_ref,
    trans_ref, featt_ref, slope_ref, sums_ref, first_ref, own_ref, bias_ref, in_ref, pay_ref, total_ref, acc_ref,
):
    hid_count, width = weight_ref.shape
    lower = rank_ref[0] == 1
    start = pl.multiple_of(block * width, width)
    here = sums_ref[...] + in_ref[:, pl.ds(start, width)].astype(f32)
    mine = (block < blocks // 2) == lower

    @pl.when(block == 0)
    def _():
        acc_ref[...] = jnp.zeros_like(acc_ref)

    @pl.when(mine)
    def _():
        sign = jnp.where(lower, 1.0, -1.0).astype(f32)
        near = forward(front_ref, jnp.where(lower, x1_ref[...], c1_ref[...]))
        far = forward(front_ref, far_ref[...])
        three = conj_times((near[:rows], near[rows:]), (far[:rows], far[rows:]))
        three = (three[0], three[1] * sign)
        half = rows // 2
        two = jnp.concatenate([three[1][:half], -three[1][half:], -three[0][:half], three[0][half:]], axis=0)
        rate = rate_ref[...]
        env = decay(rate, rows, float(rows * shards) ** -0.5)
        parts = []
        for lag, value in ((shards - 2, two), (shards - 1, jnp.concatenate(three, axis=0))):
            grad = backward(back_ref, *split(value))
            parts.append(split(grad * (env * jnp.exp(rate * (-float(lag * rows))))))
        m_high = jnp.concatenate([p[0] for p in parts], axis=0)
        m_low = jnp.concatenate([p[1] for p in parts], axis=0)
        trans = trans_ref[:, (shards - 2) * rows :]
        pay_ref[:, pl.ds(start, width)] = (here + weight_sums(trans, m_high, m_low)).astype(bf16)
        w_high, w_low = split(weight_ref[...])
        acc_ref[...] += hidden_sums(m_high, m_low, w_high, w_low)

    @pl.when(jnp.logical_not(mine))
    def _():
        pay_ref[:, pl.ds(start, width)] = here.astype(bf16)

    @pl.when(block == blocks - 1)
    def _():
        first = exact_dot(
            featt_ref[:, (shards - 2) * rows :], acc_ref[...] * slope_ref[(shards - 2) * rows :, :]
        )
        lanes = channels // 128
        own_first = get_side(own_ref[...], channels, lanes, hid_count)[1]
        in_bias, in_first = get_side(in_ref[...], channels, lanes, hid_count)
        first = first + first_ref[...] + own_first + in_first
        put_side(pay_ref, channels, fold(bias_ref[...]) + in_bias)
        total_ref[...] = first


def total_kernel(channels, hid_count, own_ref, come_ref, pay_ref):
    lanes = channels // 128
    pay_ref[:, :channels] = (own_ref[:, :channels].astype(f32) + come_ref[:, :channels].astype(f32)).astype(bf16)
    own, come = (get_side(ref[...], channels, lanes, hid_count)[0] for ref in (own_ref, come_ref))
    put_side(pay_ref, channels, own + come)


def gates_kernel(
    shards, block, blocks, rank_ref, one_ref, two_ref, val_ref, out_ref, skip_ref, conv_ref, corr_ref, late_ref, part_ref,
    grad_one_ref, grad_two_ref, grad_value_ref,
):
    rank = rank_ref[0]

    def mask(wanted):
        return jnp.where(rank == wanted, 1.0, 0.0).astype(f32)

    part = part_ref[...].astype(f32)
    late = late_ref[...]
    one = one_ref[...].astype(f32)
    val = val_ref[...].astype(f32)
    out = out_ref[...].astype(f32)
    skip = skip_ref[...]
    conv = conv_ref[...] + late * mask(2) + part * mask(shards - 1)
    corr = corr_ref[...] + late * mask(1) + part * mask(0)
    grad_two_ref[...] = (out * (conv + skip * (one * val))).astype(bf16)
    mid = corr + skip * (out * two_ref[...].astype(f32))
    grad_one_ref[...] = (mid * val).astype(bf16)
    grad_value_ref[...] = (mid * one).astype(bf16)


def finish_kernel(
    channels, shards, rank_ref, own_ref, come_ref, first_ref, first_come_ref, second_out, first_out, bias_out, second,
    first, bias, sems,
):
    rank = rank_ref[0]
    inner = jnp.logical_and(rank > 0, rank < shards - 1)
    lanes = channels // 128
    copies = [
        pltpu.make_async_copy(held, out, sems.at[i])
        for i, (held, out) in enumerate(((second, second_out), (first, first_out), (bias, bias_out)))
    ]
    picked = jnp.where(inner, own_ref[...], come_ref[...])
    second[...] = picked[:, :channels].astype(f32)
    copies[0].start()
    first[...] = jnp.where(inner, first_ref[...], first_come_ref[...])
    copies[1].start()
    rows = get_side(picked, channels, lanes, first.shape[1])[0]
    for i in range(lanes):
        bias[:, i * 128 : (i + 1) * 128] = rows[i : i + 1]
    copies[2].start()
    for copy in copies:
        copy.wait()


def few_shards_body(
    x_one, x_two, values, grad_out, first_weight, second_weight, skip_bias, decay_rate
):
    rows, channels = x_one.shape
    shards = lax.axis_size("ctx")
    feat_count, hid_count = first_weight.shape
    seq_len = rows * shards
    double = 2 * rows
    width = min(512, channels)
    blocks = channels // width
    rank = lax.axis_index("ctx").astype(jnp.int32).reshape(1)
    front, back = block_tables(rows)
    feats = feature_table(seq_len)
    featt = np.ascontiguousarray(feats.T)
    skip_row = skip_bias.reshape(1, channels)
    rate_row = decay_rate.reshape(1, channels)
    smem = pl.BlockSpec(memory_space=pltpu.SMEM)
    vmem = pl.BlockSpec(memory_space=pltpu.VMEM)
    anywhere = pl.BlockSpec(memory_space=pl.ANY)
    mebi = 1024 * 1024

    def shape(*dims, dtype=f32):
        return jax.ShapeDtypeStruct(dims, dtype)

    def call(kernel, name, units, out_shape, in_specs, out_specs=None, scratch=(), limit=16):
        return pl.pallas_call(
            kernel,
            in_specs=in_specs,
            out_specs=out_specs if out_specs is not None else [vmem] * len(out_shape),
            out_shape=out_shape,
            scratch_shapes=scratch,
            compiler_params=pltpu.CompilerParams(vmem_limit_bytes=limit * mebi),
            cost_estimate=pl.CostEstimate(
                flops=2 * units * double * double * channels, bytes_accessed=rows * channels, transcendentals=0
            ),
            name=name,
        )

    def move(array, pairs):
        return lax.ppermute(array, "ctx", pairs)

    up = [(i, i + 1) for i in range(shards - 1)]
    down = [(i + 1, i) for i in range(shards - 1)]
    inward = [(0, 1), (shards - 1, shards - 2)]
    outward = [(1, 0), (shards - 2, shards - 1)]
    across = [(1, 2), (2, 1)]
    pay_shape = (hid_count, channels + SIDE)
    block_bf16 = shape(rows, channels, dtype=bf16)
    block_f32 = shape(rows, channels)

    row_step = max(rows // 2, 16)
    gate_rows = pl.BlockSpec((row_step, channels), lambda i: (i, 0))
    x0, c0, bias = pl.pallas_call(
        products_kernel,
        grid=(rows // row_step,),
        in_specs=[gate_rows] * 4,
        out_specs=[gate_rows] * 2 + [pl.BlockSpec((1, channels), lambda i: (0, 0))],
        out_shape=[block_bf16] * 2 + [shape(1, channels)],
        compiler_params=pltpu.CompilerParams(vmem_limit_bytes=64 * mebi),
        name="products",
    )(x_one, x_two, values, grad_out)
    x1 = move(x0, up)
    c1 = move(c0, down)

    spec, trans, slope, edge = call(
        looped(
            functools.partial(filters_kernel, rows, shards),
            (None, None, None, ROWS, ROWS, None, ROWS, ROWS, CUBE, None, None, ROWS),
            blocks, width,
        ),
        "filters", 8,
        [
            shape(shards, double, channels, dtype=bf16), shape(2 * hid_count, seq_len, dtype=bf16),
            shape(seq_len, hid_count), block_bf16,
        ],
        [smem] + [vmem] * 7,
        scratch=[pltpu.VMEM((seq_len, 3 * hid_count), bf16)],
    )(rank, feats, first_weight, second_weight, rate_row, front, x0, c0)
    far = move(edge, [(0, 2), (shards - 1, shards - 3)])

    own, send = call(
        looped(
            functools.partial(own_kernel, rows, shards, channels),
            (ROWS, ROWS, ROWS, ROWS, None, None, None, None, None, None, ROWS),
            blocks, width,
        ),
        "own_pair", 8,
        [shape(hid_count, channels), shape(*pay_shape, dtype=bf16)],
        [vmem] * 10,
        scratch=[pltpu.VMEM((rows, hid_count), f32)],
    )(x0, c0, second_weight, rate_row, front, back, trans, slope, featt, bias)
    come = move(send, inward)

    conv, corr, ahead, sums, first = call(
        looped(
            functools.partial(near_kernel, rows, shards),
            (None, ROWS, ROWS, ROWS, ROWS, CUBE, ROWS, ROWS, None, None, None, None, None, ROWS, ROWS, ROWS, ROWS, ROWS),
            blocks, width,
        ),
        "near_blocks", 20,
        [block_f32] * 3 + [shape(hid_count, channels), shape(feat_count, hid_count)],
        [smem] + [vmem] * 13,
        scratch=[
            pltpu.VMEM((4, double, width), f32),
            pltpu.VMEM((3, double, width), bf16),
            pltpu.VMEM((shards - 1, double, width), bf16),
            pltpu.VMEM((shards - 1, double, width), bf16),
            pltpu.VMEM(((shards - 1) * rows, hid_count), f32),
        ],
    )(rank, x0, c0, x1, c1, spec, second_weight, rate_row, front, back, trans, featt, slope, own)

    part, late = call(
        looped(
            functools.partial(far_kernel, rows),
            (None, ROWS, (slice(2, 4), slice(None)), None, None, ROWS, ROWS, ROWS),
            blocks, width,
        ),
        "far_block", 1,
        [block_bf16, block_f32],
        [smem] + [vmem] * 5,
    )(rank, far, spec, front, back, ahead)
    part_come = move(part, outward)

    pay, first = call(
        looped(
            functools.partial(last_kernel, rows, shards, channels),
            (None, ROWS, ROWS, ROWS, ROWS, ROWS, None, None, None, None, None, ROWS),
            blocks, width,
        ),
        "last_pair", 1,
        [shape(*pay_shape, dtype=bf16), shape(feat_count, hid_count)],
        [smem] + [vmem] * 15,
        scratch=[pltpu.VMEM((2 * rows, hid_count), f32)],
    )(rank, x1, c1, far, second_weight, rate_row, front, back, trans, featt, slope, sums, first, send, bias, come)
    pay_come = move(pay, across)
    group = lax.axis_size(("ch", "sub"))
    bit = 1
    while bit < group:
        first = first + lax.ppermute(first, ("ch", "sub"), [(i, i ^ bit) for i in range(group)])
        bit *= 2
    first = first + move(first, across)
    first_come = move(first, outward)

    (total,) = call(
        functools.partial(total_kernel, channels, hid_count), "total", 0,
        [shape(*pay_shape, dtype=bf16)],
        [vmem] * 2,
    )(pay, pay_come)
    total_come = move(total, outward)

    grad_one, grad_two, grad_value = call(
        looped(
            functools.partial(gates_kernel, shards), (None,) + (ROWS,) * 12, blocks, width
        ),
        "gates", 0,
        [block_bf16] * 3,
        [smem] + [vmem] * 9,
    )(rank, x_one, x_two, values, grad_out, skip_row, conv, corr, late, part_come)

    outs = [shape(hid_count, channels), shape(feat_count, hid_count), shape(1, channels)]
    grad_second, grad_first, grad_bias = call(
        functools.partial(finish_kernel, channels, shards), "finish", 0,
        outs,
        [smem] + [vmem] * 4,
        out_specs=[anywhere] * 3,
        scratch=[pltpu.VMEM(o.shape, f32) for o in outs] + [pltpu.SemaphoreType.DMA((3,))],
    )(rank, total, total_come, first, first_come)
    return (grad_one, grad_two, grad_value, grad_first, grad_second, grad_bias.reshape(channels))


def solution(mesh):
    in_specs = (
        P(("parts", "ctx"), ("ch", "sub")),
        P(("parts", "ctx"), ("ch", "sub")),
        P(("parts", "ctx"), ("ch", "sub")),
        P(("parts", "ctx"), ("ch", "sub")),
        P(),
        P(None, ("ch", "sub")),
        P(("ch", "sub")),
        P(("ch", "sub")),
    )
    out_specs = (
        P(("parts", "ctx"), ("ch", "sub")),
        P(("parts", "ctx"), ("ch", "sub")),
        P(("parts", "ctx"), ("ch", "sub")),
        P("parts", None),
        P("parts", ("ch", "sub")),
        P(("parts", "ch", "sub")),
    )
    body = few_shards_body if mesh.shape["ctx"] == 4 else many_shards_body
    return jax.shard_map(body, mesh=mesh, in_specs=in_specs, out_specs=out_specs, check_vma=False)
```

```python
import functools
import math

import jax
import jax.numpy as jnp
import numpy as np
from jax import lax
from jax.experimental import pallas as pl
from jax.experimental.pallas import tpu as pltpu
from jax.sharding import PartitionSpec as P

band_steps = (1763, 1201, 811, 547, 367, 251, 167, 113, 79, 53, 37, 23, 17, 11, 7, 3)
highest = lax.Precision.HIGHEST
f32 = jnp.float32
bf16 = jnp.bfloat16


def features(positions):
    multiplier = jnp.array(band_steps, dtype=jnp.int32)
    phase = positions[:, None] * multiplier[None, :] % 4096
    angle = phase.astype(jnp.float32) * (2.0 * math.pi / 4096.0)
    return jnp.concatenate([jnp.cos(angle), jnp.sin(angle)], axis=1)


def tables(out_count, in_count, modulus, sign_value):
    row_index = lax.broadcasted_iota(jnp.int32, (out_count, in_count), 0)
    col_index = lax.broadcasted_iota(jnp.int32, (out_count, in_count), 1)
    angle = (row_index * col_index % modulus).astype(jnp.float32) * (2.0 * math.pi / modulus)
    return (jnp.cos(angle), sign_value * jnp.sin(angle))


def twiddle(spec_re, spec_im, freq_count, span, modulus, sign_value):
    freq_index = lax.broadcasted_iota(jnp.int32, (freq_count, span), 0)
    pos_index = lax.broadcasted_iota(jnp.int32, (freq_count, span), 1)
    angle = (freq_index * pos_index % modulus).astype(jnp.float32) * (2.0 * math.pi / modulus)
    factor_re = jnp.cos(angle)[None, None, :, :]
    factor_im = (sign_value * jnp.sin(angle))[None, None, :, :]
    return (spec_re * factor_re - spec_im * factor_im, spec_re * factor_im + spec_im * factor_re)


def contract(kernel, array):
    return jnp.einsum(
        "lj,mckj->mckl", kernel, array, precision=highest, preferred_element_type=jnp.float32
    )


def along_positions(spec_re, spec_im, kernel_re, kernel_im):
    return (
        contract(kernel_re, spec_re) - contract(kernel_im, spec_im),
        contract(kernel_re, spec_im) + contract(kernel_im, spec_re),
    )


def many_shards_body(
    x_one, x_two, values, grad_out, first_weight, second_weight, skip_bias, decay_rate
):
    row_count, chan_count = x_one.shape
    shards = lax.axis_size("ctx")
    rank = lax.axis_index("ctx")
    seq_len = row_count * shards
    total = 2 * seq_len
    narrow = chan_count // shards
    chan_weight = lax.dynamic_slice_in_dim(second_weight, rank * narrow, narrow, 1)
    chan_rate = lax.dynamic_slice_in_dim(decay_rate, rank * narrow, narrow, 0)
    source = x_one.astype(jnp.float32) * values.astype(jnp.float32)
    cotan = grad_out.astype(jnp.float32) * x_two.astype(jnp.float32)
    spread = lax.all_to_all(
        jnp.stack([source.T, cotan.T])[:, :, None, :],
        "ctx",
        split_axis=1,
        concat_axis=2,
        tiled=True,
    )
    far_source = spread[0]
    far_cotan = spread[1]
    positions = jnp.arange(seq_len, dtype=jnp.int32)
    feats = features(positions)
    pre_act = jnp.dot(feats, first_weight, precision=highest, preferred_element_type=jnp.float32)
    hidden = jnp.sin(pre_act)
    envelope = jnp.exp(-chan_rate[:, None] * positions.astype(jnp.float32)[None, :]) * float(
        seq_len
    ) ** (-0.5)
    filt = (
        jnp.einsum(
            "th,hc->ct", hidden, chan_weight, precision=highest, preferred_element_type=jnp.float32
        )
        * envelope
    )
    filt_blocks = filt.reshape(narrow, shards, row_count)
    fields = jnp.stack([far_source, far_cotan])

    def first_section(kernel):
        field_part = jnp.einsum(
            "kn,mcnj->mckj", kernel, fields, precision=highest, preferred_element_type=jnp.float32
        )
        filter_part = jnp.einsum(
            "kn,cnj->ckj",
            kernel,
            filt_blocks,
            precision=highest,
            preferred_element_type=jnp.float32,
        )
        return jnp.concatenate([field_part, filter_part[None]], axis=0)

    first_re, first_im = tables(2 * shards, shards, 2 * shards, -1.0)
    spec_re, spec_im = (first_section(first_re), first_section(first_im))
    spec_re, spec_im = twiddle(spec_re, spec_im, 2 * shards, row_count, total, -1.0)
    fwd_re, fwd_im = tables(row_count, row_count, row_count, -1.0)
    spec_re, spec_im = along_positions(spec_re, spec_im, fwd_re, fwd_im)
    source_re, source_im = (spec_re[0], spec_im[0])
    cotan_re, cotan_im = (spec_re[1], spec_im[1])
    filter_re, filter_im = (spec_re[2], spec_im[2])
    prod_re = jnp.stack(
        [
            source_re * filter_re - source_im * filter_im,
            cotan_re * filter_re + cotan_im * filter_im,
            cotan_re * source_re + cotan_im * source_im,
        ]
    )
    prod_im = jnp.stack(
        [
            source_re * filter_im + source_im * filter_re,
            cotan_im * filter_re - cotan_re * filter_im,
            cotan_im * source_re - cotan_re * source_im,
        ]
    )
    back_re, back_im = tables(row_count, row_count, row_count, 1.0)
    prod_re, prod_im = along_positions(prod_re, prod_im, back_re, back_im)
    prod_re, prod_im = twiddle(prod_re, prod_im, 2 * shards, row_count, total, 1.0)
    last_re, last_im = tables(shards, 2 * shards, 2 * shards, 1.0)
    field_out = jnp.einsum(
        "nk,mckj->mcnj", last_re, prod_re[:2], precision=highest, preferred_element_type=jnp.float32
    ) - jnp.einsum(
        "nk,mckj->mcnj", last_im, prod_im[:2], precision=highest, preferred_element_type=jnp.float32
    )
    field_out = field_out * (1.0 / total)
    filt_grad = jnp.einsum(
        "nk,ckj->cnj", last_re, prod_re[2], precision=highest, preferred_element_type=jnp.float32
    ) - jnp.einsum(
        "nk,ckj->cnj", last_im, prod_im[2], precision=highest, preferred_element_type=jnp.float32
    )
    filt_grad = (filt_grad * (1.0 / total)).reshape(narrow, seq_len)
    modulated = filt_grad * envelope
    weight_part = jnp.einsum(
        "th,ct->hc", hidden, modulated, precision=highest, preferred_element_type=jnp.float32
    )
    hidden_grad = jnp.einsum(
        "ct,hc->th", modulated, chan_weight, precision=highest, preferred_element_type=jnp.float32
    )
    first_part = jnp.dot(
        feats.T,
        hidden_grad * jnp.cos(pre_act),
        precision=highest,
        preferred_element_type=jnp.float32,
    )
    grad_first = lax.psum(first_part, ("ctx", "ch", "sub"))
    returned = lax.all_to_all(
        field_out.astype(jnp.bfloat16), "ctx", split_axis=2, concat_axis=1, tiled=True
    ).astype(field_out.dtype)
    conv_part = returned[0, :, 0, :].T
    corr_part = returned[1, :, 0, :].T
    grad_two = (grad_out.astype(jnp.float32) * (conv_part + skip_bias[None, :] * source)).astype(
        jnp.bfloat16
    )
    grad_mid = corr_part + skip_bias[None, :] * cotan
    grad_one = (grad_mid * values.astype(jnp.float32)).astype(jnp.bfloat16)
    grad_value = (grad_mid * x_one.astype(jnp.float32)).astype(jnp.bfloat16)
    grad_bias = lax.psum(jnp.sum(source * cotan, axis=0), "ctx")
    grad_second = lax.all_gather(weight_part, "ctx", axis=1, tiled=True)
    return (grad_one, grad_two, grad_value, grad_first, grad_second, grad_bias)


STEP = 16
SIDE = 256


def halves(array):
    array = np.asarray(array, np.float32)
    high = array.astype(bf16)
    low = (array - high.astype(np.float32)).astype(bf16)
    return high, low


def block_tables(rows):
    freq = np.concatenate([np.arange(0, rows, 2), np.arange(1, rows, 2)])
    phase = (2 * freq + 1)[:, None] * np.arange(rows)[None, :] % (4 * rows)
    angle = phase * (2.0 * np.pi / (4 * rows))
    forward = np.concatenate([np.cos(angle), -np.sin(angle)], axis=0)
    front = np.ascontiguousarray(np.concatenate(halves(forward), axis=1))
    back = np.ascontiguousarray(np.concatenate(halves(forward.T / rows), axis=0))
    return front, back


def feature_table(seq_len):
    phase = np.arange(seq_len)[:, None] * np.array(band_steps)[None, :] % 4096
    angle = phase * (2.0 * np.pi / 4096.0)
    return np.concatenate([np.cos(angle), np.sin(angle)], axis=1).astype(np.float32)


def split(array):
    high = array.astype(bf16)
    return high, (array - high.astype(f32)).astype(bf16)


def dot(left, right):
    return jnp.dot(left, right, preferred_element_type=f32)


def exact_dot(left, right):
    return jnp.dot(left, right, precision=highest, preferred_element_type=f32)


def dot_across(left, right):
    return lax.dot_general(left, right, (((1,), (1,)), ((), ())), preferred_element_type=f32)


def decay(rate, rows, scale):
    place = lax.broadcasted_iota(jnp.int32, (rows, rate.shape[1]), 0)
    return jnp.exp(-place.astype(f32) * rate) * scale


def times(a, b):
    return a[0] * b[0] - a[1] * b[1], a[0] * b[1] + a[1] * b[0]


def conj_times(a, b):
    return a[0] * b[0] + a[1] * b[1], a[0] * b[1] - a[1] * b[0]


def plus(a, b):
    return a[0] + b[0], a[1] + b[1]


def scaled(a, factor):
    return a[0] * factor, a[1] * factor


def choose(condition, a, b):
    return jnp.where(condition, a[0], b[0]), jnp.where(condition, a[1], b[1])


def turned(a, sign):
    return (a[1], -a[0]) if sign > 0 else (-a[1], a[0])


def forward(front_ref, block):
    return dot(front_ref[...], jnp.concatenate([block, block], axis=0))


def backward(back_ref, high, low=None):
    both = dot(back_ref[...], high)
    rows = both.shape[0] // 2
    out = both[:rows] + both[rows:]
    return out if low is None else out + dot(back_ref[:rows], low)


def row_groups(rows):
    for step in range(rows // STEP):
        sign = 1 if step * STEP < rows // 2 else -1
        yield slice(step * STEP, (step + 1) * STEP), slice(rows + step * STEP, rows + (step + 1) * STEP), sign


def weight_sums(trans, m_high, m_low):
    both = dot(trans, m_high)
    count = both.shape[0] // 2
    return both[:count] + both[count:] + dot(trans[:count], m_low)


def hidden_sums(m_high, m_low, w_high, w_low):
    left = jnp.concatenate([m_high, m_high, m_low], axis=1)
    right = jnp.concatenate([w_high, w_low, w_high], axis=1)
    return dot_across(left, right)


def looped(kernel, kinds, blocks, width):
    def over_strips(*refs):
        def step(block, carry):
            cols = pl.ds(pl.multiple_of(block * width, width), width)
            views = [
                ref if kind is None else ref.at[(*kind, cols)]
                for ref, kind in zip(refs, kinds + (None,) * (len(refs) - len(kinds)))
            ]
            kernel(block, blocks, *views)
            return carry

        lax.fori_loop(0, blocks, step, 0)

    return over_strips


ROWS = (slice(None),)
CUBE = (slice(None), slice(None))


def products_kernel(rank_ref, one_ref, two_ref, val_ref, out_ref, source_ref, cotan_ref, edge_ref, bias_ref):
    source = one_ref[...].astype(f32) * val_ref[...].astype(f32)
    cotan = out_ref[...].astype(f32) * two_ref[...].astype(f32)
    source_ref[...] = source.astype(bf16)
    cotan_ref[...] = cotan.astype(bf16)
    edge_ref[...] = jnp.where(rank_ref[0] == 0, source, cotan).astype(bf16)
    part = jnp.sum(source * cotan, axis=0, keepdims=True)

    @pl.when(pl.program_id(0) == 0)
    def _():
        bias_ref[...] = part

    @pl.when(pl.program_id(0) > 0)
    def _():
        bias_ref[...] += part


def sin_cos(angle):
    turns = jnp.floor(angle * (2.0 / math.pi) + 0.5)
    rest = ((angle - turns * 1.5703125) - turns * 4.837512969970703e-4) - turns * 7.54978995489188e-8
    square = rest * rest
    sine = rest + rest * square * (
        -1.6666654611e-1 + square * (8.3321608736e-3 + square * -1.9515295891e-4)
    )
    cosine = 1.0 - 0.5 * square + square * square * (
        4.166664568298827e-2 + square * (-1.388731625493765e-3 + square * 2.443315711809948e-5)
    )
    quarter = turns.astype(jnp.int32)
    odd = (quarter & 1) == 1
    sin_sign = jnp.where((quarter & 2) == 2, -1.0, 1.0).astype(f32)
    cos_sign = jnp.where(((quarter + 1) & 2) == 2, -1.0, 1.0).astype(f32)
    return jnp.where(odd, cosine, sine) * sin_sign, jnp.where(odd, sine, cosine) * cos_sign


def filters_kernel(rows, shards, blocks, width, *refs):
    inputs, passed, outputs, held, (hid_ref, sems) = refs[:5], refs[5:6], refs[6:10], refs[10:15], refs[15:]
    del passed
    feats_ref, first_ref, weight_ref, rate_ref, front_ref = held
    spec_ref, trans_ref, slope_ref, _ = outputs
    copies = [pltpu.make_async_copy(far, near, sems.at[i]) for i, (far, near) in enumerate(zip(inputs, held))]
    for copy in copies:
        copy.start()
    hid_count = first_ref.shape[1]
    copies[0].wait()
    copies[1].wait()
    hidden, slope = sin_cos(exact_dot(feats_ref[...], first_ref[...]))
    slope_ref[...] = slope
    high, low = split(hidden)
    hid_ref[...] = jnp.concatenate([high, high, low], axis=1)
    turned_over = jnp.concatenate([hidden, slope], axis=1).T[:hid_count]
    trans_ref[...] = jnp.concatenate(split(turned_over), axis=0)
    for copy in copies[2:]:
        copy.wait()
    strips = looped(
        functools.partial(filter_strip, rows, shards), (None, ROWS, ROWS, None, CUBE), blocks, width
    )
    strips(hid_ref, weight_ref, rate_ref, front_ref, spec_ref)


def filter_strip(rows, shards, block, blocks, hid_ref, weight_ref, rate_ref, front_ref, spec_ref):
    scale = float(rows * shards) ** -0.5
    w_high, w_low = split(weight_ref[...])
    stacked = jnp.concatenate([w_high, w_low, w_high], axis=0)
    rate = rate_ref[...]
    env = decay(rate, rows, scale)
    before = None
    for lag in range(shards):
        part = dot(hid_ref[lag * rows : (lag + 1) * rows, :], stacked)
        part = part * (env * jnp.exp(rate * (-float(lag * rows))))
        f_high, f_low = split(part)
        now = forward(front_ref, f_high) + dot(front_ref[:, :rows], f_low)
        for re, im, sign in row_groups(rows):
            here = (now[re], now[im])
            if before is not None:
                here = plus(here, turned((before[re], before[im]), -sign))
            spec_ref[lag, re, :] = here[0].astype(bf16)
            spec_ref[lag, im, :] = here[1].astype(bf16)
        before = now


def own_kernel(
    rows, shards, channels, block, blocks, source_ref, cotan_ref, weight_ref, rate_ref, front_ref, back_ref, trans_ref,
    slope_ref, featt_ref, bias_ref, sums_ref, send_ref, acc_ref,
):
    width = weight_ref.shape[1]

    @pl.when(block == 0)
    def _():
        acc_ref[...] = jnp.zeros_like(acc_ref)

    x0 = forward(front_ref, source_ref[...])
    c0 = forward(front_ref, cotan_ref[...])
    pair = conj_times((x0[:rows], x0[rows:]), (c0[:rows], c0[rows:]))
    high, low = split(jnp.concatenate(pair, axis=0))
    env = decay(rate_ref[...], rows, float(rows * shards) ** -0.5)
    m_high, m_low = split(backward(back_ref, high, low) * env)
    sums = weight_sums(trans_ref[:, :rows], m_high, m_low)
    sums_ref[...] = sums
    send_ref[:, pl.ds(pl.multiple_of(block * width, width), width)] = sums.astype(bf16)
    acc_ref[...] += hidden_sums(m_high, m_low, *split(weight_ref[...]))

    @pl.when(block == blocks - 1)
    def _():
        first = exact_dot(featt_ref[:, :rows], acc_ref[...] * slope_ref[:rows, :])
        put_side(send_ref, channels, fold(bias_ref[...]), first)


def fold(bias):
    return jnp.concatenate([bias[:, i * 128 : (i + 1) * 128] for i in range(bias.shape[1] // 128)], axis=0)


def put_side(pay_ref, channels, bias, first=None):
    half = pay_ref.shape[0] // 2
    pay_ref[:, channels:] = jnp.zeros((2 * half, SIDE), bf16)
    for start, part in zip((0, 128), split(bias)):
        pay_ref[: bias.shape[0], channels + start : channels + start + 128] = part
    if first is not None:
        for start, part in zip((0, 128), split(first)):
            pay_ref[half:, channels + start : channels + start + first.shape[1]] = part


def get_side(pay, channels, lanes, hid_count):
    half = pay.shape[0] // 2
    side = pay[:, channels : channels + 128].astype(f32) + pay[:, channels + 128 :].astype(f32)
    return side[:lanes], side[half:, :hid_count]


def near_kernel(
    rows, shards, block, blocks, rank_ref, x0_ref, c0_ref, x1_ref, c1_ref, spec_ref, weight_ref, rate_ref, front_ref, back_ref,
    trans_ref, featt_ref, slope_ref, own_ref, conv_ref, corr_ref, ahead_ref, sums_ref, first_ref, fields, fast, high_ref,
    low_ref, acc_ref,
):
    rank = rank_ref[0]
    count = shards - 1

    @pl.when(block == 0)
    def _():
        acc_ref[...] = jnp.zeros_like(acc_ref)

    lower = rank == 1
    upper = jnp.where(rank == 2, 1.0, 0.0).astype(f32)
    below_top = jnp.where(rank == shards - 1, 0.0, 1.0).astype(f32)
    side = jnp.where(rank == 2, 1.0, -1.0).astype(f32)
    for index, ref in enumerate((x0_ref, c0_ref, x1_ref, c1_ref)):
        fields[index] = forward(front_ref, ref[...])
    for re, im, sign in row_groups(rows):
        x0, c0, x1, c1 = ((fields[i, re, :], fields[i, im, :]) for i in range(4))
        w0, w1, w2 = ((spec_ref[i, re, :].astype(f32), spec_ref[i, im, :].astype(f32)) for i in range(3))
        ahead = times((w2[0], w2[1] * side), choose(lower, c1, x1))
        for index, value in enumerate(
            (plus(times(w0, x0), times(w1, x1)), plus(conj_times(w0, c0), conj_times(w1, c1)), ahead)
        ):
            fast[index, re, :] = value[0].astype(bf16)
            fast[index, im, :] = value[1].astype(bf16)
        one = plus(scaled(conj_times(x1, c0), below_top), scaled(conj_times(x0, c1), upper))
        two = conj_times(x1, c1)
        for index, value in enumerate((turned(one, sign), plus(one, turned(two, sign)), two)):
            for part, where in zip(value, (re, im)):
                high_ref[index, where, :], low_ref[index, where, :] = split(part)
    conv_ref[...] = backward(back_ref, fast[0])
    corr_ref[...] = backward(back_ref, fast[1])
    ahead_ref[...] = backward(back_ref, fast[2])
    rate = rate_ref[...]
    env = decay(rate, rows, float(rows * shards) ** -0.5)
    parts = []
    for lag in range(count):
        grad = backward(back_ref, high_ref[lag], low_ref[lag])
        parts.append(split(grad * (env * jnp.exp(rate * (-float(lag * rows))))))
    m_high = jnp.concatenate([p[0] for p in parts], axis=0)
    m_low = jnp.concatenate([p[1] for p in parts], axis=0)
    sums_ref[...] = own_ref[...] + weight_sums(trans_ref[:, : count * rows], m_high, m_low)
    w_high, w_low = split(weight_ref[...])
    acc_ref[...] += hidden_sums(m_high, m_low, w_high, w_low)

    @pl.when(block == blocks - 1)
    def _():
        first_ref[...] = exact_dot(
            featt_ref[:, : count * rows], acc_ref[...] * slope_ref[: count * rows, :]
        )


def far_kernel(rows, block, blocks, rank_ref, far_ref, spec_ref, front_ref, back_ref, ahead_ref, part_ref, late_ref):
    side = jnp.where(rank_ref[0] == 2, 1.0, -1.0).astype(f32)
    far = forward(front_ref, far_ref[...])
    far = (far[:rows], far[rows:])
    w2, w3 = ((spec_ref[i, :rows, :].astype(f32), spec_ref[i, rows:, :].astype(f32) * side) for i in range(2))
    ahead = jnp.concatenate(times(w3, far), axis=0).astype(bf16)
    part_ref[...] = (ahead_ref[...] + backward(back_ref, ahead)).astype(bf16)
    late = jnp.concatenate(times(w2, far), axis=0).astype(bf16)
    late_ref[...] = backward(back_ref, late)


def last_kernel(
    rows, shards, channels, block, blocks, after_ref, rank_ref, x1_ref, c1_ref, far_ref, weight_ref, rate_ref, front_ref, back_ref,
    trans_ref, featt_ref, slope_ref, sums_ref, first_ref, own_ref, bias_ref, in_ref, pay_ref, total_ref, acc_ref,
):
    del after_ref
    hid_count, width = weight_ref.shape
    lower = rank_ref[0] == 1
    start = pl.multiple_of(block * width, width)
    here = sums_ref[...] + in_ref[:, pl.ds(start, width)].astype(f32)
    mine = (block < blocks // 2) == lower

    @pl.when(block == 0)
    def _():
        acc_ref[...] = jnp.zeros_like(acc_ref)

    @pl.when(mine)
    def _():
        sign = jnp.where(lower, 1.0, -1.0).astype(f32)
        near = forward(front_ref, jnp.where(lower, x1_ref[...], c1_ref[...]))
        far = forward(front_ref, far_ref[...])
        three = conj_times((near[:rows], near[rows:]), (far[:rows], far[rows:]))
        three = (three[0], three[1] * sign)
        half = rows // 2
        two = jnp.concatenate([three[1][:half], -three[1][half:], -three[0][:half], three[0][half:]], axis=0)
        rate = rate_ref[...]
        env = decay(rate, rows, float(rows * shards) ** -0.5)
        parts = []
        for lag, value in ((shards - 2, two), (shards - 1, jnp.concatenate(three, axis=0))):
            grad = backward(back_ref, *split(value))
            parts.append(split(grad * (env * jnp.exp(rate * (-float(lag * rows))))))
        m_high = jnp.concatenate([p[0] for p in parts], axis=0)
        m_low = jnp.concatenate([p[1] for p in parts], axis=0)
        trans = trans_ref[:, (shards - 2) * rows :]
        pay_ref[:, pl.ds(start, width)] = (here + weight_sums(trans, m_high, m_low)).astype(bf16)
        w_high, w_low = split(weight_ref[...])
        acc_ref[...] += hidden_sums(m_high, m_low, w_high, w_low)

    @pl.when(jnp.logical_not(mine))
    def _():
        pay_ref[:, pl.ds(start, width)] = here.astype(bf16)

    @pl.when(block == blocks - 1)
    def _():
        first = exact_dot(
            featt_ref[:, (shards - 2) * rows :], acc_ref[...] * slope_ref[(shards - 2) * rows :, :]
        )
        lanes = channels // 128
        own_first = get_side(own_ref[...], channels, lanes, hid_count)[1]
        in_bias, in_first = get_side(in_ref[...], channels, lanes, hid_count)
        first = first + first_ref[...] + own_first + in_first
        put_side(pay_ref, channels, fold(bias_ref[...]) + in_bias)
        total_ref[...] = first


def total_kernel(channels, hid_count, part_ref, first_ref, own_ref, come_ref, pay_ref):
    del part_ref, first_ref
    lanes = channels // 128
    pay_ref[:, :channels] = (own_ref[:, :channels].astype(f32) + come_ref[:, :channels].astype(f32)).astype(bf16)
    own, come = (get_side(ref[...], channels, lanes, hid_count)[0] for ref in (own_ref, come_ref))
    put_side(pay_ref, channels, own + come)


def gates_kernel(
    shards, block, blocks, rank_ref, one_ref, two_ref, val_ref, out_ref, skip_ref, conv_ref, corr_ref, late_ref, part_ref,
    grad_one_ref, grad_two_ref, grad_value_ref,
):
    rank = rank_ref[0]

    def mask(wanted):
        return jnp.where(rank == wanted, 1.0, 0.0).astype(f32)

    part = part_ref[...].astype(f32)
    late = late_ref[...]
    one = one_ref[...].astype(f32)
    val = val_ref[...].astype(f32)
    out = out_ref[...].astype(f32)
    skip = skip_ref[...]
    conv = conv_ref[...] + late * mask(2) + part * mask(shards - 1)
    corr = corr_ref[...] + late * mask(1) + part * mask(0)
    grad_two_ref[...] = (out * (conv + skip * (one * val))).astype(bf16)
    mid = corr + skip * (out * two_ref[...].astype(f32))
    grad_one_ref[...] = (mid * val).astype(bf16)
    grad_value_ref[...] = (mid * one).astype(bf16)


def finish_kernel(
    channels, shards, rank_ref, own_ref, come_ref, first_ref, first_come_ref, second_out, first_out, bias_out, second,
    first, bias, sems,
):
    rank = rank_ref[0]
    inner = jnp.logical_and(rank > 0, rank < shards - 1)
    lanes = channels // 128
    copies = [
        pltpu.make_async_copy(held, out, sems.at[i])
        for i, (held, out) in enumerate(((second, second_out), (first, first_out), (bias, bias_out)))
    ]
    picked = jnp.where(inner, own_ref[...], come_ref[...])
    second[...] = picked[:, :channels].astype(f32)
    copies[0].start()
    first[...] = jnp.where(inner, first_ref[...], first_come_ref[...])
    copies[1].start()
    rows = get_side(picked, channels, lanes, first.shape[1])[0]
    for i in range(lanes):
        bias[:, i * 128 : (i + 1) * 128] = rows[i : i + 1]
    copies[2].start()
    for copy in copies:
        copy.wait()


def few_shards_body(
    x_one, x_two, values, grad_out, first_weight, second_weight, skip_bias, decay_rate
):
    rows, channels = x_one.shape
    shards = lax.axis_size("ctx")
    feat_count, hid_count = first_weight.shape
    seq_len = rows * shards
    double = 2 * rows
    width = min(512, channels)
    blocks = channels // width
    rank = lax.axis_index("ctx").astype(jnp.int32).reshape(1)
    front, back = block_tables(rows)
    feats = feature_table(seq_len)
    featt = np.ascontiguousarray(feats.T)
    skip_row = skip_bias.reshape(1, channels)
    rate_row = decay_rate.reshape(1, channels)
    smem = pl.BlockSpec(memory_space=pltpu.SMEM)
    vmem = pl.BlockSpec(memory_space=pltpu.VMEM)
    anywhere = pl.BlockSpec(memory_space=pl.ANY)
    mebi = 1024 * 1024

    def shape(*dims, dtype=f32):
        return jax.ShapeDtypeStruct(dims, dtype)

    def call(kernel, name, units, out_shape, in_specs, out_specs=None, scratch=(), limit=16, aliases={}):
        return pl.pallas_call(
            kernel,
            in_specs=in_specs,
            out_specs=out_specs if out_specs is not None else [vmem] * len(out_shape),
            out_shape=out_shape,
            scratch_shapes=scratch,
            input_output_aliases=aliases,
            compiler_params=pltpu.CompilerParams(vmem_limit_bytes=limit * mebi),
            cost_estimate=pl.CostEstimate(
                flops=2 * units * double * double * channels, bytes_accessed=rows * channels, transcendentals=0
            ),
            name=name,
        )

    def move(array, pairs):
        return lax.ppermute(array, "ctx", pairs)

    up = [(i, i + 1) for i in range(shards - 1)]
    down = [(i + 1, i) for i in range(shards - 1)]
    inward = [(0, 1), (shards - 1, shards - 2)]
    outward = [(1, 0), (shards - 2, shards - 1)]
    across = [(1, 2), (2, 1)]
    pay_shape = (hid_count, channels + SIDE)
    block_bf16 = shape(rows, channels, dtype=bf16)
    block_f32 = shape(rows, channels)

    row_step = max(rows // 2, 16)
    gate_rows = pl.BlockSpec((row_step, channels), lambda i: (i, 0))
    x0, c0, edge, bias = pl.pallas_call(
        products_kernel,
        grid=(rows // row_step,),
        in_specs=[smem] + [gate_rows] * 4,
        out_specs=[gate_rows] * 3 + [pl.BlockSpec((1, channels), lambda i: (0, 0))],
        out_shape=[block_bf16] * 3 + [shape(1, channels)],
        compiler_params=pltpu.CompilerParams(vmem_limit_bytes=64 * mebi),
        name="products",
    )(rank, x_one, x_two, values, grad_out)
    x1 = move(x0, up)
    c1 = move(c0, down)

    spec, trans, slope, edge = call(
        functools.partial(filters_kernel, rows, shards, blocks, width), "filters", 8,
        [
            shape(shards, double, channels, dtype=bf16), shape(2 * hid_count, seq_len, dtype=bf16),
            shape(seq_len, hid_count), block_bf16,
        ],
        [pl.BlockSpec(memory_space=pltpu.HBM)] * 6,
        out_specs=[vmem] * 3 + [pl.BlockSpec(memory_space=pltpu.HBM)],
        scratch=[
            pltpu.VMEM((seq_len, feat_count), f32), pltpu.VMEM((feat_count, hid_count), f32),
            pltpu.VMEM((hid_count, channels), f32), pltpu.VMEM((1, channels), f32), pltpu.VMEM((double, double), bf16),
            pltpu.VMEM((seq_len, 3 * hid_count), bf16), pltpu.SemaphoreType.DMA((5,)),
        ],
        aliases={5: 3},
    )(feats, first_weight, second_weight, rate_row, front, edge)
    far = move(edge, [(0, 2), (shards - 1, shards - 3)])

    own, send = call(
        looped(
            functools.partial(own_kernel, rows, shards, channels),
            (ROWS, ROWS, ROWS, ROWS, None, None, None, None, None, None, ROWS),
            blocks, width,
        ),
        "own_pair", 8,
        [shape(hid_count, channels), shape(*pay_shape, dtype=bf16)],
        [vmem] * 10,
        scratch=[pltpu.VMEM((rows, hid_count), f32)],
    )(x0, c0, second_weight, rate_row, front, back, trans, slope, featt, bias)
    come = move(send, inward)

    conv, corr, ahead, sums, first = call(
        looped(
            functools.partial(near_kernel, rows, shards),
            (None, ROWS, ROWS, ROWS, ROWS, CUBE, ROWS, ROWS, None, None, None, None, None, ROWS, ROWS, ROWS, ROWS, ROWS),
            blocks, width,
        ),
        "near_blocks", 20,
        [block_f32] * 3 + [shape(hid_count, channels), shape(feat_count, hid_count)],
        [smem] + [vmem] * 13,
        scratch=[
            pltpu.VMEM((4, double, width), f32),
            pltpu.VMEM((3, double, width), bf16),
            pltpu.VMEM((shards - 1, double, width), bf16),
            pltpu.VMEM((shards - 1, double, width), bf16),
            pltpu.VMEM(((shards - 1) * rows, hid_count), f32),
        ],
    )(rank, x0, c0, x1, c1, spec, second_weight, rate_row, front, back, trans, featt, slope, own)

    part, late = call(
        looped(
            functools.partial(far_kernel, rows),
            (None, ROWS, (slice(2, 4), slice(None)), None, None, ROWS, ROWS, ROWS),
            blocks, width,
        ),
        "far_block", 1,
        [block_bf16, block_f32],
        [smem] + [vmem] * 5,
    )(rank, far, spec, front, back, ahead)
    part_come = move(part, outward)

    pay, first = call(
        looped(
            functools.partial(last_kernel, rows, shards, channels),
            (None, None, ROWS, ROWS, ROWS, ROWS, ROWS, None, None, None, None, None, ROWS),
            blocks, width,
        ),
        "last_pair", 1,
        [shape(*pay_shape, dtype=bf16), shape(feat_count, hid_count)],
        [anywhere, smem] + [vmem] * 15,
        scratch=[pltpu.VMEM((2 * rows, hid_count), f32)],
    )(late, rank, x1, c1, far, second_weight, rate_row, front, back, trans, featt, slope, sums, first, send, bias, come)
    pay_come = move(pay, across)
    group = lax.axis_size(("ch", "sub"))
    bit = 1
    while bit < group:
        first = first + lax.ppermute(first, ("ch", "sub"), [(i, i ^ bit) for i in range(group)])
        bit *= 2

    (total,) = call(
        functools.partial(total_kernel, channels, hid_count), "total", 0,
        [shape(*pay_shape, dtype=bf16)],
        [anywhere] * 2 + [vmem] * 2,
    )(part_come, first, pay, pay_come)
    total_come = move(total, outward)
    first = first + move(first, across)
    first_come = move(first, outward)

    grad_one, grad_two, grad_value = call(
        looped(
            functools.partial(gates_kernel, shards), (None,) + (ROWS,) * 12, blocks, width
        ),
        "gates", 0,
        [block_bf16] * 3,
        [smem] + [vmem] * 9,
    )(rank, x_one, x_two, values, grad_out, skip_row, conv, corr, late, part_come)

    outs = [shape(hid_count, channels), shape(feat_count, hid_count), shape(1, channels)]
    grad_second, grad_first, grad_bias = call(
        functools.partial(finish_kernel, channels, shards), "finish", 0,
        outs,
        [smem] + [vmem] * 4,
        out_specs=[anywhere] * 3,
        scratch=[pltpu.VMEM(o.shape, f32) for o in outs] + [pltpu.SemaphoreType.DMA((3,))],
    )(rank, total, total_come, first, first_come)
    return (grad_one, grad_two, grad_value, grad_first, grad_second, grad_bias.reshape(channels))


def solution(mesh):
    in_specs = (
        P(("parts", "ctx"), ("ch", "sub")),
        P(("parts", "ctx"), ("ch", "sub")),
        P(("parts", "ctx"), ("ch", "sub")),
        P(("parts", "ctx"), ("ch", "sub")),
        P(),
        P(None, ("ch", "sub")),
        P(("ch", "sub")),
        P(("ch", "sub")),
    )
    out_specs = (
        P(("parts", "ctx"), ("ch", "sub")),
        P(("parts", "ctx"), ("ch", "sub")),
        P(("parts", "ctx"), ("ch", "sub")),
        P("parts", None),
        P("parts", ("ch", "sub")),
        P(("parts", "ch", "sub")),
    )
    body = few_shards_body if mesh.shape["ctx"] == 4 else many_shards_body
    return jax.shard_map(body, mesh=mesh, in_specs=in_specs, out_specs=out_specs, check_vma=False)
```

```python
import functools
import math

import jax
import jax.numpy as jnp
import numpy as np
from jax import lax
from jax.experimental import pallas as pl
from jax.experimental.pallas import tpu as pltpu
from jax.sharding import PartitionSpec as P

band_steps = (1763, 1201, 811, 547, 367, 251, 167, 113, 79, 53, 37, 23, 17, 11, 7, 3)
highest = lax.Precision.HIGHEST
f32 = jnp.float32
bf16 = jnp.bfloat16


def features(positions):
    multiplier = jnp.array(band_steps, dtype=jnp.int32)
    phase = positions[:, None] * multiplier[None, :] % 4096
    angle = phase.astype(jnp.float32) * (2.0 * math.pi / 4096.0)
    return jnp.concatenate([jnp.cos(angle), jnp.sin(angle)], axis=1)


def tables(out_count, in_count, modulus, sign_value):
    row_index = lax.broadcasted_iota(jnp.int32, (out_count, in_count), 0)
    col_index = lax.broadcasted_iota(jnp.int32, (out_count, in_count), 1)
    angle = (row_index * col_index % modulus).astype(jnp.float32) * (2.0 * math.pi / modulus)
    return (jnp.cos(angle), sign_value * jnp.sin(angle))


def twiddle(spec_re, spec_im, freq_count, span, modulus, sign_value):
    freq_index = lax.broadcasted_iota(jnp.int32, (freq_count, span), 0)
    pos_index = lax.broadcasted_iota(jnp.int32, (freq_count, span), 1)
    angle = (freq_index * pos_index % modulus).astype(jnp.float32) * (2.0 * math.pi / modulus)
    factor_re = jnp.cos(angle)[None, None, :, :]
    factor_im = (sign_value * jnp.sin(angle))[None, None, :, :]
    return (spec_re * factor_re - spec_im * factor_im, spec_re * factor_im + spec_im * factor_re)


def contract(kernel, array):
    return jnp.einsum(
        "lj,mckj->mckl", kernel, array, precision=highest, preferred_element_type=jnp.float32
    )


def along_positions(spec_re, spec_im, kernel_re, kernel_im):
    return (
        contract(kernel_re, spec_re) - contract(kernel_im, spec_im),
        contract(kernel_re, spec_im) + contract(kernel_im, spec_re),
    )


def many_shards_body(
    x_one, x_two, values, grad_out, first_weight, second_weight, skip_bias, decay_rate
):
    row_count, chan_count = x_one.shape
    shards = lax.axis_size("ctx")
    rank = lax.axis_index("ctx")
    seq_len = row_count * shards
    total = 2 * seq_len
    narrow = chan_count // shards
    chan_weight = lax.dynamic_slice_in_dim(second_weight, rank * narrow, narrow, 1)
    chan_rate = lax.dynamic_slice_in_dim(decay_rate, rank * narrow, narrow, 0)
    source = x_one.astype(jnp.float32) * values.astype(jnp.float32)
    cotan = grad_out.astype(jnp.float32) * x_two.astype(jnp.float32)
    spread = lax.all_to_all(
        jnp.stack([source.T, cotan.T])[:, :, None, :],
        "ctx",
        split_axis=1,
        concat_axis=2,
        tiled=True,
    )
    far_source = spread[0]
    far_cotan = spread[1]
    positions = jnp.arange(seq_len, dtype=jnp.int32)
    feats = features(positions)
    pre_act = jnp.dot(feats, first_weight, precision=highest, preferred_element_type=jnp.float32)
    hidden = jnp.sin(pre_act)
    envelope = jnp.exp(-chan_rate[:, None] * positions.astype(jnp.float32)[None, :]) * float(
        seq_len
    ) ** (-0.5)
    filt = (
        jnp.einsum(
            "th,hc->ct", hidden, chan_weight, precision=highest, preferred_element_type=jnp.float32
        )
        * envelope
    )
    filt_blocks = filt.reshape(narrow, shards, row_count)
    fields = jnp.stack([far_source, far_cotan])

    def first_section(kernel):
        field_part = jnp.einsum(
            "kn,mcnj->mckj", kernel, fields, precision=highest, preferred_element_type=jnp.float32
        )
        filter_part = jnp.einsum(
            "kn,cnj->ckj",
            kernel,
            filt_blocks,
            precision=highest,
            preferred_element_type=jnp.float32,
        )
        return jnp.concatenate([field_part, filter_part[None]], axis=0)

    first_re, first_im = tables(2 * shards, shards, 2 * shards, -1.0)
    spec_re, spec_im = (first_section(first_re), first_section(first_im))
    spec_re, spec_im = twiddle(spec_re, spec_im, 2 * shards, row_count, total, -1.0)
    fwd_re, fwd_im = tables(row_count, row_count, row_count, -1.0)
    spec_re, spec_im = along_positions(spec_re, spec_im, fwd_re, fwd_im)
    source_re, source_im = (spec_re[0], spec_im[0])
    cotan_re, cotan_im = (spec_re[1], spec_im[1])
    filter_re, filter_im = (spec_re[2], spec_im[2])
    prod_re = jnp.stack(
        [
            source_re * filter_re - source_im * filter_im,
            cotan_re * filter_re + cotan_im * filter_im,
            cotan_re * source_re + cotan_im * source_im,
        ]
    )
    prod_im = jnp.stack(
        [
            source_re * filter_im + source_im * filter_re,
            cotan_im * filter_re - cotan_re * filter_im,
            cotan_im * source_re - cotan_re * source_im,
        ]
    )
    back_re, back_im = tables(row_count, row_count, row_count, 1.0)
    prod_re, prod_im = along_positions(prod_re, prod_im, back_re, back_im)
    prod_re, prod_im = twiddle(prod_re, prod_im, 2 * shards, row_count, total, 1.0)
    last_re, last_im = tables(shards, 2 * shards, 2 * shards, 1.0)
    field_out = jnp.einsum(
        "nk,mckj->mcnj", last_re, prod_re[:2], precision=highest, preferred_element_type=jnp.float32
    ) - jnp.einsum(
        "nk,mckj->mcnj", last_im, prod_im[:2], precision=highest, preferred_element_type=jnp.float32
    )
    field_out = field_out * (1.0 / total)
    filt_grad = jnp.einsum(
        "nk,ckj->cnj", last_re, prod_re[2], precision=highest, preferred_element_type=jnp.float32
    ) - jnp.einsum(
        "nk,ckj->cnj", last_im, prod_im[2], precision=highest, preferred_element_type=jnp.float32
    )
    filt_grad = (filt_grad * (1.0 / total)).reshape(narrow, seq_len)
    modulated = filt_grad * envelope
    weight_part = jnp.einsum(
        "th,ct->hc", hidden, modulated, precision=highest, preferred_element_type=jnp.float32
    )
    hidden_grad = jnp.einsum(
        "ct,hc->th", modulated, chan_weight, precision=highest, preferred_element_type=jnp.float32
    )
    first_part = jnp.dot(
        feats.T,
        hidden_grad * jnp.cos(pre_act),
        precision=highest,
        preferred_element_type=jnp.float32,
    )
    grad_first = lax.psum(first_part, ("ctx", "ch", "sub"))
    returned = lax.all_to_all(
        field_out.astype(jnp.bfloat16), "ctx", split_axis=2, concat_axis=1, tiled=True
    ).astype(field_out.dtype)
    conv_part = returned[0, :, 0, :].T
    corr_part = returned[1, :, 0, :].T
    grad_two = (grad_out.astype(jnp.float32) * (conv_part + skip_bias[None, :] * source)).astype(
        jnp.bfloat16
    )
    grad_mid = corr_part + skip_bias[None, :] * cotan
    grad_one = (grad_mid * values.astype(jnp.float32)).astype(jnp.bfloat16)
    grad_value = (grad_mid * x_one.astype(jnp.float32)).astype(jnp.bfloat16)
    grad_bias = lax.psum(jnp.sum(source * cotan, axis=0), "ctx")
    grad_second = lax.all_gather(weight_part, "ctx", axis=1, tiled=True)
    return (grad_one, grad_two, grad_value, grad_first, grad_second, grad_bias)


STEP = 16
SIDE = 256


def halves(array):
    array = np.asarray(array, np.float32)
    high = array.astype(bf16)
    low = (array - high.astype(np.float32)).astype(bf16)
    return high, low


def block_tables(rows):
    freq = np.concatenate([np.arange(0, rows, 2), np.arange(1, rows, 2)])
    phase = (2 * freq + 1)[:, None] * np.arange(rows)[None, :] % (4 * rows)
    angle = phase * (2.0 * np.pi / (4 * rows))
    forward = np.concatenate([np.cos(angle), -np.sin(angle)], axis=0)
    front = np.ascontiguousarray(np.concatenate(halves(forward), axis=1))
    back = np.ascontiguousarray(np.concatenate(halves(forward.T / rows), axis=0))
    return front, back


def feature_table(seq_len):
    phase = np.arange(seq_len)[:, None] * np.array(band_steps)[None, :] % 4096
    angle = phase * (2.0 * np.pi / 4096.0)
    return np.concatenate([np.cos(angle), np.sin(angle)], axis=1).astype(np.float32)


def split(array):
    high = array.astype(bf16)
    return high, (array - high.astype(f32)).astype(bf16)


def dot(left, right):
    return jnp.dot(left, right, preferred_element_type=f32)


def exact_dot(left, right):
    return jnp.dot(left, right, precision=highest, preferred_element_type=f32)


def dot_across(left, right):
    return lax.dot_general(left, right, (((1,), (1,)), ((), ())), preferred_element_type=f32)


def decay(rate, rows, scale):
    place = lax.broadcasted_iota(jnp.int32, (rows, rate.shape[1]), 0)
    return jnp.exp(-place.astype(f32) * rate) * scale


def times(a, b):
    return a[0] * b[0] - a[1] * b[1], a[0] * b[1] + a[1] * b[0]


def conj_times(a, b):
    return a[0] * b[0] + a[1] * b[1], a[0] * b[1] - a[1] * b[0]


def plus(a, b):
    return a[0] + b[0], a[1] + b[1]


def scaled(a, factor):
    return a[0] * factor, a[1] * factor


def choose(condition, a, b):
    return jnp.where(condition, a[0], b[0]), jnp.where(condition, a[1], b[1])


def turned(a, sign):
    return (a[1], -a[0]) if sign > 0 else (-a[1], a[0])


def forward(front_ref, block):
    return dot(front_ref[...], jnp.concatenate([block, block], axis=0))


def backward(back_ref, high, low=None):
    both = dot(back_ref[...], high)
    rows = both.shape[0] // 2
    out = both[:rows] + both[rows:]
    return out if low is None else out + dot(back_ref[:rows], low)


def row_groups(rows):
    for step in range(rows // STEP):
        sign = 1 if step * STEP < rows // 2 else -1
        yield slice(step * STEP, (step + 1) * STEP), slice(rows + step * STEP, rows + (step + 1) * STEP), sign


def weight_sums(trans, m_high, m_low):
    both = dot(trans, m_high)
    count = both.shape[0] // 2
    return both[:count] + both[count:] + dot(trans[:count], m_low)


def hidden_sums(m_high, m_low, w_high, w_low):
    left = jnp.concatenate([m_high, m_high, m_low], axis=1)
    right = jnp.concatenate([w_high, w_low, w_high], axis=1)
    return dot_across(left, right)


def looped(kernel, kinds, blocks, width):
    def over_strips(*refs):
        def step(block, carry):
            cols = pl.ds(pl.multiple_of(block * width, width), width)
            views = [
                ref if kind is None else ref.at[(*kind, cols)]
                for ref, kind in zip(refs, kinds + (None,) * (len(refs) - len(kinds)))
            ]
            kernel(block, blocks, *views)
            return carry

        lax.fori_loop(0, blocks, step, 0)

    return over_strips


ROWS = (slice(None),)
CUBE = (slice(None), slice(None))


def products_kernel(rank_ref, one_ref, two_ref, val_ref, out_ref, source_ref, cotan_ref, edge_ref, bias_ref):
    source = one_ref[...].astype(f32) * val_ref[...].astype(f32)
    cotan = out_ref[...].astype(f32) * two_ref[...].astype(f32)
    source_ref[...] = source.astype(bf16)
    cotan_ref[...] = cotan.astype(bf16)
    edge_ref[...] = jnp.where(rank_ref[0] == 0, source, cotan).astype(bf16)
    part = jnp.sum(source * cotan, axis=0, keepdims=True)

    @pl.when(pl.program_id(0) == 0)
    def _():
        bias_ref[...] = part

    @pl.when(pl.program_id(0) > 0)
    def _():
        bias_ref[...] += part


def sin_cos(angle):
    turns = jnp.floor(angle * (2.0 / math.pi) + 0.5)
    rest = ((angle - turns * 1.5703125) - turns * 4.837512969970703e-4) - turns * 7.54978995489188e-8
    square = rest * rest
    sine = rest + rest * square * (
        -1.6666654611e-1 + square * (8.3321608736e-3 + square * -1.9515295891e-4)
    )
    cosine = 1.0 - 0.5 * square + square * square * (
        4.166664568298827e-2 + square * (-1.388731625493765e-3 + square * 2.443315711809948e-5)
    )
    quarter = turns.astype(jnp.int32)
    odd = (quarter & 1) == 1
    sin_sign = jnp.where((quarter & 2) == 2, -1.0, 1.0).astype(f32)
    cos_sign = jnp.where(((quarter + 1) & 2) == 2, -1.0, 1.0).astype(f32)
    return jnp.where(odd, cosine, sine) * sin_sign, jnp.where(odd, sine, cosine) * cos_sign


def filters_kernel(rows, shards, blocks, width, *refs):
    inputs, passed, outputs, held, (hid_ref, sems) = refs[:5], refs[5:6], refs[6:10], refs[10:15], refs[15:]
    del passed
    feats_ref, first_ref, weight_ref, rate_ref, front_ref = held
    spec_ref, trans_ref, slope_ref, _ = outputs
    copies = [pltpu.make_async_copy(far, near, sems.at[i]) for i, (far, near) in enumerate(zip(inputs, held))]
    for copy in copies:
        copy.start()
    hid_count = first_ref.shape[1]
    copies[0].wait()
    copies[1].wait()
    hidden, slope = sin_cos(exact_dot(feats_ref[...], first_ref[...]))
    slope_ref[...] = slope
    high, low = split(hidden)
    hid_ref[...] = jnp.concatenate([high, high, low], axis=1)
    turned_over = jnp.concatenate([hidden, slope], axis=1).T[:hid_count]
    trans_ref[...] = jnp.concatenate(split(turned_over), axis=0)
    for copy in copies[2:]:
        copy.wait()
    strips = looped(
        functools.partial(filter_strip, rows, shards), (None, ROWS, ROWS, None, CUBE), blocks, width
    )
    strips(hid_ref, weight_ref, rate_ref, front_ref, spec_ref)


def filter_strip(rows, shards, block, blocks, hid_ref, weight_ref, rate_ref, front_ref, spec_ref):
    scale = float(rows * shards) ** -0.5
    w_high, w_low = split(weight_ref[...])
    stacked = jnp.concatenate([w_high, w_low, w_high], axis=0)
    rate = rate_ref[...]
    env = decay(rate, rows, scale)
    before = None
    for lag in range(shards):
        part = dot(hid_ref[lag * rows : (lag + 1) * rows, :], stacked)
        part = part * (env * jnp.exp(rate * (-float(lag * rows))))
        f_high, f_low = split(part)
        now = forward(front_ref, f_high) + dot(front_ref[:, :rows], f_low)
        for re, im, sign in row_groups(rows):
            here = (now[re], now[im])
            if before is not None:
                here = plus(here, turned((before[re], before[im]), -sign))
            spec_ref[lag, re, :] = here[0].astype(bf16)
            spec_ref[lag, im, :] = here[1].astype(bf16)
        before = now


def own_kernel(
    rows, shards, channels, blocks, width, trans_out, slope_out, source_ref, cotan_ref, weight_ref, rate_ref, front_ref,
    back_ref, featt_ref, bias_ref, sums_ref, send_ref, trans_ref, slope_ref, acc_ref, sems,
):
    copies = [
        pltpu.make_async_copy(trans_out, trans_ref, sems.at[0]),
        pltpu.make_async_copy(slope_out, slope_ref, sems.at[1]),
    ]
    for copy in copies:
        copy.start()
    acc_ref[...] = jnp.zeros_like(acc_ref)
    copies[0].wait()
    strips = looped(
        functools.partial(own_strip, rows, shards),
        (ROWS, ROWS, ROWS, ROWS, None, None, None, ROWS, ROWS, None), blocks, width,
    )
    strips(
        source_ref, cotan_ref, weight_ref, rate_ref, front_ref, back_ref, trans_ref, sums_ref, send_ref, acc_ref
    )
    copies[1].wait()
    first = exact_dot(featt_ref[:, :rows], acc_ref[...] * slope_ref[:rows, :])
    put_side(send_ref, channels, fold(bias_ref[...]), first)


def own_strip(
    rows, shards, block, blocks, source_ref, cotan_ref, weight_ref, rate_ref, front_ref, back_ref, trans_ref, sums_ref,
    send_ref, acc_ref,
):
    x0 = forward(front_ref, source_ref[...])
    c0 = forward(front_ref, cotan_ref[...])
    pair = conj_times((x0[:rows], x0[rows:]), (c0[:rows], c0[rows:]))
    high, low = split(jnp.concatenate(pair, axis=0))
    env = decay(rate_ref[...], rows, float(rows * shards) ** -0.5)
    m_high, m_low = split(backward(back_ref, high, low) * env)
    sums = weight_sums(trans_ref[:, :rows], m_high, m_low)
    sums_ref[...] = sums
    send_ref[...] = sums.astype(bf16)
    acc_ref[...] += hidden_sums(m_high, m_low, *split(weight_ref[...]))


def fold(bias):
    return jnp.concatenate([bias[:, i * 128 : (i + 1) * 128] for i in range(bias.shape[1] // 128)], axis=0)


def put_side(pay_ref, channels, bias, first=None):
    half = pay_ref.shape[0] // 2
    pay_ref[:, channels:] = jnp.zeros((2 * half, SIDE), bf16)
    for start, part in zip((0, 128), split(bias)):
        pay_ref[: bias.shape[0], channels + start : channels + start + 128] = part
    if first is not None:
        for start, part in zip((0, 128), split(first)):
            pay_ref[half:, channels + start : channels + start + first.shape[1]] = part


def get_side(pay, channels, lanes, hid_count):
    half = pay.shape[0] // 2
    side = pay[:, channels : channels + 128].astype(f32) + pay[:, channels + 128 :].astype(f32)
    return side[:lanes], side[half:, :hid_count]


def near_kernel(
    rows, shards, block, blocks, rank_ref, x0_ref, c0_ref, x1_ref, c1_ref, spec_ref, weight_ref, rate_ref, front_ref, back_ref,
    trans_ref, featt_ref, slope_ref, own_ref, conv_ref, corr_ref, ahead_ref, sums_ref, first_ref, fields, fast, high_ref,
    low_ref, acc_ref,
):
    rank = rank_ref[0]
    count = shards - 1

    @pl.when(block == 0)
    def _():
        acc_ref[...] = jnp.zeros_like(acc_ref)

    lower = rank == 1
    upper = jnp.where(rank == 2, 1.0, 0.0).astype(f32)
    below_top = jnp.where(rank == shards - 1, 0.0, 1.0).astype(f32)
    side = jnp.where(rank == 2, 1.0, -1.0).astype(f32)
    for index, ref in enumerate((x0_ref, c0_ref, x1_ref, c1_ref)):
        fields[index] = forward(front_ref, ref[...])
    for re, im, sign in row_groups(rows):
        x0, c0, x1, c1 = ((fields[i, re, :], fields[i, im, :]) for i in range(4))
        w0, w1, w2 = ((spec_ref[i, re, :].astype(f32), spec_ref[i, im, :].astype(f32)) for i in range(3))
        ahead = times((w2[0], w2[1] * side), choose(lower, c1, x1))
        for index, value in enumerate(
            (plus(times(w0, x0), times(w1, x1)), plus(conj_times(w0, c0), conj_times(w1, c1)), ahead)
        ):
            fast[index, re, :] = value[0].astype(bf16)
            fast[index, im, :] = value[1].astype(bf16)
        one = plus(scaled(conj_times(x1, c0), below_top), scaled(conj_times(x0, c1), upper))
        two = conj_times(x1, c1)
        for index, value in enumerate((turned(one, sign), plus(one, turned(two, sign)), two)):
            for part, where in zip(value, (re, im)):
                high_ref[index, where, :], low_ref[index, where, :] = split(part)
    conv_ref[...] = backward(back_ref, fast[0])
    corr_ref[...] = backward(back_ref, fast[1])
    ahead_ref[...] = backward(back_ref, fast[2])
    rate = rate_ref[...]
    env = decay(rate, rows, float(rows * shards) ** -0.5)
    parts = []
    for lag in range(count):
        grad = backward(back_ref, high_ref[lag], low_ref[lag])
        parts.append(split(grad * (env * jnp.exp(rate * (-float(lag * rows))))))
    m_high = jnp.concatenate([p[0] for p in parts], axis=0)
    m_low = jnp.concatenate([p[1] for p in parts], axis=0)
    sums_ref[...] = own_ref[...] + weight_sums(trans_ref[:, : count * rows], m_high, m_low)
    w_high, w_low = split(weight_ref[...])
    acc_ref[...] += hidden_sums(m_high, m_low, w_high, w_low)

    @pl.when(block == blocks - 1)
    def _():
        first_ref[...] = exact_dot(
            featt_ref[:, : count * rows], acc_ref[...] * slope_ref[: count * rows, :]
        )


def far_kernel(rows, block, blocks, rank_ref, far_ref, spec_ref, front_ref, back_ref, ahead_ref, part_ref, late_ref):
    side = jnp.where(rank_ref[0] == 2, 1.0, -1.0).astype(f32)
    far = forward(front_ref, far_ref[...])
    far = (far[:rows], far[rows:])
    w2, w3 = ((spec_ref[i, :rows, :].astype(f32), spec_ref[i, rows:, :].astype(f32) * side) for i in range(2))
    ahead = jnp.concatenate(times(w3, far), axis=0).astype(bf16)
    part_ref[...] = (ahead_ref[...] + backward(back_ref, ahead)).astype(bf16)
    late = jnp.concatenate(times(w2, far), axis=0).astype(bf16)
    late_ref[...] = backward(back_ref, late)


def last_kernel(
    rows, shards, channels, block, blocks, after_ref, rank_ref, x1_ref, c1_ref, far_ref, weight_ref, rate_ref, front_ref, back_ref,
    trans_ref, featt_ref, slope_ref, sums_ref, first_ref, own_ref, bias_ref, in_ref, pay_ref, total_ref, acc_ref,
):
    del after_ref
    hid_count, width = weight_ref.shape
    lower = rank_ref[0] == 1
    start = pl.multiple_of(block * width, width)
    here = sums_ref[...] + in_ref[:, pl.ds(start, width)].astype(f32)
    mine = (block < blocks // 2) == lower

    @pl.when(block == 0)
    def _():
        acc_ref[...] = jnp.zeros_like(acc_ref)

    @pl.when(mine)
    def _():
        sign = jnp.where(lower, 1.0, -1.0).astype(f32)
        near = forward(front_ref, jnp.where(lower, x1_ref[...], c1_ref[...]))
        far = forward(front_ref, far_ref[...])
        three = conj_times((near[:rows], near[rows:]), (far[:rows], far[rows:]))
        three = (three[0], three[1] * sign)
        half = rows // 2
        two = jnp.concatenate([three[1][:half], -three[1][half:], -three[0][:half], three[0][half:]], axis=0)
        rate = rate_ref[...]
        env = decay(rate, rows, float(rows * shards) ** -0.5)
        parts = []
        for lag, value in ((shards - 2, two), (shards - 1, jnp.concatenate(three, axis=0))):
            grad = backward(back_ref, *split(value))
            parts.append(split(grad * (env * jnp.exp(rate * (-float(lag * rows))))))
        m_high = jnp.concatenate([p[0] for p in parts], axis=0)
        m_low = jnp.concatenate([p[1] for p in parts], axis=0)
        trans = trans_ref[:, (shards - 2) * rows :]
        pay_ref[:, pl.ds(start, width)] = (here + weight_sums(trans, m_high, m_low)).astype(bf16)
        w_high, w_low = split(weight_ref[...])
        acc_ref[...] += hidden_sums(m_high, m_low, w_high, w_low)

    @pl.when(jnp.logical_not(mine))
    def _():
        pay_ref[:, pl.ds(start, width)] = here.astype(bf16)

    @pl.when(block == blocks - 1)
    def _():
        first = exact_dot(
            featt_ref[:, (shards - 2) * rows :], acc_ref[...] * slope_ref[(shards - 2) * rows :, :]
        )
        lanes = channels // 128
        own_first = get_side(own_ref[...], channels, lanes, hid_count)[1]
        in_bias, in_first = get_side(in_ref[...], channels, lanes, hid_count)
        first = first + first_ref[...] + own_first + in_first
        put_side(pay_ref, channels, fold(bias_ref[...]) + in_bias)
        total_ref[...] = first


def total_kernel(channels, hid_count, part_ref, own_ref, come_ref, first_ref, first_come_ref, pay_ref):
    del part_ref
    lanes = channels // 128
    pay_ref[:, :channels] = (own_ref[:, :channels].astype(f32) + come_ref[:, :channels].astype(f32)).astype(bf16)
    own, come = (get_side(ref[...], channels, lanes, hid_count)[0] for ref in (own_ref, come_ref))
    put_side(pay_ref, channels, own + come, first_ref[...] + first_come_ref[...])


def gates_kernel(
    shards, block, blocks, rank_ref, one_ref, two_ref, val_ref, out_ref, skip_ref, conv_ref, corr_ref, late_ref, part_ref,
    grad_one_ref, grad_two_ref, grad_value_ref,
):
    rank = rank_ref[0]

    def mask(wanted):
        return jnp.where(rank == wanted, 1.0, 0.0).astype(f32)

    part = part_ref[...].astype(f32)
    late = late_ref[...]
    one = one_ref[...].astype(f32)
    val = val_ref[...].astype(f32)
    out = out_ref[...].astype(f32)
    skip = skip_ref[...]
    conv = conv_ref[...] + late * mask(2) + part * mask(shards - 1)
    corr = corr_ref[...] + late * mask(1) + part * mask(0)
    grad_two_ref[...] = (out * (conv + skip * (one * val))).astype(bf16)
    mid = corr + skip * (out * two_ref[...].astype(f32))
    grad_one_ref[...] = (mid * val).astype(bf16)
    grad_value_ref[...] = (mid * one).astype(bf16)


def finish_kernel(
    channels, shards, rank_ref, own_ref, come_ref, second_out, first_out, bias_out, second, first, bias, sems
):
    rank = rank_ref[0]
    inner = jnp.logical_and(rank > 0, rank < shards - 1)
    lanes = channels // 128
    copies = [
        pltpu.make_async_copy(held, out, sems.at[i])
        for i, (held, out) in enumerate(((second, second_out), (first, first_out), (bias, bias_out)))
    ]
    picked = jnp.where(inner, own_ref[...], come_ref[...])
    second[...] = picked[:, :channels].astype(f32)
    copies[0].start()
    rows, first[...] = get_side(picked, channels, lanes, first.shape[1])
    copies[1].start()
    for i in range(lanes):
        bias[:, i * 128 : (i + 1) * 128] = rows[i : i + 1]
    copies[2].start()
    for copy in copies:
        copy.wait()


def few_shards_body(
    x_one, x_two, values, grad_out, first_weight, second_weight, skip_bias, decay_rate
):
    rows, channels = x_one.shape
    shards = lax.axis_size("ctx")
    feat_count, hid_count = first_weight.shape
    seq_len = rows * shards
    double = 2 * rows
    width = min(512, channels)
    blocks = channels // width
    rank = lax.axis_index("ctx").astype(jnp.int32).reshape(1)
    front, back = block_tables(rows)
    feats = feature_table(seq_len)
    featt = np.ascontiguousarray(feats.T)
    skip_row = skip_bias.reshape(1, channels)
    rate_row = decay_rate.reshape(1, channels)
    smem = pl.BlockSpec(memory_space=pltpu.SMEM)
    vmem = pl.BlockSpec(memory_space=pltpu.VMEM)
    anywhere = pl.BlockSpec(memory_space=pl.ANY)
    mebi = 1024 * 1024

    def shape(*dims, dtype=f32):
        return jax.ShapeDtypeStruct(dims, dtype)

    def call(kernel, name, units, out_shape, in_specs, out_specs=None, scratch=(), limit=16, aliases={}):
        return pl.pallas_call(
            kernel,
            in_specs=in_specs,
            out_specs=out_specs if out_specs is not None else [vmem] * len(out_shape),
            out_shape=out_shape,
            scratch_shapes=scratch,
            input_output_aliases=aliases,
            compiler_params=pltpu.CompilerParams(vmem_limit_bytes=limit * mebi),
            cost_estimate=pl.CostEstimate(
                flops=2 * units * double * double * channels, bytes_accessed=rows * channels, transcendentals=0
            ),
            name=name,
        )

    def move(array, pairs):
        return lax.ppermute(array, "ctx", pairs)

    up = [(i, i + 1) for i in range(shards - 1)]
    down = [(i + 1, i) for i in range(shards - 1)]
    inward = [(0, 1), (shards - 1, shards - 2)]
    outward = [(1, 0), (shards - 2, shards - 1)]
    across = [(1, 2), (2, 1)]
    pay_shape = (hid_count, channels + SIDE)
    block_bf16 = shape(rows, channels, dtype=bf16)
    block_f32 = shape(rows, channels)

    row_step = max(rows // 2, 16)
    gate_rows = pl.BlockSpec((row_step, channels), lambda i: (i, 0))
    x0, c0, edge, bias = pl.pallas_call(
        products_kernel,
        grid=(rows // row_step,),
        in_specs=[smem] + [gate_rows] * 4,
        out_specs=[gate_rows] * 3 + [pl.BlockSpec((1, channels), lambda i: (0, 0))],
        out_shape=[block_bf16] * 3 + [shape(1, channels)],
        compiler_params=pltpu.CompilerParams(vmem_limit_bytes=64 * mebi),
        name="products",
    )(rank, x_one, x_two, values, grad_out)
    x1 = move(x0, up)
    c1 = move(c0, down)

    spec, trans, slope, edge = call(
        functools.partial(filters_kernel, rows, shards, blocks, width), "filters", 8,
        [
            shape(shards, double, channels, dtype=bf16), shape(2 * hid_count, seq_len, dtype=bf16),
            shape(seq_len, hid_count), block_bf16,
        ],
        [pl.BlockSpec(memory_space=pltpu.HBM)] * 6,
        out_specs=[vmem] * 3 + [pl.BlockSpec(memory_space=pltpu.HBM)],
        scratch=[
            pltpu.VMEM((seq_len, feat_count), f32), pltpu.VMEM((feat_count, hid_count), f32),
            pltpu.VMEM((hid_count, channels), f32), pltpu.VMEM((1, channels), f32), pltpu.VMEM((double, double), bf16),
            pltpu.VMEM((seq_len, 3 * hid_count), bf16), pltpu.SemaphoreType.DMA((5,)),
        ],
        aliases={5: 3}, limit=57,
    )(feats, first_weight, second_weight, rate_row, front, edge)
    far = move(edge, [(0, 2), (shards - 1, shards - 3)])

    own, send = call(
        functools.partial(own_kernel, rows, shards, channels, blocks, width), "own_pair", 8,
        [shape(hid_count, channels), shape(*pay_shape, dtype=bf16)],
        [anywhere] * 2 + [vmem] * 8,
        scratch=[
            pltpu.VMEM((2 * hid_count, seq_len), bf16), pltpu.VMEM((seq_len, hid_count), f32),
            pltpu.VMEM((rows, hid_count), f32), pltpu.SemaphoreType.DMA((2,)),
        ],
    )(trans, slope, x0, c0, second_weight, rate_row, front, back, featt, bias)
    come = move(send, inward)

    conv, corr, ahead, sums, first = call(
        looped(
            functools.partial(near_kernel, rows, shards),
            (None, ROWS, ROWS, ROWS, ROWS, CUBE, ROWS, ROWS, None, None, None, None, None, ROWS, ROWS, ROWS, ROWS, ROWS),
            blocks, width,
        ),
        "near_blocks", 20,
        [block_f32] * 3 + [shape(hid_count, channels), shape(feat_count, hid_count)],
        [smem] + [vmem] * 13,
        scratch=[
            pltpu.VMEM((4, double, width), f32),
            pltpu.VMEM((3, double, width), bf16),
            pltpu.VMEM((shards - 1, double, width), bf16),
            pltpu.VMEM((shards - 1, double, width), bf16),
            pltpu.VMEM(((shards - 1) * rows, hid_count), f32),
        ],
    )(rank, x0, c0, x1, c1, spec, second_weight, rate_row, front, back, trans, featt, slope, own)

    part, late = call(
        looped(
            functools.partial(far_kernel, rows),
            (None, ROWS, (slice(2, 4), slice(None)), None, None, ROWS, ROWS, ROWS),
            blocks, width,
        ),
        "far_block", 1,
        [block_bf16, block_f32],
        [smem] + [vmem] * 5,
    )(rank, far, spec, front, back, ahead)
    part_come = move(part, outward)

    pay, first = call(
        looped(
            functools.partial(last_kernel, rows, shards, channels),
            (None, None, ROWS, ROWS, ROWS, ROWS, ROWS, None, None, None, None, None, ROWS),
            blocks, width,
        ),
        "last_pair", 1,
        [shape(*pay_shape, dtype=bf16), shape(feat_count, hid_count)],
        [anywhere, smem] + [vmem] * 15,
        scratch=[pltpu.VMEM((2 * rows, hid_count), f32)],
    )(late, rank, x1, c1, far, second_weight, rate_row, front, back, trans, featt, slope, sums, first, send, bias, come)
    pay_come = move(pay, across)
    group = lax.axis_size(("ch", "sub"))
    bit = 1
    while bit < group:
        first = first + lax.ppermute(first, ("ch", "sub"), [(i, i ^ bit) for i in range(group)])
        bit *= 2

    (total,) = call(
        functools.partial(total_kernel, channels, hid_count), "total", 0,
        [shape(*pay_shape, dtype=bf16)],
        [anywhere] + [vmem] * 4,
    )(part_come, pay, pay_come, first, move(first, across))
    total_come = move(total, outward)

    grad_one, grad_two, grad_value = call(
        looped(
            functools.partial(gates_kernel, shards), (None,) + (ROWS,) * 12, blocks, width
        ),
        "gates", 0,
        [block_bf16] * 3,
        [smem] + [vmem] * 9,
    )(rank, x_one, x_two, values, grad_out, skip_row, conv, corr, late, part_come)

    outs = [shape(hid_count, channels), shape(feat_count, hid_count), shape(1, channels)]
    grad_second, grad_first, grad_bias = call(
        functools.partial(finish_kernel, channels, shards), "finish", 0,
        outs,
        [smem] + [vmem] * 2,
        out_specs=[anywhere] * 3,
        scratch=[pltpu.VMEM(o.shape, f32) for o in outs] + [pltpu.SemaphoreType.DMA((3,))],
    )(rank, total, total_come)
    return (grad_one, grad_two, grad_value, grad_first, grad_second, grad_bias.reshape(channels))


def solution(mesh):
    in_specs = (
        P(("parts", "ctx"), ("ch", "sub")),
        P(("parts", "ctx"), ("ch", "sub")),
        P(("parts", "ctx"), ("ch", "sub")),
        P(("parts", "ctx"), ("ch", "sub")),
        P(),
        P(None, ("ch", "sub")),
        P(("ch", "sub")),
        P(("ch", "sub")),
    )
    out_specs = (
        P(("parts", "ctx"), ("ch", "sub")),
        P(("parts", "ctx"), ("ch", "sub")),
        P(("parts", "ctx"), ("ch", "sub")),
        P("parts", None),
        P("parts", ("ch", "sub")),
        P(("parts", "ch", "sub")),
    )
    body = few_shards_body if mesh.shape["ctx"] == 4 else many_shards_body
    return jax.shard_map(body, mesh=mesh, in_specs=in_specs, out_specs=out_specs, check_vma=False)
```

```python
import functools
import math

import jax
import jax.numpy as jnp
import numpy as np
from jax import lax
from jax.experimental import pallas as pl
from jax.experimental.pallas import tpu as pltpu
from jax.sharding import PartitionSpec as P

band_steps = (1763, 1201, 811, 547, 367, 251, 167, 113, 79, 53, 37, 23, 17, 11, 7, 3)
highest = lax.Precision.HIGHEST
f32 = jnp.float32
bf16 = jnp.bfloat16


def features(positions):
    multiplier = jnp.array(band_steps, dtype=jnp.int32)
    phase = positions[:, None] * multiplier[None, :] % 4096
    angle = phase.astype(jnp.float32) * (2.0 * math.pi / 4096.0)
    return jnp.concatenate([jnp.cos(angle), jnp.sin(angle)], axis=1)


def tables(out_count, in_count, modulus, sign_value):
    row_index = lax.broadcasted_iota(jnp.int32, (out_count, in_count), 0)
    col_index = lax.broadcasted_iota(jnp.int32, (out_count, in_count), 1)
    angle = (row_index * col_index % modulus).astype(jnp.float32) * (2.0 * math.pi / modulus)
    return (jnp.cos(angle), sign_value * jnp.sin(angle))


def twiddle(spec_re, spec_im, freq_count, span, modulus, sign_value):
    freq_index = lax.broadcasted_iota(jnp.int32, (freq_count, span), 0)
    pos_index = lax.broadcasted_iota(jnp.int32, (freq_count, span), 1)
    angle = (freq_index * pos_index % modulus).astype(jnp.float32) * (2.0 * math.pi / modulus)
    factor_re = jnp.cos(angle)[None, None, :, :]
    factor_im = (sign_value * jnp.sin(angle))[None, None, :, :]
    return (spec_re * factor_re - spec_im * factor_im, spec_re * factor_im + spec_im * factor_re)


def contract(kernel, array):
    return jnp.einsum(
        "lj,mckj->mckl", kernel, array, precision=highest, preferred_element_type=jnp.float32
    )


def along_positions(spec_re, spec_im, kernel_re, kernel_im):
    return (
        contract(kernel_re, spec_re) - contract(kernel_im, spec_im),
        contract(kernel_re, spec_im) + contract(kernel_im, spec_re),
    )


def many_shards_body(
    x_one, x_two, values, grad_out, first_weight, second_weight, skip_bias, decay_rate
):
    row_count, chan_count = x_one.shape
    shards = lax.axis_size("ctx")
    rank = lax.axis_index("ctx")
    seq_len = row_count * shards
    total = 2 * seq_len
    narrow = chan_count // shards
    chan_weight = lax.dynamic_slice_in_dim(second_weight, rank * narrow, narrow, 1)
    chan_rate = lax.dynamic_slice_in_dim(decay_rate, rank * narrow, narrow, 0)
    source = x_one.astype(jnp.float32) * values.astype(jnp.float32)
    cotan = grad_out.astype(jnp.float32) * x_two.astype(jnp.float32)
    spread = lax.all_to_all(
        jnp.stack([source.T, cotan.T])[:, :, None, :],
        "ctx",
        split_axis=1,
        concat_axis=2,
        tiled=True,
    )
    far_source = spread[0]
    far_cotan = spread[1]
    positions = jnp.arange(seq_len, dtype=jnp.int32)
    feats = features(positions)
    pre_act = jnp.dot(feats, first_weight, precision=highest, preferred_element_type=jnp.float32)
    hidden = jnp.sin(pre_act)
    envelope = jnp.exp(-chan_rate[:, None] * positions.astype(jnp.float32)[None, :]) * float(
        seq_len
    ) ** (-0.5)
    filt = (
        jnp.einsum(
            "th,hc->ct", hidden, chan_weight, precision=highest, preferred_element_type=jnp.float32
        )
        * envelope
    )
    filt_blocks = filt.reshape(narrow, shards, row_count)
    fields = jnp.stack([far_source, far_cotan])

    def first_section(kernel):
        field_part = jnp.einsum(
            "kn,mcnj->mckj", kernel, fields, precision=highest, preferred_element_type=jnp.float32
        )
        filter_part = jnp.einsum(
            "kn,cnj->ckj",
            kernel,
            filt_blocks,
            precision=highest,
            preferred_element_type=jnp.float32,
        )
        return jnp.concatenate([field_part, filter_part[None]], axis=0)

    first_re, first_im = tables(2 * shards, shards, 2 * shards, -1.0)
    spec_re, spec_im = (first_section(first_re), first_section(first_im))
    spec_re, spec_im = twiddle(spec_re, spec_im, 2 * shards, row_count, total, -1.0)
    fwd_re, fwd_im = tables(row_count, row_count, row_count, -1.0)
    spec_re, spec_im = along_positions(spec_re, spec_im, fwd_re, fwd_im)
    source_re, source_im = (spec_re[0], spec_im[0])
    cotan_re, cotan_im = (spec_re[1], spec_im[1])
    filter_re, filter_im = (spec_re[2], spec_im[2])
    prod_re = jnp.stack(
        [
            source_re * filter_re - source_im * filter_im,
            cotan_re * filter_re + cotan_im * filter_im,
            cotan_re * source_re + cotan_im * source_im,
        ]
    )
    prod_im = jnp.stack(
        [
            source_re * filter_im + source_im * filter_re,
            cotan_im * filter_re - cotan_re * filter_im,
            cotan_im * source_re - cotan_re * source_im,
        ]
    )
    back_re, back_im = tables(row_count, row_count, row_count, 1.0)
    prod_re, prod_im = along_positions(prod_re, prod_im, back_re, back_im)
    prod_re, prod_im = twiddle(prod_re, prod_im, 2 * shards, row_count, total, 1.0)
    last_re, last_im = tables(shards, 2 * shards, 2 * shards, 1.0)
    field_out = jnp.einsum(
        "nk,mckj->mcnj", last_re, prod_re[:2], precision=highest, preferred_element_type=jnp.float32
    ) - jnp.einsum(
        "nk,mckj->mcnj", last_im, prod_im[:2], precision=highest, preferred_element_type=jnp.float32
    )
    field_out = field_out * (1.0 / total)
    filt_grad = jnp.einsum(
        "nk,ckj->cnj", last_re, prod_re[2], precision=highest, preferred_element_type=jnp.float32
    ) - jnp.einsum(
        "nk,ckj->cnj", last_im, prod_im[2], precision=highest, preferred_element_type=jnp.float32
    )
    filt_grad = (filt_grad * (1.0 / total)).reshape(narrow, seq_len)
    modulated = filt_grad * envelope
    weight_part = jnp.einsum(
        "th,ct->hc", hidden, modulated, precision=highest, preferred_element_type=jnp.float32
    )
    hidden_grad = jnp.einsum(
        "ct,hc->th", modulated, chan_weight, precision=highest, preferred_element_type=jnp.float32
    )
    first_part = jnp.dot(
        feats.T,
        hidden_grad * jnp.cos(pre_act),
        precision=highest,
        preferred_element_type=jnp.float32,
    )
    grad_first = lax.psum(first_part, ("ctx", "ch", "sub"))
    returned = lax.all_to_all(
        field_out.astype(jnp.bfloat16), "ctx", split_axis=2, concat_axis=1, tiled=True
    ).astype(field_out.dtype)
    conv_part = returned[0, :, 0, :].T
    corr_part = returned[1, :, 0, :].T
    grad_two = (grad_out.astype(jnp.float32) * (conv_part + skip_bias[None, :] * source)).astype(
        jnp.bfloat16
    )
    grad_mid = corr_part + skip_bias[None, :] * cotan
    grad_one = (grad_mid * values.astype(jnp.float32)).astype(jnp.bfloat16)
    grad_value = (grad_mid * x_one.astype(jnp.float32)).astype(jnp.bfloat16)
    grad_bias = lax.psum(jnp.sum(source * cotan, axis=0), "ctx")
    grad_second = lax.all_gather(weight_part, "ctx", axis=1, tiled=True)
    return (grad_one, grad_two, grad_value, grad_first, grad_second, grad_bias)


STEP = 16
SIDE = 256


def halves(array):
    array = np.asarray(array, np.float32)
    high = array.astype(bf16)
    low = (array - high.astype(np.float32)).astype(bf16)
    return high, low


def block_tables(rows):
    freq = np.concatenate([np.arange(0, rows, 2), np.arange(1, rows, 2)])
    phase = (2 * freq + 1)[:, None] * np.arange(rows)[None, :] % (4 * rows)
    angle = phase * (2.0 * np.pi / (4 * rows))
    forward = np.concatenate([np.cos(angle), -np.sin(angle)], axis=0)
    front = np.ascontiguousarray(np.concatenate(halves(forward), axis=1))
    back = np.ascontiguousarray(np.concatenate(halves(forward.T / rows), axis=0))
    return front, back


def feature_table(seq_len):
    phase = np.arange(seq_len)[:, None] * np.array(band_steps)[None, :] % 4096
    angle = phase * (2.0 * np.pi / 4096.0)
    return np.concatenate([np.cos(angle), np.sin(angle)], axis=1).astype(np.float32)


def split(array):
    high = array.astype(bf16)
    return high, (array - high.astype(f32)).astype(bf16)


def dot(left, right):
    return jnp.dot(left, right, preferred_element_type=f32)


def exact_dot(left, right):
    return jnp.dot(left, right, precision=highest, preferred_element_type=f32)


def dot_across(left, right):
    return lax.dot_general(left, right, (((1,), (1,)), ((), ())), preferred_element_type=f32)


def decay(rate, rows, scale):
    place = lax.broadcasted_iota(jnp.int32, (rows, rate.shape[1]), 0)
    return jnp.exp(-place.astype(f32) * rate) * scale


def times(a, b):
    return a[0] * b[0] - a[1] * b[1], a[0] * b[1] + a[1] * b[0]


def conj_times(a, b):
    return a[0] * b[0] + a[1] * b[1], a[0] * b[1] - a[1] * b[0]


def plus(a, b):
    return a[0] + b[0], a[1] + b[1]


def scaled(a, factor):
    return a[0] * factor, a[1] * factor


def choose(condition, a, b):
    return jnp.where(condition, a[0], b[0]), jnp.where(condition, a[1], b[1])


def turned(a, sign):
    return (a[1], -a[0]) if sign > 0 else (-a[1], a[0])


def forward(front_ref, block):
    return dot(front_ref[...], jnp.concatenate([block, block], axis=0))


def backward(back_ref, high, low=None):
    both = dot(back_ref[...], high)
    rows = both.shape[0] // 2
    out = both[:rows] + both[rows:]
    return out if low is None else out + dot(back_ref[:rows], low)


def row_groups(rows):
    for step in range(rows // STEP):
        sign = 1 if step * STEP < rows // 2 else -1
        yield slice(step * STEP, (step + 1) * STEP), slice(rows + step * STEP, rows + (step + 1) * STEP), sign


def weight_sums(trans, m_high, m_low):
    both = dot(trans, m_high)
    count = both.shape[0] // 2
    return both[:count] + both[count:] + dot(trans[:count], m_low)


def hidden_sums(m_high, m_low, w_high, w_low):
    left = jnp.concatenate([m_high, m_high, m_low], axis=1)
    right = jnp.concatenate([w_high, w_low, w_high], axis=1)
    return dot_across(left, right)


def looped(kernel, kinds, blocks, width):
    def over_strips(*refs):
        def step(block, carry):
            cols = pl.ds(pl.multiple_of(block * width, width), width)
            views = [
                ref if kind is None else ref.at[(*kind, cols)]
                for ref, kind in zip(refs, kinds + (None,) * (len(refs) - len(kinds)))
            ]
            kernel(block, blocks, *views)
            return carry

        lax.fori_loop(0, blocks, step, 0)

    return over_strips


ROWS = (slice(None),)
CUBE = (slice(None), slice(None))


def products_kernel(rank_ref, one_ref, two_ref, val_ref, out_ref, source_ref, cotan_ref, edge_ref, bias_ref):
    source = one_ref[...].astype(f32) * val_ref[...].astype(f32)
    cotan = out_ref[...].astype(f32) * two_ref[...].astype(f32)
    source_ref[...] = source.astype(bf16)
    cotan_ref[...] = cotan.astype(bf16)
    edge_ref[...] = jnp.where(rank_ref[0] == 0, source, cotan).astype(bf16)
    part = jnp.sum(source * cotan, axis=0, keepdims=True)

    @pl.when(pl.program_id(0) == 0)
    def _():
        bias_ref[...] = part

    @pl.when(pl.program_id(0) > 0)
    def _():
        bias_ref[...] += part


def sin_cos(angle):
    turns = jnp.floor(angle * (2.0 / math.pi) + 0.5)
    rest = ((angle - turns * 1.5703125) - turns * 4.837512969970703e-4) - turns * 7.54978995489188e-8
    square = rest * rest
    sine = rest + rest * square * (
        -1.6666654611e-1 + square * (8.3321608736e-3 + square * -1.9515295891e-4)
    )
    cosine = 1.0 - 0.5 * square + square * square * (
        4.166664568298827e-2 + square * (-1.388731625493765e-3 + square * 2.443315711809948e-5)
    )
    quarter = turns.astype(jnp.int32)
    odd = (quarter & 1) == 1
    sin_sign = jnp.where((quarter & 2) == 2, -1.0, 1.0).astype(f32)
    cos_sign = jnp.where(((quarter + 1) & 2) == 2, -1.0, 1.0).astype(f32)
    return jnp.where(odd, cosine, sine) * sin_sign, jnp.where(odd, sine, cosine) * cos_sign


def turned_over(hidden, slope):
    both = jnp.concatenate([hidden, slope], axis=1).T
    return jnp.concatenate(split(both[: hidden.shape[1]]), axis=0)


def filters_kernel(rows, shards, blocks, width, *refs):
    inputs, (spec_out, trans_ref, slope_ref), held, (spec_ref, hid_ref, sems, out_sems) = (
        refs[:5], refs[6:9], refs[10:15], refs[15:]
    )
    feats_ref, first_ref, weight_ref, rate_ref, front_ref = held
    copies = [pltpu.make_async_copy(far, near, sems.at[i]) for i, (far, near) in enumerate(zip(inputs, held))]
    for copy in copies:
        copy.start()
    copies[0].wait()
    copies[1].wait()
    hidden, slope = sin_cos(exact_dot(feats_ref[...], first_ref[...]))
    slope_ref[...] = slope
    high, low = split(hidden)
    hid_ref[...] = jnp.concatenate([high, high, low], axis=1)
    trans_ref[...] = turned_over(hidden, slope)
    for copy in copies[2:]:
        copy.wait()

    def leaving(block):
        cols = pl.ds(pl.multiple_of(block * width, width), width)
        return pltpu.make_async_copy(spec_ref.at[:, :, cols], spec_out.at[:, :, cols], out_sems.at[block])

    def strip(block, blocks, *views):
        filter_strip(rows, shards, *views)
        leaving(block).start()

    looped(strip, (None, ROWS, ROWS, None, CUBE), blocks, width)(hid_ref, weight_ref, rate_ref, front_ref, spec_ref)
    for block in range(blocks):
        leaving(block).wait()


def filter_strip(rows, shards, hid_ref, weight_ref, rate_ref, front_ref, spec_ref):
    scale = float(rows * shards) ** -0.5
    w_high, w_low = split(weight_ref[...])
    stacked = jnp.concatenate([w_high, w_low, w_high], axis=0)
    rate = rate_ref[...]
    env = decay(rate, rows, scale)
    before = None
    for lag in range(shards):
        part = dot(hid_ref[lag * rows : (lag + 1) * rows, :], stacked)
        part = part * (env * jnp.exp(rate * (-float(lag * rows))))
        f_high, f_low = split(part)
        now = forward(front_ref, f_high) + dot(front_ref[:, :rows], f_low)
        for re, im, sign in row_groups(rows):
            here = (now[re], now[im])
            if before is not None:
                here = plus(here, turned((before[re], before[im]), -sign))
            spec_ref[lag, re, :] = here[0].astype(bf16)
            spec_ref[lag, im, :] = here[1].astype(bf16)
        before = now


def own_kernel(
    rows, shards, channels, blocks, width, passed, feats_ref, first_ref, source_ref, cotan_ref, weight_ref, rate_ref,
    front_ref, back_ref, featt_ref, bias_ref, sums_ref, send_ref, passing, trans_ref, acc_ref,
):
    del passed, passing
    hidden, slope = sin_cos(exact_dot(feats_ref[...], first_ref[...]))
    trans_ref[...] = turned_over(hidden, slope)
    acc_ref[...] = jnp.zeros_like(acc_ref)
    strips = looped(
        functools.partial(own_strip, rows, shards),
        (ROWS, ROWS, ROWS, ROWS, None, None, None, ROWS, ROWS, None), blocks, width,
    )
    strips(
        source_ref, cotan_ref, weight_ref, rate_ref, front_ref, back_ref, trans_ref, sums_ref, send_ref, acc_ref
    )
    first = exact_dot(featt_ref[:, :rows], acc_ref[...] * slope)
    put_side(send_ref, channels, fold(bias_ref[...]), first)


def own_strip(
    rows, shards, block, blocks, source_ref, cotan_ref, weight_ref, rate_ref, front_ref, back_ref, trans_ref, sums_ref,
    send_ref, acc_ref,
):
    x0 = forward(front_ref, source_ref[...])
    c0 = forward(front_ref, cotan_ref[...])
    pair = conj_times((x0[:rows], x0[rows:]), (c0[:rows], c0[rows:]))
    high, low = split(jnp.concatenate(pair, axis=0))
    env = decay(rate_ref[...], rows, float(rows * shards) ** -0.5)
    m_high, m_low = split(backward(back_ref, high, low) * env)
    sums = weight_sums(trans_ref[...], m_high, m_low)
    sums_ref[...] = sums
    send_ref[...] = sums.astype(bf16)
    acc_ref[...] += hidden_sums(m_high, m_low, *split(weight_ref[...]))


def fold(bias):
    return jnp.concatenate([bias[:, i * 128 : (i + 1) * 128] for i in range(bias.shape[1] // 128)], axis=0)


def put_side(pay_ref, channels, bias, first=None):
    half = pay_ref.shape[0] // 2
    pay_ref[:, channels:] = jnp.zeros((2 * half, SIDE), bf16)
    for start, part in zip((0, 128), split(bias)):
        pay_ref[: bias.shape[0], channels + start : channels + start + 128] = part
    if first is not None:
        for start, part in zip((0, 128), split(first)):
            pay_ref[half:, channels + start : channels + start + first.shape[1]] = part


def get_side(pay, channels, lanes, hid_count):
    half = pay.shape[0] // 2
    side = pay[:, channels : channels + 128].astype(f32) + pay[:, channels + 128 :].astype(f32)
    return side[:lanes], side[half:, :hid_count]


def near_kernel(
    rows, shards, block, blocks, passed, rank_ref, x0_ref, c0_ref, x1_ref, c1_ref, spec_ref, weight_ref, rate_ref, front_ref, back_ref,
    trans_ref, featt_ref, slope_ref, own_ref, conv_ref, corr_ref, ahead_ref, sums_ref, first_ref, passing, fields, fast,
    high_ref, low_ref, acc_ref,
):
    del passed, passing
    rank = rank_ref[0]
    count = shards - 1

    @pl.when(block == 0)
    def _():
        acc_ref[...] = jnp.zeros_like(acc_ref)

    lower = rank == 1
    upper = jnp.where(rank == 2, 1.0, 0.0).astype(f32)
    below_top = jnp.where(rank == shards - 1, 0.0, 1.0).astype(f32)
    side = jnp.where(rank == 2, 1.0, -1.0).astype(f32)
    for index, ref in enumerate((x0_ref, c0_ref, x1_ref, c1_ref)):
        fields[index] = forward(front_ref, ref[...])
    for re, im, sign in row_groups(rows):
        x0, c0, x1, c1 = ((fields[i, re, :], fields[i, im, :]) for i in range(4))
        w0, w1, w2 = ((spec_ref[i, re, :].astype(f32), spec_ref[i, im, :].astype(f32)) for i in range(3))
        ahead = times((w2[0], w2[1] * side), choose(lower, c1, x1))
        for index, value in enumerate(
            (plus(times(w0, x0), times(w1, x1)), plus(conj_times(w0, c0), conj_times(w1, c1)), ahead)
        ):
            fast[index, re, :] = value[0].astype(bf16)
            fast[index, im, :] = value[1].astype(bf16)
        one = plus(scaled(conj_times(x1, c0), below_top), scaled(conj_times(x0, c1), upper))
        two = conj_times(x1, c1)
        for index, value in enumerate((turned(one, sign), plus(one, turned(two, sign)), two)):
            for part, where in zip(value, (re, im)):
                high_ref[index, where, :], low_ref[index, where, :] = split(part)
    conv_ref[...] = backward(back_ref, fast[0])
    corr_ref[...] = backward(back_ref, fast[1])
    ahead_ref[...] = backward(back_ref, fast[2])
    rate = rate_ref[...]
    env = decay(rate, rows, float(rows * shards) ** -0.5)
    parts = []
    for lag in range(count):
        grad = backward(back_ref, high_ref[lag], low_ref[lag])
        parts.append(split(grad * (env * jnp.exp(rate * (-float(lag * rows))))))
    m_high = jnp.concatenate([p[0] for p in parts], axis=0)
    m_low = jnp.concatenate([p[1] for p in parts], axis=0)
    sums_ref[...] = own_ref[...] + weight_sums(trans_ref[:, : count * rows], m_high, m_low)
    w_high, w_low = split(weight_ref[...])
    acc_ref[...] += hidden_sums(m_high, m_low, w_high, w_low)

    @pl.when(block == blocks - 1)
    def _():
        first_ref[...] = exact_dot(
            featt_ref[:, : count * rows], acc_ref[...] * slope_ref[: count * rows, :]
        )


def far_kernel(rows, block, blocks, rank_ref, far_ref, spec_ref, front_ref, back_ref, ahead_ref, part_ref, late_ref):
    side = jnp.where(rank_ref[0] == 2, 1.0, -1.0).astype(f32)
    far = forward(front_ref, far_ref[...])
    far = (far[:rows], far[rows:])
    w2, w3 = ((spec_ref[i, :rows, :].astype(f32), spec_ref[i, rows:, :].astype(f32) * side) for i in range(2))
    ahead = jnp.concatenate(times(w3, far), axis=0).astype(bf16)
    part_ref[...] = (ahead_ref[...] + backward(back_ref, ahead)).astype(bf16)
    late = jnp.concatenate(times(w2, far), axis=0).astype(bf16)
    late_ref[...] = backward(back_ref, late)


def last_kernel(
    rows, shards, channels, block, blocks, after_ref, rank_ref, x1_ref, c1_ref, far_ref, weight_ref, rate_ref, front_ref, back_ref,
    trans_ref, featt_ref, slope_ref, sums_ref, first_ref, own_ref, bias_ref, in_ref, pay_ref, total_ref, acc_ref,
):
    del after_ref
    hid_count, width = weight_ref.shape
    lower = rank_ref[0] == 1
    start = pl.multiple_of(block * width, width)
    here = sums_ref[...] + in_ref[:, pl.ds(start, width)].astype(f32)
    mine = (block < blocks // 2) == lower

    @pl.when(block == 0)
    def _():
        acc_ref[...] = jnp.zeros_like(acc_ref)

    @pl.when(mine)
    def _():
        sign = jnp.where(lower, 1.0, -1.0).astype(f32)
        near = forward(front_ref, jnp.where(lower, x1_ref[...], c1_ref[...]))
        far = forward(front_ref, far_ref[...])
        three = conj_times((near[:rows], near[rows:]), (far[:rows], far[rows:]))
        three = (three[0], three[1] * sign)
        half = rows // 2
        two = jnp.concatenate([three[1][:half], -three[1][half:], -three[0][:half], three[0][half:]], axis=0)
        rate = rate_ref[...]
        env = decay(rate, rows, float(rows * shards) ** -0.5)
        parts = []
        for lag, value in ((shards - 2, two), (shards - 1, jnp.concatenate(three, axis=0))):
            grad = backward(back_ref, *split(value))
            parts.append(split(grad * (env * jnp.exp(rate * (-float(lag * rows))))))
        m_high = jnp.concatenate([p[0] for p in parts], axis=0)
        m_low = jnp.concatenate([p[1] for p in parts], axis=0)
        trans = trans_ref[:, (shards - 2) * rows :]
        pay_ref[:, pl.ds(start, width)] = (here + weight_sums(trans, m_high, m_low)).astype(bf16)
        w_high, w_low = split(weight_ref[...])
        acc_ref[...] += hidden_sums(m_high, m_low, w_high, w_low)

    @pl.when(jnp.logical_not(mine))
    def _():
        pay_ref[:, pl.ds(start, width)] = here.astype(bf16)

    @pl.when(block == blocks - 1)
    def _():
        first = exact_dot(
            featt_ref[:, (shards - 2) * rows :], acc_ref[...] * slope_ref[(shards - 2) * rows :, :]
        )
        lanes = channels // 128
        own_first = get_side(own_ref[...], channels, lanes, hid_count)[1]
        in_bias, in_first = get_side(in_ref[...], channels, lanes, hid_count)
        first = first + first_ref[...] + own_first + in_first
        put_side(pay_ref, channels, fold(bias_ref[...]) + in_bias)
        total_ref[...] = first


def total_kernel(channels, hid_count, part_ref, own_ref, come_ref, first_ref, first_come_ref, pay_ref):
    del part_ref
    lanes = channels // 128
    pay_ref[:, :channels] = (own_ref[:, :channels].astype(f32) + come_ref[:, :channels].astype(f32)).astype(bf16)
    own, come = (get_side(ref[...], channels, lanes, hid_count)[0] for ref in (own_ref, come_ref))
    put_side(pay_ref, channels, own + come, first_ref[...] + first_come_ref[...])


def gates_kernel(
    shards, block, blocks, rank_ref, one_ref, two_ref, val_ref, out_ref, skip_ref, conv_ref, corr_ref, late_ref, part_ref,
    grad_one_ref, grad_two_ref, grad_value_ref,
):
    rank = rank_ref[0]

    def mask(wanted):
        return jnp.where(rank == wanted, 1.0, 0.0).astype(f32)

    part = part_ref[...].astype(f32)
    late = late_ref[...]
    one = one_ref[...].astype(f32)
    val = val_ref[...].astype(f32)
    out = out_ref[...].astype(f32)
    skip = skip_ref[...]
    conv = conv_ref[...] + late * mask(2) + part * mask(shards - 1)
    corr = corr_ref[...] + late * mask(1) + part * mask(0)
    grad_two_ref[...] = (out * (conv + skip * (one * val))).astype(bf16)
    mid = corr + skip * (out * two_ref[...].astype(f32))
    grad_one_ref[...] = (mid * val).astype(bf16)
    grad_value_ref[...] = (mid * one).astype(bf16)


def finish_kernel(
    channels, shards, rank_ref, own_ref, come_ref, second_out, first_out, bias_out, second, first, bias, sems
):
    rank = rank_ref[0]
    inner = jnp.logical_and(rank > 0, rank < shards - 1)
    lanes = channels // 128
    copies = [
        pltpu.make_async_copy(held, out, sems.at[i])
        for i, (held, out) in enumerate(((second, second_out), (first, first_out), (bias, bias_out)))
    ]
    picked = jnp.where(inner, own_ref[...], come_ref[...])
    second[...] = picked[:, :channels].astype(f32)
    copies[0].start()
    rows, first[...] = get_side(picked, channels, lanes, first.shape[1])
    copies[1].start()
    for i in range(lanes):
        bias[:, i * 128 : (i + 1) * 128] = rows[i : i + 1]
    copies[2].start()
    for copy in copies:
        copy.wait()


def few_shards_body(
    x_one, x_two, values, grad_out, first_weight, second_weight, skip_bias, decay_rate
):
    rows, channels = x_one.shape
    shards = lax.axis_size("ctx")
    feat_count, hid_count = first_weight.shape
    seq_len = rows * shards
    double = 2 * rows
    width = min(512, channels)
    blocks = channels // width
    rank = lax.axis_index("ctx").astype(jnp.int32).reshape(1)
    front, back = block_tables(rows)
    feats = feature_table(seq_len)
    featt = np.ascontiguousarray(feats.T)
    skip_row = skip_bias.reshape(1, channels)
    rate_row = decay_rate.reshape(1, channels)
    smem = pl.BlockSpec(memory_space=pltpu.SMEM)
    vmem = pl.BlockSpec(memory_space=pltpu.VMEM)
    anywhere = pl.BlockSpec(memory_space=pl.ANY)
    mebi = 1024 * 1024

    def shape(*dims, dtype=f32):
        return jax.ShapeDtypeStruct(dims, dtype)

    def call(kernel, name, units, out_shape, in_specs, out_specs=None, scratch=(), limit=16, aliases={}):
        return pl.pallas_call(
            kernel,
            in_specs=in_specs,
            out_specs=out_specs if out_specs is not None else [vmem] * len(out_shape),
            out_shape=out_shape,
            scratch_shapes=scratch,
            input_output_aliases=aliases,
            compiler_params=pltpu.CompilerParams(vmem_limit_bytes=limit * mebi),
            cost_estimate=pl.CostEstimate(
                flops=2 * units * double * double * channels, bytes_accessed=rows * channels, transcendentals=0
            ),
            name=name,
        )

    def move(array, pairs):
        return lax.ppermute(array, "ctx", pairs)

    up = [(i, i + 1) for i in range(shards - 1)]
    down = [(i + 1, i) for i in range(shards - 1)]
    inward = [(0, 1), (shards - 1, shards - 2)]
    outward = [(1, 0), (shards - 2, shards - 1)]
    across = [(1, 2), (2, 1)]
    pay_shape = (hid_count, channels + SIDE)
    block_bf16 = shape(rows, channels, dtype=bf16)
    block_f32 = shape(rows, channels)

    row_step = max(rows // 2, 16)
    gate_rows = pl.BlockSpec((row_step, channels), lambda i: (i, 0))
    x0, c0, edge, bias = pl.pallas_call(
        products_kernel,
        grid=(rows // row_step,),
        in_specs=[smem] + [gate_rows] * 4,
        out_specs=[gate_rows] * 3 + [pl.BlockSpec((1, channels), lambda i: (0, 0))],
        out_shape=[block_bf16] * 3 + [shape(1, channels)],
        compiler_params=pltpu.CompilerParams(vmem_limit_bytes=64 * mebi),
        name="products",
    )(rank, x_one, x_two, values, grad_out)
    x1 = move(x0, up)
    c1 = move(c0, down)

    spec, trans, slope, edge = call(
        functools.partial(filters_kernel, rows, shards, blocks, width), "filters", 8,
        [
            shape(shards, double, channels, dtype=bf16), shape(2 * hid_count, seq_len, dtype=bf16),
            shape(seq_len, hid_count), block_bf16,
        ],
        [anywhere] * 6,
        out_specs=[anywhere] + [vmem] * 2 + [anywhere],
        scratch=[
            pltpu.VMEM((seq_len, feat_count), f32), pltpu.VMEM((feat_count, hid_count), f32),
            pltpu.VMEM((hid_count, channels), f32), pltpu.VMEM((1, channels), f32), pltpu.VMEM((double, double), bf16),
            pltpu.VMEM((shards, double, channels), bf16), pltpu.VMEM((seq_len, 3 * hid_count), bf16),
            pltpu.SemaphoreType.DMA((5,)), pltpu.SemaphoreType.DMA((blocks,)),
        ],
        aliases={5: 3},
        limit=60,
    )(feats, first_weight, second_weight, rate_row, front, edge)

    own, send, edge = call(
        functools.partial(own_kernel, rows, shards, channels, blocks, width), "own_pair", 8,
        [shape(hid_count, channels), shape(*pay_shape, dtype=bf16), block_bf16],
        [anywhere] + [vmem] * 10,
        out_specs=[vmem] * 2 + [anywhere],
        scratch=[pltpu.VMEM((2 * hid_count, rows), bf16), pltpu.VMEM((rows, hid_count), f32)],
        aliases={0: 2},
    )(edge, feats[:rows], first_weight, x0, c0, second_weight, rate_row, front, back, featt, bias)
    far = move(edge, [(0, 2), (shards - 1, shards - 3)])

    conv, corr, ahead, sums, first, send = call(
        looped(
            functools.partial(near_kernel, rows, shards),
            (None, None) + (ROWS,) * 4 + (CUBE, ROWS, ROWS) + (None,) * 5 + (ROWS,) * 5,
            blocks, width,
        ),
        "near_blocks", 20,
        [block_f32] * 3
        + [shape(hid_count, channels), shape(feat_count, hid_count), shape(*pay_shape, dtype=bf16)],
        [anywhere, smem] + [vmem] * 13,
        out_specs=[vmem] * 5 + [anywhere],
        scratch=[
            pltpu.VMEM((4, double, width), f32),
            pltpu.VMEM((3, double, width), bf16),
            pltpu.VMEM((shards - 1, double, width), bf16),
            pltpu.VMEM((shards - 1, double, width), bf16),
            pltpu.VMEM(((shards - 1) * rows, hid_count), f32),
        ],
        aliases={0: 5},
    )(send, rank, x0, c0, x1, c1, spec, second_weight, rate_row, front, back, trans, featt, slope, own)

    come = move(send, inward)

    part, late = call(
        looped(
            functools.partial(far_kernel, rows),
            (None, ROWS, (slice(2, 4), slice(None)), None, None, ROWS, ROWS, ROWS),
            blocks, width,
        ),
        "far_block", 1,
        [block_bf16, block_f32],
        [smem] + [vmem] * 5,
    )(rank, far, spec, front, back, ahead)
    part_come = move(part, outward)

    pay, first = call(
        looped(
            functools.partial(last_kernel, rows, shards, channels),
            (None, None, ROWS, ROWS, ROWS, ROWS, ROWS, None, None, None, None, None, ROWS),
            blocks, width,
        ),
        "last_pair", 1,
        [shape(*pay_shape, dtype=bf16), shape(feat_count, hid_count)],
        [anywhere, smem] + [vmem] * 15,
        scratch=[pltpu.VMEM((2 * rows, hid_count), f32)],
    )(late, rank, x1, c1, far, second_weight, rate_row, front, back, trans, featt, slope, sums, first, send, bias, come)
    pay_come = move(pay, across)
    group = lax.axis_size(("ch", "sub"))
    bit = 1
    while bit < group:
        first = first + lax.ppermute(first, ("ch", "sub"), [(i, i ^ bit) for i in range(group)])
        bit *= 2

    (total,) = call(
        functools.partial(total_kernel, channels, hid_count), "total", 0,
        [shape(*pay_shape, dtype=bf16)],
        [anywhere] + [vmem] * 4,
    )(part_come, pay, pay_come, first, move(first, across))
    total_come = move(total, outward)

    grad_one, grad_two, grad_value = call(
        looped(
            functools.partial(gates_kernel, shards), (None,) + (ROWS,) * 12, blocks, width
        ),
        "gates", 0,
        [block_bf16] * 3,
        [smem] + [vmem] * 9,
    )(rank, x_one, x_two, values, grad_out, skip_row, conv, corr, late, part_come)

    outs = [shape(hid_count, channels), shape(feat_count, hid_count), shape(1, channels)]
    grad_second, grad_first, grad_bias = call(
        functools.partial(finish_kernel, channels, shards), "finish", 0,
        outs,
        [smem] + [vmem] * 2,
        out_specs=[anywhere] * 3,
        scratch=[pltpu.VMEM(o.shape, f32) for o in outs] + [pltpu.SemaphoreType.DMA((3,))],
    )(rank, total, total_come)
    return (grad_one, grad_two, grad_value, grad_first, grad_second, grad_bias.reshape(channels))


def solution(mesh):
    in_specs = (
        P(("parts", "ctx"), ("ch", "sub")),
        P(("parts", "ctx"), ("ch", "sub")),
        P(("parts", "ctx"), ("ch", "sub")),
        P(("parts", "ctx"), ("ch", "sub")),
        P(),
        P(None, ("ch", "sub")),
        P(("ch", "sub")),
        P(("ch", "sub")),
    )
    out_specs = (
        P(("parts", "ctx"), ("ch", "sub")),
        P(("parts", "ctx"), ("ch", "sub")),
        P(("parts", "ctx"), ("ch", "sub")),
        P("parts", None),
        P("parts", ("ch", "sub")),
        P(("parts", "ch", "sub")),
    )
    body = few_shards_body if mesh.shape["ctx"] == 4 else many_shards_body
    return jax.shard_map(body, mesh=mesh, in_specs=in_specs, out_specs=out_specs, check_vma=False)
```

```python
import functools
import math

import jax
import jax.numpy as jnp
import numpy as np
from jax import lax
from jax.experimental import pallas as pl
from jax.experimental.pallas import tpu as pltpu
from jax.sharding import PartitionSpec as P

band_steps = (1763, 1201, 811, 547, 367, 251, 167, 113, 79, 53, 37, 23, 17, 11, 7, 3)
highest = lax.Precision.HIGHEST
f32 = jnp.float32
bf16 = jnp.bfloat16


def features(positions):
    multiplier = jnp.array(band_steps, dtype=jnp.int32)
    phase = positions[:, None] * multiplier[None, :] % 4096
    angle = phase.astype(jnp.float32) * (2.0 * math.pi / 4096.0)
    return jnp.concatenate([jnp.cos(angle), jnp.sin(angle)], axis=1)


def tables(out_count, in_count, modulus, sign_value):
    row_index = lax.broadcasted_iota(jnp.int32, (out_count, in_count), 0)
    col_index = lax.broadcasted_iota(jnp.int32, (out_count, in_count), 1)
    angle = (row_index * col_index % modulus).astype(jnp.float32) * (2.0 * math.pi / modulus)
    return (jnp.cos(angle), sign_value * jnp.sin(angle))


def twiddle(spec_re, spec_im, freq_count, span, modulus, sign_value):
    freq_index = lax.broadcasted_iota(jnp.int32, (freq_count, span), 0)
    pos_index = lax.broadcasted_iota(jnp.int32, (freq_count, span), 1)
    angle = (freq_index * pos_index % modulus).astype(jnp.float32) * (2.0 * math.pi / modulus)
    factor_re = jnp.cos(angle)[None, None, :, :]
    factor_im = (sign_value * jnp.sin(angle))[None, None, :, :]
    return (spec_re * factor_re - spec_im * factor_im, spec_re * factor_im + spec_im * factor_re)


def contract(kernel, array):
    return jnp.einsum(
        "lj,mckj->mckl", kernel, array, precision=highest, preferred_element_type=jnp.float32
    )


def along_positions(spec_re, spec_im, kernel_re, kernel_im):
    return (
        contract(kernel_re, spec_re) - contract(kernel_im, spec_im),
        contract(kernel_re, spec_im) + contract(kernel_im, spec_re),
    )


def many_shards_body(
    x_one, x_two, values, grad_out, first_weight, second_weight, skip_bias, decay_rate
):
    row_count, chan_count = x_one.shape
    shards = lax.axis_size("ctx")
    rank = lax.axis_index("ctx")
    seq_len = row_count * shards
    total = 2 * seq_len
    narrow = chan_count // shards
    chan_weight = lax.dynamic_slice_in_dim(second_weight, rank * narrow, narrow, 1)
    chan_rate = lax.dynamic_slice_in_dim(decay_rate, rank * narrow, narrow, 0)
    source = x_one.astype(jnp.float32) * values.astype(jnp.float32)
    cotan = grad_out.astype(jnp.float32) * x_two.astype(jnp.float32)
    spread = lax.all_to_all(
        jnp.stack([source.T, cotan.T])[:, :, None, :],
        "ctx",
        split_axis=1,
        concat_axis=2,
        tiled=True,
    )
    far_source = spread[0]
    far_cotan = spread[1]
    positions = jnp.arange(seq_len, dtype=jnp.int32)
    feats = features(positions)
    pre_act = jnp.dot(feats, first_weight, precision=highest, preferred_element_type=jnp.float32)
    hidden = jnp.sin(pre_act)
    envelope = jnp.exp(-chan_rate[:, None] * positions.astype(jnp.float32)[None, :]) * float(
        seq_len
    ) ** (-0.5)
    filt = (
        jnp.einsum(
            "th,hc->ct", hidden, chan_weight, precision=highest, preferred_element_type=jnp.float32
        )
        * envelope
    )
    filt_blocks = filt.reshape(narrow, shards, row_count)
    fields = jnp.stack([far_source, far_cotan])

    def first_section(kernel):
        field_part = jnp.einsum(
            "kn,mcnj->mckj", kernel, fields, precision=highest, preferred_element_type=jnp.float32
        )
        filter_part = jnp.einsum(
            "kn,cnj->ckj",
            kernel,
            filt_blocks,
            precision=highest,
            preferred_element_type=jnp.float32,
        )
        return jnp.concatenate([field_part, filter_part[None]], axis=0)

    first_re, first_im = tables(2 * shards, shards, 2 * shards, -1.0)
    spec_re, spec_im = (first_section(first_re), first_section(first_im))
    spec_re, spec_im = twiddle(spec_re, spec_im, 2 * shards, row_count, total, -1.0)
    fwd_re, fwd_im = tables(row_count, row_count, row_count, -1.0)
    spec_re, spec_im = along_positions(spec_re, spec_im, fwd_re, fwd_im)
    source_re, source_im = (spec_re[0], spec_im[0])
    cotan_re, cotan_im = (spec_re[1], spec_im[1])
    filter_re, filter_im = (spec_re[2], spec_im[2])
    prod_re = jnp.stack(
        [
            source_re * filter_re - source_im * filter_im,
            cotan_re * filter_re + cotan_im * filter_im,
            cotan_re * source_re + cotan_im * source_im,
        ]
    )
    prod_im = jnp.stack(
        [
            source_re * filter_im + source_im * filter_re,
            cotan_im * filter_re - cotan_re * filter_im,
            cotan_im * source_re - cotan_re * source_im,
        ]
    )
    back_re, back_im = tables(row_count, row_count, row_count, 1.0)
    prod_re, prod_im = along_positions(prod_re, prod_im, back_re, back_im)
    prod_re, prod_im = twiddle(prod_re, prod_im, 2 * shards, row_count, total, 1.0)
    last_re, last_im = tables(shards, 2 * shards, 2 * shards, 1.0)
    field_out = jnp.einsum(
        "nk,mckj->mcnj", last_re, prod_re[:2], precision=highest, preferred_element_type=jnp.float32
    ) - jnp.einsum(
        "nk,mckj->mcnj", last_im, prod_im[:2], precision=highest, preferred_element_type=jnp.float32
    )
    field_out = field_out * (1.0 / total)
    filt_grad = jnp.einsum(
        "nk,ckj->cnj", last_re, prod_re[2], precision=highest, preferred_element_type=jnp.float32
    ) - jnp.einsum(
        "nk,ckj->cnj", last_im, prod_im[2], precision=highest, preferred_element_type=jnp.float32
    )
    filt_grad = (filt_grad * (1.0 / total)).reshape(narrow, seq_len)
    modulated = filt_grad * envelope
    weight_part = jnp.einsum(
        "th,ct->hc", hidden, modulated, precision=highest, preferred_element_type=jnp.float32
    )
    hidden_grad = jnp.einsum(
        "ct,hc->th", modulated, chan_weight, precision=highest, preferred_element_type=jnp.float32
    )
    first_part = jnp.dot(
        feats.T,
        hidden_grad * jnp.cos(pre_act),
        precision=highest,
        preferred_element_type=jnp.float32,
    )
    grad_first = lax.psum(first_part, ("ctx", "ch", "sub"))
    returned = lax.all_to_all(
        field_out.astype(jnp.bfloat16), "ctx", split_axis=2, concat_axis=1, tiled=True
    ).astype(field_out.dtype)
    conv_part = returned[0, :, 0, :].T
    corr_part = returned[1, :, 0, :].T
    grad_two = (grad_out.astype(jnp.float32) * (conv_part + skip_bias[None, :] * source)).astype(
        jnp.bfloat16
    )
    grad_mid = corr_part + skip_bias[None, :] * cotan
    grad_one = (grad_mid * values.astype(jnp.float32)).astype(jnp.bfloat16)
    grad_value = (grad_mid * x_one.astype(jnp.float32)).astype(jnp.bfloat16)
    grad_bias = lax.psum(jnp.sum(source * cotan, axis=0), "ctx")
    grad_second = lax.all_gather(weight_part, "ctx", axis=1, tiled=True)
    return (grad_one, grad_two, grad_value, grad_first, grad_second, grad_bias)


STEP = 16
SIDE = 256


def halves(array):
    array = np.asarray(array, np.float32)
    high = array.astype(bf16)
    low = (array - high.astype(np.float32)).astype(bf16)
    return high, low


def block_tables(rows):
    freq = np.concatenate([np.arange(0, rows, 2), np.arange(1, rows, 2)])
    phase = (2 * freq + 1)[:, None] * np.arange(rows)[None, :] % (4 * rows)
    angle = phase * (2.0 * np.pi / (4 * rows))
    forward = np.concatenate([np.cos(angle), -np.sin(angle)], axis=0)
    front = np.ascontiguousarray(np.concatenate(halves(forward), axis=1))
    back = np.ascontiguousarray(np.concatenate(halves(forward.T / rows), axis=0))
    return front, back


def feature_table(seq_len):
    phase = np.arange(seq_len)[:, None] * np.array(band_steps)[None, :] % 4096
    angle = phase * (2.0 * np.pi / 4096.0)
    return np.concatenate([np.cos(angle), np.sin(angle)], axis=1).astype(np.float32)


def split(array):
    high = array.astype(bf16)
    return high, (array - high.astype(f32)).astype(bf16)


def dot(left, right):
    return jnp.dot(left, right, preferred_element_type=f32)


def exact_dot(left, right):
    return jnp.dot(left, right, precision=highest, preferred_element_type=f32)


def dot_across(left, right):
    return lax.dot_general(left, right, (((1,), (1,)), ((), ())), preferred_element_type=f32)


def decay(rate, rows, scale):
    place = lax.broadcasted_iota(jnp.int32, (rows, rate.shape[1]), 0)
    return jnp.exp(-place.astype(f32) * rate) * scale


def times(a, b):
    return a[0] * b[0] - a[1] * b[1], a[0] * b[1] + a[1] * b[0]


def conj_times(a, b):
    return a[0] * b[0] + a[1] * b[1], a[0] * b[1] - a[1] * b[0]


def plus(a, b):
    return a[0] + b[0], a[1] + b[1]


def scaled(a, factor):
    return a[0] * factor, a[1] * factor


def choose(condition, a, b):
    return jnp.where(condition, a[0], b[0]), jnp.where(condition, a[1], b[1])


def turned(a, sign):
    return (a[1], -a[0]) if sign > 0 else (-a[1], a[0])


def forward(front_ref, block):
    return dot(front_ref[...], jnp.concatenate([block, block], axis=0))


def backward(back_ref, high, low=None):
    both = dot(back_ref[...], high)
    rows = both.shape[0] // 2
    out = both[:rows] + both[rows:]
    return out if low is None else out + dot(back_ref[:rows], low)


def row_groups(rows):
    for step in range(rows // STEP):
        sign = 1 if step * STEP < rows // 2 else -1
        yield slice(step * STEP, (step + 1) * STEP), slice(rows + step * STEP, rows + (step + 1) * STEP), sign


def weight_sums(trans, m_high, m_low):
    both = dot(trans, m_high)
    count = both.shape[0] // 2
    return both[:count] + both[count:] + dot(trans[:count], m_low)


def hidden_sums(m_high, m_low, w_high, w_low):
    left = jnp.concatenate([m_high, m_high, m_low], axis=1)
    right = jnp.concatenate([w_high, w_low, w_high], axis=1)
    return dot_across(left, right)


def looped(kernel, kinds, blocks, width):
    def over_strips(*refs):
        def step(block, carry):
            cols = pl.ds(pl.multiple_of(block * width, width), width)
            views = [
                ref if kind is None else ref.at[(*kind, cols)]
                for ref, kind in zip(refs, kinds + (None,) * (len(refs) - len(kinds)))
            ]
            kernel(block, blocks, *views)
            return carry

        lax.fori_loop(0, blocks, step, 0)

    return over_strips


ROWS = (slice(None),)
CUBE = (slice(None), slice(None))


def products_kernel(rank_ref, one_ref, two_ref, val_ref, out_ref, source_ref, cotan_ref, edge_ref, bias_ref):
    source = one_ref[...].astype(f32) * val_ref[...].astype(f32)
    cotan = out_ref[...].astype(f32) * two_ref[...].astype(f32)
    source_ref[...] = source.astype(bf16)
    cotan_ref[...] = cotan.astype(bf16)
    edge_ref[...] = jnp.where(rank_ref[0] == 0, source, cotan).astype(bf16)
    part = jnp.sum(source * cotan, axis=0, keepdims=True)

    @pl.when(pl.program_id(0) == 0)
    def _():
        bias_ref[...] = part

    @pl.when(pl.program_id(0) > 0)
    def _():
        bias_ref[...] += part


def sin_cos(angle):
    turns = jnp.floor(angle * (2.0 / math.pi) + 0.5)
    rest = ((angle - turns * 1.5703125) - turns * 4.837512969970703e-4) - turns * 7.54978995489188e-8
    square = rest * rest
    sine = rest + rest * square * (
        -1.6666654611e-1 + square * (8.3321608736e-3 + square * -1.9515295891e-4)
    )
    cosine = 1.0 - 0.5 * square + square * square * (
        4.166664568298827e-2 + square * (-1.388731625493765e-3 + square * 2.443315711809948e-5)
    )
    quarter = turns.astype(jnp.int32)
    odd = (quarter & 1) == 1
    sin_sign = jnp.where((quarter & 2) == 2, -1.0, 1.0).astype(f32)
    cos_sign = jnp.where(((quarter + 1) & 2) == 2, -1.0, 1.0).astype(f32)
    return jnp.where(odd, cosine, sine) * sin_sign, jnp.where(odd, sine, cosine) * cos_sign


def turned_over(hidden, slope):
    both = jnp.concatenate([hidden, slope], axis=1).T
    return jnp.concatenate(split(both[: hidden.shape[1]]), axis=0)


def filters_kernel(
    rows, shards, blocks, width, passed, feats_ref, first_ref, weight_ref, rate_ref, front_ref, spec_ref, trans_ref,
    slope_ref, passing, hid_ref,
):
    del passed, passing
    hidden, slope = sin_cos(exact_dot(feats_ref[...], first_ref[...]))
    slope_ref[...] = slope
    high, low = split(hidden)
    hid_ref[...] = jnp.concatenate([high, high, low], axis=1)
    trans_ref[...] = turned_over(hidden, slope)
    strips = looped(
        functools.partial(filter_strip, rows, shards), (None, ROWS, ROWS, None, CUBE), blocks, width
    )
    strips(hid_ref, weight_ref, rate_ref, front_ref, spec_ref)


def filter_strip(rows, shards, block, blocks, hid_ref, weight_ref, rate_ref, front_ref, spec_ref):
    scale = float(rows * shards) ** -0.5
    w_high, w_low = split(weight_ref[...])
    stacked = jnp.concatenate([w_high, w_low, w_high], axis=0)
    rate = rate_ref[...]
    env = decay(rate, rows, scale)
    before = None
    for lag in range(shards):
        part = dot(hid_ref[lag * rows : (lag + 1) * rows, :], stacked)
        part = part * (env * jnp.exp(rate * (-float(lag * rows))))
        f_high, f_low = split(part)
        now = forward(front_ref, f_high) + dot(front_ref[:, :rows], f_low)
        for re, im, sign in row_groups(rows):
            here = (now[re], now[im])
            if before is not None:
                here = plus(here, turned((before[re], before[im]), -sign))
            spec_ref[lag, re, :] = here[0].astype(bf16)
            spec_ref[lag, im, :] = here[1].astype(bf16)
        before = now


def own_kernel(rows, shards, channels, blocks, width, *refs):
    inputs, (sums_out, send_out), held = refs[:10], refs[11:13], refs[14:24]
    sums_ref, send_ref, trans_ref, acc_ref, sems, out_sems = refs[24:]
    (
        feats_ref, first_ref, source_ref, cotan_ref, weight_ref, rate_ref, front_ref, back_ref, featt_ref, bias_ref
    ) = held
    copies = [pltpu.make_async_copy(far, near, sems.at[i]) for i, (far, near) in enumerate(zip(inputs, held))]
    for copy in copies:
        copy.start()
    acc_ref[...] = jnp.zeros_like(acc_ref)
    copies[0].wait()
    copies[1].wait()
    hidden, slope = sin_cos(exact_dot(feats_ref[...], first_ref[...]))
    trans_ref[...] = turned_over(hidden, slope)
    for copy in copies[2:]:
        copy.wait()

    def leaving(block):
        cols = pl.ds(pl.multiple_of(block * width, width), width)
        return pltpu.make_async_copy(sums_ref.at[:, cols], sums_out.at[:, cols], out_sems.at[block])

    def strip(block, blocks, *views):
        own_strip(rows, shards, *views)
        leaving(block).start()

    kinds = (ROWS, ROWS, ROWS, ROWS, None, None, None, ROWS, ROWS, None)
    looped(strip, kinds, blocks, width)(
        source_ref, cotan_ref, weight_ref, rate_ref, front_ref, back_ref, trans_ref, sums_ref, send_ref, acc_ref
    )
    first = exact_dot(featt_ref[:, :rows], acc_ref[...] * slope)
    put_side(send_ref, channels, fold(bias_ref[...]), first)
    last = pltpu.make_async_copy(send_ref, send_out, out_sems.at[blocks])
    last.start()
    for block in range(blocks):
        leaving(block).wait()
    last.wait()


def own_strip(
    rows, shards, source_ref, cotan_ref, weight_ref, rate_ref, front_ref, back_ref, trans_ref, sums_ref,
    send_ref, acc_ref,
):
    x0 = forward(front_ref, source_ref[...])
    c0 = forward(front_ref, cotan_ref[...])
    pair = conj_times((x0[:rows], x0[rows:]), (c0[:rows], c0[rows:]))
    high, low = split(jnp.concatenate(pair, axis=0))
    env = decay(rate_ref[...], rows, float(rows * shards) ** -0.5)
    m_high, m_low = split(backward(back_ref, high, low) * env)
    sums = weight_sums(trans_ref[...], m_high, m_low)
    sums_ref[...] = sums
    send_ref[...] = sums.astype(bf16)
    acc_ref[...] += hidden_sums(m_high, m_low, *split(weight_ref[...]))


def fold(bias):
    return jnp.concatenate([bias[:, i * 128 : (i + 1) * 128] for i in range(bias.shape[1] // 128)], axis=0)


def put_side(pay_ref, channels, bias, first=None):
    half = pay_ref.shape[0] // 2
    pay_ref[:, channels:] = jnp.zeros((2 * half, SIDE), bf16)
    for start, part in zip((0, 128), split(bias)):
        pay_ref[: bias.shape[0], channels + start : channels + start + 128] = part
    if first is not None:
        for start, part in zip((0, 128), split(first)):
            pay_ref[half:, channels + start : channels + start + first.shape[1]] = part


def get_side(pay, channels, lanes, hid_count):
    half = pay.shape[0] // 2
    side = pay[:, channels : channels + 128].astype(f32) + pay[:, channels + 128 :].astype(f32)
    return side[:lanes], side[half:, :hid_count]


def near_kernel(
    rows, shards, block, blocks, passed, rank_ref, x0_ref, c0_ref, x1_ref, c1_ref, spec_ref, weight_ref, rate_ref,
    front_ref, back_ref, trans_ref, featt_ref, slope_ref, own_ref, conv_ref, corr_ref, ahead_ref, sums_ref, first_ref,
    passing, fields, fast, high_ref, low_ref, acc_ref,
):
    del passed, passing
    rank = rank_ref[0]
    count = shards - 1
    lower = rank == 1
    inner = jnp.logical_and(rank > 0, rank < shards - 1)
    upper = jnp.where(rank == 2, 1.0, 0.0).astype(f32)
    side = jnp.where(rank == 2, 1.0, -1.0).astype(f32)

    @pl.when(block == 0)
    def _():
        acc_ref[...] = jnp.zeros_like(acc_ref)

    for index, ref in enumerate((x0_ref, c0_ref, x1_ref, c1_ref)):
        fields[index] = forward(front_ref, ref[...])
    for re, im, sign in row_groups(rows):
        x0, c0, x1, c1 = ((fields[i, re, :], fields[i, im, :]) for i in range(4))
        w0, w1 = ((spec_ref[i, re, :].astype(f32), spec_ref[i, im, :].astype(f32)) for i in range(2))
        for index, value in enumerate(
            (plus(times(w0, x0), times(w1, x1)), plus(conj_times(w0, c0), conj_times(w1, c1)))
        ):
            fast[index, re, :] = value[0].astype(bf16)
            fast[index, im, :] = value[1].astype(bf16)
    conv_ref[...] = backward(back_ref, fast[0])
    corr_ref[...] = backward(back_ref, fast[1])

    @pl.when(jnp.logical_not(inner))
    def _():
        sums_ref[...] = own_ref[...]
        ahead_ref[...] = jnp.zeros_like(ahead_ref)

    @pl.when(inner)
    def _():
        for re, im, sign in row_groups(rows):
            x0, c0, x1, c1 = ((fields[i, re, :], fields[i, im, :]) for i in range(4))
            w2 = (spec_ref[2, re, :].astype(f32), spec_ref[2, im, :].astype(f32) * side)
            ahead = times(w2, choose(lower, c1, x1))
            fast[2, re, :] = ahead[0].astype(bf16)
            fast[2, im, :] = ahead[1].astype(bf16)
            one = plus(conj_times(x1, c0), scaled(conj_times(x0, c1), upper))
            two = conj_times(x1, c1)
            for index, value in enumerate((turned(one, sign), plus(one, turned(two, sign)), two)):
                for part, where in zip(value, (re, im)):
                    high_ref[index, where, :], low_ref[index, where, :] = split(part)
        ahead_ref[...] = backward(back_ref, fast[2])
        rate = rate_ref[...]
        env = decay(rate, rows, float(rows * shards) ** -0.5)
        parts = []
        for lag in range(count):
            grad = backward(back_ref, high_ref[lag], low_ref[lag])
            parts.append(split(grad * (env * jnp.exp(rate * (-float(lag * rows))))))
        m_high = jnp.concatenate([p[0] for p in parts], axis=0)
        m_low = jnp.concatenate([p[1] for p in parts], axis=0)
        sums_ref[...] = own_ref[...] + weight_sums(trans_ref[:, : count * rows], m_high, m_low)
        w_high, w_low = split(weight_ref[...])
        acc_ref[...] += hidden_sums(m_high, m_low, w_high, w_low)

    @pl.when(block == blocks - 1)
    def _():
        first_ref[...] = exact_dot(
            featt_ref[:, : count * rows], acc_ref[...] * slope_ref[: count * rows, :]
        )


def far_kernel(rows, block, blocks, rank_ref, far_ref, spec_ref, front_ref, back_ref, ahead_ref, part_ref, late_ref):
    side = jnp.where(rank_ref[0] == 2, 1.0, -1.0).astype(f32)
    far = forward(front_ref, far_ref[...])
    far = (far[:rows], far[rows:])
    w2, w3 = ((spec_ref[i, :rows, :].astype(f32), spec_ref[i, rows:, :].astype(f32) * side) for i in range(2))
    ahead = jnp.concatenate(times(w3, far), axis=0).astype(bf16)
    part_ref[...] = (ahead_ref[...] + backward(back_ref, ahead)).astype(bf16)
    late = jnp.concatenate(times(w2, far), axis=0).astype(bf16)
    late_ref[...] = backward(back_ref, late)


def last_kernel(
    rows, shards, channels, block, blocks, after_ref, rank_ref, x1_ref, c1_ref, far_ref, weight_ref, rate_ref, front_ref, back_ref,
    trans_ref, featt_ref, slope_ref, sums_ref, first_ref, own_ref, bias_ref, in_ref, pay_ref, total_ref, acc_ref,
):
    del after_ref
    hid_count, width = weight_ref.shape
    lower = rank_ref[0] == 1
    start = pl.multiple_of(block * width, width)
    here = sums_ref[...] + in_ref[:, pl.ds(start, width)].astype(f32)
    mine = (block < blocks // 2) == lower

    @pl.when(block == 0)
    def _():
        acc_ref[...] = jnp.zeros_like(acc_ref)

    @pl.when(mine)
    def _():
        sign = jnp.where(lower, 1.0, -1.0).astype(f32)
        near = forward(front_ref, jnp.where(lower, x1_ref[...], c1_ref[...]))
        far = forward(front_ref, far_ref[...])
        three = conj_times((near[:rows], near[rows:]), (far[:rows], far[rows:]))
        three = (three[0], three[1] * sign)
        half = rows // 2
        two = jnp.concatenate([three[1][:half], -three[1][half:], -three[0][:half], three[0][half:]], axis=0)
        rate = rate_ref[...]
        env = decay(rate, rows, float(rows * shards) ** -0.5)
        parts = []
        for lag, value in ((shards - 2, two), (shards - 1, jnp.concatenate(three, axis=0))):
            grad = backward(back_ref, *split(value))
            parts.append(split(grad * (env * jnp.exp(rate * (-float(lag * rows))))))
        m_high = jnp.concatenate([p[0] for p in parts], axis=0)
        m_low = jnp.concatenate([p[1] for p in parts], axis=0)
        trans = trans_ref[:, (shards - 2) * rows :]
        pay_ref[:, pl.ds(start, width)] = (here + weight_sums(trans, m_high, m_low)).astype(bf16)
        w_high, w_low = split(weight_ref[...])
        acc_ref[...] += hidden_sums(m_high, m_low, w_high, w_low)

    @pl.when(jnp.logical_not(mine))
    def _():
        pay_ref[:, pl.ds(start, width)] = here.astype(bf16)

    @pl.when(block == blocks - 1)
    def _():
        first = exact_dot(
            featt_ref[:, (shards - 2) * rows :], acc_ref[...] * slope_ref[(shards - 2) * rows :, :]
        )
        lanes = channels // 128
        own_first = get_side(own_ref[...], channels, lanes, hid_count)[1]
        in_bias, in_first = get_side(in_ref[...], channels, lanes, hid_count)
        first = first + first_ref[...] + own_first + in_first
        put_side(pay_ref, channels, fold(bias_ref[...]) + in_bias)
        total_ref[...] = first


def total_kernel(channels, hid_count, part_ref, own_ref, come_ref, first_ref, first_come_ref, pay_ref):
    del part_ref
    lanes = channels // 128
    pay_ref[:, :channels] = (own_ref[:, :channels].astype(f32) + come_ref[:, :channels].astype(f32)).astype(bf16)
    own, come = (get_side(ref[...], channels, lanes, hid_count)[0] for ref in (own_ref, come_ref))
    put_side(pay_ref, channels, own + come, first_ref[...] + first_come_ref[...])


def gates_kernel(
    shards, block, blocks, rank_ref, one_ref, two_ref, val_ref, out_ref, skip_ref, conv_ref, corr_ref, late_ref, part_ref,
    grad_one_ref, grad_two_ref, grad_value_ref,
):
    rank = rank_ref[0]

    def mask(wanted):
        return jnp.where(rank == wanted, 1.0, 0.0).astype(f32)

    part = part_ref[...].astype(f32)
    late = late_ref[...]
    one = one_ref[...].astype(f32)
    val = val_ref[...].astype(f32)
    out = out_ref[...].astype(f32)
    skip = skip_ref[...]
    conv = conv_ref[...] + late * mask(2) + part * mask(shards - 1)
    corr = corr_ref[...] + late * mask(1) + part * mask(0)
    grad_two_ref[...] = (out * (conv + skip * (one * val))).astype(bf16)
    mid = corr + skip * (out * two_ref[...].astype(f32))
    grad_one_ref[...] = (mid * val).astype(bf16)
    grad_value_ref[...] = (mid * one).astype(bf16)


def finish_kernel(
    channels, shards, rank_ref, own_ref, come_ref, second_out, first_out, bias_out, second, first, bias, sems
):
    rank = rank_ref[0]
    inner = jnp.logical_and(rank > 0, rank < shards - 1)
    lanes = channels // 128
    copies = [
        pltpu.make_async_copy(held, out, sems.at[i])
        for i, (held, out) in enumerate(((second, second_out), (first, first_out), (bias, bias_out)))
    ]
    picked = jnp.where(inner, own_ref[...], come_ref[...])
    second[...] = picked[:, :channels].astype(f32)
    copies[0].start()
    rows, first[...] = get_side(picked, channels, lanes, first.shape[1])
    copies[1].start()
    for i in range(lanes):
        bias[:, i * 128 : (i + 1) * 128] = rows[i : i + 1]
    copies[2].start()
    for copy in copies:
        copy.wait()


def few_shards_body(
    x_one, x_two, values, grad_out, first_weight, second_weight, skip_bias, decay_rate
):
    rows, channels = x_one.shape
    shards = lax.axis_size("ctx")
    feat_count, hid_count = first_weight.shape
    seq_len = rows * shards
    double = 2 * rows
    width = min(512, channels)
    blocks = channels // width
    rank = lax.axis_index("ctx").astype(jnp.int32).reshape(1)
    front, back = block_tables(rows)
    feats = feature_table(seq_len)
    featt = np.ascontiguousarray(feats.T)
    skip_row = skip_bias.reshape(1, channels)
    rate_row = decay_rate.reshape(1, channels)
    smem = pl.BlockSpec(memory_space=pltpu.SMEM)
    vmem = pl.BlockSpec(memory_space=pltpu.VMEM)
    anywhere = pl.BlockSpec(memory_space=pl.ANY)
    mebi = 1024 * 1024

    def shape(*dims, dtype=f32):
        return jax.ShapeDtypeStruct(dims, dtype)

    def call(kernel, name, units, out_shape, in_specs, out_specs=None, scratch=(), limit=16, aliases={}):
        return pl.pallas_call(
            kernel,
            in_specs=in_specs,
            out_specs=out_specs if out_specs is not None else [vmem] * len(out_shape),
            out_shape=out_shape,
            scratch_shapes=scratch,
            input_output_aliases=aliases,
            compiler_params=pltpu.CompilerParams(vmem_limit_bytes=limit * mebi),
            cost_estimate=pl.CostEstimate(
                flops=2 * units * double * double * channels, bytes_accessed=rows * channels, transcendentals=0
            ),
            name=name,
        )

    def move(array, pairs):
        return lax.ppermute(array, "ctx", pairs)

    up = [(i, i + 1) for i in range(shards - 1)]
    down = [(i + 1, i) for i in range(shards - 1)]
    inward = [(0, 1), (shards - 1, shards - 2)]
    outward = [(1, 0), (shards - 2, shards - 1)]
    across = [(1, 2), (2, 1)]
    pay_shape = (hid_count, channels + SIDE)
    block_bf16 = shape(rows, channels, dtype=bf16)
    block_f32 = shape(rows, channels)

    row_step = max(rows // 2, 16)
    gate_rows = pl.BlockSpec((row_step, channels), lambda i: (i, 0))
    x0, c0, edge, bias = pl.pallas_call(
        products_kernel,
        grid=(rows // row_step,),
        in_specs=[smem] + [gate_rows] * 4,
        out_specs=[gate_rows] * 3 + [pl.BlockSpec((1, channels), lambda i: (0, 0))],
        out_shape=[block_bf16] * 3 + [shape(1, channels)],
        compiler_params=pltpu.CompilerParams(vmem_limit_bytes=64 * mebi),
        name="products",
    )(rank, x_one, x_two, values, grad_out)
    x1 = move(x0, up)
    c1 = move(c0, down)

    own_shapes = [
        shape(rows, feat_count), shape(feat_count, hid_count), block_bf16, block_bf16, shape(hid_count, channels),
        shape(1, channels), shape(double, double, dtype=bf16), shape(double, double, dtype=bf16),
        shape(feat_count, seq_len), shape(1, channels), shape(hid_count, channels), shape(*pay_shape, dtype=bf16),
    ]
    own, send, edge = call(
        functools.partial(own_kernel, rows, shards, channels, blocks, width), "own_pair", 8,
        [shape(hid_count, channels), shape(*pay_shape, dtype=bf16), block_bf16],
        [anywhere] * 11,
        out_specs=[anywhere] * 3,
        scratch=[pltpu.VMEM(s.shape, s.dtype) for s in own_shapes]
        + [
            pltpu.VMEM((2 * hid_count, rows), bf16), pltpu.VMEM((rows, hid_count), f32),
            pltpu.SemaphoreType.DMA((10,)), pltpu.SemaphoreType.DMA((blocks + 1,)),
        ],
        aliases={10: 2},
        limit=60,
    )(feats[:rows], first_weight, x0, c0, second_weight, rate_row, front, back, featt, bias, edge)
    far = move(edge, [(0, 2), (shards - 1, shards - 3)])

    spec, trans, slope, send = call(
        functools.partial(filters_kernel, rows, shards, blocks, width), "filters", 8,
        [
            shape(shards, double, channels, dtype=bf16), shape(2 * hid_count, seq_len, dtype=bf16),
            shape(seq_len, hid_count), shape(*pay_shape, dtype=bf16),
        ],
        [anywhere] + [vmem] * 5,
        out_specs=[vmem] * 3 + [anywhere],
        scratch=[pltpu.VMEM((seq_len, 3 * hid_count), bf16)],
        aliases={0: 3},
    )(send, feats, first_weight, second_weight, rate_row, front)

    conv, corr, ahead, sums, first, send = call(
        looped(
            functools.partial(near_kernel, rows, shards),
            (None, None) + (ROWS,) * 4 + (CUBE, ROWS, ROWS) + (None,) * 5 + (ROWS,) * 5,
            blocks, width,
        ),
        "near_blocks", 20,
        [block_f32] * 3
        + [shape(hid_count, channels), shape(feat_count, hid_count), shape(*pay_shape, dtype=bf16)],
        [anywhere, smem] + [vmem] * 13,
        out_specs=[vmem] * 5 + [anywhere],
        scratch=[
            pltpu.VMEM((4, double, width), f32),
            pltpu.VMEM((3, double, width), bf16),
            pltpu.VMEM((shards - 1, double, width), bf16),
            pltpu.VMEM((shards - 1, double, width), bf16),
            pltpu.VMEM(((shards - 1) * rows, hid_count), f32),
        ],
        aliases={0: 5},
    )(send, rank, x0, c0, x1, c1, spec, second_weight, rate_row, front, back, trans, featt, slope, own)

    come = move(send, inward)

    part, late = call(
        looped(
            functools.partial(far_kernel, rows),
            (None, ROWS, (slice(2, 4), slice(None)), None, None, ROWS, ROWS, ROWS),
            blocks, width,
        ),
        "far_block", 1,
        [block_bf16, block_f32],
        [smem] + [vmem] * 5,
    )(rank, far, spec, front, back, ahead)
    part_come = move(part, outward)

    pay, first = call(
        looped(
            functools.partial(last_kernel, rows, shards, channels),
            (None, None, ROWS, ROWS, ROWS, ROWS, ROWS, None, None, None, None, None, ROWS),
            blocks, width,
        ),
        "last_pair", 1,
        [shape(*pay_shape, dtype=bf16), shape(feat_count, hid_count)],
        [anywhere, smem] + [vmem] * 15,
        scratch=[pltpu.VMEM((2 * rows, hid_count), f32)],
    )(late, rank, x1, c1, far, second_weight, rate_row, front, back, trans, featt, slope, sums, first, send, bias, come)
    pay_come = move(pay, across)
    group = lax.axis_size(("ch", "sub"))
    bit = 1
    while bit < group:
        first = first + lax.ppermute(first, ("ch", "sub"), [(i, i ^ bit) for i in range(group)])
        bit *= 2

    (total,) = call(
        functools.partial(total_kernel, channels, hid_count), "total", 0,
        [shape(*pay_shape, dtype=bf16)],
        [anywhere] + [vmem] * 4,
    )(part_come, pay, pay_come, first, move(first, across))
    total_come = move(total, outward)

    grad_one, grad_two, grad_value = call(
        looped(
            functools.partial(gates_kernel, shards), (None,) + (ROWS,) * 12, blocks, width
        ),
        "gates", 0,
        [block_bf16] * 3,
        [smem] + [vmem] * 9,
    )(rank, x_one, x_two, values, grad_out, skip_row, conv, corr, late, part_come)

    outs = [shape(hid_count, channels), shape(feat_count, hid_count), shape(1, channels)]
    grad_second, grad_first, grad_bias = call(
        functools.partial(finish_kernel, channels, shards), "finish", 0,
        outs,
        [smem] + [vmem] * 2,
        out_specs=[anywhere] * 3,
        scratch=[pltpu.VMEM(o.shape, f32) for o in outs] + [pltpu.SemaphoreType.DMA((3,))],
    )(rank, total, total_come)
    return (grad_one, grad_two, grad_value, grad_first, grad_second, grad_bias.reshape(channels))


def solution(mesh):
    in_specs = (
        P(("parts", "ctx"), ("ch", "sub")),
        P(("parts", "ctx"), ("ch", "sub")),
        P(("parts", "ctx"), ("ch", "sub")),
        P(("parts", "ctx"), ("ch", "sub")),
        P(),
        P(None, ("ch", "sub")),
        P(("ch", "sub")),
        P(("ch", "sub")),
    )
    out_specs = (
        P(("parts", "ctx"), ("ch", "sub")),
        P(("parts", "ctx"), ("ch", "sub")),
        P(("parts", "ctx"), ("ch", "sub")),
        P("parts", None),
        P("parts", ("ch", "sub")),
        P(("parts", "ch", "sub")),
    )
    body = few_shards_body if mesh.shape["ctx"] == 4 else many_shards_body
    return jax.shard_map(body, mesh=mesh, in_specs=in_specs, out_specs=out_specs, check_vma=False)
```

```python
import functools
import math

import jax
import jax.numpy as jnp
import numpy as np
from jax import lax
from jax.experimental import pallas as pl
from jax.experimental.pallas import tpu as pltpu
from jax.sharding import PartitionSpec as P

band_steps = (1763, 1201, 811, 547, 367, 251, 167, 113, 79, 53, 37, 23, 17, 11, 7, 3)
highest = lax.Precision.HIGHEST
f32 = jnp.float32
bf16 = jnp.bfloat16


def features(positions):
    multiplier = jnp.array(band_steps, dtype=jnp.int32)
    phase = positions[:, None] * multiplier[None, :] % 4096
    angle = phase.astype(jnp.float32) * (2.0 * math.pi / 4096.0)
    return jnp.concatenate([jnp.cos(angle), jnp.sin(angle)], axis=1)


def tables(out_count, in_count, modulus, sign_value):
    row_index = lax.broadcasted_iota(jnp.int32, (out_count, in_count), 0)
    col_index = lax.broadcasted_iota(jnp.int32, (out_count, in_count), 1)
    angle = (row_index * col_index % modulus).astype(jnp.float32) * (2.0 * math.pi / modulus)
    return (jnp.cos(angle), sign_value * jnp.sin(angle))


def twiddle(spec_re, spec_im, freq_count, span, modulus, sign_value):
    freq_index = lax.broadcasted_iota(jnp.int32, (freq_count, span), 0)
    pos_index = lax.broadcasted_iota(jnp.int32, (freq_count, span), 1)
    angle = (freq_index * pos_index % modulus).astype(jnp.float32) * (2.0 * math.pi / modulus)
    factor_re = jnp.cos(angle)[None, None, :, :]
    factor_im = (sign_value * jnp.sin(angle))[None, None, :, :]
    return (spec_re * factor_re - spec_im * factor_im, spec_re * factor_im + spec_im * factor_re)


def contract(kernel, array):
    return jnp.einsum(
        "lj,mckj->mckl", kernel, array, precision=highest, preferred_element_type=jnp.float32
    )


def along_positions(spec_re, spec_im, kernel_re, kernel_im):
    return (
        contract(kernel_re, spec_re) - contract(kernel_im, spec_im),
        contract(kernel_re, spec_im) + contract(kernel_im, spec_re),
    )


def many_shards_body(
    x_one, x_two, values, grad_out, first_weight, second_weight, skip_bias, decay_rate
):
    row_count, chan_count = x_one.shape
    shards = lax.axis_size("ctx")
    rank = lax.axis_index("ctx")
    seq_len = row_count * shards
    total = 2 * seq_len
    narrow = chan_count // shards
    chan_weight = lax.dynamic_slice_in_dim(second_weight, rank * narrow, narrow, 1)
    chan_rate = lax.dynamic_slice_in_dim(decay_rate, rank * narrow, narrow, 0)
    source = x_one.astype(jnp.float32) * values.astype(jnp.float32)
    cotan = grad_out.astype(jnp.float32) * x_two.astype(jnp.float32)
    spread = lax.all_to_all(
        jnp.stack([source.T, cotan.T])[:, :, None, :],
        "ctx",
        split_axis=1,
        concat_axis=2,
        tiled=True,
    )
    far_source = spread[0]
    far_cotan = spread[1]
    positions = jnp.arange(seq_len, dtype=jnp.int32)
    feats = features(positions)
    pre_act = jnp.dot(feats, first_weight, precision=highest, preferred_element_type=jnp.float32)
    hidden = jnp.sin(pre_act)
    envelope = jnp.exp(-chan_rate[:, None] * positions.astype(jnp.float32)[None, :]) * float(
        seq_len
    ) ** (-0.5)
    filt = (
        jnp.einsum(
            "th,hc->ct", hidden, chan_weight, precision=highest, preferred_element_type=jnp.float32
        )
        * envelope
    )
    filt_blocks = filt.reshape(narrow, shards, row_count)
    fields = jnp.stack([far_source, far_cotan])

    def first_section(kernel):
        field_part = jnp.einsum(
            "kn,mcnj->mckj", kernel, fields, precision=highest, preferred_element_type=jnp.float32
        )
        filter_part = jnp.einsum(
            "kn,cnj->ckj",
            kernel,
            filt_blocks,
            precision=highest,
            preferred_element_type=jnp.float32,
        )
        return jnp.concatenate([field_part, filter_part[None]], axis=0)

    first_re, first_im = tables(2 * shards, shards, 2 * shards, -1.0)
    spec_re, spec_im = (first_section(first_re), first_section(first_im))
    spec_re, spec_im = twiddle(spec_re, spec_im, 2 * shards, row_count, total, -1.0)
    fwd_re, fwd_im = tables(row_count, row_count, row_count, -1.0)
    spec_re, spec_im = along_positions(spec_re, spec_im, fwd_re, fwd_im)
    source_re, source_im = (spec_re[0], spec_im[0])
    cotan_re, cotan_im = (spec_re[1], spec_im[1])
    filter_re, filter_im = (spec_re[2], spec_im[2])
    prod_re = jnp.stack(
        [
            source_re * filter_re - source_im * filter_im,
            cotan_re * filter_re + cotan_im * filter_im,
            cotan_re * source_re + cotan_im * source_im,
        ]
    )
    prod_im = jnp.stack(
        [
            source_re * filter_im + source_im * filter_re,
            cotan_im * filter_re - cotan_re * filter_im,
            cotan_im * source_re - cotan_re * source_im,
        ]
    )
    back_re, back_im = tables(row_count, row_count, row_count, 1.0)
    prod_re, prod_im = along_positions(prod_re, prod_im, back_re, back_im)
    prod_re, prod_im = twiddle(prod_re, prod_im, 2 * shards, row_count, total, 1.0)
    last_re, last_im = tables(shards, 2 * shards, 2 * shards, 1.0)
    field_out = jnp.einsum(
        "nk,mckj->mcnj", last_re, prod_re[:2], precision=highest, preferred_element_type=jnp.float32
    ) - jnp.einsum(
        "nk,mckj->mcnj", last_im, prod_im[:2], precision=highest, preferred_element_type=jnp.float32
    )
    field_out = field_out * (1.0 / total)
    filt_grad = jnp.einsum(
        "nk,ckj->cnj", last_re, prod_re[2], precision=highest, preferred_element_type=jnp.float32
    ) - jnp.einsum(
        "nk,ckj->cnj", last_im, prod_im[2], precision=highest, preferred_element_type=jnp.float32
    )
    filt_grad = (filt_grad * (1.0 / total)).reshape(narrow, seq_len)
    modulated = filt_grad * envelope
    weight_part = jnp.einsum(
        "th,ct->hc", hidden, modulated, precision=highest, preferred_element_type=jnp.float32
    )
    hidden_grad = jnp.einsum(
        "ct,hc->th", modulated, chan_weight, precision=highest, preferred_element_type=jnp.float32
    )
    first_part = jnp.dot(
        feats.T,
        hidden_grad * jnp.cos(pre_act),
        precision=highest,
        preferred_element_type=jnp.float32,
    )
    grad_first = lax.psum(first_part, ("ctx", "ch", "sub"))
    returned = lax.all_to_all(
        field_out.astype(jnp.bfloat16), "ctx", split_axis=2, concat_axis=1, tiled=True
    ).astype(field_out.dtype)
    conv_part = returned[0, :, 0, :].T
    corr_part = returned[1, :, 0, :].T
    grad_two = (grad_out.astype(jnp.float32) * (conv_part + skip_bias[None, :] * source)).astype(
        jnp.bfloat16
    )
    grad_mid = corr_part + skip_bias[None, :] * cotan
    grad_one = (grad_mid * values.astype(jnp.float32)).astype(jnp.bfloat16)
    grad_value = (grad_mid * x_one.astype(jnp.float32)).astype(jnp.bfloat16)
    grad_bias = lax.psum(jnp.sum(source * cotan, axis=0), "ctx")
    grad_second = lax.all_gather(weight_part, "ctx", axis=1, tiled=True)
    return (grad_one, grad_two, grad_value, grad_first, grad_second, grad_bias)


STEP = 16
SIDE = 256


def halves(array):
    array = np.asarray(array, np.float32)
    high = array.astype(bf16)
    low = (array - high.astype(np.float32)).astype(bf16)
    return high, low


def block_tables(rows):
    freq = np.concatenate([np.arange(0, rows, 2), np.arange(1, rows, 2)])
    phase = (2 * freq + 1)[:, None] * np.arange(rows)[None, :] % (4 * rows)
    angle = phase * (2.0 * np.pi / (4 * rows))
    forward = np.concatenate([np.cos(angle), -np.sin(angle)], axis=0)
    front = np.ascontiguousarray(np.concatenate(halves(forward), axis=1))
    back = np.ascontiguousarray(np.concatenate(halves(forward.T / rows), axis=0))
    return front, back


def feature_table(seq_len):
    phase = np.arange(seq_len)[:, None] * np.array(band_steps)[None, :] % 4096
    angle = phase * (2.0 * np.pi / 4096.0)
    return np.concatenate([np.cos(angle), np.sin(angle)], axis=1).astype(np.float32)


def split(array):
    high = array.astype(bf16)
    return high, (array - high.astype(f32)).astype(bf16)


def dot(left, right):
    return jnp.dot(left, right, preferred_element_type=f32)


def exact_dot(left, right):
    return jnp.dot(left, right, precision=highest, preferred_element_type=f32)


def dot_across(left, right):
    return lax.dot_general(left, right, (((1,), (1,)), ((), ())), preferred_element_type=f32)


def decay(rate, rows, scale):
    place = lax.broadcasted_iota(jnp.int32, (rows, rate.shape[1]), 0)
    return jnp.exp(-place.astype(f32) * rate) * scale


def times(a, b):
    return a[0] * b[0] - a[1] * b[1], a[0] * b[1] + a[1] * b[0]


def conj_times(a, b):
    return a[0] * b[0] + a[1] * b[1], a[0] * b[1] - a[1] * b[0]


def plus(a, b):
    return a[0] + b[0], a[1] + b[1]


def scaled(a, factor):
    return a[0] * factor, a[1] * factor


def choose(condition, a, b):
    return jnp.where(condition, a[0], b[0]), jnp.where(condition, a[1], b[1])


def turned(a, sign):
    return (a[1], -a[0]) if sign > 0 else (-a[1], a[0])


def forward(front_ref, block):
    return dot(front_ref[...], jnp.concatenate([block, block], axis=0))


def backward(back_ref, high, low=None):
    both = dot(back_ref[...], high)
    rows = both.shape[0] // 2
    out = both[:rows] + both[rows:]
    return out if low is None else out + dot(back_ref[:rows], low)


def row_groups(rows):
    for step in range(rows // STEP):
        sign = 1 if step * STEP < rows // 2 else -1
        yield slice(step * STEP, (step + 1) * STEP), slice(rows + step * STEP, rows + (step + 1) * STEP), sign


def weight_sums(trans, m_high, m_low):
    both = dot(trans, m_high)
    count = both.shape[0] // 2
    return both[:count] + both[count:] + dot(trans[:count], m_low)


def hidden_sums(m_high, m_low, w_high, w_low):
    left = jnp.concatenate([m_high, m_high, m_low], axis=1)
    right = jnp.concatenate([w_high, w_low, w_high], axis=1)
    return dot_across(left, right)


def looped(kernel, kinds, blocks, width):
    def over_strips(*refs):
        def step(block, carry):
            cols = pl.ds(pl.multiple_of(block * width, width), width)
            views = [
                ref if kind is None else ref.at[(*kind, cols)]
                for ref, kind in zip(refs, kinds + (None,) * (len(refs) - len(kinds)))
            ]
            kernel(block, blocks, *views)
            return carry

        lax.fori_loop(0, blocks, step, 0)

    return over_strips


ROWS = (slice(None),)
CUBE = (slice(None), slice(None))


def products_kernel(rank_ref, one_ref, two_ref, val_ref, out_ref, source_ref, cotan_ref, edge_ref, bias_ref):
    source = one_ref[...].astype(f32) * val_ref[...].astype(f32)
    cotan = out_ref[...].astype(f32) * two_ref[...].astype(f32)
    source_ref[...] = source.astype(bf16)
    cotan_ref[...] = cotan.astype(bf16)
    edge_ref[...] = jnp.where(rank_ref[0] == 0, source, cotan).astype(bf16)
    part = jnp.sum(source * cotan, axis=0, keepdims=True)

    @pl.when(pl.program_id(0) == 0)
    def _():
        bias_ref[...] = part

    @pl.when(pl.program_id(0) > 0)
    def _():
        bias_ref[...] += part


def sin_cos(angle):
    turns = jnp.floor(angle * (2.0 / math.pi) + 0.5)
    rest = ((angle - turns * 1.5703125) - turns * 4.837512969970703e-4) - turns * 7.54978995489188e-8
    square = rest * rest
    sine = rest + rest * square * (
        -1.6666654611e-1 + square * (8.3321608736e-3 + square * -1.9515295891e-4)
    )
    cosine = 1.0 - 0.5 * square + square * square * (
        4.166664568298827e-2 + square * (-1.388731625493765e-3 + square * 2.443315711809948e-5)
    )
    quarter = turns.astype(jnp.int32)
    odd = (quarter & 1) == 1
    sin_sign = jnp.where((quarter & 2) == 2, -1.0, 1.0).astype(f32)
    cos_sign = jnp.where(((quarter + 1) & 2) == 2, -1.0, 1.0).astype(f32)
    return jnp.where(odd, cosine, sine) * sin_sign, jnp.where(odd, sine, cosine) * cos_sign


def turned_over(hidden, slope):
    both = jnp.concatenate([hidden, slope], axis=1).T
    return jnp.concatenate(split(both[: hidden.shape[1]]), axis=0)


def filters_kernel(
    rows, shards, blocks, width, feats_ref, first_ref, weight_ref, rate_ref, front_ref, spec_ref, trans_ref, slope_ref,
    hid_ref,
):
    hidden, slope = sin_cos(exact_dot(feats_ref[...], first_ref[...]))
    slope_ref[...] = slope
    high, low = split(hidden)
    hid_ref[...] = jnp.concatenate([high, high, low], axis=1)
    trans_ref[...] = turned_over(hidden, slope)
    strips = looped(
        functools.partial(filter_strip, rows, shards), (None, ROWS, ROWS, None, CUBE), blocks, width
    )
    strips(hid_ref, weight_ref, rate_ref, front_ref, spec_ref)


def filter_strip(rows, shards, block, blocks, hid_ref, weight_ref, rate_ref, front_ref, spec_ref):
    scale = float(rows * shards) ** -0.5
    w_high, w_low = split(weight_ref[...])
    stacked = jnp.concatenate([w_high, w_low, w_high], axis=0)
    rate = rate_ref[...]
    env = decay(rate, rows, scale)
    before = None
    for lag in range(shards):
        part = dot(hid_ref[lag * rows : (lag + 1) * rows, :], stacked)
        part = part * (env * jnp.exp(rate * (-float(lag * rows))))
        f_high, f_low = split(part)
        now = forward(front_ref, f_high) + dot(front_ref[:, :rows], f_low)
        for re, im, sign in row_groups(rows):
            here = (now[re], now[im])
            if before is not None:
                here = plus(here, turned((before[re], before[im]), -sign))
            spec_ref[lag, re, :] = here[0].astype(bf16)
            spec_ref[lag, im, :] = here[1].astype(bf16)
        before = now


def own_kernel(rows, shards, channels, blocks, width, *refs):
    inputs, (sums_out, send_out, first_out), held = refs[:10], refs[11:14], refs[15:25]
    sums_ref, send_ref, own_first_ref, trans_ref, acc_ref, sems, out_sems = refs[25:]
    (
        feats_ref, first_ref, source_ref, cotan_ref, weight_ref, rate_ref, front_ref, back_ref, featt_ref, bias_ref
    ) = held
    copies = [pltpu.make_async_copy(far, near, sems.at[i]) for i, (far, near) in enumerate(zip(inputs, held))]
    for copy in copies:
        copy.start()
    acc_ref[...] = jnp.zeros_like(acc_ref)
    copies[0].wait()
    copies[1].wait()
    hidden, slope = sin_cos(exact_dot(feats_ref[...], first_ref[...]))
    trans_ref[...] = turned_over(hidden, slope)
    for copy in copies[2:]:
        copy.wait()

    def leaving(block):
        cols = pl.ds(pl.multiple_of(block * width, width), width)
        return pltpu.make_async_copy(sums_ref.at[:, cols], sums_out.at[:, cols], out_sems.at[block])

    def strip(block, blocks, *views):
        own_strip(rows, shards, *views)
        leaving(block).start()

    kinds = (ROWS, ROWS, ROWS, ROWS, None, None, None, ROWS, ROWS, None)
    looped(strip, kinds, blocks, width)(
        source_ref, cotan_ref, weight_ref, rate_ref, front_ref, back_ref, trans_ref, sums_ref, send_ref, acc_ref
    )
    first = exact_dot(featt_ref[:, :rows], acc_ref[...] * slope)
    own_first_ref[...] = first
    put_side(send_ref, channels, fold(bias_ref[...]), first)
    ends = [
        pltpu.make_async_copy(own_first_ref, first_out, out_sems.at[blocks]),
        pltpu.make_async_copy(send_ref, send_out, out_sems.at[blocks + 1]),
    ]
    for end in ends:
        end.start()
    for block in range(blocks):
        leaving(block).wait()
    for end in ends:
        end.wait()


def own_strip(
    rows, shards, source_ref, cotan_ref, weight_ref, rate_ref, front_ref, back_ref, trans_ref, sums_ref,
    send_ref, acc_ref,
):
    x0 = forward(front_ref, source_ref[...])
    c0 = forward(front_ref, cotan_ref[...])
    pair = conj_times((x0[:rows], x0[rows:]), (c0[:rows], c0[rows:]))
    high, low = split(jnp.concatenate(pair, axis=0))
    env = decay(rate_ref[...], rows, float(rows * shards) ** -0.5)
    m_high, m_low = split(backward(back_ref, high, low) * env)
    sums = weight_sums(trans_ref[...], m_high, m_low)
    sums_ref[...] = sums
    send_ref[...] = sums.astype(bf16)
    acc_ref[...] += hidden_sums(m_high, m_low, *split(weight_ref[...]))


def fold(bias):
    return jnp.concatenate([bias[:, i * 128 : (i + 1) * 128] for i in range(bias.shape[1] // 128)], axis=0)


def put_side(pay_ref, channels, bias, first=None):
    half = pay_ref.shape[0] // 2
    pay_ref[:, channels:] = jnp.zeros((2 * half, SIDE), bf16)
    for start, part in zip((0, 128), split(bias)):
        pay_ref[: bias.shape[0], channels + start : channels + start + 128] = part
    if first is not None:
        for start, part in zip((0, 128), split(first)):
            pay_ref[half:, channels + start : channels + start + first.shape[1]] = part


def get_side(pay, channels, lanes, hid_count):
    half = pay.shape[0] // 2
    side = pay[:, channels : channels + 128].astype(f32) + pay[:, channels + 128 :].astype(f32)
    return side[:lanes], side[half:, :hid_count]


def near_kernel(
    rows, shards, blocks, width, rank_ref, x0_ref, c0_ref, x1_ref, c1_ref, spec_ref, weight_ref, rate_ref, front_ref,
    back_ref, trans_ref, featt_ref, slope_ref, own_ref, own_first_ref, conv_ref, corr_ref, ahead_ref, sums_ref,
    first_ref, fields, fast, high_ref, low_ref, acc_ref,
):
    rank = rank_ref[0]
    inner = jnp.logical_and(rank > 0, rank < shards - 1)
    count = shards - 1
    tables = (front_ref, back_ref)
    blocks_in = (x0_ref, c0_ref, x1_ref, c1_ref)

    @pl.when(jnp.logical_not(inner))
    def _():
        looped(
            functools.partial(near_strip, rows, shards, False),
            (None, None, None) + (ROWS,) * 4 + (CUBE, ROWS, ROWS), blocks, width,
        )(rank_ref, *tables, *blocks_in, spec_ref, conv_ref, corr_ref, fields, fast)

    @pl.when(inner)
    def _():
        acc_ref[...] = jnp.zeros_like(acc_ref)
        looped(
            functools.partial(near_strip, rows, shards, True),
            (None, None, None) + (ROWS,) * 4 + (CUBE, ROWS, ROWS) + (None, None, None) + (ROWS,) * 5, blocks, width,
        )(
            rank_ref, *tables, *blocks_in, spec_ref, conv_ref, corr_ref, fields, fast, trans_ref, weight_ref, rate_ref,
            own_ref, ahead_ref, sums_ref, high_ref, low_ref, acc_ref,
        )
        first_ref[...] = own_first_ref[...] + exact_dot(
            featt_ref[:, : count * rows], acc_ref[...] * slope_ref[: count * rows, :]
        )


def near_strip(
    rows, shards, inner, block, blocks, rank_ref, front_ref, back_ref, x0_ref, c0_ref, x1_ref, c1_ref, spec_ref,
    conv_ref, corr_ref, fields, fast, *rest
):
    rank = rank_ref[0]
    count = shards - 1
    if inner:
        trans_ref, weight_ref, rate_ref, own_ref, ahead_ref, sums_ref, high_ref, low_ref, acc_ref = rest
        lower = rank == 1
        upper = jnp.where(rank == 2, 1.0, 0.0).astype(f32)
        side = jnp.where(rank == 2, 1.0, -1.0).astype(f32)
    for index, ref in enumerate((x0_ref, c0_ref, x1_ref, c1_ref)):
        fields[index] = forward(front_ref, ref[...])
    for re, im, sign in row_groups(rows):
        x0, c0, x1, c1 = ((fields[i, re, :], fields[i, im, :]) for i in range(4))
        w0, w1, w2 = ((spec_ref[i, re, :].astype(f32), spec_ref[i, im, :].astype(f32)) for i in range(3))
        values = [plus(times(w0, x0), times(w1, x1)), plus(conj_times(w0, c0), conj_times(w1, c1))]
        if inner:
            values.append(times((w2[0], w2[1] * side), choose(lower, c1, x1)))
        for index, value in enumerate(values):
            fast[index, re, :] = value[0].astype(bf16)
            fast[index, im, :] = value[1].astype(bf16)
        if inner:
            one = plus(conj_times(x1, c0), scaled(conj_times(x0, c1), upper))
            two = conj_times(x1, c1)
            for index, value in enumerate((turned(one, sign), plus(one, turned(two, sign)), two)):
                for part, where in zip(value, (re, im)):
                    high_ref[index, where, :], low_ref[index, where, :] = split(part)
    conv_ref[...] = backward(back_ref, fast[0])
    corr_ref[...] = backward(back_ref, fast[1])
    if not inner:
        return
    ahead_ref[...] = backward(back_ref, fast[2])
    rate = rate_ref[...]
    env = decay(rate, rows, float(rows * shards) ** -0.5)
    parts = []
    for lag in range(count):
        grad = backward(back_ref, high_ref[lag], low_ref[lag])
        parts.append(split(grad * (env * jnp.exp(rate * (-float(lag * rows))))))
    m_high = jnp.concatenate([p[0] for p in parts], axis=0)
    m_low = jnp.concatenate([p[1] for p in parts], axis=0)
    sums_ref[...] = own_ref[...] + weight_sums(trans_ref[:, : count * rows], m_high, m_low)
    acc_ref[...] += hidden_sums(m_high, m_low, *split(weight_ref[...]))


def on_inner(shards, rank_at, kernel):
    def run(*refs):
        rank = refs[rank_at][0]

        @pl.when(jnp.logical_and(rank > 0, rank < shards - 1))
        def _():
            kernel(*refs)

    return run


def far_kernel(rows, block, blocks, rank_ref, far_ref, spec_ref, front_ref, back_ref, ahead_ref, part_ref, late_ref):
    side = jnp.where(rank_ref[0] == 2, 1.0, -1.0).astype(f32)
    far = forward(front_ref, far_ref[...])
    far = (far[:rows], far[rows:])
    w2, w3 = ((spec_ref[i, :rows, :].astype(f32), spec_ref[i, rows:, :].astype(f32) * side) for i in range(2))
    ahead = jnp.concatenate(times(w3, far), axis=0).astype(bf16)
    part_ref[...] = (ahead_ref[...] + backward(back_ref, ahead)).astype(bf16)
    late = jnp.concatenate(times(w2, far), axis=0).astype(bf16)
    late_ref[...] = backward(back_ref, late)


def last_kernel(
    rows, shards, channels, block, blocks, after_ref, rank_ref, x1_ref, c1_ref, far_ref, weight_ref, rate_ref, front_ref, back_ref,
    trans_ref, featt_ref, slope_ref, sums_ref, first_ref, bias_ref, in_ref, pay_ref, total_ref, acc_ref,
):
    del after_ref
    hid_count, width = weight_ref.shape
    lower = rank_ref[0] == 1
    start = pl.multiple_of(block * width, width)
    here = sums_ref[...] + in_ref[:, pl.ds(start, width)].astype(f32)
    mine = (block < blocks // 2) == lower

    @pl.when(block == 0)
    def _():
        acc_ref[...] = jnp.zeros_like(acc_ref)

    @pl.when(mine)
    def _():
        sign = jnp.where(lower, 1.0, -1.0).astype(f32)
        near = forward(front_ref, jnp.where(lower, x1_ref[...], c1_ref[...]))
        far = forward(front_ref, far_ref[...])
        three = conj_times((near[:rows], near[rows:]), (far[:rows], far[rows:]))
        three = (three[0], three[1] * sign)
        half = rows // 2
        two = jnp.concatenate([three[1][:half], -three[1][half:], -three[0][:half], three[0][half:]], axis=0)
        rate = rate_ref[...]
        env = decay(rate, rows, float(rows * shards) ** -0.5)
        parts = []
        for lag, value in ((shards - 2, two), (shards - 1, jnp.concatenate(three, axis=0))):
            grad = backward(back_ref, *split(value))
            parts.append(split(grad * (env * jnp.exp(rate * (-float(lag * rows))))))
        m_high = jnp.concatenate([p[0] for p in parts], axis=0)
        m_low = jnp.concatenate([p[1] for p in parts], axis=0)
        trans = trans_ref[:, (shards - 2) * rows :]
        pay_ref[:, pl.ds(start, width)] = (here + weight_sums(trans, m_high, m_low)).astype(bf16)
        w_high, w_low = split(weight_ref[...])
        acc_ref[...] += hidden_sums(m_high, m_low, w_high, w_low)

    @pl.when(jnp.logical_not(mine))
    def _():
        pay_ref[:, pl.ds(start, width)] = here.astype(bf16)

    @pl.when(block == blocks - 1)
    def _():
        first = exact_dot(
            featt_ref[:, (shards - 2) * rows :], acc_ref[...] * slope_ref[(shards - 2) * rows :, :]
        )
        lanes = channels // 128
        in_bias, in_first = get_side(in_ref[...], channels, lanes, hid_count)
        first = first + first_ref[...] + in_first
        put_side(pay_ref, channels, fold(bias_ref[...]) + in_bias)
        total_ref[...] = first


def total_kernel(channels, hid_count, part_ref, own_ref, come_ref, first_ref, pay_ref):
    del part_ref
    lanes = channels // 128
    pay_ref[:, :channels] = (own_ref[:, :channels].astype(f32) + come_ref[:, :channels].astype(f32)).astype(bf16)
    own, come = (get_side(ref[...], channels, lanes, hid_count)[0] for ref in (own_ref, come_ref))
    put_side(pay_ref, channels, own + come, first_ref[...])


def gates_kernel(
    shards, block, blocks, rank_ref, one_ref, two_ref, val_ref, out_ref, skip_ref, conv_ref, corr_ref, late_ref, part_ref,
    grad_one_ref, grad_two_ref, grad_value_ref,
):
    rank = rank_ref[0]

    def on(wanted, value):
        return jnp.where(rank == wanted, value, jnp.zeros_like(value))

    part = part_ref[...].astype(f32)
    late = late_ref[...]
    one = one_ref[...].astype(f32)
    val = val_ref[...].astype(f32)
    out = out_ref[...].astype(f32)
    skip = skip_ref[...]
    conv = conv_ref[...] + on(2, late) + on(shards - 1, part)
    corr = corr_ref[...] + on(1, late) + on(0, part)
    grad_two_ref[...] = (out * (conv + skip * (one * val))).astype(bf16)
    mid = corr + skip * (out * two_ref[...].astype(f32))
    grad_one_ref[...] = (mid * val).astype(bf16)
    grad_value_ref[...] = (mid * one).astype(bf16)


def finish_kernel(
    channels, shards, rank_ref, own_ref, come_ref, second_out, first_out, bias_out, second, first, bias, sems
):
    rank = rank_ref[0]
    inner = jnp.logical_and(rank > 0, rank < shards - 1)
    lanes = channels // 128
    copies = [
        pltpu.make_async_copy(held, out, sems.at[i])
        for i, (held, out) in enumerate(((second, second_out), (first, first_out), (bias, bias_out)))
    ]
    picked = jnp.where(inner, own_ref[...], come_ref[...])
    second[...] = picked[:, :channels].astype(f32)
    copies[0].start()
    rows, first[...] = get_side(picked, channels, lanes, first.shape[1])
    copies[1].start()
    for i in range(lanes):
        bias[:, i * 128 : (i + 1) * 128] = rows[i : i + 1]
    copies[2].start()
    for copy in copies:
        copy.wait()


def few_shards_body(
    x_one, x_two, values, grad_out, first_weight, second_weight, skip_bias, decay_rate
):
    rows, channels = x_one.shape
    shards = lax.axis_size("ctx")
    feat_count, hid_count = first_weight.shape
    seq_len = rows * shards
    double = 2 * rows
    width = min(512, channels)
    blocks = channels // width
    rank = lax.axis_index("ctx").astype(jnp.int32).reshape(1)
    front, back = block_tables(rows)
    feats = feature_table(seq_len)
    featt = np.ascontiguousarray(feats.T)
    skip_row = skip_bias.reshape(1, channels)
    rate_row = decay_rate.reshape(1, channels)
    smem = pl.BlockSpec(memory_space=pltpu.SMEM)
    vmem = pl.BlockSpec(memory_space=pltpu.VMEM)
    anywhere = pl.BlockSpec(memory_space=pl.ANY)
    mebi = 1024 * 1024

    def shape(*dims, dtype=f32):
        return jax.ShapeDtypeStruct(dims, dtype)

    def call(kernel, name, units, out_shape, in_specs, out_specs=None, scratch=(), limit=16, aliases={}):
        return pl.pallas_call(
            kernel,
            in_specs=in_specs,
            out_specs=out_specs if out_specs is not None else [vmem] * len(out_shape),
            out_shape=out_shape,
            scratch_shapes=scratch,
            input_output_aliases=aliases,
            compiler_params=pltpu.CompilerParams(vmem_limit_bytes=limit * mebi),
            cost_estimate=pl.CostEstimate(
                flops=2 * units * double * double * channels, bytes_accessed=rows * channels, transcendentals=0
            ),
            name=name,
        )

    def move(array, pairs):
        return lax.ppermute(array, "ctx", pairs)

    up = [(i, i + 1) for i in range(shards - 1)]
    down = [(i + 1, i) for i in range(shards - 1)]
    inward = [(0, 1), (shards - 1, shards - 2)]
    outward = [(1, 0), (shards - 2, shards - 1)]
    across = [(1, 2), (2, 1)]
    pay_shape = (hid_count, channels + SIDE)
    block_bf16 = shape(rows, channels, dtype=bf16)
    block_f32 = shape(rows, channels)

    row_step = max(rows // 2, 16)
    gate_rows = pl.BlockSpec((row_step, channels), lambda i: (i, 0))
    x0, c0, edge, bias = pl.pallas_call(
        products_kernel,
        grid=(rows // row_step,),
        in_specs=[smem] + [gate_rows] * 4,
        out_specs=[gate_rows] * 3 + [pl.BlockSpec((1, channels), lambda i: (0, 0))],
        out_shape=[block_bf16] * 3 + [shape(1, channels)],
        compiler_params=pltpu.CompilerParams(vmem_limit_bytes=64 * mebi),
        name="products",
    )(rank, x_one, x_two, values, grad_out)
    x1 = move(x0, up)
    c1 = move(c0, down)

    own_shapes = [
        shape(rows, feat_count), shape(feat_count, hid_count), block_bf16, block_bf16, shape(hid_count, channels),
        shape(1, channels), shape(double, double, dtype=bf16), shape(double, double, dtype=bf16),
        shape(feat_count, seq_len), shape(1, channels), shape(hid_count, channels), shape(*pay_shape, dtype=bf16),
        shape(feat_count, hid_count),
    ]
    own, send, own_first, edge = call(
        functools.partial(own_kernel, rows, shards, channels, blocks, width), "own_pair", 8,
        [shape(hid_count, channels), shape(*pay_shape, dtype=bf16), shape(feat_count, hid_count), block_bf16],
        [anywhere] * 11,
        out_specs=[anywhere] * 4,
        scratch=[pltpu.VMEM(s.shape, s.dtype) for s in own_shapes]
        + [
            pltpu.VMEM((2 * hid_count, rows), bf16), pltpu.VMEM((rows, hid_count), f32),
            pltpu.SemaphoreType.DMA((10,)), pltpu.SemaphoreType.DMA((blocks + 2,)),
        ],
        aliases={10: 3},
        limit=60,
    )(feats[:rows], first_weight, x0, c0, second_weight, rate_row, front, back, featt, bias, edge)
    far = move(edge, [(0, 2), (shards - 1, shards - 3)])

    spec, trans, slope = call(
        functools.partial(filters_kernel, rows, shards, blocks, width), "filters", 8,
        [
            shape(shards, double, channels, dtype=bf16), shape(2 * hid_count, seq_len, dtype=bf16),
            shape(seq_len, hid_count),
        ],
        [vmem] * 5,
        scratch=[pltpu.VMEM((seq_len, 3 * hid_count), bf16)],
    )(feats, first_weight, second_weight, rate_row, front)

    conv, corr, ahead, sums, first = call(
        functools.partial(near_kernel, rows, shards, blocks, width), "near_blocks", 20,
        [block_f32] * 3 + [shape(hid_count, channels), shape(feat_count, hid_count)],
        [smem] + [vmem] * 14,
        scratch=[
            pltpu.VMEM((4, double, width), f32),
            pltpu.VMEM((3, double, width), bf16),
            pltpu.VMEM((shards - 1, double, width), bf16),
            pltpu.VMEM((shards - 1, double, width), bf16),
            pltpu.VMEM(((shards - 1) * rows, hid_count), f32),
        ],
    )(rank, x0, c0, x1, c1, spec, second_weight, rate_row, front, back, trans, featt, slope, own, own_first)
    come = move(send, inward)

    part, late = call(
        on_inner(
            shards, 0,
            looped(
                functools.partial(far_kernel, rows),
                (None, ROWS, (slice(2, 4), slice(None)), None, None, ROWS, ROWS, ROWS),
                blocks, width,
            ),
        ),
        "far_block", 1,
        [block_bf16, block_f32],
        [smem] + [vmem] * 5,
    )(rank, far, spec, front, back, ahead)
    part_come = move(part, outward)

    pay, first = call(
        on_inner(
            shards, 1,
            looped(
                functools.partial(last_kernel, rows, shards, channels),
                (None, None, ROWS, ROWS, ROWS, ROWS, ROWS, None, None, None, None, None, ROWS),
                blocks, width,
            ),
        ),
        "last_pair", 1,
        [shape(*pay_shape, dtype=bf16), shape(feat_count, hid_count)],
        [anywhere, smem] + [vmem] * 14,
        scratch=[pltpu.VMEM((2 * rows, hid_count), f32)],
    )(late, rank, x1, c1, far, second_weight, rate_row, front, back, trans, featt, slope, sums, first, bias, come)
    first = first + move(first, across)
    pay_come = move(pay, across)
    group = lax.axis_size(("ch", "sub"))
    bit = 1
    while bit < group:
        first = first + lax.ppermute(first, ("ch", "sub"), [(i, i ^ bit) for i in range(group)])
        bit *= 2

    (total,) = call(
        functools.partial(total_kernel, channels, hid_count), "total", 0,
        [shape(*pay_shape, dtype=bf16)],
        [anywhere] + [vmem] * 3,
    )(part_come, pay, pay_come, first)
    total_come = move(total, outward)

    grad_one, grad_two, grad_value = call(
        looped(
            functools.partial(gates_kernel, shards), (None,) + (ROWS,) * 12, blocks, width
        ),
        "gates", 0,
        [block_bf16] * 3,
        [smem] + [vmem] * 9,
    )(rank, x_one, x_two, values, grad_out, skip_row, conv, corr, late, part_come)

    outs = [shape(hid_count, channels), shape(feat_count, hid_count), shape(1, channels)]
    grad_second, grad_first, grad_bias = call(
        functools.partial(finish_kernel, channels, shards), "finish", 0,
        outs,
        [smem] + [vmem] * 2,
        out_specs=[anywhere] * 3,
        scratch=[pltpu.VMEM(o.shape, f32) for o in outs] + [pltpu.SemaphoreType.DMA((3,))],
    )(rank, total, total_come)
    return (grad_one, grad_two, grad_value, grad_first, grad_second, grad_bias.reshape(channels))


def solution(mesh):
    in_specs = (
        P(("parts", "ctx"), ("ch", "sub")),
        P(("parts", "ctx"), ("ch", "sub")),
        P(("parts", "ctx"), ("ch", "sub")),
        P(("parts", "ctx"), ("ch", "sub")),
        P(),
        P(None, ("ch", "sub")),
        P(("ch", "sub")),
        P(("ch", "sub")),
    )
    out_specs = (
        P(("parts", "ctx"), ("ch", "sub")),
        P(("parts", "ctx"), ("ch", "sub")),
        P(("parts", "ctx"), ("ch", "sub")),
        P("parts", None),
        P("parts", ("ch", "sub")),
        P(("parts", "ch", "sub")),
    )
    body = few_shards_body if mesh.shape["ctx"] == 4 else many_shards_body
    return jax.shard_map(body, mesh=mesh, in_specs=in_specs, out_specs=out_specs, check_vma=False)
```

```python
import functools
import math

import jax
import jax.numpy as jnp
import numpy as np
from jax import lax
from jax.experimental import pallas as pl
from jax.experimental.pallas import tpu as pltpu
from jax.sharding import PartitionSpec as P

band_steps = (1763, 1201, 811, 547, 367, 251, 167, 113, 79, 53, 37, 23, 17, 11, 7, 3)
highest = lax.Precision.HIGHEST
f32 = jnp.float32
bf16 = jnp.bfloat16


def features(positions):
    multiplier = jnp.array(band_steps, dtype=jnp.int32)
    phase = positions[:, None] * multiplier[None, :] % 4096
    angle = phase.astype(jnp.float32) * (2.0 * math.pi / 4096.0)
    return jnp.concatenate([jnp.cos(angle), jnp.sin(angle)], axis=1)


def tables(out_count, in_count, modulus, sign_value):
    row_index = lax.broadcasted_iota(jnp.int32, (out_count, in_count), 0)
    col_index = lax.broadcasted_iota(jnp.int32, (out_count, in_count), 1)
    angle = (row_index * col_index % modulus).astype(jnp.float32) * (2.0 * math.pi / modulus)
    return (jnp.cos(angle), sign_value * jnp.sin(angle))


def twiddle(spec_re, spec_im, freq_count, span, modulus, sign_value):
    freq_index = lax.broadcasted_iota(jnp.int32, (freq_count, span), 0)
    pos_index = lax.broadcasted_iota(jnp.int32, (freq_count, span), 1)
    angle = (freq_index * pos_index % modulus).astype(jnp.float32) * (2.0 * math.pi / modulus)
    factor_re = jnp.cos(angle)[None, None, :, :]
    factor_im = (sign_value * jnp.sin(angle))[None, None, :, :]
    return (spec_re * factor_re - spec_im * factor_im, spec_re * factor_im + spec_im * factor_re)


def contract(kernel, array):
    return jnp.einsum(
        "lj,mckj->mckl", kernel, array, precision=highest, preferred_element_type=jnp.float32
    )


def along_positions(spec_re, spec_im, kernel_re, kernel_im):
    return (
        contract(kernel_re, spec_re) - contract(kernel_im, spec_im),
        contract(kernel_re, spec_im) + contract(kernel_im, spec_re),
    )


def many_shards_body(
    x_one, x_two, values, grad_out, first_weight, second_weight, skip_bias, decay_rate
):
    row_count, chan_count = x_one.shape
    shards = lax.axis_size("ctx")
    rank = lax.axis_index("ctx")
    seq_len = row_count * shards
    total = 2 * seq_len
    narrow = chan_count // shards
    chan_weight = lax.dynamic_slice_in_dim(second_weight, rank * narrow, narrow, 1)
    chan_rate = lax.dynamic_slice_in_dim(decay_rate, rank * narrow, narrow, 0)
    source = x_one.astype(jnp.float32) * values.astype(jnp.float32)
    cotan = grad_out.astype(jnp.float32) * x_two.astype(jnp.float32)
    spread = lax.all_to_all(
        jnp.stack([source.T, cotan.T])[:, :, None, :],
        "ctx",
        split_axis=1,
        concat_axis=2,
        tiled=True,
    )
    far_source = spread[0]
    far_cotan = spread[1]
    positions = jnp.arange(seq_len, dtype=jnp.int32)
    feats = features(positions)
    pre_act = jnp.dot(feats, first_weight, precision=highest, preferred_element_type=jnp.float32)
    hidden = jnp.sin(pre_act)
    envelope = jnp.exp(-chan_rate[:, None] * positions.astype(jnp.float32)[None, :]) * float(
        seq_len
    ) ** (-0.5)
    filt = (
        jnp.einsum(
            "th,hc->ct", hidden, chan_weight, precision=highest, preferred_element_type=jnp.float32
        )
        * envelope
    )
    filt_blocks = filt.reshape(narrow, shards, row_count)
    fields = jnp.stack([far_source, far_cotan])

    def first_section(kernel):
        field_part = jnp.einsum(
            "kn,mcnj->mckj", kernel, fields, precision=highest, preferred_element_type=jnp.float32
        )
        filter_part = jnp.einsum(
            "kn,cnj->ckj",
            kernel,
            filt_blocks,
            precision=highest,
            preferred_element_type=jnp.float32,
        )
        return jnp.concatenate([field_part, filter_part[None]], axis=0)

    first_re, first_im = tables(2 * shards, shards, 2 * shards, -1.0)
    spec_re, spec_im = (first_section(first_re), first_section(first_im))
    spec_re, spec_im = twiddle(spec_re, spec_im, 2 * shards, row_count, total, -1.0)
    fwd_re, fwd_im = tables(row_count, row_count, row_count, -1.0)
    spec_re, spec_im = along_positions(spec_re, spec_im, fwd_re, fwd_im)
    source_re, source_im = (spec_re[0], spec_im[0])
    cotan_re, cotan_im = (spec_re[1], spec_im[1])
    filter_re, filter_im = (spec_re[2], spec_im[2])
    prod_re = jnp.stack(
        [
            source_re * filter_re - source_im * filter_im,
            cotan_re * filter_re + cotan_im * filter_im,
            cotan_re * source_re + cotan_im * source_im,
        ]
    )
    prod_im = jnp.stack(
        [
            source_re * filter_im + source_im * filter_re,
            cotan_im * filter_re - cotan_re * filter_im,
            cotan_im * source_re - cotan_re * source_im,
        ]
    )
    back_re, back_im = tables(row_count, row_count, row_count, 1.0)
    prod_re, prod_im = along_positions(prod_re, prod_im, back_re, back_im)
    prod_re, prod_im = twiddle(prod_re, prod_im, 2 * shards, row_count, total, 1.0)
    last_re, last_im = tables(shards, 2 * shards, 2 * shards, 1.0)
    field_out = jnp.einsum(
        "nk,mckj->mcnj", last_re, prod_re[:2], precision=highest, preferred_element_type=jnp.float32
    ) - jnp.einsum(
        "nk,mckj->mcnj", last_im, prod_im[:2], precision=highest, preferred_element_type=jnp.float32
    )
    field_out = field_out * (1.0 / total)
    filt_grad = jnp.einsum(
        "nk,ckj->cnj", last_re, prod_re[2], precision=highest, preferred_element_type=jnp.float32
    ) - jnp.einsum(
        "nk,ckj->cnj", last_im, prod_im[2], precision=highest, preferred_element_type=jnp.float32
    )
    filt_grad = (filt_grad * (1.0 / total)).reshape(narrow, seq_len)
    modulated = filt_grad * envelope
    weight_part = jnp.einsum(
        "th,ct->hc", hidden, modulated, precision=highest, preferred_element_type=jnp.float32
    )
    hidden_grad = jnp.einsum(
        "ct,hc->th", modulated, chan_weight, precision=highest, preferred_element_type=jnp.float32
    )
    first_part = jnp.dot(
        feats.T,
        hidden_grad * jnp.cos(pre_act),
        precision=highest,
        preferred_element_type=jnp.float32,
    )
    grad_first = lax.psum(first_part, ("ctx", "ch", "sub"))
    returned = lax.all_to_all(
        field_out.astype(jnp.bfloat16), "ctx", split_axis=2, concat_axis=1, tiled=True
    ).astype(field_out.dtype)
    conv_part = returned[0, :, 0, :].T
    corr_part = returned[1, :, 0, :].T
    grad_two = (grad_out.astype(jnp.float32) * (conv_part + skip_bias[None, :] * source)).astype(
        jnp.bfloat16
    )
    grad_mid = corr_part + skip_bias[None, :] * cotan
    grad_one = (grad_mid * values.astype(jnp.float32)).astype(jnp.bfloat16)
    grad_value = (grad_mid * x_one.astype(jnp.float32)).astype(jnp.bfloat16)
    grad_bias = lax.psum(jnp.sum(source * cotan, axis=0), "ctx")
    grad_second = lax.all_gather(weight_part, "ctx", axis=1, tiled=True)
    return (grad_one, grad_two, grad_value, grad_first, grad_second, grad_bias)


STEP = 16
SIDE = 256


def halves(array):
    array = np.asarray(array, np.float32)
    high = array.astype(bf16)
    low = (array - high.astype(np.float32)).astype(bf16)
    return high, low


def block_tables(rows):
    freq = np.concatenate([np.arange(0, rows, 2), np.arange(1, rows, 2)])
    phase = (2 * freq + 1)[:, None] * np.arange(rows)[None, :] % (4 * rows)
    angle = phase * (2.0 * np.pi / (4 * rows))
    forward = np.concatenate([np.cos(angle), -np.sin(angle)], axis=0)
    front = np.ascontiguousarray(np.concatenate(halves(forward), axis=1))
    back = np.ascontiguousarray(np.concatenate(halves(forward.T / rows), axis=0))
    return front, back


def feature_table(seq_len):
    phase = np.arange(seq_len)[:, None] * np.array(band_steps)[None, :] % 4096
    angle = phase * (2.0 * np.pi / 4096.0)
    return np.concatenate([np.cos(angle), np.sin(angle)], axis=1).astype(np.float32)


def split(array):
    high = array.astype(bf16)
    return high, (array - high.astype(f32)).astype(bf16)


def dot(left, right):
    return jnp.dot(left, right, preferred_element_type=f32)


def exact_dot(left, right):
    return jnp.dot(left, right, precision=highest, preferred_element_type=f32)


def dot_across(left, right):
    return lax.dot_general(left, right, (((1,), (1,)), ((), ())), preferred_element_type=f32)


def decay(rate, rows, scale):
    place = lax.broadcasted_iota(jnp.int32, (rows, rate.shape[1]), 0)
    return jnp.exp(-place.astype(f32) * rate) * scale


def times(a, b):
    return a[0] * b[0] - a[1] * b[1], a[0] * b[1] + a[1] * b[0]


def conj_times(a, b):
    return a[0] * b[0] + a[1] * b[1], a[0] * b[1] - a[1] * b[0]


def plus(a, b):
    return a[0] + b[0], a[1] + b[1]


def scaled(a, factor):
    return a[0] * factor, a[1] * factor


def choose(condition, a, b):
    return jnp.where(condition, a[0], b[0]), jnp.where(condition, a[1], b[1])


def turned(a, sign):
    return (a[1], -a[0]) if sign > 0 else (-a[1], a[0])


def forward(front_ref, block):
    return dot(front_ref[...], jnp.concatenate([block, block], axis=0))


def backward(back_ref, high, low=None):
    both = dot(back_ref[...], high)
    rows = both.shape[0] // 2
    out = both[:rows] + both[rows:]
    return out if low is None else out + dot(back_ref[:rows], low)


def row_groups(rows):
    for step in range(rows // STEP):
        sign = 1 if step * STEP < rows // 2 else -1
        yield slice(step * STEP, (step + 1) * STEP), slice(rows + step * STEP, rows + (step + 1) * STEP), sign


def weight_sums(trans, m_high, m_low):
    both = dot(trans, m_high)
    count = both.shape[0] // 2
    return both[:count] + both[count:] + dot(trans[:count], m_low)


def hidden_sums(m_high, m_low, w_high, w_low):
    left = jnp.concatenate([m_high, m_high, m_low], axis=1)
    right = jnp.concatenate([w_high, w_low, w_high], axis=1)
    return dot_across(left, right)


def looped(kernel, kinds, blocks, width):
    def over_strips(*refs):
        def step(block, carry):
            cols = pl.ds(pl.multiple_of(block * width, width), width)
            views = [
                ref if kind is None else ref.at[(*kind, cols)]
                for ref, kind in zip(refs, kinds + (None,) * (len(refs) - len(kinds)))
            ]
            kernel(block, blocks, *views)
            return carry

        lax.fori_loop(0, blocks, step, 0)

    return over_strips


ROWS = (slice(None),)
CUBE = (slice(None), slice(None))


def products_kernel(rank_ref, one_ref, two_ref, val_ref, out_ref, source_ref, cotan_ref, edge_ref, bias_ref):
    source = one_ref[...].astype(f32) * val_ref[...].astype(f32)
    cotan = out_ref[...].astype(f32) * two_ref[...].astype(f32)
    source_ref[...] = source.astype(bf16)
    cotan_ref[...] = cotan.astype(bf16)
    edge_ref[...] = jnp.where(rank_ref[0] == 0, source, cotan).astype(bf16)
    part = jnp.sum(source * cotan, axis=0, keepdims=True)

    @pl.when(pl.program_id(0) == 0)
    def _():
        bias_ref[...] = part

    @pl.when(pl.program_id(0) > 0)
    def _():
        bias_ref[...] += part


def sin_cos(angle):
    turns = jnp.floor(angle * (2.0 / math.pi) + 0.5)
    rest = ((angle - turns * 1.5703125) - turns * 4.837512969970703e-4) - turns * 7.54978995489188e-8
    square = rest * rest
    sine = rest + rest * square * (
        -1.6666654611e-1 + square * (8.3321608736e-3 + square * -1.9515295891e-4)
    )
    cosine = 1.0 - 0.5 * square + square * square * (
        4.166664568298827e-2 + square * (-1.388731625493765e-3 + square * 2.443315711809948e-5)
    )
    quarter = turns.astype(jnp.int32)
    odd = (quarter & 1) == 1
    sin_sign = jnp.where((quarter & 2) == 2, -1.0, 1.0).astype(f32)
    cos_sign = jnp.where(((quarter + 1) & 2) == 2, -1.0, 1.0).astype(f32)
    return jnp.where(odd, cosine, sine) * sin_sign, jnp.where(odd, sine, cosine) * cos_sign


def turned_over(hidden, slope):
    both = jnp.concatenate([hidden, slope], axis=1).T
    return jnp.concatenate(split(both[: hidden.shape[1]]), axis=0)


def filters_kernel(
    rows, shards, blocks, width, feats_ref, first_ref, weight_ref, rate_ref, front_ref, spec_ref, trans_ref, slope_ref,
    hid_ref,
):
    hidden, slope = sin_cos(exact_dot(feats_ref[...], first_ref[...]))
    slope_ref[...] = slope
    high, low = split(hidden)
    hid_ref[...] = jnp.concatenate([high, high, low], axis=1)
    trans_ref[...] = turned_over(hidden, slope)
    strips = looped(
        functools.partial(filter_strip, rows, shards), (None, ROWS, ROWS, None, CUBE), blocks, width
    )
    strips(hid_ref, weight_ref, rate_ref, front_ref, spec_ref)


def filter_strip(rows, shards, block, blocks, hid_ref, weight_ref, rate_ref, front_ref, spec_ref):
    scale = float(rows * shards) ** -0.5
    w_high, w_low = split(weight_ref[...])
    stacked = jnp.concatenate([w_high, w_low, w_high], axis=0)
    rate = rate_ref[...]
    env = decay(rate, rows, scale)
    before = None
    for lag in range(shards):
        part = dot(hid_ref[lag * rows : (lag + 1) * rows, :], stacked)
        part = part * (env * jnp.exp(rate * (-float(lag * rows))))
        f_high, f_low = split(part)
        now = forward(front_ref, f_high) + dot(front_ref[:, :rows], f_low)
        for re, im, sign in row_groups(rows):
            here = (now[re], now[im])
            if before is not None:
                here = plus(here, turned((before[re], before[im]), -sign))
            spec_ref[lag, re, :] = here[0].astype(bf16)
            spec_ref[lag, im, :] = here[1].astype(bf16)
        before = now


def own_kernel(rows, shards, channels, blocks, width, *refs):
    inputs, (sums_out, send_out, first_out), held = refs[:10], refs[11:14], refs[15:25]
    sums_ref, send_ref, own_first_ref, trans_ref, acc_ref, sems, out_sems = refs[25:]
    (
        feats_ref, first_ref, source_ref, cotan_ref, weight_ref, rate_ref, front_ref, back_ref, featt_ref, bias_ref
    ) = held
    copies = [pltpu.make_async_copy(far, near, sems.at[i]) for i, (far, near) in enumerate(zip(inputs, held))]
    for copy in copies:
        copy.start()
    acc_ref[...] = jnp.zeros_like(acc_ref)
    copies[0].wait()
    copies[1].wait()
    hidden, slope = sin_cos(exact_dot(feats_ref[...], first_ref[...]))
    trans_ref[...] = turned_over(hidden, slope)
    for copy in copies[2:]:
        copy.wait()

    def leaving(block):
        cols = pl.ds(pl.multiple_of(block * width, width), width)
        return pltpu.make_async_copy(sums_ref.at[:, cols], sums_out.at[:, cols], out_sems.at[block])

    def strip(block, blocks, *views):
        own_strip(rows, shards, *views)
        leaving(block).start()

    kinds = (ROWS, ROWS, ROWS, ROWS, None, None, None, ROWS, ROWS, None)
    looped(strip, kinds, blocks, width)(
        source_ref, cotan_ref, weight_ref, rate_ref, front_ref, back_ref, trans_ref, sums_ref, send_ref, acc_ref
    )
    first = exact_dot(featt_ref[:, :rows], acc_ref[...] * slope)
    own_first_ref[...] = first
    put_side(send_ref, channels, fold(bias_ref[...]), first)
    ends = [
        pltpu.make_async_copy(own_first_ref, first_out, out_sems.at[blocks]),
        pltpu.make_async_copy(send_ref, send_out, out_sems.at[blocks + 1]),
    ]
    for end in ends:
        end.start()
    for block in range(blocks):
        leaving(block).wait()
    for end in ends:
        end.wait()


def own_strip(
    rows, shards, source_ref, cotan_ref, weight_ref, rate_ref, front_ref, back_ref, trans_ref, sums_ref,
    send_ref, acc_ref,
):
    x0 = forward(front_ref, source_ref[...])
    c0 = forward(front_ref, cotan_ref[...])
    pair = conj_times((x0[:rows], x0[rows:]), (c0[:rows], c0[rows:]))
    high, low = split(jnp.concatenate(pair, axis=0))
    env = decay(rate_ref[...], rows, float(rows * shards) ** -0.5)
    m_high, m_low = split(backward(back_ref, high, low) * env)
    sums = weight_sums(trans_ref[...], m_high, m_low)
    sums_ref[...] = sums
    send_ref[...] = sums.astype(bf16)
    acc_ref[...] += hidden_sums(m_high, m_low, *split(weight_ref[...]))


def fold(bias):
    return jnp.concatenate([bias[:, i * 128 : (i + 1) * 128] for i in range(bias.shape[1] // 128)], axis=0)


def put_side(pay_ref, channels, bias, first=None):
    half = pay_ref.shape[0] // 2
    pay_ref[:, channels:] = jnp.zeros((2 * half, SIDE), bf16)
    for start, part in zip((0, 128), split(bias)):
        pay_ref[: bias.shape[0], channels + start : channels + start + 128] = part
    if first is not None:
        for start, part in zip((0, 128), split(first)):
            pay_ref[half:, channels + start : channels + start + first.shape[1]] = part


def get_side(pay, channels, lanes, hid_count):
    half = pay.shape[0] // 2
    side = pay[:, channels : channels + 128].astype(f32) + pay[:, channels + 128 :].astype(f32)
    return side[:lanes], side[half:, :hid_count]


def near_kernel(
    rows, shards, blocks, width, rank_ref, x0_ref, c0_ref, x1_ref, c1_ref, spec_ref, weight_ref, rate_ref, front_ref,
    back_ref, trans_ref, featt_ref, slope_ref, own_ref, own_first_ref, conv_ref, corr_ref, ahead_ref, sums_ref,
    first_ref, fields, fast, high_ref, low_ref, acc_ref,
):
    rank = rank_ref[0]
    inner = jnp.logical_and(rank > 0, rank < shards - 1)
    count = shards - 1
    tables = (front_ref, back_ref)
    blocks_in = (x0_ref, c0_ref, x1_ref, c1_ref)

    @pl.when(jnp.logical_not(inner))
    def _():
        looped(
            functools.partial(near_strip, rows, shards, False),
            (None, None, None) + (ROWS,) * 4 + (CUBE, ROWS, ROWS), blocks, width,
        )(rank_ref, *tables, *blocks_in, spec_ref, conv_ref, corr_ref, fields, fast)

    @pl.when(inner)
    def _():
        acc_ref[...] = jnp.zeros_like(acc_ref)
        looped(
            functools.partial(near_strip, rows, shards, True),
            (None, None, None) + (ROWS,) * 4 + (CUBE, ROWS, ROWS) + (None, None, None) + (ROWS,) * 5, blocks, width,
        )(
            rank_ref, *tables, *blocks_in, spec_ref, conv_ref, corr_ref, fields, fast, trans_ref, weight_ref, rate_ref,
            own_ref, ahead_ref, sums_ref, high_ref, low_ref, acc_ref,
        )
        first_ref[...] = own_first_ref[...] + exact_dot(
            featt_ref[:, : count * rows], acc_ref[...] * slope_ref[: count * rows, :]
        )


def near_strip(
    rows, shards, inner, block, blocks, rank_ref, front_ref, back_ref, x0_ref, c0_ref, x1_ref, c1_ref, spec_ref,
    conv_ref, corr_ref, fields, fast, *rest
):
    rank = rank_ref[0]
    count = shards - 1
    if inner:
        trans_ref, weight_ref, rate_ref, own_ref, ahead_ref, sums_ref, high_ref, low_ref, acc_ref = rest
        lower = rank == 1
        upper = jnp.where(rank == 2, 1.0, 0.0).astype(f32)
        side = jnp.where(rank == 2, 1.0, -1.0).astype(f32)
    for index, ref in enumerate((x0_ref, c0_ref, x1_ref, c1_ref)):
        fields[index] = forward(front_ref, ref[...])
    for re, im, sign in row_groups(rows):
        x0, c0, x1, c1 = ((fields[i, re, :], fields[i, im, :]) for i in range(4))
        w0, w1, w2 = ((spec_ref[i, re, :].astype(f32), spec_ref[i, im, :].astype(f32)) for i in range(3))
        values = [plus(times(w0, x0), times(w1, x1)), plus(conj_times(w0, c0), conj_times(w1, c1))]
        if inner:
            values.append(times((w2[0], w2[1] * side), choose(lower, c1, x1)))
        for index, value in enumerate(values):
            fast[index, re, :] = value[0].astype(bf16)
            fast[index, im, :] = value[1].astype(bf16)
        if inner:
            one = plus(conj_times(x1, c0), scaled(conj_times(x0, c1), upper))
            two = conj_times(x1, c1)
            for index, value in enumerate((turned(one, sign), plus(one, turned(two, sign)), two)):
                for part, where in zip(value, (re, im)):
                    high_ref[index, where, :], low_ref[index, where, :] = split(part)
    conv_ref[...] = backward(back_ref, fast[0])
    corr_ref[...] = backward(back_ref, fast[1])
    if not inner:
        return
    ahead_ref[...] = backward(back_ref, fast[2])
    rate = rate_ref[...]
    env = decay(rate, rows, float(rows * shards) ** -0.5)
    parts = []
    for lag in range(count):
        grad = backward(back_ref, high_ref[lag], low_ref[lag])
        parts.append(split(grad * (env * jnp.exp(rate * (-float(lag * rows))))))
    m_high = jnp.concatenate([p[0] for p in parts], axis=0)
    m_low = jnp.concatenate([p[1] for p in parts], axis=0)
    sums_ref[...] = own_ref[...] + weight_sums(trans_ref[:, : count * rows], m_high, m_low)
    acc_ref[...] += hidden_sums(m_high, m_low, *split(weight_ref[...]))


def on_inner(shards, rank_at, kernel):
    def run(*refs):
        rank = refs[rank_at][0]

        @pl.when(jnp.logical_and(rank > 0, rank < shards - 1))
        def _():
            kernel(*refs)

    return run


def far_kernel(rows, block, blocks, rank_ref, far_ref, spec_ref, front_ref, back_ref, ahead_ref, part_ref, late_ref):
    side = jnp.where(rank_ref[0] == 2, 1.0, -1.0).astype(f32)
    far = forward(front_ref, far_ref[...])
    far = (far[:rows], far[rows:])
    w2, w3 = ((spec_ref[i, :rows, :].astype(f32), spec_ref[i, rows:, :].astype(f32) * side) for i in range(2))
    ahead = jnp.concatenate(times(w3, far), axis=0).astype(bf16)
    part_ref[...] = (ahead_ref[...] + backward(back_ref, ahead)).astype(bf16)
    late = jnp.concatenate(times(w2, far), axis=0).astype(bf16)
    late_ref[...] = backward(back_ref, late)


def last_kernel(
    rows, shards, channels, block, blocks, after_ref, rank_ref, x1_ref, c1_ref, far_ref, weight_ref, rate_ref, front_ref, back_ref,
    trans_ref, featt_ref, slope_ref, sums_ref, first_ref, bias_ref, in_ref, pay_ref, total_ref, acc_ref,
):
    del after_ref
    hid_count, width = weight_ref.shape
    lower = rank_ref[0] == 1
    start = pl.multiple_of(block * width, width)
    here = sums_ref[...] + in_ref[:, pl.ds(start, width)].astype(f32)
    mine = (block < blocks // 2) == lower

    @pl.when(block == 0)
    def _():
        acc_ref[...] = jnp.zeros_like(acc_ref)

    @pl.when(mine)
    def _():
        sign = jnp.where(lower, 1.0, -1.0).astype(f32)
        near = forward(front_ref, jnp.where(lower, x1_ref[...], c1_ref[...]))
        far = forward(front_ref, far_ref[...])
        three = conj_times((near[:rows], near[rows:]), (far[:rows], far[rows:]))
        three = (three[0], three[1] * sign)
        half = rows // 2
        two = jnp.concatenate([three[1][:half], -three[1][half:], -three[0][:half], three[0][half:]], axis=0)
        rate = rate_ref[...]
        env = decay(rate, rows, float(rows * shards) ** -0.5)
        parts = []
        for lag, value in ((shards - 2, two), (shards - 1, jnp.concatenate(three, axis=0))):
            grad = backward(back_ref, *split(value))
            parts.append(split(grad * (env * jnp.exp(rate * (-float(lag * rows))))))
        m_high = jnp.concatenate([p[0] for p in parts], axis=0)
        m_low = jnp.concatenate([p[1] for p in parts], axis=0)
        trans = trans_ref[:, (shards - 2) * rows :]
        pay_ref[:, pl.ds(start, width)] = (here + weight_sums(trans, m_high, m_low)).astype(bf16)
        w_high, w_low = split(weight_ref[...])
        acc_ref[...] += hidden_sums(m_high, m_low, w_high, w_low)

    @pl.when(jnp.logical_not(mine))
    def _():
        pay_ref[:, pl.ds(start, width)] = here.astype(bf16)

    @pl.when(block == blocks - 1)
    def _():
        first = exact_dot(
            featt_ref[:, (shards - 2) * rows :], acc_ref[...] * slope_ref[(shards - 2) * rows :, :]
        )
        lanes = channels // 128
        in_bias, in_first = get_side(in_ref[...], channels, lanes, hid_count)
        first = first + first_ref[...] + in_first
        put_side(pay_ref, channels, fold(bias_ref[...]) + in_bias)
        total_ref[...] = first


def total_kernel(channels, hid_count, part_ref, first_ref, own_ref, come_ref, pay_ref):
    del part_ref, first_ref
    lanes = channels // 128
    pay_ref[:, :channels] = (own_ref[:, :channels].astype(f32) + come_ref[:, :channels].astype(f32)).astype(bf16)
    own, come = (get_side(ref[...], channels, lanes, hid_count)[0] for ref in (own_ref, come_ref))
    put_side(pay_ref, channels, own + come)


def gates_kernel(
    shards, block, blocks, rank_ref, one_ref, two_ref, val_ref, out_ref, skip_ref, conv_ref, corr_ref, late_ref, part_ref,
    grad_one_ref, grad_two_ref, grad_value_ref,
):
    rank = rank_ref[0]

    def on(wanted, value):
        return jnp.where(rank == wanted, value, jnp.zeros_like(value))

    part = part_ref[...].astype(f32)
    late = late_ref[...]
    one = one_ref[...].astype(f32)
    val = val_ref[...].astype(f32)
    out = out_ref[...].astype(f32)
    skip = skip_ref[...]
    conv = conv_ref[...] + on(2, late) + on(shards - 1, part)
    corr = corr_ref[...] + on(1, late) + on(0, part)
    grad_two_ref[...] = (out * (conv + skip * (one * val))).astype(bf16)
    mid = corr + skip * (out * two_ref[...].astype(f32))
    grad_one_ref[...] = (mid * val).astype(bf16)
    grad_value_ref[...] = (mid * one).astype(bf16)


def finish_kernel(
    channels, shards, rank_ref, own_ref, come_ref, first_ref, first_come_ref, second_out, first_out, bias_out, second,
    first, bias, sems,
):
    rank = rank_ref[0]
    inner = jnp.logical_and(rank > 0, rank < shards - 1)
    lanes = channels // 128
    copies = [
        pltpu.make_async_copy(held, out, sems.at[i])
        for i, (held, out) in enumerate(((second, second_out), (first, first_out), (bias, bias_out)))
    ]
    picked = jnp.where(inner, own_ref[...], come_ref[...])
    second[...] = picked[:, :channels].astype(f32)
    copies[0].start()
    first[...] = jnp.where(inner, first_ref[...], first_come_ref[...])
    copies[1].start()
    rows = get_side(picked, channels, lanes, first.shape[1])[0]
    for i in range(lanes):
        bias[:, i * 128 : (i + 1) * 128] = rows[i : i + 1]
    copies[2].start()
    for copy in copies:
        copy.wait()


def few_shards_body(
    x_one, x_two, values, grad_out, first_weight, second_weight, skip_bias, decay_rate
):
    rows, channels = x_one.shape
    shards = lax.axis_size("ctx")
    feat_count, hid_count = first_weight.shape
    seq_len = rows * shards
    double = 2 * rows
    width = min(512, channels)
    blocks = channels // width
    rank = lax.axis_index("ctx").astype(jnp.int32).reshape(1)
    front, back = block_tables(rows)
    feats = feature_table(seq_len)
    featt = np.ascontiguousarray(feats.T)
    skip_row = skip_bias.reshape(1, channels)
    rate_row = decay_rate.reshape(1, channels)
    smem = pl.BlockSpec(memory_space=pltpu.SMEM)
    vmem = pl.BlockSpec(memory_space=pltpu.VMEM)
    anywhere = pl.BlockSpec(memory_space=pl.ANY)
    mebi = 1024 * 1024

    def shape(*dims, dtype=f32):
        return jax.ShapeDtypeStruct(dims, dtype)

    def call(kernel, name, units, out_shape, in_specs, out_specs=None, scratch=(), limit=16, aliases={}):
        return pl.pallas_call(
            kernel,
            in_specs=in_specs,
            out_specs=out_specs if out_specs is not None else [vmem] * len(out_shape),
            out_shape=out_shape,
            scratch_shapes=scratch,
            input_output_aliases=aliases,
            compiler_params=pltpu.CompilerParams(vmem_limit_bytes=limit * mebi),
            cost_estimate=pl.CostEstimate(
                flops=2 * units * double * double * channels, bytes_accessed=rows * channels, transcendentals=0
            ),
            name=name,
        )

    def move(array, pairs):
        return lax.ppermute(array, "ctx", pairs)

    up = [(i, i + 1) for i in range(shards - 1)]
    down = [(i + 1, i) for i in range(shards - 1)]
    inward = [(0, 1), (shards - 1, shards - 2)]
    outward = [(1, 0), (shards - 2, shards - 1)]
    across = [(1, 2), (2, 1)]
    pay_shape = (hid_count, channels + SIDE)
    block_bf16 = shape(rows, channels, dtype=bf16)
    block_f32 = shape(rows, channels)

    row_step = max(rows // 2, 16)
    gate_rows = pl.BlockSpec((row_step, channels), lambda i: (i, 0))
    x0, c0, edge, bias = pl.pallas_call(
        products_kernel,
        grid=(rows // row_step,),
        in_specs=[smem] + [gate_rows] * 4,
        out_specs=[gate_rows] * 3 + [pl.BlockSpec((1, channels), lambda i: (0, 0))],
        out_shape=[block_bf16] * 3 + [shape(1, channels)],
        compiler_params=pltpu.CompilerParams(vmem_limit_bytes=64 * mebi),
        name="products",
    )(rank, x_one, x_two, values, grad_out)
    x1 = move(x0, up)
    c1 = move(c0, down)

    own_shapes = [
        shape(rows, feat_count), shape(feat_count, hid_count), block_bf16, block_bf16, shape(hid_count, channels),
        shape(1, channels), shape(double, double, dtype=bf16), shape(double, double, dtype=bf16),
        shape(feat_count, seq_len), shape(1, channels), shape(hid_count, channels), shape(*pay_shape, dtype=bf16),
        shape(feat_count, hid_count),
    ]
    own, send, own_first, edge = call(
        functools.partial(own_kernel, rows, shards, channels, blocks, width), "own_pair", 8,
        [shape(hid_count, channels), shape(*pay_shape, dtype=bf16), shape(feat_count, hid_count), block_bf16],
        [anywhere] * 11,
        out_specs=[anywhere] * 4,
        scratch=[pltpu.VMEM(s.shape, s.dtype) for s in own_shapes]
        + [
            pltpu.VMEM((2 * hid_count, rows), bf16), pltpu.VMEM((rows, hid_count), f32),
            pltpu.SemaphoreType.DMA((10,)), pltpu.SemaphoreType.DMA((blocks + 2,)),
        ],
        aliases={10: 3},
        limit=60,
    )(feats[:rows], first_weight, x0, c0, second_weight, rate_row, front, back, featt, bias, edge)
    far = move(edge, [(0, 2), (shards - 1, shards - 3)])

    spec, trans, slope = call(
        functools.partial(filters_kernel, rows, shards, blocks, width), "filters", 8,
        [
            shape(shards, double, channels, dtype=bf16), shape(2 * hid_count, seq_len, dtype=bf16),
            shape(seq_len, hid_count),
        ],
        [vmem] * 5,
        scratch=[pltpu.VMEM((seq_len, 3 * hid_count), bf16)],
    )(feats, first_weight, second_weight, rate_row, front)

    send, _ = lax.optimization_barrier((send, slope))
    come = move(send, inward)

    conv, corr, ahead, sums, first = call(
        functools.partial(near_kernel, rows, shards, blocks, width), "near_blocks", 20,
        [block_f32] * 3 + [shape(hid_count, channels), shape(feat_count, hid_count)],
        [smem] + [vmem] * 14,
        scratch=[
            pltpu.VMEM((4, double, width), f32),
            pltpu.VMEM((3, double, width), bf16),
            pltpu.VMEM((shards - 1, double, width), bf16),
            pltpu.VMEM((shards - 1, double, width), bf16),
            pltpu.VMEM(((shards - 1) * rows, hid_count), f32),
        ],
    )(rank, x0, c0, x1, c1, spec, second_weight, rate_row, front, back, trans, featt, slope, own, own_first)
    part, late = call(
        on_inner(
            shards, 0,
            looped(
                functools.partial(far_kernel, rows),
                (None, ROWS, (slice(2, 4), slice(None)), None, None, ROWS, ROWS, ROWS),
                blocks, width,
            ),
        ),
        "far_block", 1,
        [block_bf16, block_f32],
        [smem] + [vmem] * 5,
    )(rank, far, spec, front, back, ahead)
    part_come = move(part, outward)

    pay, first = call(
        on_inner(
            shards, 1,
            looped(
                functools.partial(last_kernel, rows, shards, channels),
                (None, None, ROWS, ROWS, ROWS, ROWS, ROWS, None, None, None, None, None, ROWS),
                blocks, width,
            ),
        ),
        "last_pair", 1,
        [shape(*pay_shape, dtype=bf16), shape(feat_count, hid_count)],
        [anywhere, smem] + [vmem] * 14,
        scratch=[pltpu.VMEM((2 * rows, hid_count), f32)],
    )(late, rank, x1, c1, far, second_weight, rate_row, front, back, trans, featt, slope, sums, first, bias, come)
    pay_come = move(pay, across)
    group = lax.axis_size(("ch", "sub"))
    bit = 1
    while bit < group:
        first = first + lax.ppermute(first, ("ch", "sub"), [(i, i ^ bit) for i in range(group)])
        bit *= 2

    (total,) = call(
        functools.partial(total_kernel, channels, hid_count), "total", 0,
        [shape(*pay_shape, dtype=bf16)],
        [anywhere] * 2 + [vmem] * 2,
    )(part_come, first, pay, pay_come)
    total_come = move(total, outward)
    first = first + move(first, across)
    first_come = move(first, outward)

    grad_one, grad_two, grad_value = call(
        looped(
            functools.partial(gates_kernel, shards), (None,) + (ROWS,) * 12, blocks, width
        ),
        "gates", 0,
        [block_bf16] * 3,
        [smem] + [vmem] * 9,
    )(rank, x_one, x_two, values, grad_out, skip_row, conv, corr, late, part_come)

    outs = [shape(hid_count, channels), shape(feat_count, hid_count), shape(1, channels)]
    grad_second, grad_first, grad_bias = call(
        functools.partial(finish_kernel, channels, shards), "finish", 0,
        outs,
        [smem] + [vmem] * 4,
        out_specs=[anywhere] * 3,
        scratch=[pltpu.VMEM(o.shape, f32) for o in outs] + [pltpu.SemaphoreType.DMA((3,))],
    )(rank, total, total_come, first, first_come)
    return (grad_one, grad_two, grad_value, grad_first, grad_second, grad_bias.reshape(channels))


def solution(mesh):
    in_specs = (
        P(("parts", "ctx"), ("ch", "sub")),
        P(("parts", "ctx"), ("ch", "sub")),
        P(("parts", "ctx"), ("ch", "sub")),
        P(("parts", "ctx"), ("ch", "sub")),
        P(),
        P(None, ("ch", "sub")),
        P(("ch", "sub")),
        P(("ch", "sub")),
    )
    out_specs = (
        P(("parts", "ctx"), ("ch", "sub")),
        P(("parts", "ctx"), ("ch", "sub")),
        P(("parts", "ctx"), ("ch", "sub")),
        P("parts", None),
        P("parts", ("ch", "sub")),
        P(("parts", "ch", "sub")),
    )
    body = few_shards_body if mesh.shape["ctx"] == 4 else many_shards_body
    return jax.shard_map(body, mesh=mesh, in_specs=in_specs, out_specs=out_specs, check_vma=False)
```

```python
import functools
import math

import jax
import jax.numpy as jnp
import numpy as np
from jax import lax
from jax.experimental import pallas as pl
from jax.experimental.pallas import tpu as pltpu
from jax.sharding import PartitionSpec as P

band_steps = (1763, 1201, 811, 547, 367, 251, 167, 113, 79, 53, 37, 23, 17, 11, 7, 3)
highest = lax.Precision.HIGHEST
f32 = jnp.float32
bf16 = jnp.bfloat16


def features(positions):
    multiplier = jnp.array(band_steps, dtype=jnp.int32)
    phase = positions[:, None] * multiplier[None, :] % 4096
    angle = phase.astype(jnp.float32) * (2.0 * math.pi / 4096.0)
    return jnp.concatenate([jnp.cos(angle), jnp.sin(angle)], axis=1)


def tables(out_count, in_count, modulus, sign_value):
    row_index = lax.broadcasted_iota(jnp.int32, (out_count, in_count), 0)
    col_index = lax.broadcasted_iota(jnp.int32, (out_count, in_count), 1)
    angle = (row_index * col_index % modulus).astype(jnp.float32) * (2.0 * math.pi / modulus)
    return (jnp.cos(angle), sign_value * jnp.sin(angle))


def twiddle(spec_re, spec_im, freq_count, span, modulus, sign_value):
    freq_index = lax.broadcasted_iota(jnp.int32, (freq_count, span), 0)
    pos_index = lax.broadcasted_iota(jnp.int32, (freq_count, span), 1)
    angle = (freq_index * pos_index % modulus).astype(jnp.float32) * (2.0 * math.pi / modulus)
    factor_re = jnp.cos(angle)[None, None, :, :]
    factor_im = (sign_value * jnp.sin(angle))[None, None, :, :]
    return (spec_re * factor_re - spec_im * factor_im, spec_re * factor_im + spec_im * factor_re)


def contract(kernel, array):
    return jnp.einsum(
        "lj,mckj->mckl", kernel, array, precision=highest, preferred_element_type=jnp.float32
    )


def along_positions(spec_re, spec_im, kernel_re, kernel_im):
    return (
        contract(kernel_re, spec_re) - contract(kernel_im, spec_im),
        contract(kernel_re, spec_im) + contract(kernel_im, spec_re),
    )


def many_shards_body(
    x_one, x_two, values, grad_out, first_weight, second_weight, skip_bias, decay_rate
):
    row_count, chan_count = x_one.shape
    shards = lax.axis_size("ctx")
    rank = lax.axis_index("ctx")
    seq_len = row_count * shards
    total = 2 * seq_len
    narrow = chan_count // shards
    chan_weight = lax.dynamic_slice_in_dim(second_weight, rank * narrow, narrow, 1)
    chan_rate = lax.dynamic_slice_in_dim(decay_rate, rank * narrow, narrow, 0)
    source = x_one.astype(jnp.float32) * values.astype(jnp.float32)
    cotan = grad_out.astype(jnp.float32) * x_two.astype(jnp.float32)
    spread = lax.all_to_all(
        jnp.stack([source.T, cotan.T])[:, :, None, :],
        "ctx",
        split_axis=1,
        concat_axis=2,
        tiled=True,
    )
    far_source = spread[0]
    far_cotan = spread[1]
    positions = jnp.arange(seq_len, dtype=jnp.int32)
    feats = features(positions)
    pre_act = jnp.dot(feats, first_weight, precision=highest, preferred_element_type=jnp.float32)
    hidden = jnp.sin(pre_act)
    envelope = jnp.exp(-chan_rate[:, None] * positions.astype(jnp.float32)[None, :]) * float(
        seq_len
    ) ** (-0.5)
    filt = (
        jnp.einsum(
            "th,hc->ct", hidden, chan_weight, precision=highest, preferred_element_type=jnp.float32
        )
        * envelope
    )
    filt_blocks = filt.reshape(narrow, shards, row_count)
    fields = jnp.stack([far_source, far_cotan])

    def first_section(kernel):
        field_part = jnp.einsum(
            "kn,mcnj->mckj", kernel, fields, precision=highest, preferred_element_type=jnp.float32
        )
        filter_part = jnp.einsum(
            "kn,cnj->ckj",
            kernel,
            filt_blocks,
            precision=highest,
            preferred_element_type=jnp.float32,
        )
        return jnp.concatenate([field_part, filter_part[None]], axis=0)

    first_re, first_im = tables(2 * shards, shards, 2 * shards, -1.0)
    spec_re, spec_im = (first_section(first_re), first_section(first_im))
    spec_re, spec_im = twiddle(spec_re, spec_im, 2 * shards, row_count, total, -1.0)
    fwd_re, fwd_im = tables(row_count, row_count, row_count, -1.0)
    spec_re, spec_im = along_positions(spec_re, spec_im, fwd_re, fwd_im)
    source_re, source_im = (spec_re[0], spec_im[0])
    cotan_re, cotan_im = (spec_re[1], spec_im[1])
    filter_re, filter_im = (spec_re[2], spec_im[2])
    prod_re = jnp.stack(
        [
            source_re * filter_re - source_im * filter_im,
            cotan_re * filter_re + cotan_im * filter_im,
            cotan_re * source_re + cotan_im * source_im,
        ]
    )
    prod_im = jnp.stack(
        [
            source_re * filter_im + source_im * filter_re,
            cotan_im * filter_re - cotan_re * filter_im,
            cotan_im * source_re - cotan_re * source_im,
        ]
    )
    back_re, back_im = tables(row_count, row_count, row_count, 1.0)
    prod_re, prod_im = along_positions(prod_re, prod_im, back_re, back_im)
    prod_re, prod_im = twiddle(prod_re, prod_im, 2 * shards, row_count, total, 1.0)
    last_re, last_im = tables(shards, 2 * shards, 2 * shards, 1.0)
    field_out = jnp.einsum(
        "nk,mckj->mcnj", last_re, prod_re[:2], precision=highest, preferred_element_type=jnp.float32
    ) - jnp.einsum(
        "nk,mckj->mcnj", last_im, prod_im[:2], precision=highest, preferred_element_type=jnp.float32
    )
    field_out = field_out * (1.0 / total)
    filt_grad = jnp.einsum(
        "nk,ckj->cnj", last_re, prod_re[2], precision=highest, preferred_element_type=jnp.float32
    ) - jnp.einsum(
        "nk,ckj->cnj", last_im, prod_im[2], precision=highest, preferred_element_type=jnp.float32
    )
    filt_grad = (filt_grad * (1.0 / total)).reshape(narrow, seq_len)
    modulated = filt_grad * envelope
    weight_part = jnp.einsum(
        "th,ct->hc", hidden, modulated, precision=highest, preferred_element_type=jnp.float32
    )
    hidden_grad = jnp.einsum(
        "ct,hc->th", modulated, chan_weight, precision=highest, preferred_element_type=jnp.float32
    )
    first_part = jnp.dot(
        feats.T,
        hidden_grad * jnp.cos(pre_act),
        precision=highest,
        preferred_element_type=jnp.float32,
    )
    grad_first = lax.psum(first_part, ("ctx", "ch", "sub"))
    returned = lax.all_to_all(
        field_out.astype(jnp.bfloat16), "ctx", split_axis=2, concat_axis=1, tiled=True
    ).astype(field_out.dtype)
    conv_part = returned[0, :, 0, :].T
    corr_part = returned[1, :, 0, :].T
    grad_two = (grad_out.astype(jnp.float32) * (conv_part + skip_bias[None, :] * source)).astype(
        jnp.bfloat16
    )
    grad_mid = corr_part + skip_bias[None, :] * cotan
    grad_one = (grad_mid * values.astype(jnp.float32)).astype(jnp.bfloat16)
    grad_value = (grad_mid * x_one.astype(jnp.float32)).astype(jnp.bfloat16)
    grad_bias = lax.psum(jnp.sum(source * cotan, axis=0), "ctx")
    grad_second = lax.all_gather(weight_part, "ctx", axis=1, tiled=True)
    return (grad_one, grad_two, grad_value, grad_first, grad_second, grad_bias)


STEP = 16
SIDE = 256


def halves(array):
    array = np.asarray(array, np.float32)
    high = array.astype(bf16)
    low = (array - high.astype(np.float32)).astype(bf16)
    return high, low


def block_tables(rows):
    freq = np.concatenate([np.arange(0, rows, 2), np.arange(1, rows, 2)])
    phase = (2 * freq + 1)[:, None] * np.arange(rows)[None, :] % (4 * rows)
    angle = phase * (2.0 * np.pi / (4 * rows))
    forward = np.concatenate([np.cos(angle), -np.sin(angle)], axis=0)
    front = np.ascontiguousarray(np.concatenate(halves(forward), axis=1))
    back = np.ascontiguousarray(np.concatenate(halves(forward.T / rows), axis=0))
    return front, back


def feature_table(seq_len):
    phase = np.arange(seq_len)[:, None] * np.array(band_steps)[None, :] % 4096
    angle = phase * (2.0 * np.pi / 4096.0)
    return np.concatenate([np.cos(angle), np.sin(angle)], axis=1).astype(np.float32)


def split(array):
    high = array.astype(bf16)
    return high, (array - high.astype(f32)).astype(bf16)


def dot(left, right):
    return jnp.dot(left, right, preferred_element_type=f32)


def exact_dot(left, right):
    return jnp.dot(left, right, precision=highest, preferred_element_type=f32)


def dot_across(left, right):
    return lax.dot_general(left, right, (((1,), (1,)), ((), ())), preferred_element_type=f32)


def decay(rate, rows, scale):
    place = lax.broadcasted_iota(jnp.int32, (rows, rate.shape[1]), 0)
    return jnp.exp(-place.astype(f32) * rate) * scale


def times(a, b):
    return a[0] * b[0] - a[1] * b[1], a[0] * b[1] + a[1] * b[0]


def conj_times(a, b):
    return a[0] * b[0] + a[1] * b[1], a[0] * b[1] - a[1] * b[0]


def plus(a, b):
    return a[0] + b[0], a[1] + b[1]


def scaled(a, factor):
    return a[0] * factor, a[1] * factor


def choose(condition, a, b):
    return jnp.where(condition, a[0], b[0]), jnp.where(condition, a[1], b[1])


def turned(a, sign):
    return (a[1], -a[0]) if sign > 0 else (-a[1], a[0])


def forward(front_ref, block):
    return dot(front_ref[...], jnp.concatenate([block, block], axis=0))


def backward(back_ref, high, low=None):
    both = dot(back_ref[...], high)
    rows = both.shape[0] // 2
    out = both[:rows] + both[rows:]
    return out if low is None else out + dot(back_ref[:rows], low)


def row_groups(rows):
    for step in range(rows // STEP):
        sign = 1 if step * STEP < rows // 2 else -1
        yield slice(step * STEP, (step + 1) * STEP), slice(rows + step * STEP, rows + (step + 1) * STEP), sign


def weight_sums(trans, m_high, m_low):
    both = dot(trans, m_high)
    count = both.shape[0] // 2
    return both[:count] + both[count:] + dot(trans[:count], m_low)


def hidden_sums(m_high, m_low, w_high, w_low):
    left = jnp.concatenate([m_high, m_high, m_low], axis=1)
    right = jnp.concatenate([w_high, w_low, w_high], axis=1)
    return dot_across(left, right)


def looped(kernel, kinds, blocks, width):
    def over_strips(*refs):
        def step(block, carry):
            cols = pl.ds(pl.multiple_of(block * width, width), width)
            views = [
                ref if kind is None else ref.at[(*kind, cols)]
                for ref, kind in zip(refs, kinds + (None,) * (len(refs) - len(kinds)))
            ]
            kernel(block, blocks, *views)
            return carry

        lax.fori_loop(0, blocks, step, 0)

    return over_strips


ROWS = (slice(None),)
CUBE = (slice(None), slice(None))


def products_kernel(rank_ref, one_ref, two_ref, val_ref, out_ref, pair_ref, other_ref, edge_ref, bias_ref):
    source = one_ref[...].astype(f32) * val_ref[...].astype(f32)
    cotan = out_ref[...].astype(f32) * two_ref[...].astype(f32)
    even = rank_ref[0] % 2 == 0
    pair_ref[...] = jnp.where(even, source, cotan).astype(bf16)
    edge_ref[...] = pair_ref[...]
    other_ref[...] = jnp.where(even, cotan, source).astype(bf16)
    part = jnp.sum(source * cotan, axis=0, keepdims=True)

    @pl.when(pl.program_id(0) == 0)
    def _():
        bias_ref[...] = part

    @pl.when(pl.program_id(0) > 0)
    def _():
        bias_ref[...] += part


def ordered(first, a, b):
    return (jnp.where(first, a, b), jnp.where(first, b, a))


def sin_cos(angle):
    turns = jnp.floor(angle * (2.0 / math.pi) + 0.5)
    rest = ((angle - turns * 1.5703125) - turns * 4.837512969970703e-4) - turns * 7.54978995489188e-8
    square = rest * rest
    sine = rest + rest * square * (
        -1.6666654611e-1 + square * (8.3321608736e-3 + square * -1.9515295891e-4)
    )
    cosine = 1.0 - 0.5 * square + square * square * (
        4.166664568298827e-2 + square * (-1.388731625493765e-3 + square * 2.443315711809948e-5)
    )
    quarter = turns.astype(jnp.int32)
    odd = (quarter & 1) == 1
    sin_sign = jnp.where((quarter & 2) == 2, -1.0, 1.0).astype(f32)
    cos_sign = jnp.where(((quarter + 1) & 2) == 2, -1.0, 1.0).astype(f32)
    return jnp.where(odd, cosine, sine) * sin_sign, jnp.where(odd, sine, cosine) * cos_sign


def turned_over(hidden, slope):
    both = jnp.concatenate([hidden, slope], axis=1).T
    return jnp.concatenate(split(both[: hidden.shape[1]]), axis=0)


def filters_kernel(
    rows, shards, blocks, width, feats_ref, first_ref, weight_ref, rate_ref, front_ref, spec_ref, trans_ref, slope_ref,
    hid_ref,
):
    hidden, slope = sin_cos(exact_dot(feats_ref[...], first_ref[...]))
    slope_ref[...] = slope
    high, low = split(hidden)
    hid_ref[...] = jnp.concatenate([high, high, low], axis=1)
    trans_ref[...] = turned_over(hidden, slope)
    strips = looped(
        functools.partial(filter_strip, rows, shards), (None, ROWS, ROWS, None, CUBE), blocks, width
    )
    strips(hid_ref, weight_ref, rate_ref, front_ref, spec_ref)


def filter_strip(rows, shards, block, blocks, hid_ref, weight_ref, rate_ref, front_ref, spec_ref):
    scale = float(rows * shards) ** -0.5
    w_high, w_low = split(weight_ref[...])
    stacked = jnp.concatenate([w_high, w_low, w_high], axis=0)
    rate = rate_ref[...]
    env = decay(rate, rows, scale)
    before = None
    for lag in range(shards):
        part = dot(hid_ref[lag * rows : (lag + 1) * rows, :], stacked)
        part = part * (env * jnp.exp(rate * (-float(lag * rows))))
        f_high, f_low = split(part)
        now = forward(front_ref, f_high) + dot(front_ref[:, :rows], f_low)
        for re, im, sign in row_groups(rows):
            here = (now[re], now[im])
            if before is not None:
                here = plus(here, turned((before[re], before[im]), -sign))
            spec_ref[lag, re, :] = here[0].astype(bf16)
            spec_ref[lag, im, :] = here[1].astype(bf16)
        before = now


def own_kernel(rows, shards, channels, blocks, width, rank_ref, *refs):
    inputs, send_out, held = refs[:10], refs[10], refs[11:21]
    send_ref, trans_ref, acc_ref, sems, out_sem = refs[21:]
    (
        feats_ref, first_ref, pair_ref, other_ref, weight_ref, rate_ref, front_ref, back_ref, featt_ref, bias_ref
    ) = held
    copies = [pltpu.make_async_copy(far, near, sems.at[i]) for i, (far, near) in enumerate(zip(inputs, held))]
    for copy in copies:
        copy.start()
    acc_ref[...] = jnp.zeros_like(acc_ref)
    copies[0].wait()
    copies[1].wait()
    hidden, slope = sin_cos(exact_dot(feats_ref[...], first_ref[...]))
    trans_ref[...] = turned_over(hidden, slope)
    for copy in copies[2:]:
        copy.wait()
    kinds = (None, ROWS, ROWS, ROWS, ROWS, None, None, None, ROWS, None)
    looped(functools.partial(own_strip, rows, shards), kinds, blocks, width)(
        rank_ref, pair_ref, other_ref, weight_ref, rate_ref, front_ref, back_ref, trans_ref, send_ref, acc_ref
    )
    first = exact_dot(featt_ref[:, :rows], acc_ref[...] * slope)
    put_side(send_ref, channels, fold(bias_ref[...]), first)
    last = pltpu.make_async_copy(send_ref, send_out, out_sem)
    last.start()
    last.wait()


def own_strip(
    rows, shards, block, blocks, rank_ref, pair_ref, other_ref, weight_ref, rate_ref, front_ref, back_ref, trans_ref,
    send_ref, acc_ref,
):
    source, cotan = ordered(rank_ref[0] % 2 == 0, pair_ref[...], other_ref[...])
    x0 = forward(front_ref, source)
    c0 = forward(front_ref, cotan)
    pair = conj_times((x0[:rows], x0[rows:]), (c0[:rows], c0[rows:]))
    high, low = split(jnp.concatenate(pair, axis=0))
    env = decay(rate_ref[...], rows, float(rows * shards) ** -0.5)
    m_high, m_low = split(backward(back_ref, high, low) * env)
    send_ref[...] = weight_sums(trans_ref[...], m_high, m_low).astype(bf16)
    acc_ref[...] += hidden_sums(m_high, m_low, *split(weight_ref[...]))


def fold(bias):
    return jnp.concatenate([bias[:, i * 128 : (i + 1) * 128] for i in range(bias.shape[1] // 128)], axis=0)


def put_side(pay_ref, channels, bias, first=None):
    half = pay_ref.shape[0] // 2
    pay_ref[:, channels:] = jnp.zeros((2 * half, SIDE), bf16)
    for start, part in zip((0, 128), split(bias)):
        pay_ref[: bias.shape[0], channels + start : channels + start + 128] = part
    if first is not None:
        for start, part in zip((0, 128), split(first)):
            pay_ref[half:, channels + start : channels + start + first.shape[1]] = part


def get_side(pay, channels, lanes, hid_count):
    half = pay.shape[0] // 2
    side = pay[:, channels : channels + 128].astype(f32) + pay[:, channels + 128 :].astype(f32)
    return side[:lanes], side[half:, :hid_count]


def near_kernel(
    rows, shards, blocks, width, rank_ref, pair_ref, other_ref, pair_in_ref, middle_in_ref, spec_ref, weight_ref,
    rate_ref, front_ref, back_ref, trans_ref, featt_ref, slope_ref, conv_ref, corr_ref, ahead_ref, sums_ref, first_ref,
    fields, fast, high_ref, low_ref, acc_ref,
):
    rank = rank_ref[0]
    inner = jnp.logical_and(rank > 0, rank < shards - 1)
    count = shards - 1
    kinds = (None, None, None) + (ROWS,) * 4 + (CUBE, ROWS, ROWS)
    common = (
        rank_ref, front_ref, back_ref, pair_ref, other_ref, pair_in_ref, middle_in_ref, spec_ref, conv_ref, corr_ref,
        fields, fast,
    )

    @pl.when(jnp.logical_not(inner))
    def _():
        looped(functools.partial(edge_strip, rows, shards), kinds, blocks, width)(*common)

    @pl.when(inner)
    def _():
        acc_ref[...] = jnp.zeros_like(acc_ref)
        looped(
            functools.partial(inner_strip, rows, shards), kinds + (None, None, None) + (ROWS,) * 4, blocks, width
        )(*common, trans_ref, weight_ref, rate_ref, ahead_ref, sums_ref, high_ref, low_ref, acc_ref)
        first_ref[...] = exact_dot(
            featt_ref[:, : count * rows], acc_ref[...] * slope_ref[: count * rows, :]
        )


def edge_strip(
    rows, shards, block, blocks, rank_ref, front_ref, back_ref, pair_ref, other_ref, pair_in_ref, middle_in_ref,
    spec_ref, conv_ref, corr_ref, fields, fast,
):
    del middle_in_ref
    top = rank_ref[0] == shards - 1
    source, cotan = ordered(rank_ref[0] % 2 == 0, pair_ref[...], other_ref[...])
    for index, block_in in enumerate((source, cotan, pair_in_ref[...])):
        fields[index] = forward(front_ref, block_in)
    on_conv = jnp.where(top, 1.0, 0.0).astype(f32)
    on_corr = jnp.where(top, 0.0, 1.0).astype(f32)
    for re, im, sign in row_groups(rows):
        x0, c0, near = ((fields[i, re, :], fields[i, im, :]) for i in range(3))
        w0, w1 = ((spec_ref[i, re, :].astype(f32), spec_ref[i, im, :].astype(f32)) for i in range(2))
        values = (
            plus(times(w0, x0), scaled(times(w1, near), on_conv)),
            plus(conj_times(w0, c0), scaled(conj_times(w1, near), on_corr)),
        )
        for index, value in enumerate(values):
            fast[index, re, :] = value[0].astype(bf16)
            fast[index, im, :] = value[1].astype(bf16)
    conv_ref[...] = backward(back_ref, fast[0])
    corr_ref[...] = backward(back_ref, fast[1])


def inner_strip(
    rows, shards, block, blocks, rank_ref, front_ref, back_ref, pair_ref, other_ref, pair_in_ref, middle_in_ref,
    spec_ref, conv_ref, corr_ref, fields, fast, trans_ref, weight_ref, rate_ref, ahead_ref, sums_ref, high_ref, low_ref,
    acc_ref,
):
    lower = rank_ref[0] == 1
    upper = jnp.where(lower, 0.0, 1.0).astype(f32)
    side = jnp.where(lower, -1.0, 1.0).astype(f32)
    count = shards - 1
    blocks_in = (
        *ordered(lower, other_ref[...], pair_ref[...]), *ordered(lower, pair_in_ref[...], middle_in_ref[...])
    )
    for index, block_in in enumerate(blocks_in):
        fields[index] = forward(front_ref, block_in)
    for re, im, sign in row_groups(rows):
        x0, c0, x1, c1 = ((fields[i, re, :], fields[i, im, :]) for i in range(4))
        w0, w1, w2 = ((spec_ref[i, re, :].astype(f32), spec_ref[i, im, :].astype(f32)) for i in range(3))
        values = (
            plus(times(w0, x0), times(w1, x1)),
            plus(conj_times(w0, c0), conj_times(w1, c1)),
            times((w2[0], w2[1] * side), choose(lower, c1, x1)),
        )
        for index, value in enumerate(values):
            fast[index, re, :] = value[0].astype(bf16)
            fast[index, im, :] = value[1].astype(bf16)
        zero = conj_times(x0, c0)
        one = plus(conj_times(x1, c0), scaled(conj_times(x0, c1), upper))
        two = conj_times(x1, c1)
        for index, value in enumerate((plus(zero, turned(one, sign)), plus(one, turned(two, sign)), two)):
            for part, where in zip(value, (re, im)):
                high_ref[index, where, :], low_ref[index, where, :] = split(part)
    conv_ref[...] = backward(back_ref, fast[0])
    corr_ref[...] = backward(back_ref, fast[1])
    ahead_ref[...] = backward(back_ref, fast[2])
    rate = rate_ref[...]
    env = decay(rate, rows, float(rows * shards) ** -0.5)
    parts = []
    for lag in range(count):
        grad = backward(back_ref, high_ref[lag], low_ref[lag])
        parts.append(split(grad * (env * jnp.exp(rate * (-float(lag * rows))))))
    m_high = jnp.concatenate([p[0] for p in parts], axis=0)
    m_low = jnp.concatenate([p[1] for p in parts], axis=0)
    sums_ref[...] = weight_sums(trans_ref[:, : count * rows], m_high, m_low)
    acc_ref[...] += hidden_sums(m_high, m_low, *split(weight_ref[...]))


def only(inner, shards, rank_at, kernel):
    def run(*refs):
        rank = refs[rank_at][0]

        @pl.when(jnp.logical_and(rank > 0, rank < shards - 1) == inner)
        def _():
            kernel(*refs)

    return run


def far_kernel(rows, block, blocks, rank_ref, far_ref, spec_ref, front_ref, back_ref, ahead_ref, part_ref, late_ref):
    side = jnp.where(rank_ref[0] == 2, 1.0, -1.0).astype(f32)
    far = forward(front_ref, far_ref[...])
    far = (far[:rows], far[rows:])
    w2, w3 = ((spec_ref[i, :rows, :].astype(f32), spec_ref[i, rows:, :].astype(f32) * side) for i in range(2))
    ahead = jnp.concatenate(times(w3, far), axis=0).astype(bf16)
    part_ref[...] = (ahead_ref[...] + backward(back_ref, ahead)).astype(bf16)
    late = jnp.concatenate(times(w2, far), axis=0).astype(bf16)
    late_ref[...] = backward(back_ref, late)


def last_kernel(
    rows, shards, channels, block, blocks, after_ref, rank_ref, near_ref, far_ref, weight_ref, rate_ref, front_ref, back_ref,
    trans_ref, featt_ref, slope_ref, sums_ref, first_ref, bias_ref, in_ref, pay_ref, total_ref, acc_ref,
):
    del after_ref
    hid_count, width = weight_ref.shape
    lower = rank_ref[0] == 1
    start = pl.multiple_of(block * width, width)
    here = sums_ref[...] + in_ref[:, pl.ds(start, width)].astype(f32)
    mine = (block < blocks // 2) == lower

    @pl.when(block == 0)
    def _():
        acc_ref[...] = jnp.zeros_like(acc_ref)

    @pl.when(mine)
    def _():
        sign = jnp.where(lower, 1.0, -1.0).astype(f32)
        near = forward(front_ref, near_ref[...])
        far = forward(front_ref, far_ref[...])
        three = conj_times((near[:rows], near[rows:]), (far[:rows], far[rows:]))
        three = (three[0], three[1] * sign)
        half = rows // 2
        two = jnp.concatenate([three[1][:half], -three[1][half:], -three[0][:half], three[0][half:]], axis=0)
        rate = rate_ref[...]
        env = decay(rate, rows, float(rows * shards) ** -0.5)
        parts = []
        for lag, value in ((shards - 2, two), (shards - 1, jnp.concatenate(three, axis=0))):
            grad = backward(back_ref, *split(value))
            parts.append(split(grad * (env * jnp.exp(rate * (-float(lag * rows))))))
        m_high = jnp.concatenate([p[0] for p in parts], axis=0)
        m_low = jnp.concatenate([p[1] for p in parts], axis=0)
        trans = trans_ref[:, (shards - 2) * rows :]
        pay_ref[:, pl.ds(start, width)] = (here + weight_sums(trans, m_high, m_low)).astype(bf16)
        w_high, w_low = split(weight_ref[...])
        acc_ref[...] += hidden_sums(m_high, m_low, w_high, w_low)

    @pl.when(jnp.logical_not(mine))
    def _():
        pay_ref[:, pl.ds(start, width)] = here.astype(bf16)

    @pl.when(block == blocks - 1)
    def _():
        first = exact_dot(
            featt_ref[:, (shards - 2) * rows :], acc_ref[...] * slope_ref[(shards - 2) * rows :, :]
        )
        lanes = channels // 128
        in_bias, in_first = get_side(in_ref[...], channels, lanes, hid_count)
        first = first + first_ref[...] + in_first
        put_side(pay_ref, channels, fold(bias_ref[...]) + in_bias)
        total_ref[...] = first


def total_kernel(channels, hid_count, part_ref, first_ref, own_ref, come_ref, pay_ref):
    del part_ref, first_ref
    lanes = channels // 128
    pay_ref[:, :channels] = (own_ref[:, :channels].astype(f32) + come_ref[:, :channels].astype(f32)).astype(bf16)
    own, come = (get_side(ref[...], channels, lanes, hid_count)[0] for ref in (own_ref, come_ref))
    put_side(pay_ref, channels, own + come)


def gates_kernel(
    shards, block, blocks, rank_ref, one_ref, two_ref, val_ref, out_ref, skip_ref, conv_ref, corr_ref, late_ref, part_ref,
    grad_one_ref, grad_two_ref, grad_value_ref,
):
    rank = rank_ref[0]

    def on(wanted, value):
        return jnp.where(rank == wanted, value, jnp.zeros_like(value))

    part = part_ref[...].astype(f32)
    late = late_ref[...]
    one = one_ref[...].astype(f32)
    val = val_ref[...].astype(f32)
    out = out_ref[...].astype(f32)
    skip = skip_ref[...]
    conv = conv_ref[...] + on(2, late) + on(shards - 1, part)
    corr = corr_ref[...] + on(1, late) + on(0, part)
    grad_two_ref[...] = (out * (conv + skip * (one * val))).astype(bf16)
    mid = corr + skip * (out * two_ref[...].astype(f32))
    grad_one_ref[...] = (mid * val).astype(bf16)
    grad_value_ref[...] = (mid * one).astype(bf16)


def finish_kernel(
    channels, shards, rank_ref, own_ref, come_ref, first_ref, first_come_ref, second_out, first_out, bias_out, second,
    first, bias, sems,
):
    rank = rank_ref[0]
    inner = jnp.logical_and(rank > 0, rank < shards - 1)
    lanes = channels // 128
    copies = [
        pltpu.make_async_copy(held, out, sems.at[i])
        for i, (held, out) in enumerate(((second, second_out), (first, first_out), (bias, bias_out)))
    ]
    picked = jnp.where(inner, own_ref[...], come_ref[...])
    second[...] = picked[:, :channels].astype(f32)
    copies[0].start()
    first[...] = jnp.where(inner, first_ref[...], first_come_ref[...])
    copies[1].start()
    rows = get_side(picked, channels, lanes, first.shape[1])[0]
    for i in range(lanes):
        bias[:, i * 128 : (i + 1) * 128] = rows[i : i + 1]
    copies[2].start()
    for copy in copies:
        copy.wait()


def few_shards_body(
    x_one, x_two, values, grad_out, first_weight, second_weight, skip_bias, decay_rate
):
    rows, channels = x_one.shape
    shards = lax.axis_size("ctx")
    feat_count, hid_count = first_weight.shape
    seq_len = rows * shards
    double = 2 * rows
    width = min(512, channels)
    blocks = channels // width
    rank = lax.axis_index("ctx").astype(jnp.int32).reshape(1)
    front, back = block_tables(rows)
    feats = feature_table(seq_len)
    featt = np.ascontiguousarray(feats.T)
    skip_row = skip_bias.reshape(1, channels)
    rate_row = decay_rate.reshape(1, channels)
    smem = pl.BlockSpec(memory_space=pltpu.SMEM)
    vmem = pl.BlockSpec(memory_space=pltpu.VMEM)
    anywhere = pl.BlockSpec(memory_space=pl.ANY)
    mebi = 1024 * 1024

    def shape(*dims, dtype=f32):
        return jax.ShapeDtypeStruct(dims, dtype)

    def call(kernel, name, units, out_shape, in_specs, out_specs=None, scratch=(), limit=16, aliases={}):
        return pl.pallas_call(
            kernel,
            in_specs=in_specs,
            out_specs=out_specs if out_specs is not None else [vmem] * len(out_shape),
            out_shape=out_shape,
            scratch_shapes=scratch,
            input_output_aliases=aliases,
            compiler_params=pltpu.CompilerParams(vmem_limit_bytes=limit * mebi),
            cost_estimate=pl.CostEstimate(
                flops=2 * units * double * double * channels, bytes_accessed=rows * channels, transcendentals=0
            ),
            name=name,
        )

    def move(array, pairs):
        return lax.ppermute(array, "ctx", pairs)

    inward = [(0, 1), (shards - 1, shards - 2)]
    outward = [(1, 0), (shards - 2, shards - 1)]
    across = [(1, 2), (2, 1)]
    pay_shape = (hid_count, channels + SIDE)
    block_bf16 = shape(rows, channels, dtype=bf16)
    block_f32 = shape(rows, channels)

    row_step = max(rows // 2, 16)
    gate_rows = pl.BlockSpec((row_step, channels), lambda i: (i, 0))
    pair, other, edge, bias = pl.pallas_call(
        products_kernel,
        grid=(rows // row_step,),
        in_specs=[smem] + [gate_rows] * 4,
        out_specs=[gate_rows] * 3 + [pl.BlockSpec((1, channels), lambda i: (0, 0))],
        out_shape=[block_bf16] * 3 + [shape(1, channels)],
        compiler_params=pltpu.CompilerParams(vmem_limit_bytes=64 * mebi),
        name="products",
    )(rank, x_one, x_two, values, grad_out)
    pair_in = move(pair, inward + outward)
    middle_in = move(other, across)

    own_shapes = [
        shape(rows, feat_count), shape(feat_count, hid_count), block_bf16, block_bf16, shape(hid_count, channels),
        shape(1, channels), shape(double, double, dtype=bf16), shape(double, double, dtype=bf16),
        shape(feat_count, seq_len), shape(1, channels), shape(*pay_shape, dtype=bf16),
    ]
    (send,) = call(
        only(False, shards, 0, functools.partial(own_kernel, rows, shards, channels, blocks, width)), "own_pair", 8,
        [shape(*pay_shape, dtype=bf16)],
        [smem] + [anywhere] * 10,
        out_specs=[anywhere],
        scratch=[pltpu.VMEM(s.shape, s.dtype) for s in own_shapes]
        + [
            pltpu.VMEM((2 * hid_count, rows), bf16), pltpu.VMEM((rows, hid_count), f32),
            pltpu.SemaphoreType.DMA((10,)), pltpu.SemaphoreType.DMA,
        ],
        limit=60,
    )(rank, feats[:rows], first_weight, pair, other, second_weight, rate_row, front, back, featt, bias)
    edge, _ = lax.optimization_barrier((edge, send))
    far = move(edge, [(0, 2), (shards - 1, shards - 3)])

    spec, trans, slope = call(
        functools.partial(filters_kernel, rows, shards, blocks, width), "filters", 8,
        [
            shape(shards, double, channels, dtype=bf16), shape(2 * hid_count, seq_len, dtype=bf16),
            shape(seq_len, hid_count),
        ],
        [vmem] * 5,
        scratch=[pltpu.VMEM((seq_len, 3 * hid_count), bf16)],
    )(feats, first_weight, second_weight, rate_row, front)

    send, _ = lax.optimization_barrier((send, slope))
    come = move(send, inward)

    conv, corr, ahead, sums, first = call(
        functools.partial(near_kernel, rows, shards, blocks, width), "near_blocks", 20,
        [block_f32] * 3 + [shape(hid_count, channels), shape(feat_count, hid_count)],
        [smem] + [vmem] * 12,
        scratch=[
            pltpu.VMEM((4, double, width), f32),
            pltpu.VMEM((3, double, width), bf16),
            pltpu.VMEM((shards - 1, double, width), bf16),
            pltpu.VMEM((shards - 1, double, width), bf16),
            pltpu.VMEM(((shards - 1) * rows, hid_count), f32),
        ],
    )(rank, pair, other, pair_in, middle_in, spec, second_weight, rate_row, front, back, trans, featt, slope)

    part, late = call(
        only(
            True, shards, 0,
            looped(
                functools.partial(far_kernel, rows),
                (None, ROWS, (slice(2, 4), slice(None)), None, None, ROWS, ROWS, ROWS),
                blocks, width,
            ),
        ),
        "far_block", 1,
        [block_bf16, block_f32],
        [smem] + [vmem] * 5,
    )(rank, far, spec, front, back, ahead)
    part_come = move(part, outward)

    pay, first = call(
        only(
            True, shards, 1,
            looped(
                functools.partial(last_kernel, rows, shards, channels),
                (None, None, ROWS, ROWS, ROWS, ROWS, None, None, None, None, None, ROWS),
                blocks, width,
            ),
        ),
        "last_pair", 1,
        [shape(*pay_shape, dtype=bf16), shape(feat_count, hid_count)],
        [anywhere, smem] + [vmem] * 13,
        scratch=[pltpu.VMEM((2 * rows, hid_count), f32)],
    )(late, rank, pair_in, far, second_weight, rate_row, front, back, trans, featt, slope, sums, first, bias, come)
    pay_come = move(pay, across)
    group = lax.axis_size(("ch", "sub"))
    bit = 1
    while bit < group:
        first = first + lax.ppermute(first, ("ch", "sub"), [(i, i ^ bit) for i in range(group)])
        bit *= 2

    (total,) = call(
        functools.partial(total_kernel, channels, hid_count), "total", 0,
        [shape(*pay_shape, dtype=bf16)],
        [anywhere] * 2 + [vmem] * 2,
    )(part_come, first, pay, pay_come)
    total_come = move(total, outward)
    first = first + move(first, across)
    first_come = move(first, outward)

    grad_one, grad_two, grad_value = call(
        looped(
            functools.partial(gates_kernel, shards), (None,) + (ROWS,) * 12, blocks, width
        ),
        "gates", 0,
        [block_bf16] * 3,
        [smem] + [vmem] * 9,
    )(rank, x_one, x_two, values, grad_out, skip_row, conv, corr, late, part_come)

    outs = [shape(hid_count, channels), shape(feat_count, hid_count), shape(1, channels)]
    grad_second, grad_first, grad_bias = call(
        functools.partial(finish_kernel, channels, shards), "finish", 0,
        outs,
        [smem] + [vmem] * 4,
        out_specs=[anywhere] * 3,
        scratch=[pltpu.VMEM(o.shape, f32) for o in outs] + [pltpu.SemaphoreType.DMA((3,))],
    )(rank, total, total_come, first, first_come)
    return (grad_one, grad_two, grad_value, grad_first, grad_second, grad_bias.reshape(channels))


def solution(mesh):
    in_specs = (
        P(("parts", "ctx"), ("ch", "sub")),
        P(("parts", "ctx"), ("ch", "sub")),
        P(("parts", "ctx"), ("ch", "sub")),
        P(("parts", "ctx"), ("ch", "sub")),
        P(),
        P(None, ("ch", "sub")),
        P(("ch", "sub")),
        P(("ch", "sub")),
    )
    out_specs = (
        P(("parts", "ctx"), ("ch", "sub")),
        P(("parts", "ctx"), ("ch", "sub")),
        P(("parts", "ctx"), ("ch", "sub")),
        P("parts", None),
        P("parts", ("ch", "sub")),
        P(("parts", "ch", "sub")),
    )
    body = few_shards_body if mesh.shape["ctx"] == 4 else many_shards_body
    return jax.shard_map(body, mesh=mesh, in_specs=in_specs, out_specs=out_specs, check_vma=False)
```

```python
import functools
import math

import jax
import jax.numpy as jnp
import numpy as np
from jax import lax
from jax.experimental import pallas as pl
from jax.experimental.pallas import tpu as pltpu
from jax.sharding import PartitionSpec as P

band_steps = (1763, 1201, 811, 547, 367, 251, 167, 113, 79, 53, 37, 23, 17, 11, 7, 3)
highest = lax.Precision.HIGHEST
f32 = jnp.float32
bf16 = jnp.bfloat16


def features(positions):
    multiplier = jnp.array(band_steps, dtype=jnp.int32)
    phase = positions[:, None] * multiplier[None, :] % 4096
    angle = phase.astype(jnp.float32) * (2.0 * math.pi / 4096.0)
    return jnp.concatenate([jnp.cos(angle), jnp.sin(angle)], axis=1)


def tables(out_count, in_count, modulus, sign_value):
    row_index = lax.broadcasted_iota(jnp.int32, (out_count, in_count), 0)
    col_index = lax.broadcasted_iota(jnp.int32, (out_count, in_count), 1)
    angle = (row_index * col_index % modulus).astype(jnp.float32) * (2.0 * math.pi / modulus)
    return (jnp.cos(angle), sign_value * jnp.sin(angle))


def twiddle(spec_re, spec_im, freq_count, span, modulus, sign_value):
    freq_index = lax.broadcasted_iota(jnp.int32, (freq_count, span), 0)
    pos_index = lax.broadcasted_iota(jnp.int32, (freq_count, span), 1)
    angle = (freq_index * pos_index % modulus).astype(jnp.float32) * (2.0 * math.pi / modulus)
    factor_re = jnp.cos(angle)[None, None, :, :]
    factor_im = (sign_value * jnp.sin(angle))[None, None, :, :]
    return (spec_re * factor_re - spec_im * factor_im, spec_re * factor_im + spec_im * factor_re)


def contract(kernel, array):
    return jnp.einsum(
        "lj,mckj->mckl", kernel, array, precision=highest, preferred_element_type=jnp.float32
    )


def along_positions(spec_re, spec_im, kernel_re, kernel_im):
    return (
        contract(kernel_re, spec_re) - contract(kernel_im, spec_im),
        contract(kernel_re, spec_im) + contract(kernel_im, spec_re),
    )


def many_shards_body(
    x_one, x_two, values, grad_out, first_weight, second_weight, skip_bias, decay_rate
):
    row_count, chan_count = x_one.shape
    shards = lax.axis_size("ctx")
    rank = lax.axis_index("ctx")
    seq_len = row_count * shards
    total = 2 * seq_len
    narrow = chan_count // shards
    chan_weight = lax.dynamic_slice_in_dim(second_weight, rank * narrow, narrow, 1)
    chan_rate = lax.dynamic_slice_in_dim(decay_rate, rank * narrow, narrow, 0)
    source = x_one.astype(jnp.float32) * values.astype(jnp.float32)
    cotan = grad_out.astype(jnp.float32) * x_two.astype(jnp.float32)
    spread = lax.all_to_all(
        jnp.stack([source.T, cotan.T])[:, :, None, :],
        "ctx",
        split_axis=1,
        concat_axis=2,
        tiled=True,
    )
    far_source = spread[0]
    far_cotan = spread[1]
    positions = jnp.arange(seq_len, dtype=jnp.int32)
    feats = features(positions)
    pre_act = jnp.dot(feats, first_weight, precision=highest, preferred_element_type=jnp.float32)
    hidden = jnp.sin(pre_act)
    envelope = jnp.exp(-chan_rate[:, None] * positions.astype(jnp.float32)[None, :]) * float(
        seq_len
    ) ** (-0.5)
    filt = (
        jnp.einsum(
            "th,hc->ct", hidden, chan_weight, precision=highest, preferred_element_type=jnp.float32
        )
        * envelope
    )
    filt_blocks = filt.reshape(narrow, shards, row_count)
    fields = jnp.stack([far_source, far_cotan])

    def first_section(kernel):
        field_part = jnp.einsum(
            "kn,mcnj->mckj", kernel, fields, precision=highest, preferred_element_type=jnp.float32
        )
        filter_part = jnp.einsum(
            "kn,cnj->ckj",
            kernel,
            filt_blocks,
            precision=highest,
            preferred_element_type=jnp.float32,
        )
        return jnp.concatenate([field_part, filter_part[None]], axis=0)

    first_re, first_im = tables(2 * shards, shards, 2 * shards, -1.0)
    spec_re, spec_im = (first_section(first_re), first_section(first_im))
    spec_re, spec_im = twiddle(spec_re, spec_im, 2 * shards, row_count, total, -1.0)
    fwd_re, fwd_im = tables(row_count, row_count, row_count, -1.0)
    spec_re, spec_im = along_positions(spec_re, spec_im, fwd_re, fwd_im)
    source_re, source_im = (spec_re[0], spec_im[0])
    cotan_re, cotan_im = (spec_re[1], spec_im[1])
    filter_re, filter_im = (spec_re[2], spec_im[2])
    prod_re = jnp.stack(
        [
            source_re * filter_re - source_im * filter_im,
            cotan_re * filter_re + cotan_im * filter_im,
            cotan_re * source_re + cotan_im * source_im,
        ]
    )
    prod_im = jnp.stack(
        [
            source_re * filter_im + source_im * filter_re,
            cotan_im * filter_re - cotan_re * filter_im,
            cotan_im * source_re - cotan_re * source_im,
        ]
    )
    back_re, back_im = tables(row_count, row_count, row_count, 1.0)
    prod_re, prod_im = along_positions(prod_re, prod_im, back_re, back_im)
    prod_re, prod_im = twiddle(prod_re, prod_im, 2 * shards, row_count, total, 1.0)
    last_re, last_im = tables(shards, 2 * shards, 2 * shards, 1.0)
    field_out = jnp.einsum(
        "nk,mckj->mcnj", last_re, prod_re[:2], precision=highest, preferred_element_type=jnp.float32
    ) - jnp.einsum(
        "nk,mckj->mcnj", last_im, prod_im[:2], precision=highest, preferred_element_type=jnp.float32
    )
    field_out = field_out * (1.0 / total)
    filt_grad = jnp.einsum(
        "nk,ckj->cnj", last_re, prod_re[2], precision=highest, preferred_element_type=jnp.float32
    ) - jnp.einsum(
        "nk,ckj->cnj", last_im, prod_im[2], precision=highest, preferred_element_type=jnp.float32
    )
    filt_grad = (filt_grad * (1.0 / total)).reshape(narrow, seq_len)
    modulated = filt_grad * envelope
    weight_part = jnp.einsum(
        "th,ct->hc", hidden, modulated, precision=highest, preferred_element_type=jnp.float32
    )
    hidden_grad = jnp.einsum(
        "ct,hc->th", modulated, chan_weight, precision=highest, preferred_element_type=jnp.float32
    )
    first_part = jnp.dot(
        feats.T,
        hidden_grad * jnp.cos(pre_act),
        precision=highest,
        preferred_element_type=jnp.float32,
    )
    grad_first = lax.psum(first_part, ("ctx", "ch", "sub"))
    returned = lax.all_to_all(
        field_out.astype(jnp.bfloat16), "ctx", split_axis=2, concat_axis=1, tiled=True
    ).astype(field_out.dtype)
    conv_part = returned[0, :, 0, :].T
    corr_part = returned[1, :, 0, :].T
    grad_two = (grad_out.astype(jnp.float32) * (conv_part + skip_bias[None, :] * source)).astype(
        jnp.bfloat16
    )
    grad_mid = corr_part + skip_bias[None, :] * cotan
    grad_one = (grad_mid * values.astype(jnp.float32)).astype(jnp.bfloat16)
    grad_value = (grad_mid * x_one.astype(jnp.float32)).astype(jnp.bfloat16)
    grad_bias = lax.psum(jnp.sum(source * cotan, axis=0), "ctx")
    grad_second = lax.all_gather(weight_part, "ctx", axis=1, tiled=True)
    return (grad_one, grad_two, grad_value, grad_first, grad_second, grad_bias)


STEP = 16
SIDE = 256


def halves(array):
    array = np.asarray(array, np.float32)
    high = array.astype(bf16)
    low = (array - high.astype(np.float32)).astype(bf16)
    return high, low


def block_tables(rows):
    freq = np.concatenate([np.arange(0, rows, 2), np.arange(1, rows, 2)])
    phase = (2 * freq + 1)[:, None] * np.arange(rows)[None, :] % (4 * rows)
    angle = phase * (2.0 * np.pi / (4 * rows))
    forward = np.concatenate([np.cos(angle), -np.sin(angle)], axis=0)
    front = np.ascontiguousarray(np.concatenate(halves(forward), axis=1))
    back = np.ascontiguousarray(np.concatenate(halves(forward.T / rows), axis=0))
    return front, back


def feature_table(seq_len):
    phase = np.arange(seq_len)[:, None] * np.array(band_steps)[None, :] % 4096
    angle = phase * (2.0 * np.pi / 4096.0)
    return np.concatenate([np.cos(angle), np.sin(angle)], axis=1).astype(np.float32)


def split(array):
    high = array.astype(bf16)
    return high, (array - high.astype(f32)).astype(bf16)


def dot(left, right):
    return jnp.dot(left, right, preferred_element_type=f32)


def exact_dot(left, right):
    return jnp.dot(left, right, precision=highest, preferred_element_type=f32)


def dot_across(left, right):
    return lax.dot_general(left, right, (((1,), (1,)), ((), ())), preferred_element_type=f32)


def decay(rate, rows, scale):
    place = lax.broadcasted_iota(jnp.int32, (rows, rate.shape[1]), 0)
    return jnp.exp(-place.astype(f32) * rate) * scale


def times(a, b):
    return a[0] * b[0] - a[1] * b[1], a[0] * b[1] + a[1] * b[0]


def conj_times(a, b):
    return a[0] * b[0] + a[1] * b[1], a[0] * b[1] - a[1] * b[0]


def plus(a, b):
    return a[0] + b[0], a[1] + b[1]


def scaled(a, factor):
    return a[0] * factor, a[1] * factor


def choose(condition, a, b):
    return jnp.where(condition, a[0], b[0]), jnp.where(condition, a[1], b[1])


def turned(a, sign):
    return (a[1], -a[0]) if sign > 0 else (-a[1], a[0])


def forward(front_ref, block):
    return dot(front_ref[...], jnp.concatenate([block, block], axis=0))


def backward(back_ref, high, low=None):
    both = dot(back_ref[...], high)
    rows = both.shape[0] // 2
    out = both[:rows] + both[rows:]
    return out if low is None else out + dot(back_ref[:rows], low)


def row_groups(rows):
    for step in range(rows // STEP):
        sign = 1 if step * STEP < rows // 2 else -1
        yield slice(step * STEP, (step + 1) * STEP), slice(rows + step * STEP, rows + (step + 1) * STEP), sign


def weight_sums(trans, m_high, m_low):
    both = dot(trans, m_high)
    count = both.shape[0] // 2
    return both[:count] + both[count:] + dot(trans[:count], m_low)


def hidden_sums(m_high, m_low, w_high, w_low):
    left = jnp.concatenate([m_high, m_high, m_low], axis=1)
    right = jnp.concatenate([w_high, w_low, w_high], axis=1)
    return dot_across(left, right)


def looped(kernel, kinds, blocks, width):
    def over_strips(*refs):
        def step(block, carry):
            cols = pl.ds(pl.multiple_of(block * width, width), width)
            views = [
                ref if kind is None else ref.at[(*kind, cols)]
                for ref, kind in zip(refs, kinds + (None,) * (len(refs) - len(kinds)))
            ]
            kernel(block, blocks, *views)
            return carry

        lax.fori_loop(0, blocks, step, 0)

    return over_strips


ROWS = (slice(None),)
CUBE = (slice(None), slice(None))


def products_kernel(rank_ref, one_ref, two_ref, val_ref, out_ref, pair_ref, other_ref, edge_ref, bias_ref):
    source = one_ref[...].astype(f32) * val_ref[...].astype(f32)
    cotan = out_ref[...].astype(f32) * two_ref[...].astype(f32)
    even = rank_ref[0] % 2 == 0
    pair_ref[...] = jnp.where(even, source, cotan).astype(bf16)
    edge_ref[...] = pair_ref[...]
    other_ref[...] = jnp.where(even, cotan, source).astype(bf16)
    part = jnp.sum(source * cotan, axis=0, keepdims=True)

    @pl.when(pl.program_id(0) == 0)
    def _():
        bias_ref[...] = part

    @pl.when(pl.program_id(0) > 0)
    def _():
        bias_ref[...] += part


def ordered(first, a, b):
    return (jnp.where(first, a, b), jnp.where(first, b, a))


def sin_cos(angle):
    turns = jnp.floor(angle * (2.0 / math.pi) + 0.5)
    rest = ((angle - turns * 1.5703125) - turns * 4.837512969970703e-4) - turns * 7.54978995489188e-8
    square = rest * rest
    sine = rest + rest * square * (
        -1.6666654611e-1 + square * (8.3321608736e-3 + square * -1.9515295891e-4)
    )
    cosine = 1.0 - 0.5 * square + square * square * (
        4.166664568298827e-2 + square * (-1.388731625493765e-3 + square * 2.443315711809948e-5)
    )
    quarter = turns.astype(jnp.int32)
    odd = (quarter & 1) == 1
    sin_sign = jnp.where((quarter & 2) == 2, -1.0, 1.0).astype(f32)
    cos_sign = jnp.where(((quarter + 1) & 2) == 2, -1.0, 1.0).astype(f32)
    return jnp.where(odd, cosine, sine) * sin_sign, jnp.where(odd, sine, cosine) * cos_sign


def turned_over(hidden, slope):
    both = jnp.concatenate([hidden, slope], axis=1).T
    return jnp.concatenate(split(both[: hidden.shape[1]]), axis=0)


def filters_kernel(
    rows, shards, blocks, width, feats_ref, first_ref, weight_ref, rate_ref, front_ref, spec_ref, trans_ref, slope_ref,
    hid_ref,
):
    hidden, slope = sin_cos(exact_dot(feats_ref[...], first_ref[...]))
    slope_ref[...] = slope
    high, low = split(hidden)
    hid_ref[...] = jnp.concatenate([high, high, low], axis=1)
    trans_ref[...] = turned_over(hidden, slope)
    strips = looped(
        functools.partial(filter_strip, rows, shards), (None, ROWS, ROWS, None, CUBE), blocks, width
    )
    strips(hid_ref, weight_ref, rate_ref, front_ref, spec_ref)


def filter_strip(rows, shards, block, blocks, hid_ref, weight_ref, rate_ref, front_ref, spec_ref):
    scale = float(rows * shards) ** -0.5
    w_high, w_low = split(weight_ref[...])
    stacked = jnp.concatenate([w_high, w_low, w_high], axis=0)
    rate = rate_ref[...]
    env = decay(rate, rows, scale)
    before = None
    for lag in range(shards):
        part = dot(hid_ref[lag * rows : (lag + 1) * rows, :], stacked)
        part = part * (env * jnp.exp(rate * (-float(lag * rows))))
        f_high, f_low = split(part)
        now = forward(front_ref, f_high) + dot(front_ref[:, :rows], f_low)
        for re, im, sign in row_groups(rows):
            here = (now[re], now[im])
            if before is not None:
                here = plus(here, turned((before[re], before[im]), -sign))
            spec_ref[lag, re, :] = here[0].astype(bf16)
            spec_ref[lag, im, :] = here[1].astype(bf16)
        before = now


def own_kernel(rows, shards, channels, blocks, width, rank_ref, *refs):
    inputs, send_out, held = refs[:10], refs[10], refs[11:21]
    send_ref, trans_ref, acc_ref, sems, out_sem = refs[21:]
    (
        feats_ref, first_ref, pair_ref, other_ref, weight_ref, rate_ref, front_ref, back_ref, featt_ref, bias_ref
    ) = held
    copies = [pltpu.make_async_copy(far, near, sems.at[i]) for i, (far, near) in enumerate(zip(inputs, held))]
    for copy in copies:
        copy.start()
    acc_ref[...] = jnp.zeros_like(acc_ref)
    copies[0].wait()
    copies[1].wait()
    hidden, slope = sin_cos(exact_dot(feats_ref[...], first_ref[...]))
    trans_ref[...] = turned_over(hidden, slope)
    for copy in copies[2:]:
        copy.wait()
    kinds = (None, ROWS, ROWS, ROWS, ROWS, None, None, None, ROWS, None)
    looped(functools.partial(own_strip, rows, shards), kinds, blocks, width)(
        rank_ref, pair_ref, other_ref, weight_ref, rate_ref, front_ref, back_ref, trans_ref, send_ref, acc_ref
    )
    first = exact_dot(featt_ref[:, :rows], acc_ref[...] * slope)
    put_side(send_ref, channels, fold(bias_ref[...]), first)
    last = pltpu.make_async_copy(send_ref, send_out, out_sem)
    last.start()
    last.wait()


def own_strip(
    rows, shards, block, blocks, rank_ref, pair_ref, other_ref, weight_ref, rate_ref, front_ref, back_ref, trans_ref,
    send_ref, acc_ref,
):
    source, cotan = ordered(rank_ref[0] % 2 == 0, pair_ref[...], other_ref[...])
    x0 = forward(front_ref, source)
    c0 = forward(front_ref, cotan)
    pair = conj_times((x0[:rows], x0[rows:]), (c0[:rows], c0[rows:]))
    high, low = split(jnp.concatenate(pair, axis=0))
    env = decay(rate_ref[...], rows, float(rows * shards) ** -0.5)
    m_high, m_low = split(backward(back_ref, high, low) * env)
    send_ref[...] = weight_sums(trans_ref[...], m_high, m_low).astype(bf16)
    acc_ref[...] += hidden_sums(m_high, m_low, *split(weight_ref[...]))


def fold(bias):
    return jnp.concatenate([bias[:, i * 128 : (i + 1) * 128] for i in range(bias.shape[1] // 128)], axis=0)


def put_side(pay_ref, channels, bias, first=None):
    half = pay_ref.shape[0] // 2
    pay_ref[:, channels:] = jnp.zeros((2 * half, SIDE), bf16)
    for start, part in zip((0, 128), split(bias)):
        pay_ref[: bias.shape[0], channels + start : channels + start + 128] = part
    if first is not None:
        for start, part in zip((0, 128), split(first)):
            pay_ref[half:, channels + start : channels + start + first.shape[1]] = part


def get_side(pay, channels, lanes, hid_count):
    half = pay.shape[0] // 2
    side = pay[:, channels : channels + 128].astype(f32) + pay[:, channels + 128 :].astype(f32)
    return side[:lanes], side[half:, :hid_count]


def near_kernel(
    rows, shards, blocks, width, rank_ref, pair_ref, other_ref, pair_in_ref, middle_in_ref, spec_ref, weight_ref,
    rate_ref, front_ref, back_ref, trans_ref, featt_ref, slope_ref, conv_ref, corr_ref, ahead_ref, sums_ref, first_ref,
    fields, fast, high_ref, low_ref, acc_ref,
):
    rank = rank_ref[0]
    inner = jnp.logical_and(rank > 0, rank < shards - 1)
    count = shards - 1
    kinds = (None, None, None) + (ROWS,) * 4 + (CUBE, ROWS, ROWS)
    common = (
        rank_ref, front_ref, back_ref, pair_ref, other_ref, pair_in_ref, middle_in_ref, spec_ref, conv_ref, corr_ref,
        fields, fast,
    )

    @pl.when(jnp.logical_not(inner))
    def _():
        looped(functools.partial(edge_strip, rows, shards), kinds, blocks, width)(*common)

    @pl.when(inner)
    def _():
        acc_ref[...] = jnp.zeros_like(acc_ref)
        looped(
            functools.partial(inner_strip, rows, shards), kinds + (None, None, None) + (ROWS,) * 4, blocks, width
        )(*common, trans_ref, weight_ref, rate_ref, ahead_ref, sums_ref, high_ref, low_ref, acc_ref)
        first_ref[...] = exact_dot(
            featt_ref[:, : count * rows], acc_ref[...] * slope_ref[: count * rows, :]
        )


def edge_strip(
    rows, shards, block, blocks, rank_ref, front_ref, back_ref, pair_ref, other_ref, pair_in_ref, middle_in_ref,
    spec_ref, conv_ref, corr_ref, fields, fast,
):
    del middle_in_ref
    top = rank_ref[0] == shards - 1
    source, cotan = ordered(rank_ref[0] % 2 == 0, pair_ref[...], other_ref[...])
    for index, block_in in enumerate((source, cotan, pair_in_ref[...])):
        fields[index] = forward(front_ref, block_in)
    on_conv = jnp.where(top, 1.0, 0.0).astype(f32)
    on_corr = jnp.where(top, 0.0, 1.0).astype(f32)
    for re, im, sign in row_groups(rows):
        x0, c0, near = ((fields[i, re, :], fields[i, im, :]) for i in range(3))
        w0, w1 = ((spec_ref[i, re, :].astype(f32), spec_ref[i, im, :].astype(f32)) for i in range(2))
        values = (
            plus(times(w0, x0), scaled(times(w1, near), on_conv)),
            plus(conj_times(w0, c0), scaled(conj_times(w1, near), on_corr)),
        )
        for index, value in enumerate(values):
            fast[index, re, :] = value[0].astype(bf16)
            fast[index, im, :] = value[1].astype(bf16)
    conv_ref[...] = backward(back_ref, fast[0])
    corr_ref[...] = backward(back_ref, fast[1])


def inner_strip(
    rows, shards, block, blocks, rank_ref, front_ref, back_ref, pair_ref, other_ref, pair_in_ref, middle_in_ref,
    spec_ref, conv_ref, corr_ref, fields, fast, trans_ref, weight_ref, rate_ref, ahead_ref, sums_ref, high_ref, low_ref,
    acc_ref,
):
    lower = rank_ref[0] == 1
    upper = jnp.where(lower, 0.0, 1.0).astype(f32)
    side = jnp.where(lower, -1.0, 1.0).astype(f32)
    count = shards - 1
    blocks_in = (
        *ordered(lower, other_ref[...], pair_ref[...]), *ordered(lower, pair_in_ref[...], middle_in_ref[...])
    )
    for index, block_in in enumerate(blocks_in):
        fields[index] = forward(front_ref, block_in)
    for re, im, sign in row_groups(rows):
        x0, c0, x1, c1 = ((fields[i, re, :], fields[i, im, :]) for i in range(4))
        w0, w1, w2 = ((spec_ref[i, re, :].astype(f32), spec_ref[i, im, :].astype(f32)) for i in range(3))
        values = (
            plus(times(w0, x0), times(w1, x1)),
            plus(conj_times(w0, c0), conj_times(w1, c1)),
            times((w2[0], w2[1] * side), choose(lower, c1, x1)),
        )
        for index, value in enumerate(values):
            fast[index, re, :] = value[0].astype(bf16)
            fast[index, im, :] = value[1].astype(bf16)
        zero = conj_times(x0, c0)
        one = plus(conj_times(x1, c0), scaled(conj_times(x0, c1), upper))
        two = conj_times(x1, c1)
        for index, value in enumerate((plus(zero, turned(one, sign)), plus(one, turned(two, sign)), two)):
            for part, where in zip(value, (re, im)):
                high_ref[index, where, :], low_ref[index, where, :] = split(part)
    conv_ref[...] = backward(back_ref, fast[0])
    corr_ref[...] = backward(back_ref, fast[1])
    ahead_ref[...] = backward(back_ref, fast[2])
    rate = rate_ref[...]
    env = decay(rate, rows, float(rows * shards) ** -0.5)
    parts = []
    for lag in range(count):
        grad = backward(back_ref, high_ref[lag], low_ref[lag])
        parts.append(split(grad * (env * jnp.exp(rate * (-float(lag * rows))))))
    m_high = jnp.concatenate([p[0] for p in parts], axis=0)
    m_low = jnp.concatenate([p[1] for p in parts], axis=0)
    sums_ref[...] = weight_sums(trans_ref[:, : count * rows], m_high, m_low)
    acc_ref[...] += hidden_sums(m_high, m_low, *split(weight_ref[...]))


def only(inner, shards, rank_at, kernel):
    def run(*refs):
        rank = refs[rank_at][0]

        @pl.when(jnp.logical_and(rank > 0, rank < shards - 1) == inner)
        def _():
            kernel(*refs)

    return run


def far_kernel(rows, block, blocks, rank_ref, far_ref, spec_ref, front_ref, back_ref, ahead_ref, part_ref, late_ref):
    side = jnp.where(rank_ref[0] == 2, 1.0, -1.0).astype(f32)
    far = forward(front_ref, far_ref[...])
    far = (far[:rows], far[rows:])
    w2, w3 = ((spec_ref[i, :rows, :].astype(f32), spec_ref[i, rows:, :].astype(f32) * side) for i in range(2))
    ahead = jnp.concatenate(times(w3, far), axis=0).astype(bf16)
    part_ref[...] = (ahead_ref[...] + backward(back_ref, ahead)).astype(bf16)
    late = jnp.concatenate(times(w2, far), axis=0).astype(bf16)
    late_ref[...] = backward(back_ref, late)


def last_kernel(
    rows, shards, channels, block, blocks, after_ref, rank_ref, near_ref, far_ref, weight_ref, rate_ref, front_ref, back_ref,
    trans_ref, featt_ref, slope_ref, sums_ref, first_ref, bias_ref, in_ref, pay_ref, total_ref, acc_ref,
):
    del after_ref
    hid_count, width = weight_ref.shape
    lower = rank_ref[0] == 1
    start = pl.multiple_of(block * width, width)
    here = sums_ref[...] + in_ref[:, pl.ds(start, width)].astype(f32)
    mine = (block < blocks // 2) == lower

    @pl.when(block == 0)
    def _():
        acc_ref[...] = jnp.zeros_like(acc_ref)

    @pl.when(mine)
    def _():
        sign = jnp.where(lower, 1.0, -1.0).astype(f32)
        near = forward(front_ref, near_ref[...])
        far = forward(front_ref, far_ref[...])
        three = conj_times((near[:rows], near[rows:]), (far[:rows], far[rows:]))
        three = (three[0], three[1] * sign)
        half = rows // 2
        two = jnp.concatenate([three[1][:half], -three[1][half:], -three[0][:half], three[0][half:]], axis=0)
        rate = rate_ref[...]
        env = decay(rate, rows, float(rows * shards) ** -0.5)
        parts = []
        for lag, value in ((shards - 2, two), (shards - 1, jnp.concatenate(three, axis=0))):
            grad = backward(back_ref, *split(value))
            parts.append(split(grad * (env * jnp.exp(rate * (-float(lag * rows))))))
        m_high = jnp.concatenate([p[0] for p in parts], axis=0)
        m_low = jnp.concatenate([p[1] for p in parts], axis=0)
        trans = trans_ref[:, (shards - 2) * rows :]
        pay_ref[:, pl.ds(start, width)] = (here + weight_sums(trans, m_high, m_low)).astype(bf16)
        w_high, w_low = split(weight_ref[...])
        acc_ref[...] += hidden_sums(m_high, m_low, w_high, w_low)

    @pl.when(jnp.logical_not(mine))
    def _():
        pay_ref[:, pl.ds(start, width)] = here.astype(bf16)

    @pl.when(block == blocks - 1)
    def _():
        first = exact_dot(
            featt_ref[:, (shards - 2) * rows :], acc_ref[...] * slope_ref[(shards - 2) * rows :, :]
        )
        lanes = channels // 128
        in_bias, in_first = get_side(in_ref[...], channels, lanes, hid_count)
        first = first + first_ref[...] + in_first
        put_side(pay_ref, channels, fold(bias_ref[...]) + in_bias)
        total_ref[...] = first


def total_kernel(channels, hid_count, part_ref, first_ref, own_ref, come_ref, pay_ref):
    del part_ref, first_ref
    lanes = channels // 128
    pay_ref[:, :channels] = (own_ref[:, :channels].astype(f32) + come_ref[:, :channels].astype(f32)).astype(bf16)
    own, come = (get_side(ref[...], channels, lanes, hid_count)[0] for ref in (own_ref, come_ref))
    put_side(pay_ref, channels, own + come)


def gates_kernel(
    shards, block, blocks, rank_ref, one_ref, two_ref, val_ref, out_ref, skip_ref, conv_ref, corr_ref, late_ref, part_ref,
    grad_one_ref, grad_two_ref, grad_value_ref,
):
    rank = rank_ref[0]

    def on(wanted, value):
        return jnp.where(rank == wanted, value, jnp.zeros_like(value))

    part = part_ref[...].astype(f32)
    late = late_ref[...]
    one = one_ref[...].astype(f32)
    val = val_ref[...].astype(f32)
    out = out_ref[...].astype(f32)
    skip = skip_ref[...]
    conv = conv_ref[...] + on(2, late) + on(shards - 1, part)
    corr = corr_ref[...] + on(1, late) + on(0, part)
    grad_two_ref[...] = (out * (conv + skip * (one * val))).astype(bf16)
    mid = corr + skip * (out * two_ref[...].astype(f32))
    grad_one_ref[...] = (mid * val).astype(bf16)
    grad_value_ref[...] = (mid * one).astype(bf16)


def finish_kernel(
    channels, shards, rank_ref, own_ref, come_ref, first_ref, first_come_ref, second_out, first_out, bias_out, second,
    first, bias, sems,
):
    rank = rank_ref[0]
    inner = jnp.logical_and(rank > 0, rank < shards - 1)
    lanes = channels // 128
    copies = [
        pltpu.make_async_copy(held, out, sems.at[i])
        for i, (held, out) in enumerate(((second, second_out), (first, first_out), (bias, bias_out)))
    ]
    picked = jnp.where(inner, own_ref[...], come_ref[...])
    second[...] = picked[:, :channels].astype(f32)
    copies[0].start()
    first[...] = jnp.where(inner, first_ref[...], first_come_ref[...])
    copies[1].start()
    rows = get_side(picked, channels, lanes, first.shape[1])[0]
    for i in range(lanes):
        bias[:, i * 128 : (i + 1) * 128] = rows[i : i + 1]
    copies[2].start()
    for copy in copies:
        copy.wait()


def few_shards_body(
    x_one, x_two, values, grad_out, first_weight, second_weight, skip_bias, decay_rate
):
    rows, channels = x_one.shape
    shards = lax.axis_size("ctx")
    feat_count, hid_count = first_weight.shape
    seq_len = rows * shards
    double = 2 * rows
    width = min(512, channels)
    blocks = channels // width
    rank = lax.axis_index("ctx").astype(jnp.int32).reshape(1)
    front, back = block_tables(rows)
    feats = feature_table(seq_len)
    featt = np.ascontiguousarray(feats.T)
    skip_row = skip_bias.reshape(1, channels)
    rate_row = decay_rate.reshape(1, channels)
    smem = pl.BlockSpec(memory_space=pltpu.SMEM)
    vmem = pl.BlockSpec(memory_space=pltpu.VMEM)
    anywhere = pl.BlockSpec(memory_space=pl.ANY)
    mebi = 1024 * 1024

    def shape(*dims, dtype=f32):
        return jax.ShapeDtypeStruct(dims, dtype)

    def call(kernel, name, units, out_shape, in_specs, out_specs=None, scratch=(), limit=16, aliases={}):
        return pl.pallas_call(
            kernel,
            in_specs=in_specs,
            out_specs=out_specs if out_specs is not None else [vmem] * len(out_shape),
            out_shape=out_shape,
            scratch_shapes=scratch,
            input_output_aliases=aliases,
            compiler_params=pltpu.CompilerParams(vmem_limit_bytes=limit * mebi),
            cost_estimate=pl.CostEstimate(
                flops=2 * units * double * double * channels, bytes_accessed=rows * channels, transcendentals=0
            ),
            name=name,
        )

    def move(array, pairs):
        return lax.ppermute(array, "ctx", pairs)

    inward = [(0, 1), (shards - 1, shards - 2)]
    outward = [(1, 0), (shards - 2, shards - 1)]
    across = [(1, 2), (2, 1)]
    pay_shape = (hid_count, channels + SIDE)
    block_bf16 = shape(rows, channels, dtype=bf16)
    block_f32 = shape(rows, channels)

    row_step = max(rows // 2, 16)
    gate_rows = pl.BlockSpec((row_step, channels), lambda i: (i, 0))
    pair, other, edge, bias = pl.pallas_call(
        products_kernel,
        grid=(rows // row_step,),
        in_specs=[smem] + [gate_rows] * 4,
        out_specs=[gate_rows] * 3 + [pl.BlockSpec((1, channels), lambda i: (0, 0))],
        out_shape=[block_bf16] * 3 + [shape(1, channels)],
        compiler_params=pltpu.CompilerParams(vmem_limit_bytes=64 * mebi),
        name="products",
    )(rank, x_one, x_two, values, grad_out)
    pair_in = move(pair, inward + outward)
    middle_in = move(other, across)

    own_shapes = [
        shape(rows, feat_count), shape(feat_count, hid_count), block_bf16, block_bf16, shape(hid_count, channels),
        shape(1, channels), shape(double, double, dtype=bf16), shape(double, double, dtype=bf16),
        shape(feat_count, seq_len), shape(1, channels), shape(*pay_shape, dtype=bf16),
    ]
    (send,) = call(
        only(False, shards, 0, functools.partial(own_kernel, rows, shards, channels, blocks, width)), "own_pair", 8,
        [shape(*pay_shape, dtype=bf16)],
        [smem] + [anywhere] * 10,
        out_specs=[anywhere],
        scratch=[pltpu.VMEM(s.shape, s.dtype) for s in own_shapes]
        + [
            pltpu.VMEM((2 * hid_count, rows), bf16), pltpu.VMEM((rows, hid_count), f32),
            pltpu.SemaphoreType.DMA((10,)), pltpu.SemaphoreType.DMA,
        ],
        limit=60,
    )(rank, feats[:rows], first_weight, pair, other, second_weight, rate_row, front, back, featt, bias)
    late_feats, _ = lax.optimization_barrier((jnp.asarray(feats), send))
    spec, trans, slope = call(
        functools.partial(filters_kernel, rows, shards, blocks, width), "filters", 8,
        [
            shape(shards, double, channels, dtype=bf16), shape(2 * hid_count, seq_len, dtype=bf16),
            shape(seq_len, hid_count),
        ],
        [vmem] * 5,
        scratch=[pltpu.VMEM((seq_len, 3 * hid_count), bf16)],
    )(late_feats, first_weight, second_weight, rate_row, front)

    edge, _ = lax.optimization_barrier((edge, slope))
    far = move(edge, [(0, 2), (shards - 1, shards - 3)])
    send, _ = lax.optimization_barrier((send, pair_in))
    come = move(send, inward)

    conv, corr, ahead, sums, first = call(
        functools.partial(near_kernel, rows, shards, blocks, width), "near_blocks", 20,
        [block_f32] * 3 + [shape(hid_count, channels), shape(feat_count, hid_count)],
        [smem] + [vmem] * 12,
        scratch=[
            pltpu.VMEM((4, double, width), f32),
            pltpu.VMEM((3, double, width), bf16),
            pltpu.VMEM((shards - 1, double, width), bf16),
            pltpu.VMEM((shards - 1, double, width), bf16),
            pltpu.VMEM(((shards - 1) * rows, hid_count), f32),
        ],
    )(rank, pair, other, pair_in, middle_in, spec, second_weight, rate_row, front, back, trans, featt, slope)

    part, late = call(
        only(
            True, shards, 0,
            looped(
                functools.partial(far_kernel, rows),
                (None, ROWS, (slice(2, 4), slice(None)), None, None, ROWS, ROWS, ROWS),
                blocks, width,
            ),
        ),
        "far_block", 1,
        [block_bf16, block_f32],
        [smem] + [vmem] * 5,
    )(rank, far, spec, front, back, ahead)
    part_come = move(part, outward)

    pay, first = call(
        only(
            True, shards, 1,
            looped(
                functools.partial(last_kernel, rows, shards, channels),
                (None, None, ROWS, ROWS, ROWS, ROWS, None, None, None, None, None, ROWS),
                blocks, width,
            ),
        ),
        "last_pair", 1,
        [shape(*pay_shape, dtype=bf16), shape(feat_count, hid_count)],
        [anywhere, smem] + [vmem] * 13,
        scratch=[pltpu.VMEM((2 * rows, hid_count), f32)],
    )(late, rank, pair_in, far, second_weight, rate_row, front, back, trans, featt, slope, sums, first, bias, come)
    pay_come = move(pay, across + [(0, 0), (shards - 1, shards - 1)])
    group = lax.axis_size(("ch", "sub"))
    bit = 1
    while bit < group:
        first = first + lax.ppermute(first, ("ch", "sub"), [(i, i ^ bit) for i in range(group)])
        bit *= 2

    (total,) = call(
        functools.partial(total_kernel, channels, hid_count), "total", 0,
        [shape(*pay_shape, dtype=bf16)],
        [anywhere] * 2 + [vmem] * 2,
    )(part_come, first, pay, pay_come)
    total_come = move(total, inward + outward)
    first = first + move(first, [(i, shards - 1 - i) for i in range(shards)])
    first_come = move(first, inward + outward)

    grad_one, grad_two, grad_value = call(
        looped(
            functools.partial(gates_kernel, shards), (None,) + (ROWS,) * 12, blocks, width
        ),
        "gates", 0,
        [block_bf16] * 3,
        [smem] + [vmem] * 9,
    )(rank, x_one, x_two, values, grad_out, skip_row, conv, corr, late, part_come)

    outs = [shape(hid_count, channels), shape(feat_count, hid_count), shape(1, channels)]
    grad_second, grad_first, grad_bias = call(
        functools.partial(finish_kernel, channels, shards), "finish", 0,
        outs,
        [smem] + [vmem] * 4,
        out_specs=[anywhere] * 3,
        scratch=[pltpu.VMEM(o.shape, f32) for o in outs] + [pltpu.SemaphoreType.DMA((3,))],
    )(rank, total, total_come, first, first_come)
    return (grad_one, grad_two, grad_value, grad_first, grad_second, grad_bias.reshape(channels))


def solution(mesh):
    in_specs = (
        P(("parts", "ctx"), ("ch", "sub")),
        P(("parts", "ctx"), ("ch", "sub")),
        P(("parts", "ctx"), ("ch", "sub")),
        P(("parts", "ctx"), ("ch", "sub")),
        P(),
        P(None, ("ch", "sub")),
        P(("ch", "sub")),
        P(("ch", "sub")),
    )
    out_specs = (
        P(("parts", "ctx"), ("ch", "sub")),
        P(("parts", "ctx"), ("ch", "sub")),
        P(("parts", "ctx"), ("ch", "sub")),
        P("parts", None),
        P("parts", ("ch", "sub")),
        P(("parts", "ch", "sub")),
    )
    body = few_shards_body if mesh.shape["ctx"] == 4 else many_shards_body
    return jax.shard_map(body, mesh=mesh, in_specs=in_specs, out_specs=out_specs, check_vma=False)
```

```python
import functools
import math

import jax
import jax.numpy as jnp
import numpy as np
from jax import lax
from jax.experimental import pallas as pl
from jax.experimental.pallas import tpu as pltpu
from jax.sharding import PartitionSpec as P

band_steps = (1763, 1201, 811, 547, 367, 251, 167, 113, 79, 53, 37, 23, 17, 11, 7, 3)
highest = lax.Precision.HIGHEST
f32 = jnp.float32
bf16 = jnp.bfloat16


def features(positions):
    multiplier = jnp.array(band_steps, dtype=jnp.int32)
    phase = positions[:, None] * multiplier[None, :] % 4096
    angle = phase.astype(jnp.float32) * (2.0 * math.pi / 4096.0)
    return jnp.concatenate([jnp.cos(angle), jnp.sin(angle)], axis=1)


def tables(out_count, in_count, modulus, sign_value):
    row_index = lax.broadcasted_iota(jnp.int32, (out_count, in_count), 0)
    col_index = lax.broadcasted_iota(jnp.int32, (out_count, in_count), 1)
    angle = (row_index * col_index % modulus).astype(jnp.float32) * (2.0 * math.pi / modulus)
    return (jnp.cos(angle), sign_value * jnp.sin(angle))


def twiddle(spec_re, spec_im, freq_count, span, modulus, sign_value):
    freq_index = lax.broadcasted_iota(jnp.int32, (freq_count, span), 0)
    pos_index = lax.broadcasted_iota(jnp.int32, (freq_count, span), 1)
    angle = (freq_index * pos_index % modulus).astype(jnp.float32) * (2.0 * math.pi / modulus)
    factor_re = jnp.cos(angle)[None, None, :, :]
    factor_im = (sign_value * jnp.sin(angle))[None, None, :, :]
    return (spec_re * factor_re - spec_im * factor_im, spec_re * factor_im + spec_im * factor_re)


def contract(kernel, array):
    return jnp.einsum(
        "lj,mckj->mckl", kernel, array, precision=highest, preferred_element_type=jnp.float32
    )


def along_positions(spec_re, spec_im, kernel_re, kernel_im):
    return (
        contract(kernel_re, spec_re) - contract(kernel_im, spec_im),
        contract(kernel_re, spec_im) + contract(kernel_im, spec_re),
    )


def many_shards_body(
    x_one, x_two, values, grad_out, first_weight, second_weight, skip_bias, decay_rate
):
    row_count, chan_count = x_one.shape
    shards = lax.axis_size("ctx")
    rank = lax.axis_index("ctx")
    seq_len = row_count * shards
    total = 2 * seq_len
    narrow = chan_count // shards
    chan_weight = lax.dynamic_slice_in_dim(second_weight, rank * narrow, narrow, 1)
    chan_rate = lax.dynamic_slice_in_dim(decay_rate, rank * narrow, narrow, 0)
    source = x_one.astype(jnp.float32) * values.astype(jnp.float32)
    cotan = grad_out.astype(jnp.float32) * x_two.astype(jnp.float32)
    spread = lax.all_to_all(
        jnp.stack([source.T, cotan.T])[:, :, None, :],
        "ctx",
        split_axis=1,
        concat_axis=2,
        tiled=True,
    )
    far_source = spread[0]
    far_cotan = spread[1]
    positions = jnp.arange(seq_len, dtype=jnp.int32)
    feats = features(positions)
    pre_act = jnp.dot(feats, first_weight, precision=highest, preferred_element_type=jnp.float32)
    hidden = jnp.sin(pre_act)
    envelope = jnp.exp(-chan_rate[:, None] * positions.astype(jnp.float32)[None, :]) * float(
        seq_len
    ) ** (-0.5)
    filt = (
        jnp.einsum(
            "th,hc->ct", hidden, chan_weight, precision=highest, preferred_element_type=jnp.float32
        )
        * envelope
    )
    filt_blocks = filt.reshape(narrow, shards, row_count)
    fields = jnp.stack([far_source, far_cotan])

    def first_section(kernel):
        field_part = jnp.einsum(
            "kn,mcnj->mckj", kernel, fields, precision=highest, preferred_element_type=jnp.float32
        )
        filter_part = jnp.einsum(
            "kn,cnj->ckj",
            kernel,
            filt_blocks,
            precision=highest,
            preferred_element_type=jnp.float32,
        )
        return jnp.concatenate([field_part, filter_part[None]], axis=0)

    first_re, first_im = tables(2 * shards, shards, 2 * shards, -1.0)
    spec_re, spec_im = (first_section(first_re), first_section(first_im))
    spec_re, spec_im = twiddle(spec_re, spec_im, 2 * shards, row_count, total, -1.0)
    fwd_re, fwd_im = tables(row_count, row_count, row_count, -1.0)
    spec_re, spec_im = along_positions(spec_re, spec_im, fwd_re, fwd_im)
    source_re, source_im = (spec_re[0], spec_im[0])
    cotan_re, cotan_im = (spec_re[1], spec_im[1])
    filter_re, filter_im = (spec_re[2], spec_im[2])
    prod_re = jnp.stack(
        [
            source_re * filter_re - source_im * filter_im,
            cotan_re * filter_re + cotan_im * filter_im,
            cotan_re * source_re + cotan_im * source_im,
        ]
    )
    prod_im = jnp.stack(
        [
            source_re * filter_im + source_im * filter_re,
            cotan_im * filter_re - cotan_re * filter_im,
            cotan_im * source_re - cotan_re * source_im,
        ]
    )
    back_re, back_im = tables(row_count, row_count, row_count, 1.0)
    prod_re, prod_im = along_positions(prod_re, prod_im, back_re, back_im)
    prod_re, prod_im = twiddle(prod_re, prod_im, 2 * shards, row_count, total, 1.0)
    last_re, last_im = tables(shards, 2 * shards, 2 * shards, 1.0)
    field_out = jnp.einsum(
        "nk,mckj->mcnj", last_re, prod_re[:2], precision=highest, preferred_element_type=jnp.float32
    ) - jnp.einsum(
        "nk,mckj->mcnj", last_im, prod_im[:2], precision=highest, preferred_element_type=jnp.float32
    )
    field_out = field_out * (1.0 / total)
    filt_grad = jnp.einsum(
        "nk,ckj->cnj", last_re, prod_re[2], precision=highest, preferred_element_type=jnp.float32
    ) - jnp.einsum(
        "nk,ckj->cnj", last_im, prod_im[2], precision=highest, preferred_element_type=jnp.float32
    )
    filt_grad = (filt_grad * (1.0 / total)).reshape(narrow, seq_len)
    modulated = filt_grad * envelope
    weight_part = jnp.einsum(
        "th,ct->hc", hidden, modulated, precision=highest, preferred_element_type=jnp.float32
    )
    hidden_grad = jnp.einsum(
        "ct,hc->th", modulated, chan_weight, precision=highest, preferred_element_type=jnp.float32
    )
    first_part = jnp.dot(
        feats.T,
        hidden_grad * jnp.cos(pre_act),
        precision=highest,
        preferred_element_type=jnp.float32,
    )
    grad_first = lax.psum(first_part, ("ctx", "ch", "sub"))
    returned = lax.all_to_all(
        field_out.astype(jnp.bfloat16), "ctx", split_axis=2, concat_axis=1, tiled=True
    ).astype(field_out.dtype)
    conv_part = returned[0, :, 0, :].T
    corr_part = returned[1, :, 0, :].T
    grad_two = (grad_out.astype(jnp.float32) * (conv_part + skip_bias[None, :] * source)).astype(
        jnp.bfloat16
    )
    grad_mid = corr_part + skip_bias[None, :] * cotan
    grad_one = (grad_mid * values.astype(jnp.float32)).astype(jnp.bfloat16)
    grad_value = (grad_mid * x_one.astype(jnp.float32)).astype(jnp.bfloat16)
    grad_bias = lax.psum(jnp.sum(source * cotan, axis=0), "ctx")
    grad_second = lax.all_gather(weight_part, "ctx", axis=1, tiled=True)
    return (grad_one, grad_two, grad_value, grad_first, grad_second, grad_bias)


STEP = 16
SIDE = 128


def halves(array):
    array = np.asarray(array, np.float32)
    high = array.astype(bf16)
    low = (array - high.astype(np.float32)).astype(bf16)
    return high, low


def block_tables(rows):
    freq = np.concatenate([np.arange(0, rows, 2), np.arange(1, rows, 2)])
    phase = (2 * freq + 1)[:, None] * np.arange(rows)[None, :] % (4 * rows)
    angle = phase * (2.0 * np.pi / (4 * rows))
    forward = np.concatenate([np.cos(angle), -np.sin(angle)], axis=0)
    front = np.ascontiguousarray(np.concatenate(halves(forward), axis=1))
    back = np.ascontiguousarray(np.concatenate(halves(forward.T / rows), axis=0))
    return front, back


def feature_table(seq_len):
    phase = np.arange(seq_len)[:, None] * np.array(band_steps)[None, :] % 4096
    angle = phase * (2.0 * np.pi / 4096.0)
    return np.concatenate([np.cos(angle), np.sin(angle)], axis=1).astype(np.float32)


def split(array):
    high = array.astype(bf16)
    return high, (array - high.astype(f32)).astype(bf16)


def dot(left, right):
    return jnp.dot(left, right, preferred_element_type=f32)


def exact_dot(left, right):
    return jnp.dot(left, right, precision=highest, preferred_element_type=f32)


def dot_across(left, right):
    return lax.dot_general(left, right, (((1,), (1,)), ((), ())), preferred_element_type=f32)


def decay(rate, rows, scale):
    place = lax.broadcasted_iota(jnp.int32, (rows, rate.shape[1]), 0)
    return jnp.exp(-place.astype(f32) * rate) * scale


def times(a, b):
    return a[0] * b[0] - a[1] * b[1], a[0] * b[1] + a[1] * b[0]


def conj_times(a, b):
    return a[0] * b[0] + a[1] * b[1], a[0] * b[1] - a[1] * b[0]


def plus(a, b):
    return a[0] + b[0], a[1] + b[1]


def scaled(a, factor):
    return a[0] * factor, a[1] * factor


def choose(condition, a, b):
    return jnp.where(condition, a[0], b[0]), jnp.where(condition, a[1], b[1])


def turned(a, sign):
    return (a[1], -a[0]) if sign > 0 else (-a[1], a[0])


def forward(front_ref, block):
    return dot(front_ref[...], jnp.concatenate([block, block], axis=0))


def backward(back_ref, high, low=None):
    both = dot(back_ref[...], high)
    rows = both.shape[0] // 2
    out = both[:rows] + both[rows:]
    return out if low is None else out + dot(back_ref[:rows], low)


def row_groups(rows):
    for step in range(rows // STEP):
        sign = 1 if step * STEP < rows // 2 else -1
        yield slice(step * STEP, (step + 1) * STEP), slice(rows + step * STEP, rows + (step + 1) * STEP), sign


def weight_sums(trans, m_high, m_low):
    both = dot(trans, m_high)
    count = both.shape[0] // 2
    return both[:count] + both[count:] + dot(trans[:count], m_low)


def hidden_sums(m_high, m_low, w_high, w_low):
    left = jnp.concatenate([m_high, m_high, m_low], axis=1)
    right = jnp.concatenate([w_high, w_low, w_high], axis=1)
    return dot_across(left, right)


def looped(kernel, kinds, blocks, width):
    def over_strips(*refs):
        def step(block, carry):
            cols = pl.ds(pl.multiple_of(block * width, width), width)
            views = [
                ref if kind is None else ref.at[(*kind, cols)]
                for ref, kind in zip(refs, kinds + (None,) * (len(refs) - len(kinds)))
            ]
            kernel(block, blocks, *views)
            return carry

        lax.fori_loop(0, blocks, step, 0)

    return over_strips


ROWS = (slice(None),)
CUBE = (slice(None), slice(None))


def products_kernel(rank_ref, one_ref, two_ref, val_ref, out_ref, pair_ref, other_ref, edge_ref, bias_ref):
    source = one_ref[...].astype(f32) * val_ref[...].astype(f32)
    cotan = out_ref[...].astype(f32) * two_ref[...].astype(f32)
    even = rank_ref[0] % 2 == 0
    pair_ref[...] = jnp.where(even, source, cotan).astype(bf16)
    edge_ref[...] = pair_ref[...]
    other_ref[...] = jnp.where(even, cotan, source).astype(bf16)
    part = jnp.sum(source * cotan, axis=0, keepdims=True)

    @pl.when(pl.program_id(0) == 0)
    def _():
        bias_ref[...] = part

    @pl.when(pl.program_id(0) > 0)
    def _():
        bias_ref[...] += part


def ordered(first, a, b):
    return (jnp.where(first, a, b), jnp.where(first, b, a))


def sin_cos(angle):
    turns = jnp.floor(angle * (2.0 / math.pi) + 0.5)
    rest = ((angle - turns * 1.5703125) - turns * 4.837512969970703e-4) - turns * 7.54978995489188e-8
    square = rest * rest
    sine = rest + rest * square * (
        -1.6666654611e-1 + square * (8.3321608736e-3 + square * -1.9515295891e-4)
    )
    cosine = 1.0 - 0.5 * square + square * square * (
        4.166664568298827e-2 + square * (-1.388731625493765e-3 + square * 2.443315711809948e-5)
    )
    quarter = turns.astype(jnp.int32)
    odd = (quarter & 1) == 1
    sin_sign = jnp.where((quarter & 2) == 2, -1.0, 1.0).astype(f32)
    cos_sign = jnp.where(((quarter + 1) & 2) == 2, -1.0, 1.0).astype(f32)
    return jnp.where(odd, cosine, sine) * sin_sign, jnp.where(odd, sine, cosine) * cos_sign


def turned_over(hidden, slope):
    both = jnp.concatenate([hidden, slope], axis=1).T
    return jnp.concatenate(split(both[: hidden.shape[1]]), axis=0)


def filters_kernel(
    rows, shards, blocks, width, feats_ref, first_ref, weight_ref, rate_ref, front_ref, spec_ref, trans_ref, slope_ref,
    hid_ref,
):
    hidden, slope = sin_cos(exact_dot(feats_ref[...], first_ref[...]))
    slope_ref[...] = slope
    high, low = split(hidden)
    hid_ref[...] = jnp.concatenate([high, high, low], axis=1)
    trans_ref[...] = turned_over(hidden, slope)
    strips = looped(
        functools.partial(filter_strip, rows, shards), (None, ROWS, ROWS, None, CUBE), blocks, width
    )
    strips(hid_ref, weight_ref, rate_ref, front_ref, spec_ref)


def filter_strip(rows, shards, block, blocks, hid_ref, weight_ref, rate_ref, front_ref, spec_ref):
    scale = float(rows * shards) ** -0.5
    w_high, w_low = split(weight_ref[...])
    stacked = jnp.concatenate([w_high, w_low, w_high], axis=0)
    rate = rate_ref[...]
    env = decay(rate, rows, scale)
    before = None
    for lag in range(shards):
        part = dot(hid_ref[lag * rows : (lag + 1) * rows, :], stacked)
        part = part * (env * jnp.exp(rate * (-float(lag * rows))))
        f_high, f_low = split(part)
        now = forward(front_ref, f_high) + dot(front_ref[:, :rows], f_low)
        for re, im, sign in row_groups(rows):
            here = (now[re], now[im])
            if before is not None:
                here = plus(here, turned((before[re], before[im]), -sign))
            spec_ref[lag, re, :] = here[0].astype(bf16)
            spec_ref[lag, im, :] = here[1].astype(bf16)
        before = now


def own_kernel(rows, shards, channels, blocks, width, rank_ref, *refs):
    inputs, send_out, held = refs[:10], refs[10], refs[11:21]
    send_ref, trans_ref, acc_ref, sems, out_sem = refs[21:]
    (
        feats_ref, first_ref, pair_ref, other_ref, weight_ref, rate_ref, front_ref, back_ref, featt_ref, bias_ref
    ) = held
    copies = [pltpu.make_async_copy(far, near, sems.at[i]) for i, (far, near) in enumerate(zip(inputs, held))]
    for copy in copies:
        copy.start()
    acc_ref[...] = jnp.zeros_like(acc_ref)
    copies[0].wait()
    copies[1].wait()
    hidden, slope = sin_cos(exact_dot(feats_ref[...], first_ref[...]))
    trans_ref[...] = turned_over(hidden, slope)
    for copy in copies[2:]:
        copy.wait()
    kinds = (None, ROWS, ROWS, ROWS, ROWS, None, None, None, ROWS, None)
    looped(functools.partial(own_strip, rows, shards), kinds, blocks, width)(
        rank_ref, pair_ref, other_ref, weight_ref, rate_ref, front_ref, back_ref, trans_ref, send_ref, acc_ref
    )
    first = exact_dot(featt_ref[:, :rows], acc_ref[...] * slope)
    put_side(send_ref, channels, fold(bias_ref[...]), first)
    last = pltpu.make_async_copy(send_ref, send_out, out_sem)
    last.start()
    last.wait()


def own_strip(
    rows, shards, block, blocks, rank_ref, pair_ref, other_ref, weight_ref, rate_ref, front_ref, back_ref, trans_ref,
    send_ref, acc_ref,
):
    source, cotan = ordered(rank_ref[0] % 2 == 0, pair_ref[...], other_ref[...])
    x0 = forward(front_ref, source)
    c0 = forward(front_ref, cotan)
    pair = conj_times((x0[:rows], x0[rows:]), (c0[:rows], c0[rows:]))
    high, low = split(jnp.concatenate(pair, axis=0))
    env = decay(rate_ref[...], rows, float(rows * shards) ** -0.5)
    m_high, m_low = split(backward(back_ref, high, low) * env)
    send_ref[...] = weight_sums(trans_ref[...], m_high, m_low).astype(bf16)
    acc_ref[...] += hidden_sums(m_high, m_low, *split(weight_ref[...]))


def fold(bias):
    return jnp.concatenate([bias[:, i * 128 : (i + 1) * 128] for i in range(bias.shape[1] // 128)], axis=0)


def put_side(pay_ref, channels, bias, first=None):
    half = pay_ref.shape[0] // 2
    pay_ref[:, channels:] = jnp.zeros((2 * half, SIDE), bf16)
    for start, part in zip((0, half // 2), split(bias)):
        pay_ref[start : start + bias.shape[0], channels:] = part
    if first is not None:
        pay_ref[half:, channels:] = jnp.concatenate(split(first), axis=1)


def get_side(pay, channels, lanes, hid_count):
    half = pay.shape[0] // 2
    side = pay[:, channels:].astype(f32)
    low = side[half:]
    return side[:lanes] + side[half // 2 : half // 2 + lanes], low[:, :hid_count] + low[:, hid_count:]


def near_kernel(
    rows, shards, blocks, width, rank_ref, pair_ref, other_ref, pair_in_ref, middle_in_ref, spec_ref, weight_ref,
    rate_ref, front_ref, back_ref, trans_ref, featt_ref, slope_ref, conv_ref, corr_ref, ahead_ref, sums_ref, first_ref,
    fields, fast, high_ref, low_ref, acc_ref,
):
    rank = rank_ref[0]
    inner = jnp.logical_and(rank > 0, rank < shards - 1)
    count = shards - 1
    kinds = (None, None, None) + (ROWS,) * 4 + (CUBE, ROWS, ROWS)
    common = (
        rank_ref, front_ref, back_ref, pair_ref, other_ref, pair_in_ref, middle_in_ref, spec_ref, conv_ref, corr_ref,
        fields, fast,
    )

    @pl.when(jnp.logical_not(inner))
    def _():
        looped(functools.partial(edge_strip, rows, shards), kinds, blocks, width)(*common)

    @pl.when(inner)
    def _():
        acc_ref[...] = jnp.zeros_like(acc_ref)
        looped(
            functools.partial(inner_strip, rows, shards), kinds + (None, None, None) + (ROWS,) * 4, blocks, width
        )(*common, trans_ref, weight_ref, rate_ref, ahead_ref, sums_ref, high_ref, low_ref, acc_ref)
        first_ref[...] = exact_dot(
            featt_ref[:, : count * rows], acc_ref[...] * slope_ref[: count * rows, :]
        )


def edge_strip(
    rows, shards, block, blocks, rank_ref, front_ref, back_ref, pair_ref, other_ref, pair_in_ref, middle_in_ref,
    spec_ref, conv_ref, corr_ref, fields, fast,
):
    del middle_in_ref
    top = rank_ref[0] == shards - 1
    source, cotan = ordered(rank_ref[0] % 2 == 0, pair_ref[...], other_ref[...])
    for index, block_in in enumerate((source, cotan, pair_in_ref[...])):
        fields[index] = forward(front_ref, block_in)
    on_conv = jnp.where(top, 1.0, 0.0).astype(f32)
    on_corr = jnp.where(top, 0.0, 1.0).astype(f32)
    for re, im, sign in row_groups(rows):
        x0, c0, near = ((fields[i, re, :], fields[i, im, :]) for i in range(3))
        w0, w1 = ((spec_ref[i, re, :].astype(f32), spec_ref[i, im, :].astype(f32)) for i in range(2))
        values = (
            plus(times(w0, x0), scaled(times(w1, near), on_conv)),
            plus(conj_times(w0, c0), scaled(conj_times(w1, near), on_corr)),
        )
        for index, value in enumerate(values):
            fast[index, re, :] = value[0].astype(bf16)
            fast[index, im, :] = value[1].astype(bf16)
    conv_ref[...] = backward(back_ref, fast[0])
    corr_ref[...] = backward(back_ref, fast[1])


def inner_strip(
    rows, shards, block, blocks, rank_ref, front_ref, back_ref, pair_ref, other_ref, pair_in_ref, middle_in_ref,
    spec_ref, conv_ref, corr_ref, fields, fast, trans_ref, weight_ref, rate_ref, ahead_ref, sums_ref, high_ref, low_ref,
    acc_ref,
):
    lower = rank_ref[0] == 1
    upper = jnp.where(lower, 0.0, 1.0).astype(f32)
    side = jnp.where(lower, -1.0, 1.0).astype(f32)
    count = shards - 1
    blocks_in = (
        *ordered(lower, other_ref[...], pair_ref[...]), *ordered(lower, pair_in_ref[...], middle_in_ref[...])
    )
    for index, block_in in enumerate(blocks_in):
        fields[index] = forward(front_ref, block_in)
    for re, im, sign in row_groups(rows):
        x0, c0, x1, c1 = ((fields[i, re, :], fields[i, im, :]) for i in range(4))
        w0, w1, w2 = ((spec_ref[i, re, :].astype(f32), spec_ref[i, im, :].astype(f32)) for i in range(3))
        values = (
            plus(times(w0, x0), times(w1, x1)),
            plus(conj_times(w0, c0), conj_times(w1, c1)),
            times((w2[0], w2[1] * side), choose(lower, c1, x1)),
        )
        for index, value in enumerate(values):
            fast[index, re, :] = value[0].astype(bf16)
            fast[index, im, :] = value[1].astype(bf16)
        zero = conj_times(x0, c0)
        one = plus(conj_times(x1, c0), scaled(conj_times(x0, c1), upper))
        two = conj_times(x1, c1)
        for index, value in enumerate((plus(zero, turned(one, sign)), plus(one, turned(two, sign)), two)):
            for part, where in zip(value, (re, im)):
                high_ref[index, where, :], low_ref[index, where, :] = split(part)
    conv_ref[...] = backward(back_ref, fast[0])
    corr_ref[...] = backward(back_ref, fast[1])
    ahead_ref[...] = backward(back_ref, fast[2])
    rate = rate_ref[...]
    env = decay(rate, rows, float(rows * shards) ** -0.5)
    parts = []
    for lag in range(count):
        grad = backward(back_ref, high_ref[lag], low_ref[lag])
        parts.append(split(grad * (env * jnp.exp(rate * (-float(lag * rows))))))
    m_high = jnp.concatenate([p[0] for p in parts], axis=0)
    m_low = jnp.concatenate([p[1] for p in parts], axis=0)
    sums_ref[...] = weight_sums(trans_ref[:, : count * rows], m_high, m_low)
    acc_ref[...] += hidden_sums(m_high, m_low, *split(weight_ref[...]))


def only(inner, shards, rank_at, kernel):
    def run(*refs):
        rank = refs[rank_at][0]

        @pl.when(jnp.logical_and(rank > 0, rank < shards - 1) == inner)
        def _():
            kernel(*refs)

    return run


def far_kernel(rows, block, blocks, rank_ref, far_ref, spec_ref, front_ref, back_ref, ahead_ref, part_ref, late_ref):
    side = jnp.where(rank_ref[0] == 2, 1.0, -1.0).astype(f32)
    far = forward(front_ref, far_ref[...])
    far = (far[:rows], far[rows:])
    w2, w3 = ((spec_ref[i, :rows, :].astype(f32), spec_ref[i, rows:, :].astype(f32) * side) for i in range(2))
    ahead = jnp.concatenate(times(w3, far), axis=0).astype(bf16)
    part_ref[...] = (ahead_ref[...] + backward(back_ref, ahead)).astype(bf16)
    late = jnp.concatenate(times(w2, far), axis=0).astype(bf16)
    late_ref[...] = backward(back_ref, late)


def last_kernel(
    rows, shards, channels, block, blocks, after_ref, rank_ref, near_ref, far_ref, weight_ref, rate_ref, front_ref, back_ref,
    trans_ref, featt_ref, slope_ref, sums_ref, first_ref, bias_ref, in_ref, pay_ref, total_ref, acc_ref,
):
    del after_ref
    hid_count, width = weight_ref.shape
    lower = rank_ref[0] == 1
    start = pl.multiple_of(block * width, width)
    here = sums_ref[...] + in_ref[:, pl.ds(start, width)].astype(f32)
    mine = (block < blocks // 2) == lower

    @pl.when(block == 0)
    def _():
        acc_ref[...] = jnp.zeros_like(acc_ref)

    @pl.when(mine)
    def _():
        sign = jnp.where(lower, 1.0, -1.0).astype(f32)
        near = forward(front_ref, near_ref[...])
        far = forward(front_ref, far_ref[...])
        three = conj_times((near[:rows], near[rows:]), (far[:rows], far[rows:]))
        three = (three[0], three[1] * sign)
        half = rows // 2
        two = jnp.concatenate([three[1][:half], -three[1][half:], -three[0][:half], three[0][half:]], axis=0)
        rate = rate_ref[...]
        env = decay(rate, rows, float(rows * shards) ** -0.5)
        parts = []
        for lag, value in ((shards - 2, two), (shards - 1, jnp.concatenate(three, axis=0))):
            grad = backward(back_ref, *split(value))
            parts.append(split(grad * (env * jnp.exp(rate * (-float(lag * rows))))))
        m_high = jnp.concatenate([p[0] for p in parts], axis=0)
        m_low = jnp.concatenate([p[1] for p in parts], axis=0)
        trans = trans_ref[:, (shards - 2) * rows :]
        pay_ref[:, pl.ds(start, width)] = (here + weight_sums(trans, m_high, m_low)).astype(bf16)
        w_high, w_low = split(weight_ref[...])
        acc_ref[...] += hidden_sums(m_high, m_low, w_high, w_low)

    @pl.when(jnp.logical_not(mine))
    def _():
        pay_ref[:, pl.ds(start, width)] = here.astype(bf16)

    @pl.when(block == blocks - 1)
    def _():
        first = exact_dot(
            featt_ref[:, (shards - 2) * rows :], acc_ref[...] * slope_ref[(shards - 2) * rows :, :]
        )
        lanes = channels // 128
        in_bias, in_first = get_side(in_ref[...], channels, lanes, hid_count)
        first = first + first_ref[...] + in_first
        put_side(pay_ref, channels, fold(bias_ref[...]) + in_bias)
        total_ref[...] = first


def total_kernel(channels, hid_count, part_ref, first_ref, own_ref, come_ref, pay_ref):
    del part_ref, first_ref
    lanes = channels // 128
    pay_ref[:, :channels] = (own_ref[:, :channels].astype(f32) + come_ref[:, :channels].astype(f32)).astype(bf16)
    own, come = (get_side(ref[...], channels, lanes, hid_count)[0] for ref in (own_ref, come_ref))
    put_side(pay_ref, channels, own + come)


def gates_kernel(
    shards, block, blocks, rank_ref, one_ref, two_ref, val_ref, out_ref, skip_ref, conv_ref, corr_ref, late_ref, part_ref,
    grad_one_ref, grad_two_ref, grad_value_ref,
):
    rank = rank_ref[0]

    def on(wanted, value):
        return jnp.where(rank == wanted, value, jnp.zeros_like(value))

    part = part_ref[...].astype(f32)
    late = late_ref[...]
    one = one_ref[...].astype(f32)
    val = val_ref[...].astype(f32)
    out = out_ref[...].astype(f32)
    skip = skip_ref[...]
    conv = conv_ref[...] + on(2, late) + on(shards - 1, part)
    corr = corr_ref[...] + on(1, late) + on(0, part)
    grad_two_ref[...] = (out * (conv + skip * (one * val))).astype(bf16)
    mid = corr + skip * (out * two_ref[...].astype(f32))
    grad_one_ref[...] = (mid * val).astype(bf16)
    grad_value_ref[...] = (mid * one).astype(bf16)


def finish_kernel(
    channels, shards, rank_ref, own_ref, come_ref, first_ref, first_come_ref, second_out, first_out, bias_out, second,
    first, bias, sems,
):
    rank = rank_ref[0]
    inner = jnp.logical_and(rank > 0, rank < shards - 1)
    lanes = channels // 128
    copies = [
        pltpu.make_async_copy(held, out, sems.at[i])
        for i, (held, out) in enumerate(((second, second_out), (first, first_out), (bias, bias_out)))
    ]
    picked = jnp.where(inner, own_ref[...], come_ref[...])
    second[...] = picked[:, :channels].astype(f32)
    copies[0].start()
    first[...] = jnp.where(inner, first_ref[...], first_come_ref[...])
    copies[1].start()
    rows = get_side(picked, channels, lanes, first.shape[1])[0]
    for i in range(lanes):
        bias[:, i * 128 : (i + 1) * 128] = rows[i : i + 1]
    copies[2].start()
    for copy in copies:
        copy.wait()


def few_shards_body(
    x_one, x_two, values, grad_out, first_weight, second_weight, skip_bias, decay_rate
):
    rows, channels = x_one.shape
    shards = lax.axis_size("ctx")
    feat_count, hid_count = first_weight.shape
    seq_len = rows * shards
    double = 2 * rows
    width = min(512, channels)
    blocks = channels // width
    rank = lax.axis_index("ctx").astype(jnp.int32).reshape(1)
    front, back = block_tables(rows)
    feats = feature_table(seq_len)
    featt = np.ascontiguousarray(feats.T)
    skip_row = skip_bias.reshape(1, channels)
    rate_row = decay_rate.reshape(1, channels)
    smem = pl.BlockSpec(memory_space=pltpu.SMEM)
    vmem = pl.BlockSpec(memory_space=pltpu.VMEM)
    anywhere = pl.BlockSpec(memory_space=pl.ANY)
    mebi = 1024 * 1024

    def shape(*dims, dtype=f32):
        return jax.ShapeDtypeStruct(dims, dtype)

    def call(kernel, name, units, out_shape, in_specs, out_specs=None, scratch=(), limit=16, aliases={}):
        return pl.pallas_call(
            kernel,
            in_specs=in_specs,
            out_specs=out_specs if out_specs is not None else [vmem] * len(out_shape),
            out_shape=out_shape,
            scratch_shapes=scratch,
            input_output_aliases=aliases,
            compiler_params=pltpu.CompilerParams(vmem_limit_bytes=limit * mebi),
            cost_estimate=pl.CostEstimate(
                flops=2 * units * double * double * channels, bytes_accessed=rows * channels, transcendentals=0
            ),
            name=name,
        )

    def move(array, pairs):
        return lax.ppermute(array, "ctx", pairs)

    inward = [(0, 1), (shards - 1, shards - 2)]
    outward = [(1, 0), (shards - 2, shards - 1)]
    across = [(1, 2), (2, 1)]
    alone = [(0, 0), (shards - 1, shards - 1)]
    pay_shape = (hid_count, channels + SIDE)
    block_bf16 = shape(rows, channels, dtype=bf16)
    block_f32 = shape(rows, channels)

    row_step = max(rows // 2, 16)
    gate_rows = pl.BlockSpec((row_step, channels), lambda i: (i, 0))
    pair, other, edge, bias = pl.pallas_call(
        products_kernel,
        grid=(rows // row_step,),
        in_specs=[smem] + [gate_rows] * 4,
        out_specs=[gate_rows] * 3 + [pl.BlockSpec((1, channels), lambda i: (0, 0))],
        out_shape=[block_bf16] * 3 + [shape(1, channels)],
        compiler_params=pltpu.CompilerParams(vmem_limit_bytes=64 * mebi),
        name="products",
    )(rank, x_one, x_two, values, grad_out)
    pair_in = move(pair, inward + outward)
    middle_in = move(other, across)

    own_shapes = [
        shape(rows, feat_count), shape(feat_count, hid_count), block_bf16, block_bf16, shape(hid_count, channels),
        shape(1, channels), shape(double, double, dtype=bf16), shape(double, double, dtype=bf16),
        shape(feat_count, seq_len), shape(1, channels), shape(*pay_shape, dtype=bf16),
    ]
    (send,) = call(
        only(False, shards, 0, functools.partial(own_kernel, rows, shards, channels, blocks, width)), "own_pair", 8,
        [shape(*pay_shape, dtype=bf16)],
        [smem] + [anywhere] * 10,
        out_specs=[anywhere],
        scratch=[pltpu.VMEM(s.shape, s.dtype) for s in own_shapes]
        + [
            pltpu.VMEM((2 * hid_count, rows), bf16), pltpu.VMEM((rows, hid_count), f32),
            pltpu.SemaphoreType.DMA((10,)), pltpu.SemaphoreType.DMA,
        ],
        limit=60,
    )(rank, feats[:rows], first_weight, pair, other, second_weight, rate_row, front, back, featt, bias)
    come = move(send, inward)
    late_feats, _ = lax.optimization_barrier((jnp.asarray(feats), send))
    spec, trans, slope = call(
        functools.partial(filters_kernel, rows, shards, blocks, width), "filters", 8,
        [
            shape(shards, double, channels, dtype=bf16), shape(2 * hid_count, seq_len, dtype=bf16),
            shape(seq_len, hid_count),
        ],
        [vmem] * 5,
        scratch=[pltpu.VMEM((seq_len, 3 * hid_count), bf16)],
    )(late_feats, first_weight, second_weight, rate_row, front)

    edge, _ = lax.optimization_barrier((edge, slope))
    far = move(edge, [(0, 2), (shards - 1, shards - 3)])
    conv, corr, ahead, sums, first = call(
        functools.partial(near_kernel, rows, shards, blocks, width), "near_blocks", 20,
        [block_f32] * 3 + [shape(hid_count, channels), shape(feat_count, hid_count)],
        [smem] + [vmem] * 12,
        scratch=[
            pltpu.VMEM((4, double, width), f32),
            pltpu.VMEM((3, double, width), bf16),
            pltpu.VMEM((shards - 1, double, width), bf16),
            pltpu.VMEM((shards - 1, double, width), bf16),
            pltpu.VMEM(((shards - 1) * rows, hid_count), f32),
        ],
    )(rank, pair, other, pair_in, middle_in, spec, second_weight, rate_row, front, back, trans, featt, slope)

    part, late = call(
        only(
            True, shards, 0,
            looped(
                functools.partial(far_kernel, rows),
                (None, ROWS, (slice(2, 4), slice(None)), None, None, ROWS, ROWS, ROWS),
                blocks, width,
            ),
        ),
        "far_block", 1,
        [block_bf16, block_f32],
        [smem] + [vmem] * 5,
    )(rank, far, spec, front, back, ahead)
    part_come = move(part, outward)

    pay, first = call(
        only(
            True, shards, 1,
            looped(
                functools.partial(last_kernel, rows, shards, channels),
                (None, None, ROWS, ROWS, ROWS, ROWS, None, None, None, None, None, ROWS),
                blocks, width,
            ),
        ),
        "last_pair", 1,
        [shape(*pay_shape, dtype=bf16), shape(feat_count, hid_count)],
        [anywhere, smem] + [vmem] * 13,
        scratch=[pltpu.VMEM((2 * rows, hid_count), f32)],
    )(late, rank, pair_in, far, second_weight, rate_row, front, back, trans, featt, slope, sums, first, bias, come)
    pay_come = move(pay, across + alone)
    group = lax.axis_size(("ch", "sub"))
    bit = 1
    while bit < group:
        first = first + lax.ppermute(first, ("ch", "sub"), [(i, i ^ bit) for i in range(group)])
        bit *= 2

    (total,) = call(
        functools.partial(total_kernel, channels, hid_count), "total", 0,
        [shape(*pay_shape, dtype=bf16)],
        [anywhere] * 2 + [vmem] * 2,
    )(part_come, first, pay, pay_come)
    total_come = move(total, inward + outward)
    first = first + move(first, across + alone)
    first_come = move(first, inward + outward)

    grad_one, grad_two, grad_value = call(
        looped(
            functools.partial(gates_kernel, shards), (None,) + (ROWS,) * 12, blocks, width
        ),
        "gates", 0,
        [block_bf16] * 3,
        [smem] + [vmem] * 9,
    )(rank, x_one, x_two, values, grad_out, skip_row, conv, corr, late, part_come)

    outs = [shape(hid_count, channels), shape(feat_count, hid_count), shape(1, channels)]
    grad_second, grad_first, grad_bias = call(
        functools.partial(finish_kernel, channels, shards), "finish", 0,
        outs,
        [smem] + [vmem] * 4,
        out_specs=[anywhere] * 3,
        scratch=[pltpu.VMEM(o.shape, f32) for o in outs] + [pltpu.SemaphoreType.DMA((3,))],
    )(rank, total, total_come, first, first_come)
    return (grad_one, grad_two, grad_value, grad_first, grad_second, grad_bias.reshape(channels))


def solution(mesh):
    in_specs = (
        P(("parts", "ctx"), ("ch", "sub")),
        P(("parts", "ctx"), ("ch", "sub")),
        P(("parts", "ctx"), ("ch", "sub")),
        P(("parts", "ctx"), ("ch", "sub")),
        P(),
        P(None, ("ch", "sub")),
        P(("ch", "sub")),
        P(("ch", "sub")),
    )
    out_specs = (
        P(("parts", "ctx"), ("ch", "sub")),
        P(("parts", "ctx"), ("ch", "sub")),
        P(("parts", "ctx"), ("ch", "sub")),
        P("parts", None),
        P("parts", ("ch", "sub")),
        P(("parts", "ch", "sub")),
    )
    body = few_shards_body if mesh.shape["ctx"] == 4 else many_shards_body
    return jax.shard_map(body, mesh=mesh, in_specs=in_specs, out_specs=out_specs, check_vma=False)
```

```python
import functools
import math

import jax
import jax.numpy as jnp
import numpy as np
from jax import lax
from jax.experimental import pallas as pl
from jax.experimental.pallas import tpu as pltpu
from jax.sharding import PartitionSpec as P

band_steps = (1763, 1201, 811, 547, 367, 251, 167, 113, 79, 53, 37, 23, 17, 11, 7, 3)
highest = lax.Precision.HIGHEST
f32 = jnp.float32
bf16 = jnp.bfloat16


def features(positions):
    multiplier = jnp.array(band_steps, dtype=jnp.int32)
    phase = positions[:, None] * multiplier[None, :] % 4096
    angle = phase.astype(jnp.float32) * (2.0 * math.pi / 4096.0)
    return jnp.concatenate([jnp.cos(angle), jnp.sin(angle)], axis=1)


def tables(out_count, in_count, modulus, sign_value):
    row_index = lax.broadcasted_iota(jnp.int32, (out_count, in_count), 0)
    col_index = lax.broadcasted_iota(jnp.int32, (out_count, in_count), 1)
    angle = (row_index * col_index % modulus).astype(jnp.float32) * (2.0 * math.pi / modulus)
    return (jnp.cos(angle), sign_value * jnp.sin(angle))


def twiddle(spec_re, spec_im, freq_count, span, modulus, sign_value):
    freq_index = lax.broadcasted_iota(jnp.int32, (freq_count, span), 0)
    pos_index = lax.broadcasted_iota(jnp.int32, (freq_count, span), 1)
    angle = (freq_index * pos_index % modulus).astype(jnp.float32) * (2.0 * math.pi / modulus)
    factor_re = jnp.cos(angle)[None, None, :, :]
    factor_im = (sign_value * jnp.sin(angle))[None, None, :, :]
    return (spec_re * factor_re - spec_im * factor_im, spec_re * factor_im + spec_im * factor_re)


def contract(kernel, array):
    return jnp.einsum(
        "lj,mckj->mckl", kernel, array, precision=highest, preferred_element_type=jnp.float32
    )


def along_positions(spec_re, spec_im, kernel_re, kernel_im):
    return (
        contract(kernel_re, spec_re) - contract(kernel_im, spec_im),
        contract(kernel_re, spec_im) + contract(kernel_im, spec_re),
    )


def many_shards_body(
    x_one, x_two, values, grad_out, first_weight, second_weight, skip_bias, decay_rate
):
    row_count, chan_count = x_one.shape
    shards = lax.axis_size("ctx")
    rank = lax.axis_index("ctx")
    seq_len = row_count * shards
    total = 2 * seq_len
    narrow = chan_count // shards
    chan_weight = lax.dynamic_slice_in_dim(second_weight, rank * narrow, narrow, 1)
    chan_rate = lax.dynamic_slice_in_dim(decay_rate, rank * narrow, narrow, 0)
    source = x_one.astype(jnp.float32) * values.astype(jnp.float32)
    cotan = grad_out.astype(jnp.float32) * x_two.astype(jnp.float32)
    spread = lax.all_to_all(
        jnp.stack([source.T, cotan.T])[:, :, None, :],
        "ctx",
        split_axis=1,
        concat_axis=2,
        tiled=True,
    )
    far_source = spread[0]
    far_cotan = spread[1]
    positions = jnp.arange(seq_len, dtype=jnp.int32)
    feats = features(positions)
    pre_act = jnp.dot(feats, first_weight, precision=highest, preferred_element_type=jnp.float32)
    hidden = jnp.sin(pre_act)
    envelope = jnp.exp(-chan_rate[:, None] * positions.astype(jnp.float32)[None, :]) * float(
        seq_len
    ) ** (-0.5)
    filt = (
        jnp.einsum(
            "th,hc->ct", hidden, chan_weight, precision=highest, preferred_element_type=jnp.float32
        )
        * envelope
    )
    filt_blocks = filt.reshape(narrow, shards, row_count)
    fields = jnp.stack([far_source, far_cotan])

    def first_section(kernel):
        field_part = jnp.einsum(
            "kn,mcnj->mckj", kernel, fields, precision=highest, preferred_element_type=jnp.float32
        )
        filter_part = jnp.einsum(
            "kn,cnj->ckj",
            kernel,
            filt_blocks,
            precision=highest,
            preferred_element_type=jnp.float32,
        )
        return jnp.concatenate([field_part, filter_part[None]], axis=0)

    first_re, first_im = tables(2 * shards, shards, 2 * shards, -1.0)
    spec_re, spec_im = (first_section(first_re), first_section(first_im))
    spec_re, spec_im = twiddle(spec_re, spec_im, 2 * shards, row_count, total, -1.0)
    fwd_re, fwd_im = tables(row_count, row_count, row_count, -1.0)
    spec_re, spec_im = along_positions(spec_re, spec_im, fwd_re, fwd_im)
    source_re, source_im = (spec_re[0], spec_im[0])
    cotan_re, cotan_im = (spec_re[1], spec_im[1])
    filter_re, filter_im = (spec_re[2], spec_im[2])
    prod_re = jnp.stack(
        [
            source_re * filter_re - source_im * filter_im,
            cotan_re * filter_re + cotan_im * filter_im,
            cotan_re * source_re + cotan_im * source_im,
        ]
    )
    prod_im = jnp.stack(
        [
            source_re * filter_im + source_im * filter_re,
            cotan_im * filter_re - cotan_re * filter_im,
            cotan_im * source_re - cotan_re * source_im,
        ]
    )
    back_re, back_im = tables(row_count, row_count, row_count, 1.0)
    prod_re, prod_im = along_positions(prod_re, prod_im, back_re, back_im)
    prod_re, prod_im = twiddle(prod_re, prod_im, 2 * shards, row_count, total, 1.0)
    last_re, last_im = tables(shards, 2 * shards, 2 * shards, 1.0)
    field_out = jnp.einsum(
        "nk,mckj->mcnj", last_re, prod_re[:2], precision=highest, preferred_element_type=jnp.float32
    ) - jnp.einsum(
        "nk,mckj->mcnj", last_im, prod_im[:2], precision=highest, preferred_element_type=jnp.float32
    )
    field_out = field_out * (1.0 / total)
    filt_grad = jnp.einsum(
        "nk,ckj->cnj", last_re, prod_re[2], precision=highest, preferred_element_type=jnp.float32
    ) - jnp.einsum(
        "nk,ckj->cnj", last_im, prod_im[2], precision=highest, preferred_element_type=jnp.float32
    )
    filt_grad = (filt_grad * (1.0 / total)).reshape(narrow, seq_len)
    modulated = filt_grad * envelope
    weight_part = jnp.einsum(
        "th,ct->hc", hidden, modulated, precision=highest, preferred_element_type=jnp.float32
    )
    hidden_grad = jnp.einsum(
        "ct,hc->th", modulated, chan_weight, precision=highest, preferred_element_type=jnp.float32
    )
    first_part = jnp.dot(
        feats.T,
        hidden_grad * jnp.cos(pre_act),
        precision=highest,
        preferred_element_type=jnp.float32,
    )
    grad_first = lax.psum(first_part, ("ctx", "ch", "sub"))
    returned = lax.all_to_all(
        field_out.astype(jnp.bfloat16), "ctx", split_axis=2, concat_axis=1, tiled=True
    ).astype(field_out.dtype)
    conv_part = returned[0, :, 0, :].T
    corr_part = returned[1, :, 0, :].T
    grad_two = (grad_out.astype(jnp.float32) * (conv_part + skip_bias[None, :] * source)).astype(
        jnp.bfloat16
    )
    grad_mid = corr_part + skip_bias[None, :] * cotan
    grad_one = (grad_mid * values.astype(jnp.float32)).astype(jnp.bfloat16)
    grad_value = (grad_mid * x_one.astype(jnp.float32)).astype(jnp.bfloat16)
    grad_bias = lax.psum(jnp.sum(source * cotan, axis=0), "ctx")
    grad_second = lax.all_gather(weight_part, "ctx", axis=1, tiled=True)
    return (grad_one, grad_two, grad_value, grad_first, grad_second, grad_bias)


STEP = 16
SIDE = 128


def halves(array):
    array = np.asarray(array, np.float32)
    high = array.astype(bf16)
    low = (array - high.astype(np.float32)).astype(bf16)
    return high, low


def block_tables(rows):
    freq = np.concatenate([np.arange(0, rows, 2), np.arange(1, rows, 2)])
    phase = (2 * freq + 1)[:, None] * np.arange(rows)[None, :] % (4 * rows)
    angle = phase * (2.0 * np.pi / (4 * rows))
    forward = np.concatenate([np.cos(angle), -np.sin(angle)], axis=0)
    front = np.ascontiguousarray(np.concatenate(halves(forward), axis=1))
    back = np.ascontiguousarray(np.concatenate(halves(forward.T / rows), axis=0))
    return front, back


def feature_table(seq_len):
    phase = np.arange(seq_len)[:, None] * np.array(band_steps)[None, :] % 4096
    angle = phase * (2.0 * np.pi / 4096.0)
    return np.concatenate([np.cos(angle), np.sin(angle)], axis=1).astype(np.float32)


def split(array):
    high = array.astype(bf16)
    return high, (array - high.astype(f32)).astype(bf16)


def dot(left, right):
    return jnp.dot(left, right, preferred_element_type=f32)


def exact_dot(left, right):
    return jnp.dot(left, right, precision=highest, preferred_element_type=f32)


def dot_across(left, right):
    return lax.dot_general(left, right, (((1,), (1,)), ((), ())), preferred_element_type=f32)


def decay(rate, rows, scale):
    place = lax.broadcasted_iota(jnp.int32, (rows, rate.shape[1]), 0)
    return jnp.exp(-place.astype(f32) * rate) * scale


def times(a, b):
    return a[0] * b[0] - a[1] * b[1], a[0] * b[1] + a[1] * b[0]


def conj_times(a, b):
    return a[0] * b[0] + a[1] * b[1], a[0] * b[1] - a[1] * b[0]


def plus(a, b):
    return a[0] + b[0], a[1] + b[1]


def scaled(a, factor):
    return a[0] * factor, a[1] * factor


def choose(condition, a, b):
    return jnp.where(condition, a[0], b[0]), jnp.where(condition, a[1], b[1])


def turned(a, sign):
    return (a[1], -a[0]) if sign > 0 else (-a[1], a[0])


def forward(front_ref, block):
    return dot(front_ref[...], jnp.concatenate([block, block], axis=0))


def backward(back_ref, high, low=None):
    both = dot(back_ref[...], high)
    rows = both.shape[0] // 2
    out = both[:rows] + both[rows:]
    return out if low is None else out + dot(back_ref[:rows], low)


def row_groups(rows):
    for step in range(rows // STEP):
        sign = 1 if step * STEP < rows // 2 else -1
        yield slice(step * STEP, (step + 1) * STEP), slice(rows + step * STEP, rows + (step + 1) * STEP), sign


def weight_sums(trans, m_high, m_low):
    both = dot(trans, m_high)
    count = both.shape[0] // 2
    return both[:count] + both[count:] + dot(trans[:count], m_low)


def hidden_sums(m_high, m_low, w_high, w_low):
    left = jnp.concatenate([m_high, m_high, m_low], axis=1)
    right = jnp.concatenate([w_high, w_low, w_high], axis=1)
    return dot_across(left, right)


def looped(kernel, kinds, blocks, width):
    def over_strips(*refs):
        def step(block, carry):
            cols = pl.ds(pl.multiple_of(block * width, width), width)
            views = [
                ref if kind is None else ref.at[(*kind, cols)]
                for ref, kind in zip(refs, kinds + (None,) * (len(refs) - len(kinds)))
            ]
            kernel(block, blocks, *views)
            return carry

        lax.fori_loop(0, blocks, step, 0)

    return over_strips


ROWS = (slice(None),)
CUBE = (slice(None), slice(None))


def products_kernel(rank_ref, one_ref, two_ref, val_ref, out_ref, pair_ref, other_ref, edge_ref, bias_ref):
    source = one_ref[...].astype(f32) * val_ref[...].astype(f32)
    cotan = out_ref[...].astype(f32) * two_ref[...].astype(f32)
    even = rank_ref[0] % 2 == 0
    pair_ref[...] = jnp.where(even, source, cotan).astype(bf16)
    edge_ref[...] = pair_ref[...]
    other_ref[...] = jnp.where(even, cotan, source).astype(bf16)
    part = jnp.sum(source * cotan, axis=0, keepdims=True)

    @pl.when(pl.program_id(0) == 0)
    def _():
        bias_ref[...] = part

    @pl.when(pl.program_id(0) > 0)
    def _():
        bias_ref[...] += part


def ordered(first, a, b):
    return (jnp.where(first, a, b), jnp.where(first, b, a))


def sin_cos(angle):
    turns = jnp.floor(angle * (2.0 / math.pi) + 0.5)
    rest = ((angle - turns * 1.5703125) - turns * 4.837512969970703e-4) - turns * 7.54978995489188e-8
    square = rest * rest
    sine = rest + rest * square * (
        -1.6666654611e-1 + square * (8.3321608736e-3 + square * -1.9515295891e-4)
    )
    cosine = 1.0 - 0.5 * square + square * square * (
        4.166664568298827e-2 + square * (-1.388731625493765e-3 + square * 2.443315711809948e-5)
    )
    quarter = turns.astype(jnp.int32)
    odd = (quarter & 1) == 1
    sin_sign = jnp.where((quarter & 2) == 2, -1.0, 1.0).astype(f32)
    cos_sign = jnp.where(((quarter + 1) & 2) == 2, -1.0, 1.0).astype(f32)
    return jnp.where(odd, cosine, sine) * sin_sign, jnp.where(odd, sine, cosine) * cos_sign


def turned_over(hidden, slope):
    both = jnp.concatenate([hidden, slope], axis=1).T
    return jnp.concatenate(split(both[: hidden.shape[1]]), axis=0)


def filters_kernel(
    rows, shards, blocks, width, feats_ref, first_ref, weight_ref, rate_ref, front_ref, spec_ref, trans_ref, slope_ref,
    hid_ref,
):
    hidden, slope = sin_cos(exact_dot(feats_ref[...], first_ref[...]))
    slope_ref[...] = slope
    high, low = split(hidden)
    hid_ref[...] = jnp.concatenate([high, high, low], axis=1)
    trans_ref[...] = turned_over(hidden, slope)
    strips = looped(
        functools.partial(filter_strip, rows, shards), (None, ROWS, ROWS, None, CUBE), blocks, width
    )
    strips(hid_ref, weight_ref, rate_ref, front_ref, spec_ref)


def filter_strip(rows, shards, block, blocks, hid_ref, weight_ref, rate_ref, front_ref, spec_ref):
    scale = float(rows * shards) ** -0.5
    w_high, w_low = split(weight_ref[...])
    stacked = jnp.concatenate([w_high, w_low, w_high], axis=0)
    rate = rate_ref[...]
    env = decay(rate, rows, scale)
    before = None
    for lag in range(shards):
        part = dot(hid_ref[lag * rows : (lag + 1) * rows, :], stacked)
        part = part * (env * jnp.exp(rate * (-float(lag * rows))))
        f_high, f_low = split(part)
        now = forward(front_ref, f_high) + dot(front_ref[:, :rows], f_low)
        for re, im, sign in row_groups(rows):
            here = (now[re], now[im])
            if before is not None:
                here = plus(here, turned((before[re], before[im]), -sign))
            spec_ref[lag, re, :] = here[0].astype(bf16)
            spec_ref[lag, im, :] = here[1].astype(bf16)
        before = now


def own_kernel(rows, shards, channels, blocks, width, rank_ref, *refs):
    inputs, send_out, held = refs[:10], refs[10], refs[11:21]
    send_ref, trans_ref, acc_ref, sems, out_sem = refs[21:]
    (
        feats_ref, first_ref, pair_ref, other_ref, weight_ref, rate_ref, front_ref, back_ref, featt_ref, bias_ref
    ) = held
    copies = [pltpu.make_async_copy(far, near, sems.at[i]) for i, (far, near) in enumerate(zip(inputs, held))]
    for copy in copies:
        copy.start()
    acc_ref[...] = jnp.zeros_like(acc_ref)
    copies[0].wait()
    copies[1].wait()
    hidden, slope = sin_cos(exact_dot(feats_ref[...], first_ref[...]))
    trans_ref[...] = turned_over(hidden, slope)
    for copy in copies[2:]:
        copy.wait()
    kinds = (None, ROWS, ROWS, ROWS, ROWS, None, None, None, ROWS, None)
    looped(functools.partial(own_strip, rows, shards), kinds, blocks, width)(
        rank_ref, pair_ref, other_ref, weight_ref, rate_ref, front_ref, back_ref, trans_ref, send_ref, acc_ref
    )
    first = exact_dot(featt_ref[:, :rows], acc_ref[...] * slope)
    put_side(send_ref, channels, fold(bias_ref[...]), first)
    last = pltpu.make_async_copy(send_ref, send_out, out_sem)
    last.start()
    last.wait()


def own_strip(
    rows, shards, block, blocks, rank_ref, pair_ref, other_ref, weight_ref, rate_ref, front_ref, back_ref, trans_ref,
    send_ref, acc_ref,
):
    source, cotan = ordered(rank_ref[0] % 2 == 0, pair_ref[...], other_ref[...])
    x0 = forward(front_ref, source)
    c0 = forward(front_ref, cotan)
    pair = conj_times((x0[:rows], x0[rows:]), (c0[:rows], c0[rows:]))
    high, low = split(jnp.concatenate(pair, axis=0))
    env = decay(rate_ref[...], rows, float(rows * shards) ** -0.5)
    m_high, m_low = split(backward(back_ref, high, low) * env)
    send_ref[...] = weight_sums(trans_ref[...], m_high, m_low).astype(bf16)
    acc_ref[...] += hidden_sums(m_high, m_low, *split(weight_ref[...]))


def fold(bias):
    return jnp.concatenate([bias[:, i * 128 : (i + 1) * 128] for i in range(bias.shape[1] // 128)], axis=0)


def put_side(pay_ref, channels, bias, first=None):
    half = pay_ref.shape[0] // 2
    pay_ref[:, channels:] = jnp.zeros((2 * half, SIDE), bf16)
    for start, part in zip((0, half // 2), split(bias)):
        pay_ref[start : start + bias.shape[0], channels:] = part
    if first is not None:
        pay_ref[half:, channels:] = jnp.concatenate(split(first), axis=1)


def get_side(pay, channels, lanes, hid_count):
    half = pay.shape[0] // 2
    side = pay[:, channels:].astype(f32)
    low = side[half:]
    return side[:lanes] + side[half // 2 : half // 2 + lanes], low[:, :hid_count] + low[:, hid_count:]


def near_kernel(
    rows, shards, blocks, width, rank_ref, pair_ref, other_ref, pair_in_ref, middle_in_ref, spec_ref, weight_ref,
    rate_ref, front_ref, back_ref, trans_ref, featt_ref, slope_ref, conv_ref, corr_ref, ahead_ref, sums_ref, first_ref,
    fields, fast, high_ref, low_ref, acc_ref,
):
    rank = rank_ref[0]
    inner = jnp.logical_and(rank > 0, rank < shards - 1)
    count = shards - 1
    kinds = (None, None, None) + (ROWS,) * 4 + (CUBE, ROWS, ROWS)
    common = (
        rank_ref, front_ref, back_ref, pair_ref, other_ref, pair_in_ref, middle_in_ref, spec_ref, conv_ref, corr_ref,
        fields, fast,
    )

    @pl.when(jnp.logical_not(inner))
    def _():
        looped(functools.partial(edge_strip, rows, shards), kinds, blocks, width)(*common)

    @pl.when(inner)
    def _():
        acc_ref[...] = jnp.zeros_like(acc_ref)
        looped(
            functools.partial(inner_strip, rows, shards), kinds + (None, None, None) + (ROWS,) * 4, blocks, width
        )(*common, trans_ref, weight_ref, rate_ref, ahead_ref, sums_ref, high_ref, low_ref, acc_ref)
        first_ref[...] = exact_dot(
            featt_ref[:, : count * rows], acc_ref[...] * slope_ref[: count * rows, :]
        )


def edge_strip(
    rows, shards, block, blocks, rank_ref, front_ref, back_ref, pair_ref, other_ref, pair_in_ref, middle_in_ref,
    spec_ref, conv_ref, corr_ref, fields, fast,
):
    del middle_in_ref
    top = rank_ref[0] == shards - 1
    source, cotan = ordered(rank_ref[0] % 2 == 0, pair_ref[...], other_ref[...])
    for index, block_in in enumerate((source, cotan, pair_in_ref[...])):
        fields[index] = forward(front_ref, block_in)
    on_conv = jnp.where(top, 1.0, 0.0).astype(f32)
    on_corr = jnp.where(top, 0.0, 1.0).astype(f32)
    for re, im, sign in row_groups(rows):
        x0, c0, near = ((fields[i, re, :], fields[i, im, :]) for i in range(3))
        w0, w1 = ((spec_ref[i, re, :].astype(f32), spec_ref[i, im, :].astype(f32)) for i in range(2))
        values = (
            plus(times(w0, x0), scaled(times(w1, near), on_conv)),
            plus(conj_times(w0, c0), scaled(conj_times(w1, near), on_corr)),
        )
        for index, value in enumerate(values):
            fast[index, re, :] = value[0].astype(bf16)
            fast[index, im, :] = value[1].astype(bf16)
    conv_ref[...] = backward(back_ref, fast[0])
    corr_ref[...] = backward(back_ref, fast[1])


def inner_strip(
    rows, shards, block, blocks, rank_ref, front_ref, back_ref, pair_ref, other_ref, pair_in_ref, middle_in_ref,
    spec_ref, conv_ref, corr_ref, fields, fast, trans_ref, weight_ref, rate_ref, ahead_ref, sums_ref, high_ref, low_ref,
    acc_ref,
):
    lower = rank_ref[0] == 1
    upper = jnp.where(lower, 0.0, 1.0).astype(f32)
    side = jnp.where(lower, -1.0, 1.0).astype(f32)
    count = shards - 1
    blocks_in = (
        *ordered(lower, other_ref[...], pair_ref[...]), *ordered(lower, pair_in_ref[...], middle_in_ref[...])
    )
    for index, block_in in enumerate(blocks_in):
        fields[index] = forward(front_ref, block_in)
    for re, im, sign in row_groups(rows):
        x0, c0, x1, c1 = ((fields[i, re, :], fields[i, im, :]) for i in range(4))
        w0, w1, w2 = ((spec_ref[i, re, :].astype(f32), spec_ref[i, im, :].astype(f32)) for i in range(3))
        values = (
            plus(times(w0, x0), times(w1, x1)),
            plus(conj_times(w0, c0), conj_times(w1, c1)),
            times((w2[0], w2[1] * side), choose(lower, c1, x1)),
        )
        for index, value in enumerate(values):
            fast[index, re, :] = value[0].astype(bf16)
            fast[index, im, :] = value[1].astype(bf16)
        zero = conj_times(x0, c0)
        one = plus(conj_times(x1, c0), scaled(conj_times(x0, c1), upper))
        two = conj_times(x1, c1)
        for index, value in enumerate((plus(zero, turned(one, sign)), plus(one, turned(two, sign)), two)):
            for part, where in zip(value, (re, im)):
                high_ref[index, where, :], low_ref[index, where, :] = split(part)
    conv_ref[...] = backward(back_ref, fast[0])
    corr_ref[...] = backward(back_ref, fast[1])
    ahead_ref[...] = backward(back_ref, fast[2])
    rate = rate_ref[...]
    env = decay(rate, rows, float(rows * shards) ** -0.5)
    parts = []
    for lag in range(count):
        grad = backward(back_ref, high_ref[lag], low_ref[lag])
        parts.append(split(grad * (env * jnp.exp(rate * (-float(lag * rows))))))
    m_high = jnp.concatenate([p[0] for p in parts], axis=0)
    m_low = jnp.concatenate([p[1] for p in parts], axis=0)
    sums_ref[...] = weight_sums(trans_ref[:, : count * rows], m_high, m_low)
    acc_ref[...] += hidden_sums(m_high, m_low, *split(weight_ref[...]))


def only(inner, shards, rank_at, kernel):
    def run(*refs):
        rank = refs[rank_at][0]

        @pl.when(jnp.logical_and(rank > 0, rank < shards - 1) == inner)
        def _():
            kernel(*refs)

    return run


def far_kernel(rows, block, blocks, rank_ref, far_ref, spec_ref, front_ref, back_ref, ahead_ref, part_ref):
    side = jnp.where(rank_ref[0] == 2, 1.0, -1.0).astype(f32)
    far = forward(front_ref, far_ref[...])
    w3 = (spec_ref[0, :rows, :].astype(f32), spec_ref[0, rows:, :].astype(f32) * side)
    ahead = jnp.concatenate(times(w3, (far[:rows], far[rows:])), axis=0).astype(bf16)
    part_ref[...] = (ahead_ref[...] + backward(back_ref, ahead)).astype(bf16)


def late_kernel(rows, block, blocks, rank_ref, far_ref, spec_ref, front_ref, back_ref, late_ref):
    side = jnp.where(rank_ref[0] == 2, 1.0, -1.0).astype(f32)
    far = forward(front_ref, far_ref[...])
    w2 = (spec_ref[0, :rows, :].astype(f32), spec_ref[0, rows:, :].astype(f32) * side)
    late = jnp.concatenate(times(w2, (far[:rows], far[rows:])), axis=0).astype(bf16)
    late_ref[...] = backward(back_ref, late)


def last_kernel(
    rows, shards, channels, block, blocks, after_ref, rank_ref, near_ref, far_ref, weight_ref, rate_ref, front_ref, back_ref,
    trans_ref, featt_ref, slope_ref, sums_ref, first_ref, bias_ref, in_ref, pay_ref, total_ref, acc_ref,
):
    del after_ref
    hid_count, width = weight_ref.shape
    lower = rank_ref[0] == 1
    start = pl.multiple_of(block * width, width)
    here = sums_ref[...] + in_ref[:, pl.ds(start, width)].astype(f32)
    mine = (block < blocks // 2) == lower

    @pl.when(block == 0)
    def _():
        acc_ref[...] = jnp.zeros_like(acc_ref)

    @pl.when(mine)
    def _():
        sign = jnp.where(lower, 1.0, -1.0).astype(f32)
        near = forward(front_ref, near_ref[...])
        far = forward(front_ref, far_ref[...])
        three = conj_times((near[:rows], near[rows:]), (far[:rows], far[rows:]))
        three = (three[0], three[1] * sign)
        half = rows // 2
        two = jnp.concatenate([three[1][:half], -three[1][half:], -three[0][:half], three[0][half:]], axis=0)
        rate = rate_ref[...]
        env = decay(rate, rows, float(rows * shards) ** -0.5)
        parts = []
        for lag, value in ((shards - 2, two), (shards - 1, jnp.concatenate(three, axis=0))):
            grad = backward(back_ref, *split(value))
            parts.append(split(grad * (env * jnp.exp(rate * (-float(lag * rows))))))
        m_high = jnp.concatenate([p[0] for p in parts], axis=0)
        m_low = jnp.concatenate([p[1] for p in parts], axis=0)
        trans = trans_ref[:, (shards - 2) * rows :]
        pay_ref[:, pl.ds(start, width)] = (here + weight_sums(trans, m_high, m_low)).astype(bf16)
        w_high, w_low = split(weight_ref[...])
        acc_ref[...] += hidden_sums(m_high, m_low, w_high, w_low)

    @pl.when(jnp.logical_not(mine))
    def _():
        pay_ref[:, pl.ds(start, width)] = here.astype(bf16)

    @pl.when(block == blocks - 1)
    def _():
        first = exact_dot(
            featt_ref[:, (shards - 2) * rows :], acc_ref[...] * slope_ref[(shards - 2) * rows :, :]
        )
        lanes = channels // 128
        in_bias, in_first = get_side(in_ref[...], channels, lanes, hid_count)
        first = first + first_ref[...] + in_first
        put_side(pay_ref, channels, fold(bias_ref[...]) + in_bias)
        total_ref[...] = first


def total_kernel(channels, hid_count, part_ref, first_ref, late_ref, own_ref, come_ref, pay_ref):
    del part_ref, first_ref, late_ref
    lanes = channels // 128
    pay_ref[:, :channels] = (own_ref[:, :channels].astype(f32) + come_ref[:, :channels].astype(f32)).astype(bf16)
    own, come = (get_side(ref[...], channels, lanes, hid_count)[0] for ref in (own_ref, come_ref))
    put_side(pay_ref, channels, own + come)


def gates_kernel(inner, shards, blocks, width, before, *refs):
    refs = refs[before:]
    inputs, outs, held, sems = refs[:10], refs[10:13], refs[13:16], refs[16]

    def leaving(block, i):
        cols = pl.ds(pl.multiple_of(block * width, width), width)
        return pltpu.make_async_copy(held[i].at[:, cols], outs[i].at[:, cols], sems.at[block, i])

    def strip(block, blocks, *views):
        gates_strip(inner, shards, *views)
        for i in range(3):
            leaving(block, i).start()

    looped(strip, (None,) + (ROWS,) * 12, blocks, width)(*inputs, *held)
    for block in range(blocks):
        for i in range(3):
            leaving(block, i).wait()


def gates_strip(
    inner, shards, rank_ref, one_ref, two_ref, val_ref, out_ref, skip_ref, conv_ref, corr_ref, late_ref, part_ref,
    grad_one_ref, grad_two_ref, grad_value_ref,
):
    late = late_ref[...] if inner else part_ref[...].astype(f32)
    upper = rank_ref[0] >= shards // 2
    zero = jnp.zeros_like(late)
    one = one_ref[...].astype(f32)
    val = val_ref[...].astype(f32)
    out = out_ref[...].astype(f32)
    skip = skip_ref[...]
    conv = conv_ref[...] + jnp.where(upper, late, zero)
    corr = corr_ref[...] + jnp.where(upper, zero, late)
    grad_two_ref[...] = (out * (conv + skip * (one * val))).astype(bf16)
    mid = corr + skip * (out * two_ref[...].astype(f32))
    grad_one_ref[...] = (mid * val).astype(bf16)
    grad_value_ref[...] = (mid * one).astype(bf16)


def finish_kernel(
    channels, shards, rank_ref, own_ref, come_ref, first_ref, first_come_ref, second_out, first_out, bias_out, second,
    first, bias, sems,
):
    rank = rank_ref[0]
    inner = jnp.logical_and(rank > 0, rank < shards - 1)
    lanes = channels // 128
    copies = [
        pltpu.make_async_copy(held, out, sems.at[i])
        for i, (held, out) in enumerate(((second, second_out), (first, first_out), (bias, bias_out)))
    ]
    picked = jnp.where(inner, own_ref[...], come_ref[...])
    second[...] = picked[:, :channels].astype(f32)
    copies[0].start()
    first[...] = jnp.where(inner, first_ref[...], first_come_ref[...])
    copies[1].start()
    rows = get_side(picked, channels, lanes, first.shape[1])[0]
    for i in range(lanes):
        bias[:, i * 128 : (i + 1) * 128] = rows[i : i + 1]
    copies[2].start()
    for copy in copies:
        copy.wait()


def few_shards_body(
    x_one, x_two, values, grad_out, first_weight, second_weight, skip_bias, decay_rate
):
    rows, channels = x_one.shape
    shards = lax.axis_size("ctx")
    feat_count, hid_count = first_weight.shape
    seq_len = rows * shards
    double = 2 * rows
    width = min(512, channels)
    blocks = channels // width
    rank = lax.axis_index("ctx").astype(jnp.int32).reshape(1)
    front, back = block_tables(rows)
    feats = feature_table(seq_len)
    featt = np.ascontiguousarray(feats.T)
    skip_row = skip_bias.reshape(1, channels)
    rate_row = decay_rate.reshape(1, channels)
    smem = pl.BlockSpec(memory_space=pltpu.SMEM)
    vmem = pl.BlockSpec(memory_space=pltpu.VMEM)
    anywhere = pl.BlockSpec(memory_space=pl.ANY)
    mebi = 1024 * 1024

    def shape(*dims, dtype=f32):
        return jax.ShapeDtypeStruct(dims, dtype)

    def call(kernel, name, units, out_shape, in_specs, out_specs=None, scratch=(), limit=16, aliases={}):
        return pl.pallas_call(
            kernel,
            in_specs=in_specs,
            out_specs=out_specs if out_specs is not None else [vmem] * len(out_shape),
            out_shape=out_shape,
            scratch_shapes=scratch,
            input_output_aliases=aliases,
            compiler_params=pltpu.CompilerParams(vmem_limit_bytes=limit * mebi),
            cost_estimate=pl.CostEstimate(
                flops=2 * units * double * double * channels, bytes_accessed=rows * channels, transcendentals=0
            ),
            name=name,
        )

    def move(array, pairs):
        return lax.ppermute(array, "ctx", pairs)

    inward = [(0, 1), (shards - 1, shards - 2)]
    outward = [(1, 0), (shards - 2, shards - 1)]
    across = [(1, 2), (2, 1)]
    alone = [(0, 0), (shards - 1, shards - 1)]
    pay_shape = (hid_count, channels + SIDE)
    block_bf16 = shape(rows, channels, dtype=bf16)
    block_f32 = shape(rows, channels)

    row_step = max(rows // 2, 16)
    gate_rows = pl.BlockSpec((row_step, channels), lambda i: (i, 0))
    pair, other, edge, bias = pl.pallas_call(
        products_kernel,
        grid=(rows // row_step,),
        in_specs=[smem] + [gate_rows] * 4,
        out_specs=[gate_rows] * 3 + [pl.BlockSpec((1, channels), lambda i: (0, 0))],
        out_shape=[block_bf16] * 3 + [shape(1, channels)],
        compiler_params=pltpu.CompilerParams(vmem_limit_bytes=64 * mebi),
        name="products",
    )(rank, x_one, x_two, values, grad_out)
    pair_in = move(pair, inward + outward)
    middle_in = move(other, across)

    own_shapes = [
        shape(rows, feat_count), shape(feat_count, hid_count), block_bf16, block_bf16, shape(hid_count, channels),
        shape(1, channels), shape(double, double, dtype=bf16), shape(double, double, dtype=bf16),
        shape(feat_count, seq_len), shape(1, channels), shape(*pay_shape, dtype=bf16),
    ]
    (send,) = call(
        only(False, shards, 0, functools.partial(own_kernel, rows, shards, channels, blocks, width)), "own_pair", 8,
        [shape(*pay_shape, dtype=bf16)],
        [smem] + [anywhere] * 10,
        out_specs=[anywhere],
        scratch=[pltpu.VMEM(s.shape, s.dtype) for s in own_shapes]
        + [
            pltpu.VMEM((2 * hid_count, rows), bf16), pltpu.VMEM((rows, hid_count), f32),
            pltpu.SemaphoreType.DMA((10,)), pltpu.SemaphoreType.DMA,
        ],
        limit=60,
    )(rank, feats[:rows], first_weight, pair, other, second_weight, rate_row, front, back, featt, bias)
    come = move(send, inward)
    late_feats, _ = lax.optimization_barrier((jnp.asarray(feats), send))
    spec, trans, slope = call(
        functools.partial(filters_kernel, rows, shards, blocks, width), "filters", 8,
        [
            shape(shards, double, channels, dtype=bf16), shape(2 * hid_count, seq_len, dtype=bf16),
            shape(seq_len, hid_count),
        ],
        [vmem] * 5,
        scratch=[pltpu.VMEM((seq_len, 3 * hid_count), bf16)],
    )(late_feats, first_weight, second_weight, rate_row, front)

    edge, _ = lax.optimization_barrier((edge, slope))
    far = move(edge, [(0, 2), (shards - 1, shards - 3)])
    conv, corr, ahead, sums, first = call(
        functools.partial(near_kernel, rows, shards, blocks, width), "near_blocks", 20,
        [block_f32] * 3 + [shape(hid_count, channels), shape(feat_count, hid_count)],
        [smem] + [vmem] * 12,
        scratch=[
            pltpu.VMEM((4, double, width), f32),
            pltpu.VMEM((3, double, width), bf16),
            pltpu.VMEM((shards - 1, double, width), bf16),
            pltpu.VMEM((shards - 1, double, width), bf16),
            pltpu.VMEM(((shards - 1) * rows, hid_count), f32),
        ],
    )(rank, pair, other, pair_in, middle_in, spec, second_weight, rate_row, front, back, trans, featt, slope)

    (part,) = call(
        only(
            True, shards, 0,
            looped(
                functools.partial(far_kernel, rows),
                (None, ROWS, (slice(3, 4), slice(None)), None, None, ROWS, ROWS),
                blocks, width,
            ),
        ),
        "far_block", 1,
        [block_bf16],
        [smem] + [vmem] * 5,
    )(rank, far, spec, front, back, ahead)
    (late,) = call(
        only(
            True, shards, 0,
            looped(
                functools.partial(late_kernel, rows),
                (None, ROWS, (slice(2, 3), slice(None)), None, None, ROWS),
                blocks, width,
            ),
        ),
        "late_block", 1,
        [block_f32],
        [smem] + [vmem] * 4,
    )(rank, far, spec, front, back)
    part_come = move(part, outward)

    pay, first = call(
        only(
            True, shards, 1,
            looped(
                functools.partial(last_kernel, rows, shards, channels),
                (None, None, ROWS, ROWS, ROWS, ROWS, None, None, None, None, None, ROWS),
                blocks, width,
            ),
        ),
        "last_pair", 1,
        [shape(*pay_shape, dtype=bf16), shape(feat_count, hid_count)],
        [anywhere, smem] + [vmem] * 13,
        scratch=[pltpu.VMEM((2 * rows, hid_count), f32)],
    )(part, rank, pair_in, far, second_weight, rate_row, front, back, trans, featt, slope, sums, first, bias, come)
    pay_come = move(pay, across + alone)
    group = lax.axis_size(("ch", "sub"))
    bit = 1
    while bit < group:
        first = first + lax.ppermute(first, ("ch", "sub"), [(i, i ^ bit) for i in range(group)])
        bit *= 2

    (total,) = call(
        functools.partial(total_kernel, channels, hid_count), "total", 0,
        [shape(*pay_shape, dtype=bf16)],
        [anywhere] * 3 + [vmem] * 2,
    )(part_come, first, late, pay, pay_come)
    total_come = move(total, inward + outward)

    def gates(inner, *before):
        return call(
            only(
                inner, shards, len(before),
                functools.partial(gates_kernel, inner, shards, blocks, width, len(before)),
            ),
            "gates", 0,
            [block_bf16] * 3,
            [anywhere] * len(before) + [smem] + [vmem] * 9,
            out_specs=[anywhere] * 3,
            scratch=[pltpu.VMEM((rows, channels), bf16)] * 3 + [pltpu.SemaphoreType.DMA((blocks, 3))],
            aliases={i: i for i in range(3)} if inner else {},
        )(*before, rank, x_one, x_two, values, grad_out, skip_row, conv, corr, late, part_come)

    grads = gates(False, total)
    first, _ = lax.optimization_barrier((first, grads[0]))
    first = first + move(first, across + alone)
    first_come = move(first, inward + outward)
    grad_one, grad_two, grad_value = gates(True, *grads)

    outs = [shape(hid_count, channels), shape(feat_count, hid_count), shape(1, channels)]
    grad_second, grad_first, grad_bias = call(
        functools.partial(finish_kernel, channels, shards), "finish", 0,
        outs,
        [smem] + [vmem] * 4,
        out_specs=[anywhere] * 3,
        scratch=[pltpu.VMEM(o.shape, f32) for o in outs] + [pltpu.SemaphoreType.DMA((3,))],
    )(rank, total, total_come, first, first_come)
    return (grad_one, grad_two, grad_value, grad_first, grad_second, grad_bias.reshape(channels))


def solution(mesh):
    in_specs = (
        P(("parts", "ctx"), ("ch", "sub")),
        P(("parts", "ctx"), ("ch", "sub")),
        P(("parts", "ctx"), ("ch", "sub")),
        P(("parts", "ctx"), ("ch", "sub")),
        P(),
        P(None, ("ch", "sub")),
        P(("ch", "sub")),
        P(("ch", "sub")),
    )
    out_specs = (
        P(("parts", "ctx"), ("ch", "sub")),
        P(("parts", "ctx"), ("ch", "sub")),
        P(("parts", "ctx"), ("ch", "sub")),
        P("parts", None),
        P("parts", ("ch", "sub")),
        P(("parts", "ch", "sub")),
    )
    body = few_shards_body if mesh.shape["ctx"] == 4 else many_shards_body
    return jax.shard_map(body, mesh=mesh, in_specs=in_specs, out_specs=out_specs, check_vma=False)
```

```python
import functools
import math

import jax
import jax.numpy as jnp
import numpy as np
from jax import lax
from jax.experimental import pallas as pl
from jax.experimental.pallas import tpu as pltpu
from jax.sharding import PartitionSpec as P

band_steps = (1763, 1201, 811, 547, 367, 251, 167, 113, 79, 53, 37, 23, 17, 11, 7, 3)
highest = lax.Precision.HIGHEST
f32 = jnp.float32
bf16 = jnp.bfloat16


def features(positions):
    multiplier = jnp.array(band_steps, dtype=jnp.int32)
    phase = positions[:, None] * multiplier[None, :] % 4096
    angle = phase.astype(jnp.float32) * (2.0 * math.pi / 4096.0)
    return jnp.concatenate([jnp.cos(angle), jnp.sin(angle)], axis=1)


def tables(out_count, in_count, modulus, sign_value):
    row_index = lax.broadcasted_iota(jnp.int32, (out_count, in_count), 0)
    col_index = lax.broadcasted_iota(jnp.int32, (out_count, in_count), 1)
    angle = (row_index * col_index % modulus).astype(jnp.float32) * (2.0 * math.pi / modulus)
    return (jnp.cos(angle), sign_value * jnp.sin(angle))


def twiddle(spec_re, spec_im, freq_count, span, modulus, sign_value):
    freq_index = lax.broadcasted_iota(jnp.int32, (freq_count, span), 0)
    pos_index = lax.broadcasted_iota(jnp.int32, (freq_count, span), 1)
    angle = (freq_index * pos_index % modulus).astype(jnp.float32) * (2.0 * math.pi / modulus)
    factor_re = jnp.cos(angle)[None, None, :, :]
    factor_im = (sign_value * jnp.sin(angle))[None, None, :, :]
    return (spec_re * factor_re - spec_im * factor_im, spec_re * factor_im + spec_im * factor_re)


def contract(kernel, array):
    return jnp.einsum(
        "lj,mckj->mckl", kernel, array, precision=highest, preferred_element_type=jnp.float32
    )


def along_positions(spec_re, spec_im, kernel_re, kernel_im):
    return (
        contract(kernel_re, spec_re) - contract(kernel_im, spec_im),
        contract(kernel_re, spec_im) + contract(kernel_im, spec_re),
    )


def many_shards_body(
    x_one, x_two, values, grad_out, first_weight, second_weight, skip_bias, decay_rate
):
    row_count, chan_count = x_one.shape
    shards = lax.axis_size("ctx")
    rank = lax.axis_index("ctx")
    seq_len = row_count * shards
    total = 2 * seq_len
    narrow = chan_count // shards
    chan_weight = lax.dynamic_slice_in_dim(second_weight, rank * narrow, narrow, 1)
    chan_rate = lax.dynamic_slice_in_dim(decay_rate, rank * narrow, narrow, 0)
    source = x_one.astype(jnp.float32) * values.astype(jnp.float32)
    cotan = grad_out.astype(jnp.float32) * x_two.astype(jnp.float32)
    spread = lax.all_to_all(
        jnp.stack([source.T, cotan.T])[:, :, None, :],
        "ctx",
        split_axis=1,
        concat_axis=2,
        tiled=True,
    )
    far_source = spread[0]
    far_cotan = spread[1]
    positions = jnp.arange(seq_len, dtype=jnp.int32)
    feats = features(positions)
    pre_act = jnp.dot(feats, first_weight, precision=highest, preferred_element_type=jnp.float32)
    hidden = jnp.sin(pre_act)
    envelope = jnp.exp(-chan_rate[:, None] * positions.astype(jnp.float32)[None, :]) * float(
        seq_len
    ) ** (-0.5)
    filt = (
        jnp.einsum(
            "th,hc->ct", hidden, chan_weight, precision=highest, preferred_element_type=jnp.float32
        )
        * envelope
    )
    filt_blocks = filt.reshape(narrow, shards, row_count)
    fields = jnp.stack([far_source, far_cotan])

    def first_section(kernel):
        field_part = jnp.einsum(
            "kn,mcnj->mckj", kernel, fields, precision=highest, preferred_element_type=jnp.float32
        )
        filter_part = jnp.einsum(
            "kn,cnj->ckj",
            kernel,
            filt_blocks,
            precision=highest,
            preferred_element_type=jnp.float32,
        )
        return jnp.concatenate([field_part, filter_part[None]], axis=0)

    first_re, first_im = tables(2 * shards, shards, 2 * shards, -1.0)
    spec_re, spec_im = (first_section(first_re), first_section(first_im))
    spec_re, spec_im = twiddle(spec_re, spec_im, 2 * shards, row_count, total, -1.0)
    fwd_re, fwd_im = tables(row_count, row_count, row_count, -1.0)
    spec_re, spec_im = along_positions(spec_re, spec_im, fwd_re, fwd_im)
    source_re, source_im = (spec_re[0], spec_im[0])
    cotan_re, cotan_im = (spec_re[1], spec_im[1])
    filter_re, filter_im = (spec_re[2], spec_im[2])
    prod_re = jnp.stack(
        [
            source_re * filter_re - source_im * filter_im,
            cotan_re * filter_re + cotan_im * filter_im,
            cotan_re * source_re + cotan_im * source_im,
        ]
    )
    prod_im = jnp.stack(
        [
            source_re * filter_im + source_im * filter_re,
            cotan_im * filter_re - cotan_re * filter_im,
            cotan_im * source_re - cotan_re * source_im,
        ]
    )
    back_re, back_im = tables(row_count, row_count, row_count, 1.0)
    prod_re, prod_im = along_positions(prod_re, prod_im, back_re, back_im)
    prod_re, prod_im = twiddle(prod_re, prod_im, 2 * shards, row_count, total, 1.0)
    last_re, last_im = tables(shards, 2 * shards, 2 * shards, 1.0)
    field_out = jnp.einsum(
        "nk,mckj->mcnj", last_re, prod_re[:2], precision=highest, preferred_element_type=jnp.float32
    ) - jnp.einsum(
        "nk,mckj->mcnj", last_im, prod_im[:2], precision=highest, preferred_element_type=jnp.float32
    )
    field_out = field_out * (1.0 / total)
    filt_grad = jnp.einsum(
        "nk,ckj->cnj", last_re, prod_re[2], precision=highest, preferred_element_type=jnp.float32
    ) - jnp.einsum(
        "nk,ckj->cnj", last_im, prod_im[2], precision=highest, preferred_element_type=jnp.float32
    )
    filt_grad = (filt_grad * (1.0 / total)).reshape(narrow, seq_len)
    modulated = filt_grad * envelope
    weight_part = jnp.einsum(
        "th,ct->hc", hidden, modulated, precision=highest, preferred_element_type=jnp.float32
    )
    hidden_grad = jnp.einsum(
        "ct,hc->th", modulated, chan_weight, precision=highest, preferred_element_type=jnp.float32
    )
    first_part = jnp.dot(
        feats.T,
        hidden_grad * jnp.cos(pre_act),
        precision=highest,
        preferred_element_type=jnp.float32,
    )
    grad_first = lax.psum(first_part, ("ctx", "ch", "sub"))
    returned = lax.all_to_all(
        field_out.astype(jnp.bfloat16), "ctx", split_axis=2, concat_axis=1, tiled=True
    ).astype(field_out.dtype)
    conv_part = returned[0, :, 0, :].T
    corr_part = returned[1, :, 0, :].T
    grad_two = (grad_out.astype(jnp.float32) * (conv_part + skip_bias[None, :] * source)).astype(
        jnp.bfloat16
    )
    grad_mid = corr_part + skip_bias[None, :] * cotan
    grad_one = (grad_mid * values.astype(jnp.float32)).astype(jnp.bfloat16)
    grad_value = (grad_mid * x_one.astype(jnp.float32)).astype(jnp.bfloat16)
    grad_bias = lax.psum(jnp.sum(source * cotan, axis=0), "ctx")
    grad_second = lax.all_gather(weight_part, "ctx", axis=1, tiled=True)
    return (grad_one, grad_two, grad_value, grad_first, grad_second, grad_bias)


STEP = 16
SIDE = 128


def halves(array):
    array = np.asarray(array, np.float32)
    high = array.astype(bf16)
    low = (array - high.astype(np.float32)).astype(bf16)
    return high, low


def block_tables(rows):
    freq = np.concatenate([np.arange(0, rows, 2), np.arange(1, rows, 2)])
    phase = (2 * freq + 1)[:, None] * np.arange(rows)[None, :] % (4 * rows)
    angle = phase * (2.0 * np.pi / (4 * rows))
    forward = np.concatenate([np.cos(angle), -np.sin(angle)], axis=0)
    front = np.ascontiguousarray(np.concatenate(halves(forward), axis=1))
    back = np.ascontiguousarray(np.concatenate(halves(forward.T / rows), axis=0))
    return front, back


def feature_table(seq_len):
    phase = np.arange(seq_len)[:, None] * np.array(band_steps)[None, :] % 4096
    angle = phase * (2.0 * np.pi / 4096.0)
    return np.concatenate([np.cos(angle), np.sin(angle)], axis=1).astype(np.float32)


def split(array):
    high = array.astype(bf16)
    return high, (array - high.astype(f32)).astype(bf16)


def dot(left, right):
    return jnp.dot(left, right, preferred_element_type=f32)


def exact_dot(left, right):
    return jnp.dot(left, right, precision=highest, preferred_element_type=f32)


def dot_across(left, right):
    return lax.dot_general(left, right, (((1,), (1,)), ((), ())), preferred_element_type=f32)


def decay(rate, rows, scale):
    place = lax.broadcasted_iota(jnp.int32, (rows, rate.shape[1]), 0)
    return jnp.exp(-place.astype(f32) * rate) * scale


def times(a, b):
    return a[0] * b[0] - a[1] * b[1], a[0] * b[1] + a[1] * b[0]


def conj_times(a, b):
    return a[0] * b[0] + a[1] * b[1], a[0] * b[1] - a[1] * b[0]


def plus(a, b):
    return a[0] + b[0], a[1] + b[1]


def scaled(a, factor):
    return a[0] * factor, a[1] * factor


def choose(condition, a, b):
    return jnp.where(condition, a[0], b[0]), jnp.where(condition, a[1], b[1])


def turned(a, sign):
    return (a[1], -a[0]) if sign > 0 else (-a[1], a[0])


def forward(front_ref, block):
    return dot(front_ref[...], jnp.concatenate([block, block], axis=0))


def backward(back_ref, high, low=None):
    both = dot(back_ref[...], high)
    rows = both.shape[0] // 2
    out = both[:rows] + both[rows:]
    return out if low is None else out + dot(back_ref[:rows], low)


def row_groups(rows):
    for step in range(rows // STEP):
        sign = 1 if step * STEP < rows // 2 else -1
        yield slice(step * STEP, (step + 1) * STEP), slice(rows + step * STEP, rows + (step + 1) * STEP), sign


def weight_sums(trans, m_high, m_low):
    both = dot(trans, m_high)
    count = both.shape[0] // 2
    return both[:count] + both[count:] + dot(trans[:count], m_low)


def hidden_sums(m_high, m_low, w_high, w_low):
    left = jnp.concatenate([m_high, m_high, m_low], axis=1)
    right = jnp.concatenate([w_high, w_low, w_high], axis=1)
    return dot_across(left, right)


def looped(kernel, kinds, blocks, width):
    def over_strips(*refs):
        def step(block, carry):
            cols = pl.ds(pl.multiple_of(block * width, width), width)
            views = [
                ref if kind is None else ref.at[(*kind, cols)]
                for ref, kind in zip(refs, kinds + (None,) * (len(refs) - len(kinds)))
            ]
            kernel(block, blocks, *views)
            return carry

        lax.fori_loop(0, blocks, step, 0)

    return over_strips


ROWS = (slice(None),)
CUBE = (slice(None), slice(None))


def products_kernel(rank_ref, one_ref, two_ref, val_ref, out_ref, pair_ref, other_ref, edge_ref, bias_ref):
    source = one_ref[...].astype(f32) * val_ref[...].astype(f32)
    cotan = out_ref[...].astype(f32) * two_ref[...].astype(f32)
    even = rank_ref[0] % 2 == 0
    pair_ref[...] = jnp.where(even, source, cotan).astype(bf16)
    edge_ref[...] = pair_ref[...]
    other_ref[...] = jnp.where(even, cotan, source).astype(bf16)
    part = jnp.sum(source * cotan, axis=0, keepdims=True)

    @pl.when(pl.program_id(0) == 0)
    def _():
        bias_ref[...] = part

    @pl.when(pl.program_id(0) > 0)
    def _():
        bias_ref[...] += part


def ordered(first, a, b):
    return (jnp.where(first, a, b), jnp.where(first, b, a))


def sin_cos(angle):
    turns = jnp.floor(angle * (2.0 / math.pi) + 0.5)
    rest = ((angle - turns * 1.5703125) - turns * 4.837512969970703e-4) - turns * 7.54978995489188e-8
    square = rest * rest
    sine = rest + rest * square * (
        -1.6666654611e-1 + square * (8.3321608736e-3 + square * -1.9515295891e-4)
    )
    cosine = 1.0 - 0.5 * square + square * square * (
        4.166664568298827e-2 + square * (-1.388731625493765e-3 + square * 2.443315711809948e-5)
    )
    quarter = turns.astype(jnp.int32)
    odd = (quarter & 1) == 1
    sin_sign = jnp.where((quarter & 2) == 2, -1.0, 1.0).astype(f32)
    cos_sign = jnp.where(((quarter + 1) & 2) == 2, -1.0, 1.0).astype(f32)
    return jnp.where(odd, cosine, sine) * sin_sign, jnp.where(odd, sine, cosine) * cos_sign


def turned_over(hidden, slope):
    both = jnp.concatenate([hidden, slope], axis=1).T
    return jnp.concatenate(split(both[: hidden.shape[1]]), axis=0)


def filters_kernel(
    rows, shards, blocks, width, feats_ref, first_ref, weight_ref, rate_ref, front_ref, spec_ref, trans_ref, slope_ref,
    hid_ref,
):
    hidden, slope = sin_cos(exact_dot(feats_ref[...], first_ref[...]))
    slope_ref[...] = slope
    high, low = split(hidden)
    hid_ref[...] = jnp.concatenate([high, high, low], axis=1)
    trans_ref[...] = turned_over(hidden, slope)
    strips = looped(
        functools.partial(filter_strip, rows, shards), (None, ROWS, ROWS, None, CUBE), blocks, width
    )
    strips(hid_ref, weight_ref, rate_ref, front_ref, spec_ref)


def filter_strip(rows, shards, block, blocks, hid_ref, weight_ref, rate_ref, front_ref, spec_ref):
    scale = float(rows * shards) ** -0.5
    w_high, w_low = split(weight_ref[...])
    stacked = jnp.concatenate([w_high, w_low, w_high], axis=0)
    rate = rate_ref[...]
    env = decay(rate, rows, scale)
    before = None
    for lag in range(shards):
        part = dot(hid_ref[lag * rows : (lag + 1) * rows, :], stacked)
        part = part * (env * jnp.exp(rate * (-float(lag * rows))))
        f_high, f_low = split(part)
        now = forward(front_ref, f_high) + dot(front_ref[:, :rows], f_low)
        for re, im, sign in row_groups(rows):
            here = (now[re], now[im])
            if before is not None:
                here = plus(here, turned((before[re], before[im]), -sign))
            spec_ref[lag, re, :] = here[0].astype(bf16)
            spec_ref[lag, im, :] = here[1].astype(bf16)
        before = now


def own_kernel(rows, shards, channels, blocks, width, rank_ref, *refs):
    inputs, send_out, held = refs[:10], refs[10], refs[11:21]
    send_ref, trans_ref, acc_ref, sems, out_sem = refs[21:]
    (
        feats_ref, first_ref, pair_ref, other_ref, weight_ref, rate_ref, front_ref, back_ref, featt_ref, bias_ref
    ) = held
    copies = [pltpu.make_async_copy(far, near, sems.at[i]) for i, (far, near) in enumerate(zip(inputs, held))]
    for copy in copies:
        copy.start()
    acc_ref[...] = jnp.zeros_like(acc_ref)
    copies[0].wait()
    copies[1].wait()
    hidden, slope = sin_cos(exact_dot(feats_ref[...], first_ref[...]))
    trans_ref[...] = turned_over(hidden, slope)
    for copy in copies[2:]:
        copy.wait()
    kinds = (None, ROWS, ROWS, ROWS, ROWS, None, None, None, ROWS, None)
    looped(functools.partial(own_strip, rows, shards), kinds, blocks, width)(
        rank_ref, pair_ref, other_ref, weight_ref, rate_ref, front_ref, back_ref, trans_ref, send_ref, acc_ref
    )
    first = exact_dot(featt_ref[:, :rows], acc_ref[...] * slope)
    put_side(send_ref, channels, fold(bias_ref[...]), first)
    last = pltpu.make_async_copy(send_ref, send_out, out_sem)
    last.start()
    last.wait()


def own_strip(
    rows, shards, block, blocks, rank_ref, pair_ref, other_ref, weight_ref, rate_ref, front_ref, back_ref, trans_ref,
    send_ref, acc_ref,
):
    source, cotan = ordered(rank_ref[0] % 2 == 0, pair_ref[...], other_ref[...])
    x0 = forward(front_ref, source)
    c0 = forward(front_ref, cotan)
    pair = conj_times((x0[:rows], x0[rows:]), (c0[:rows], c0[rows:]))
    high, low = split(jnp.concatenate(pair, axis=0))
    env = decay(rate_ref[...], rows, float(rows * shards) ** -0.5)
    m_high, m_low = split(backward(back_ref, high, low) * env)
    send_ref[...] = weight_sums(trans_ref[...], m_high, m_low).astype(bf16)
    acc_ref[...] += hidden_sums(m_high, m_low, *split(weight_ref[...]))


def fold(bias):
    return jnp.concatenate([bias[:, i * 128 : (i + 1) * 128] for i in range(bias.shape[1] // 128)], axis=0)


def put_side(pay_ref, channels, bias, first=None):
    half = pay_ref.shape[0] // 2
    pay_ref[:, channels:] = jnp.zeros((2 * half, SIDE), bf16)
    for start, part in zip((0, half // 2), split(bias)):
        pay_ref[start : start + bias.shape[0], channels:] = part
    if first is not None:
        pay_ref[half:, channels:] = jnp.concatenate(split(first), axis=1)


def get_side(pay, channels, lanes, hid_count):
    half = pay.shape[0] // 2
    side = pay[:, channels:].astype(f32)
    low = side[half:]
    return side[:lanes] + side[half // 2 : half // 2 + lanes], low[:, :hid_count] + low[:, hid_count:]


def near_kernel(
    rows, shards, blocks, width, rank_ref, pair_ref, other_ref, pair_in_ref, middle_in_ref, spec_ref, weight_ref,
    rate_ref, front_ref, back_ref, trans_ref, featt_ref, slope_ref, conv_ref, corr_ref, ahead_ref, sums_ref, first_ref,
    near_ref, fields, fast, high_ref, low_ref, acc_ref,
):
    rank = rank_ref[0]
    inner = jnp.logical_and(rank > 0, rank < shards - 1)
    count = shards - 1
    kinds = (None, None, None) + (ROWS,) * 4 + (CUBE, ROWS, ROWS)
    common = (
        rank_ref, front_ref, back_ref, pair_ref, other_ref, pair_in_ref, middle_in_ref, spec_ref, conv_ref, corr_ref,
        fields, fast,
    )

    @pl.when(jnp.logical_not(inner))
    def _():
        looped(functools.partial(edge_strip, rows, shards), kinds, blocks, width)(*common)

    @pl.when(inner)
    def _():
        acc_ref[...] = jnp.zeros_like(acc_ref)
        looped(
            functools.partial(inner_strip, rows, shards), kinds + (None,) * 3 + (ROWS,) * 5, blocks, width
        )(*common, trans_ref, weight_ref, rate_ref, ahead_ref, sums_ref, near_ref, high_ref, low_ref, acc_ref)
        first_ref[...] = exact_dot(
            featt_ref[:, : count * rows], acc_ref[...] * slope_ref[: count * rows, :]
        )


def edge_strip(
    rows, shards, block, blocks, rank_ref, front_ref, back_ref, pair_ref, other_ref, pair_in_ref, middle_in_ref,
    spec_ref, conv_ref, corr_ref, fields, fast,
):
    del middle_in_ref
    top = rank_ref[0] == shards - 1
    source, cotan = ordered(rank_ref[0] % 2 == 0, pair_ref[...], other_ref[...])
    for index, block_in in enumerate((source, cotan, pair_in_ref[...])):
        fields[index] = forward(front_ref, block_in)
    on_conv = jnp.where(top, 1.0, 0.0).astype(f32)
    on_corr = jnp.where(top, 0.0, 1.0).astype(f32)
    for re, im, sign in row_groups(rows):
        x0, c0, near = ((fields[i, re, :], fields[i, im, :]) for i in range(3))
        w0, w1 = ((spec_ref[i, re, :].astype(f32), spec_ref[i, im, :].astype(f32)) for i in range(2))
        values = (
            plus(times(w0, x0), scaled(times(w1, near), on_conv)),
            plus(conj_times(w0, c0), scaled(conj_times(w1, near), on_corr)),
        )
        for index, value in enumerate(values):
            fast[index, re, :] = value[0].astype(bf16)
            fast[index, im, :] = value[1].astype(bf16)
    conv_ref[...] = backward(back_ref, fast[0])
    corr_ref[...] = backward(back_ref, fast[1])


def inner_strip(
    rows, shards, block, blocks, rank_ref, front_ref, back_ref, pair_ref, other_ref, pair_in_ref, middle_in_ref,
    spec_ref, conv_ref, corr_ref, fields, fast, trans_ref, weight_ref, rate_ref, ahead_ref, sums_ref, near_ref, high_ref,
    low_ref, acc_ref,
):
    lower = rank_ref[0] == 1
    upper = jnp.where(lower, 0.0, 1.0).astype(f32)
    side = jnp.where(lower, -1.0, 1.0).astype(f32)
    count = shards - 1
    blocks_in = (
        *ordered(lower, other_ref[...], pair_ref[...]), *ordered(lower, pair_in_ref[...], middle_in_ref[...])
    )
    for index, block_in in enumerate(blocks_in):
        fields[index] = forward(front_ref, block_in)
    for re, im, sign in row_groups(rows):
        x0, c0, x1, c1 = ((fields[i, re, :], fields[i, im, :]) for i in range(4))
        w0, w1, w2 = ((spec_ref[i, re, :].astype(f32), spec_ref[i, im, :].astype(f32)) for i in range(3))
        values = (
            plus(times(w0, x0), times(w1, x1)),
            plus(conj_times(w0, c0), conj_times(w1, c1)),
            times((w2[0], w2[1] * side), choose(lower, c1, x1)),
        )
        for index, value in enumerate(values):
            fast[index, re, :] = value[0].astype(bf16)
            fast[index, im, :] = value[1].astype(bf16)
        near_ref[re, :], near_ref[im, :] = choose(lower, x1, c1)
        zero = conj_times(x0, c0)
        one = plus(conj_times(x1, c0), scaled(conj_times(x0, c1), upper))
        two = conj_times(x1, c1)
        for index, value in enumerate((plus(zero, turned(one, sign)), plus(one, turned(two, sign)), two)):
            for part, where in zip(value, (re, im)):
                high_ref[index, where, :], low_ref[index, where, :] = split(part)
    conv_ref[...] = backward(back_ref, fast[0])
    corr_ref[...] = backward(back_ref, fast[1])
    ahead_ref[...] = backward(back_ref, fast[2])
    rate = rate_ref[...]
    env = decay(rate, rows, float(rows * shards) ** -0.5)
    parts = []
    for lag in range(count):
        grad = backward(back_ref, high_ref[lag], low_ref[lag])
        parts.append(split(grad * (env * jnp.exp(rate * (-float(lag * rows))))))
    m_high = jnp.concatenate([p[0] for p in parts], axis=0)
    m_low = jnp.concatenate([p[1] for p in parts], axis=0)
    sums_ref[...] = weight_sums(trans_ref[:, : count * rows], m_high, m_low)
    acc_ref[...] += hidden_sums(m_high, m_low, *split(weight_ref[...]))


def only(inner, shards, rank_at, kernel):
    def run(*refs):
        rank = refs[rank_at][0]

        @pl.when(jnp.logical_and(rank > 0, rank < shards - 1) == inner)
        def _():
            kernel(*refs)

    return run


def far_kernel(
    rows, block, blocks, rank_ref, far_ref, spec_ref, front_ref, back_ref, ahead_ref, part_ref, far_spec_ref
):
    side = jnp.where(rank_ref[0] == 2, 1.0, -1.0).astype(f32)
    far = forward(front_ref, far_ref[...])
    far_spec_ref[...] = far
    w3 = (spec_ref[0, :rows, :].astype(f32), spec_ref[0, rows:, :].astype(f32) * side)
    ahead = jnp.concatenate(times(w3, (far[:rows], far[rows:])), axis=0).astype(bf16)
    part_ref[...] = (ahead_ref[...] + backward(back_ref, ahead)).astype(bf16)


def late_kernel(rows, block, blocks, rank_ref, far_ref, spec_ref, back_ref, late_ref):
    side = jnp.where(rank_ref[0] == 2, 1.0, -1.0).astype(f32)
    w2 = (spec_ref[0, :rows, :].astype(f32), spec_ref[0, rows:, :].astype(f32) * side)
    late = jnp.concatenate(times(w2, (far_ref[:rows, :], far_ref[rows:, :])), axis=0).astype(bf16)
    late_ref[...] = backward(back_ref, late)


def last_kernel(
    rows, shards, channels, block, blocks, after_ref, rank_ref, near_ref, far_ref, weight_ref, rate_ref, back_ref,
    trans_ref, featt_ref, slope_ref, sums_ref, first_ref, bias_ref, in_ref, pay_ref, total_ref, acc_ref,
):
    del after_ref
    hid_count, width = weight_ref.shape
    lower = rank_ref[0] == 1
    start = pl.multiple_of(block * width, width)
    here = sums_ref[...] + in_ref[:, pl.ds(start, width)].astype(f32)
    mine = (block < blocks // 2) == lower

    @pl.when(block == 0)
    def _():
        acc_ref[...] = jnp.zeros_like(acc_ref)

    @pl.when(mine)
    def _():
        sign = jnp.where(lower, 1.0, -1.0).astype(f32)
        three = conj_times((near_ref[:rows, :], near_ref[rows:, :]), (far_ref[:rows, :], far_ref[rows:, :]))
        three = (three[0], three[1] * sign)
        half = rows // 2
        two = jnp.concatenate([three[1][:half], -three[1][half:], -three[0][:half], three[0][half:]], axis=0)
        rate = rate_ref[...]
        env = decay(rate, rows, float(rows * shards) ** -0.5)
        parts = []
        for lag, value in ((shards - 2, two), (shards - 1, jnp.concatenate(three, axis=0))):
            grad = backward(back_ref, *split(value))
            parts.append(split(grad * (env * jnp.exp(rate * (-float(lag * rows))))))
        m_high = jnp.concatenate([p[0] for p in parts], axis=0)
        m_low = jnp.concatenate([p[1] for p in parts], axis=0)
        trans = trans_ref[:, (shards - 2) * rows :]
        pay_ref[:, pl.ds(start, width)] = (here + weight_sums(trans, m_high, m_low)).astype(bf16)
        w_high, w_low = split(weight_ref[...])
        acc_ref[...] += hidden_sums(m_high, m_low, w_high, w_low)

    @pl.when(jnp.logical_not(mine))
    def _():
        pay_ref[:, pl.ds(start, width)] = here.astype(bf16)

    @pl.when(block == blocks - 1)
    def _():
        first = exact_dot(
            featt_ref[:, (shards - 2) * rows :], acc_ref[...] * slope_ref[(shards - 2) * rows :, :]
        )
        lanes = channels // 128
        in_bias, in_first = get_side(in_ref[...], channels, lanes, hid_count)
        first = first + first_ref[...] + in_first
        put_side(pay_ref, channels, fold(bias_ref[...]) + in_bias)
        total_ref[...] = first


def total_kernel(channels, hid_count, part_ref, first_ref, late_ref, own_ref, come_ref, pay_ref):
    del part_ref, first_ref, late_ref
    lanes = channels // 128
    pay_ref[:, :channels] = (own_ref[:, :channels].astype(f32) + come_ref[:, :channels].astype(f32)).astype(bf16)
    own, come = (get_side(ref[...], channels, lanes, hid_count)[0] for ref in (own_ref, come_ref))
    put_side(pay_ref, channels, own + come)


def gates_kernel(inner, shards, blocks, width, before, *refs):
    refs = refs[before:]
    inputs, outs, held, sems = refs[:10], refs[10:13], refs[13:16], refs[16]

    def leaving(block, i):
        cols = pl.ds(pl.multiple_of(block * width, width), width)
        return pltpu.make_async_copy(held[i].at[:, cols], outs[i].at[:, cols], sems.at[block, i])

    def strip(block, blocks, *views):
        gates_strip(inner, shards, *views)
        for i in range(3):
            leaving(block, i).start()

    looped(strip, (None,) + (ROWS,) * 12, blocks, width)(*inputs, *held)
    for block in range(blocks):
        for i in range(3):
            leaving(block, i).wait()


def gates_strip(
    inner, shards, rank_ref, one_ref, two_ref, val_ref, out_ref, skip_ref, conv_ref, corr_ref, late_ref, part_ref,
    grad_one_ref, grad_two_ref, grad_value_ref,
):
    late = late_ref[...] if inner else part_ref[...].astype(f32)
    upper = rank_ref[0] >= shards // 2
    zero = jnp.zeros_like(late)
    one = one_ref[...].astype(f32)
    val = val_ref[...].astype(f32)
    out = out_ref[...].astype(f32)
    skip = skip_ref[...]
    conv = conv_ref[...] + jnp.where(upper, late, zero)
    corr = corr_ref[...] + jnp.where(upper, zero, late)
    grad_two_ref[...] = (out * (conv + skip * (one * val))).astype(bf16)
    mid = corr + skip * (out * two_ref[...].astype(f32))
    grad_one_ref[...] = (mid * val).astype(bf16)
    grad_value_ref[...] = (mid * one).astype(bf16)


def finish_kernel(
    channels, shards, rank_ref, own_ref, come_ref, first_ref, first_come_ref, second_out, first_out, bias_out, second,
    first, bias, sems,
):
    rank = rank_ref[0]
    inner = jnp.logical_and(rank > 0, rank < shards - 1)
    lanes = channels // 128
    copies = [
        pltpu.make_async_copy(held, out, sems.at[i])
        for i, (held, out) in enumerate(((second, second_out), (first, first_out), (bias, bias_out)))
    ]
    picked = jnp.where(inner, own_ref[...], come_ref[...])
    second[...] = picked[:, :channels].astype(f32)
    copies[0].start()
    first[...] = jnp.where(inner, first_ref[...], first_come_ref[...])
    copies[1].start()
    rows = get_side(picked, channels, lanes, first.shape[1])[0]
    for i in range(lanes):
        bias[:, i * 128 : (i + 1) * 128] = rows[i : i + 1]
    copies[2].start()
    for copy in copies:
        copy.wait()


def few_shards_body(
    x_one, x_two, values, grad_out, first_weight, second_weight, skip_bias, decay_rate
):
    rows, channels = x_one.shape
    shards = lax.axis_size("ctx")
    feat_count, hid_count = first_weight.shape
    seq_len = rows * shards
    double = 2 * rows
    width = min(512, channels)
    blocks = channels // width
    wide = 2 * width if blocks % 4 == 0 else width
    few = channels // wide
    rank = lax.axis_index("ctx").astype(jnp.int32).reshape(1)
    front, back = block_tables(rows)
    feats = feature_table(seq_len)
    featt = np.ascontiguousarray(feats.T)
    skip_row = skip_bias.reshape(1, channels)
    rate_row = decay_rate.reshape(1, channels)
    smem = pl.BlockSpec(memory_space=pltpu.SMEM)
    vmem = pl.BlockSpec(memory_space=pltpu.VMEM)
    anywhere = pl.BlockSpec(memory_space=pl.ANY)
    mebi = 1024 * 1024

    def shape(*dims, dtype=f32):
        return jax.ShapeDtypeStruct(dims, dtype)

    def call(kernel, name, units, out_shape, in_specs, out_specs=None, scratch=(), limit=16, aliases={}):
        return pl.pallas_call(
            kernel,
            in_specs=in_specs,
            out_specs=out_specs if out_specs is not None else [vmem] * len(out_shape),
            out_shape=out_shape,
            scratch_shapes=scratch,
            input_output_aliases=aliases,
            compiler_params=pltpu.CompilerParams(vmem_limit_bytes=limit * mebi),
            cost_estimate=pl.CostEstimate(
                flops=2 * units * double * double * channels, bytes_accessed=rows * channels, transcendentals=0
            ),
            name=name,
        )

    def move(array, pairs):
        return lax.ppermute(array, "ctx", pairs)

    inward = [(0, 1), (shards - 1, shards - 2)]
    outward = [(1, 0), (shards - 2, shards - 1)]
    across = [(1, 2), (2, 1)]
    alone = [(0, 0), (shards - 1, shards - 1)]
    pay_shape = (hid_count, channels + SIDE)
    block_bf16 = shape(rows, channels, dtype=bf16)
    block_f32 = shape(rows, channels)

    row_step = max(rows // 2, 16)
    gate_rows = pl.BlockSpec((row_step, channels), lambda i: (i, 0))
    pair, other, edge, bias = pl.pallas_call(
        products_kernel,
        grid=(rows // row_step,),
        in_specs=[smem] + [gate_rows] * 4,
        out_specs=[gate_rows] * 3 + [pl.BlockSpec((1, channels), lambda i: (0, 0))],
        out_shape=[block_bf16] * 3 + [shape(1, channels)],
        compiler_params=pltpu.CompilerParams(vmem_limit_bytes=64 * mebi),
        name="products",
    )(rank, x_one, x_two, values, grad_out)
    pair_in = move(pair, inward + outward)
    middle_in = move(other, across)

    own_shapes = [
        shape(rows, feat_count), shape(feat_count, hid_count), block_bf16, block_bf16, shape(hid_count, channels),
        shape(1, channels), shape(double, double, dtype=bf16), shape(double, double, dtype=bf16),
        shape(feat_count, seq_len), shape(1, channels), shape(*pay_shape, dtype=bf16),
    ]
    (send,) = call(
        only(False, shards, 0, functools.partial(own_kernel, rows, shards, channels, blocks, width)), "own_pair", 8,
        [shape(*pay_shape, dtype=bf16)],
        [smem] + [anywhere] * 10,
        out_specs=[anywhere],
        scratch=[pltpu.VMEM(s.shape, s.dtype) for s in own_shapes]
        + [
            pltpu.VMEM((2 * hid_count, rows), bf16), pltpu.VMEM((rows, hid_count), f32),
            pltpu.SemaphoreType.DMA((10,)), pltpu.SemaphoreType.DMA,
        ],
        limit=60,
    )(rank, feats[:rows], first_weight, pair, other, second_weight, rate_row, front, back, featt, bias)
    come = move(send, inward)
    late_feats, _ = lax.optimization_barrier((jnp.asarray(feats), send))
    spec, trans, slope = call(
        functools.partial(filters_kernel, rows, shards, blocks, width), "filters", 8,
        [
            shape(shards, double, channels, dtype=bf16), shape(2 * hid_count, seq_len, dtype=bf16),
            shape(seq_len, hid_count),
        ],
        [vmem] * 5,
        scratch=[pltpu.VMEM((seq_len, 3 * hid_count), bf16)],
    )(late_feats, first_weight, second_weight, rate_row, front)

    edge, _ = lax.optimization_barrier((edge, slope))
    far = move(edge, [(0, 2), (shards - 1, shards - 3)])
    conv, corr, ahead, sums, first, near_spec = call(
        functools.partial(near_kernel, rows, shards, blocks, width), "near_blocks", 20,
        [block_f32] * 3
        + [shape(hid_count, channels), shape(feat_count, hid_count), shape(double, channels)],
        [smem] + [vmem] * 12,
        scratch=[
            pltpu.VMEM((4, double, width), f32),
            pltpu.VMEM((3, double, width), bf16),
            pltpu.VMEM((shards - 1, double, width), bf16),
            pltpu.VMEM((shards - 1, double, width), bf16),
            pltpu.VMEM(((shards - 1) * rows, hid_count), f32),
        ],
    )(rank, pair, other, pair_in, middle_in, spec, second_weight, rate_row, front, back, trans, featt, slope)

    part, far_spec = call(
        only(
            True, shards, 0,
            looped(
                functools.partial(far_kernel, rows),
                (None, ROWS, (slice(3, 4), slice(None)), None, None, ROWS, ROWS, ROWS),
                few, wide,
            ),
        ),
        "far_block", 1,
        [block_bf16, shape(double, channels)],
        [smem] + [vmem] * 5,
    )(rank, far, spec, front, back, ahead)
    (late,) = call(
        only(
            True, shards, 0,
            looped(
                functools.partial(late_kernel, rows),
                (None, ROWS, (slice(2, 3), slice(None)), None, ROWS),
                few, wide,
            ),
        ),
        "late_block", 1,
        [block_f32],
        [smem] + [vmem] * 3,
    )(rank, far_spec, spec, back)
    part_come = move(part, outward)

    pay, first = call(
        only(
            True, shards, 1,
            looped(
                functools.partial(last_kernel, rows, shards, channels),
                (None, None, ROWS, ROWS, ROWS, ROWS, None, None, None, None, ROWS),
                few, wide,
            ),
        ),
        "last_pair", 1,
        [shape(*pay_shape, dtype=bf16), shape(feat_count, hid_count)],
        [anywhere, smem] + [vmem] * 12,
        scratch=[pltpu.VMEM((2 * rows, hid_count), f32)],
    )(part, rank, near_spec, far_spec, second_weight, rate_row, back, trans, featt, slope, sums, first, bias, come)
    pay_come = move(pay, across + alone)
    group = lax.axis_size(("ch", "sub"))
    bit = 1
    while bit < group:
        first = first + lax.ppermute(first, ("ch", "sub"), [(i, i ^ bit) for i in range(group)])
        bit *= 2

    (total,) = call(
        functools.partial(total_kernel, channels, hid_count), "total", 0,
        [shape(*pay_shape, dtype=bf16)],
        [anywhere] * 3 + [vmem] * 2,
    )(part_come, first, late, pay, pay_come)
    total_come = move(total, inward + outward)

    def gates(inner, *before):
        return call(
            only(
                inner, shards, len(before),
                functools.partial(gates_kernel, inner, shards, blocks, width, len(before)),
            ),
            "gates", 0,
            [block_bf16] * 3,
            [anywhere] * len(before) + [smem] + [vmem] * 9,
            out_specs=[anywhere] * 3,
            scratch=[pltpu.VMEM((rows, channels), bf16)] * 3 + [pltpu.SemaphoreType.DMA((blocks, 3))],
            aliases={i: i for i in range(3)} if inner else {},
        )(*before, rank, x_one, x_two, values, grad_out, skip_row, conv, corr, late, part_come)

    grads = gates(False, total)
    first, _ = lax.optimization_barrier((first, grads[0]))
    first = first + move(first, across + alone)
    first_come = move(first, inward + outward)
    grad_one, grad_two, grad_value = gates(True, *grads)

    outs = [shape(hid_count, channels), shape(feat_count, hid_count), shape(1, channels)]
    grad_second, grad_first, grad_bias = call(
        functools.partial(finish_kernel, channels, shards), "finish", 0,
        outs,
        [smem] + [vmem] * 4,
        out_specs=[anywhere] * 3,
        scratch=[pltpu.VMEM(o.shape, f32) for o in outs] + [pltpu.SemaphoreType.DMA((3,))],
    )(rank, total, total_come, first, first_come)
    return (grad_one, grad_two, grad_value, grad_first, grad_second, grad_bias.reshape(channels))


def solution(mesh):
    in_specs = (
        P(("parts", "ctx"), ("ch", "sub")),
        P(("parts", "ctx"), ("ch", "sub")),
        P(("parts", "ctx"), ("ch", "sub")),
        P(("parts", "ctx"), ("ch", "sub")),
        P(),
        P(None, ("ch", "sub")),
        P(("ch", "sub")),
        P(("ch", "sub")),
    )
    out_specs = (
        P(("parts", "ctx"), ("ch", "sub")),
        P(("parts", "ctx"), ("ch", "sub")),
        P(("parts", "ctx"), ("ch", "sub")),
        P("parts", None),
        P("parts", ("ch", "sub")),
        P(("parts", "ch", "sub")),
    )
    body = few_shards_body if mesh.shape["ctx"] == 4 else many_shards_body
    return jax.shard_map(body, mesh=mesh, in_specs=in_specs, out_specs=out_specs, check_vma=False)
```

```python
import functools
import math

import jax
import jax.numpy as jnp
import numpy as np
from jax import lax
from jax.experimental import pallas as pl
from jax.experimental.pallas import tpu as pltpu
from jax.sharding import PartitionSpec as P

band_steps = (1763, 1201, 811, 547, 367, 251, 167, 113, 79, 53, 37, 23, 17, 11, 7, 3)
highest = lax.Precision.HIGHEST
f32 = jnp.float32
bf16 = jnp.bfloat16


def features(positions):
    multiplier = jnp.array(band_steps, dtype=jnp.int32)
    phase = positions[:, None] * multiplier[None, :] % 4096
    angle = phase.astype(jnp.float32) * (2.0 * math.pi / 4096.0)
    return jnp.concatenate([jnp.cos(angle), jnp.sin(angle)], axis=1)


def tables(out_count, in_count, modulus, sign_value):
    row_index = lax.broadcasted_iota(jnp.int32, (out_count, in_count), 0)
    col_index = lax.broadcasted_iota(jnp.int32, (out_count, in_count), 1)
    angle = (row_index * col_index % modulus).astype(jnp.float32) * (2.0 * math.pi / modulus)
    return (jnp.cos(angle), sign_value * jnp.sin(angle))


def twiddle(spec_re, spec_im, freq_count, span, modulus, sign_value):
    freq_index = lax.broadcasted_iota(jnp.int32, (freq_count, span), 0)
    pos_index = lax.broadcasted_iota(jnp.int32, (freq_count, span), 1)
    angle = (freq_index * pos_index % modulus).astype(jnp.float32) * (2.0 * math.pi / modulus)
    factor_re = jnp.cos(angle)[None, None, :, :]
    factor_im = (sign_value * jnp.sin(angle))[None, None, :, :]
    return (spec_re * factor_re - spec_im * factor_im, spec_re * factor_im + spec_im * factor_re)


def contract(kernel, array):
    return jnp.einsum(
        "lj,mckj->mckl", kernel, array, precision=highest, preferred_element_type=jnp.float32
    )


def along_positions(spec_re, spec_im, kernel_re, kernel_im):
    return (
        contract(kernel_re, spec_re) - contract(kernel_im, spec_im),
        contract(kernel_re, spec_im) + contract(kernel_im, spec_re),
    )


def many_shards_body(
    x_one, x_two, values, grad_out, first_weight, second_weight, skip_bias, decay_rate
):
    row_count, chan_count = x_one.shape
    shards = lax.axis_size("ctx")
    rank = lax.axis_index("ctx")
    seq_len = row_count * shards
    total = 2 * seq_len
    narrow = chan_count // shards
    chan_weight = lax.dynamic_slice_in_dim(second_weight, rank * narrow, narrow, 1)
    chan_rate = lax.dynamic_slice_in_dim(decay_rate, rank * narrow, narrow, 0)
    source = x_one.astype(jnp.float32) * values.astype(jnp.float32)
    cotan = grad_out.astype(jnp.float32) * x_two.astype(jnp.float32)
    spread = lax.all_to_all(
        jnp.stack([source.T, cotan.T])[:, :, None, :],
        "ctx",
        split_axis=1,
        concat_axis=2,
        tiled=True,
    )
    far_source = spread[0]
    far_cotan = spread[1]
    positions = jnp.arange(seq_len, dtype=jnp.int32)
    feats = features(positions)
    pre_act = jnp.dot(feats, first_weight, precision=highest, preferred_element_type=jnp.float32)
    hidden = jnp.sin(pre_act)
    envelope = jnp.exp(-chan_rate[:, None] * positions.astype(jnp.float32)[None, :]) * float(
        seq_len
    ) ** (-0.5)
    filt = (
        jnp.einsum(
            "th,hc->ct", hidden, chan_weight, precision=highest, preferred_element_type=jnp.float32
        )
        * envelope
    )
    filt_blocks = filt.reshape(narrow, shards, row_count)
    fields = jnp.stack([far_source, far_cotan])

    def first_section(kernel):
        field_part = jnp.einsum(
            "kn,mcnj->mckj", kernel, fields, precision=highest, preferred_element_type=jnp.float32
        )
        filter_part = jnp.einsum(
            "kn,cnj->ckj",
            kernel,
            filt_blocks,
            precision=highest,
            preferred_element_type=jnp.float32,
        )
        return jnp.concatenate([field_part, filter_part[None]], axis=0)

    first_re, first_im = tables(2 * shards, shards, 2 * shards, -1.0)
    spec_re, spec_im = (first_section(first_re), first_section(first_im))
    spec_re, spec_im = twiddle(spec_re, spec_im, 2 * shards, row_count, total, -1.0)
    fwd_re, fwd_im = tables(row_count, row_count, row_count, -1.0)
    spec_re, spec_im = along_positions(spec_re, spec_im, fwd_re, fwd_im)
    source_re, source_im = (spec_re[0], spec_im[0])
    cotan_re, cotan_im = (spec_re[1], spec_im[1])
    filter_re, filter_im = (spec_re[2], spec_im[2])
    prod_re = jnp.stack(
        [
            source_re * filter_re - source_im * filter_im,
            cotan_re * filter_re + cotan_im * filter_im,
            cotan_re * source_re + cotan_im * source_im,
        ]
    )
    prod_im = jnp.stack(
        [
            source_re * filter_im + source_im * filter_re,
            cotan_im * filter_re - cotan_re * filter_im,
            cotan_im * source_re - cotan_re * source_im,
        ]
    )
    back_re, back_im = tables(row_count, row_count, row_count, 1.0)
    prod_re, prod_im = along_positions(prod_re, prod_im, back_re, back_im)
    prod_re, prod_im = twiddle(prod_re, prod_im, 2 * shards, row_count, total, 1.0)
    last_re, last_im = tables(shards, 2 * shards, 2 * shards, 1.0)
    field_out = jnp.einsum(
        "nk,mckj->mcnj", last_re, prod_re[:2], precision=highest, preferred_element_type=jnp.float32
    ) - jnp.einsum(
        "nk,mckj->mcnj", last_im, prod_im[:2], precision=highest, preferred_element_type=jnp.float32
    )
    field_out = field_out * (1.0 / total)
    filt_grad = jnp.einsum(
        "nk,ckj->cnj", last_re, prod_re[2], precision=highest, preferred_element_type=jnp.float32
    ) - jnp.einsum(
        "nk,ckj->cnj", last_im, prod_im[2], precision=highest, preferred_element_type=jnp.float32
    )
    filt_grad = (filt_grad * (1.0 / total)).reshape(narrow, seq_len)
    modulated = filt_grad * envelope
    weight_part = jnp.einsum(
        "th,ct->hc", hidden, modulated, precision=highest, preferred_element_type=jnp.float32
    )
    hidden_grad = jnp.einsum(
        "ct,hc->th", modulated, chan_weight, precision=highest, preferred_element_type=jnp.float32
    )
    first_part = jnp.dot(
        feats.T,
        hidden_grad * jnp.cos(pre_act),
        precision=highest,
        preferred_element_type=jnp.float32,
    )
    grad_first = lax.psum(first_part, ("ctx", "ch", "sub"))
    returned = lax.all_to_all(
        field_out.astype(jnp.bfloat16), "ctx", split_axis=2, concat_axis=1, tiled=True
    ).astype(field_out.dtype)
    conv_part = returned[0, :, 0, :].T
    corr_part = returned[1, :, 0, :].T
    grad_two = (grad_out.astype(jnp.float32) * (conv_part + skip_bias[None, :] * source)).astype(
        jnp.bfloat16
    )
    grad_mid = corr_part + skip_bias[None, :] * cotan
    grad_one = (grad_mid * values.astype(jnp.float32)).astype(jnp.bfloat16)
    grad_value = (grad_mid * x_one.astype(jnp.float32)).astype(jnp.bfloat16)
    grad_bias = lax.psum(jnp.sum(source * cotan, axis=0), "ctx")
    grad_second = lax.all_gather(weight_part, "ctx", axis=1, tiled=True)
    return (grad_one, grad_two, grad_value, grad_first, grad_second, grad_bias)


STEP = 16
SIDE = 128


def halves(array):
    array = np.asarray(array, np.float32)
    high = array.astype(bf16)
    low = (array - high.astype(np.float32)).astype(bf16)
    return high, low


def block_tables(rows):
    freq = np.concatenate([np.arange(0, rows, 2), np.arange(1, rows, 2)])
    phase = (2 * freq + 1)[:, None] * np.arange(rows)[None, :] % (4 * rows)
    angle = phase * (2.0 * np.pi / (4 * rows))
    forward = np.concatenate([np.cos(angle), -np.sin(angle)], axis=0)
    front = np.ascontiguousarray(np.concatenate(halves(forward), axis=1))
    back = np.ascontiguousarray(np.concatenate(halves(forward.T / rows), axis=0))
    return front, back


def feature_table(seq_len):
    phase = np.arange(seq_len)[:, None] * np.array(band_steps)[None, :] % 4096
    angle = phase * (2.0 * np.pi / 4096.0)
    return np.concatenate([np.cos(angle), np.sin(angle)], axis=1).astype(np.float32)


def split(array):
    high = array.astype(bf16)
    return high, (array - high.astype(f32)).astype(bf16)


def dot(left, right):
    return jnp.dot(left, right, preferred_element_type=f32)


def exact_dot(left, right):
    return jnp.dot(left, right, precision=highest, preferred_element_type=f32)


def dot_across(left, right):
    return lax.dot_general(left, right, (((1,), (1,)), ((), ())), preferred_element_type=f32)


def decay(rate, rows, scale):
    place = lax.broadcasted_iota(jnp.int32, (rows, rate.shape[1]), 0)
    return jnp.exp(-place.astype(f32) * rate) * scale


def times(a, b):
    return a[0] * b[0] - a[1] * b[1], a[0] * b[1] + a[1] * b[0]


def conj_times(a, b):
    return a[0] * b[0] + a[1] * b[1], a[0] * b[1] - a[1] * b[0]


def plus(a, b):
    return a[0] + b[0], a[1] + b[1]


def scaled(a, factor):
    return a[0] * factor, a[1] * factor


def choose(condition, a, b):
    return jnp.where(condition, a[0], b[0]), jnp.where(condition, a[1], b[1])


def turned(a, sign):
    return (a[1], -a[0]) if sign > 0 else (-a[1], a[0])


def forward(front_ref, block):
    return dot(front_ref[...], jnp.concatenate([block, block], axis=0))


def backward(back_ref, high, low=None):
    both = dot(back_ref[...], high)
    rows = both.shape[0] // 2
    out = both[:rows] + both[rows:]
    return out if low is None else out + dot(back_ref[:rows], low)


def row_groups(rows):
    for step in range(rows // STEP):
        sign = 1 if step * STEP < rows // 2 else -1
        yield slice(step * STEP, (step + 1) * STEP), slice(rows + step * STEP, rows + (step + 1) * STEP), sign


def weight_sums(trans, m_high, m_low):
    both = dot(trans, m_high)
    count = both.shape[0] // 2
    return both[:count] + both[count:] + dot(trans[:count], m_low)


def hidden_sums(m_high, m_low, w_high, w_low):
    left = jnp.concatenate([m_high, m_high, m_low], axis=1)
    right = jnp.concatenate([w_high, w_low, w_high], axis=1)
    return dot_across(left, right)


def looped(kernel, kinds, blocks, width):
    def over_strips(*refs):
        def step(block, carry):
            cols = pl.ds(pl.multiple_of(block * width, width), width)
            views = [
                ref if kind is None else ref.at[(*kind, cols)]
                for ref, kind in zip(refs, kinds + (None,) * (len(refs) - len(kinds)))
            ]
            kernel(block, blocks, *views)
            return carry

        lax.fori_loop(0, blocks, step, 0)

    return over_strips


ROWS = (slice(None),)
CUBE = (slice(None), slice(None))


def products_kernel(rank_ref, one_ref, two_ref, val_ref, out_ref, pair_ref, other_ref, edge_ref, bias_ref):
    source = one_ref[...].astype(f32) * val_ref[...].astype(f32)
    cotan = out_ref[...].astype(f32) * two_ref[...].astype(f32)
    even = rank_ref[0] % 2 == 0
    pair_ref[...] = jnp.where(even, source, cotan).astype(bf16)
    edge_ref[...] = pair_ref[...]
    other_ref[...] = jnp.where(even, cotan, source).astype(bf16)
    part = jnp.sum(source * cotan, axis=0, keepdims=True)

    @pl.when(pl.program_id(0) == 0)
    def _():
        bias_ref[...] = part

    @pl.when(pl.program_id(0) > 0)
    def _():
        bias_ref[...] += part


def ordered(first, a, b):
    return (jnp.where(first, a, b), jnp.where(first, b, a))


def sin_cos(angle):
    turns = jnp.floor(angle * (2.0 / math.pi) + 0.5)
    rest = ((angle - turns * 1.5703125) - turns * 4.837512969970703e-4) - turns * 7.54978995489188e-8
    square = rest * rest
    sine = rest + rest * square * (
        -1.6666654611e-1 + square * (8.3321608736e-3 + square * -1.9515295891e-4)
    )
    cosine = 1.0 - 0.5 * square + square * square * (
        4.166664568298827e-2 + square * (-1.388731625493765e-3 + square * 2.443315711809948e-5)
    )
    quarter = turns.astype(jnp.int32)
    odd = (quarter & 1) == 1
    sin_sign = jnp.where((quarter & 2) == 2, -1.0, 1.0).astype(f32)
    cos_sign = jnp.where(((quarter + 1) & 2) == 2, -1.0, 1.0).astype(f32)
    return jnp.where(odd, cosine, sine) * sin_sign, jnp.where(odd, sine, cosine) * cos_sign


def turned_over(hidden, slope):
    both = jnp.concatenate([hidden, slope], axis=1).T
    return jnp.concatenate(split(both[: hidden.shape[1]]), axis=0)


def filters_kernel(
    rows, shards, blocks, width, feats_ref, first_ref, weight_ref, rate_ref, front_ref, spec_ref, trans_ref, slope_ref,
    hid_ref,
):
    hidden, slope = sin_cos(exact_dot(feats_ref[...], first_ref[...]))
    slope_ref[...] = slope
    high, low = split(hidden)
    hid_ref[...] = jnp.concatenate([high, high, low], axis=1)
    trans_ref[...] = turned_over(hidden, slope)
    strips = looped(
        functools.partial(filter_strip, rows, shards), (None, ROWS, ROWS, None, CUBE), blocks, width
    )
    strips(hid_ref, weight_ref, rate_ref, front_ref, spec_ref)


def filter_strip(rows, shards, block, blocks, hid_ref, weight_ref, rate_ref, front_ref, spec_ref):
    scale = float(rows * shards) ** -0.5
    w_high, w_low = split(weight_ref[...])
    stacked = jnp.concatenate([w_high, w_low, w_high], axis=0)
    rate = rate_ref[...]
    env = decay(rate, rows, scale)
    before = None
    for lag in range(shards):
        part = dot(hid_ref[lag * rows : (lag + 1) * rows, :], stacked)
        part = part * (env * jnp.exp(rate * (-float(lag * rows))))
        f_high, f_low = split(part)
        now = forward(front_ref, f_high) + dot(front_ref[:, :rows], f_low)
        for re, im, sign in row_groups(rows):
            here = (now[re], now[im])
            if before is not None:
                here = plus(here, turned((before[re], before[im]), -sign))
            spec_ref[lag, re, :] = here[0].astype(bf16)
            spec_ref[lag, im, :] = here[1].astype(bf16)
        before = now


def own_kernel(rows, shards, channels, blocks, width, rank_ref, *refs):
    inputs, send_out, held = refs[:10], refs[10], refs[11:21]
    send_ref, trans_ref, acc_ref, sems, out_sem = refs[21:]
    (
        feats_ref, first_ref, pair_ref, other_ref, weight_ref, rate_ref, front_ref, back_ref, featt_ref, bias_ref
    ) = held
    copies = [pltpu.make_async_copy(far, near, sems.at[i]) for i, (far, near) in enumerate(zip(inputs, held))]
    for copy in copies:
        copy.start()
    acc_ref[...] = jnp.zeros_like(acc_ref)
    copies[0].wait()
    copies[1].wait()
    hidden, slope = sin_cos(exact_dot(feats_ref[...], first_ref[...]))
    trans_ref[...] = turned_over(hidden, slope)
    for copy in copies[2:]:
        copy.wait()
    kinds = (None, ROWS, ROWS, ROWS, ROWS, None, None, None, ROWS, None)
    looped(functools.partial(own_strip, rows, shards), kinds, blocks, width)(
        rank_ref, pair_ref, other_ref, weight_ref, rate_ref, front_ref, back_ref, trans_ref, send_ref, acc_ref
    )
    first = exact_dot(featt_ref[:, :rows], acc_ref[...] * slope)
    put_side(send_ref, channels, fold(bias_ref[...]), first)
    last = pltpu.make_async_copy(send_ref, send_out, out_sem)
    last.start()
    last.wait()


def own_strip(
    rows, shards, block, blocks, rank_ref, pair_ref, other_ref, weight_ref, rate_ref, front_ref, back_ref, trans_ref,
    send_ref, acc_ref,
):
    source, cotan = ordered(rank_ref[0] % 2 == 0, pair_ref[...], other_ref[...])
    x0 = forward(front_ref, source)
    c0 = forward(front_ref, cotan)
    pair = conj_times((x0[:rows], x0[rows:]), (c0[:rows], c0[rows:]))
    high, low = split(jnp.concatenate(pair, axis=0))
    env = decay(rate_ref[...], rows, float(rows * shards) ** -0.5)
    m_high, m_low = split(backward(back_ref, high, low) * env)
    send_ref[...] = weight_sums(trans_ref[...], m_high, m_low).astype(bf16)
    acc_ref[...] += hidden_sums(m_high, m_low, *split(weight_ref[...]))


def fold(bias):
    return jnp.concatenate([bias[:, i * 128 : (i + 1) * 128] for i in range(bias.shape[1] // 128)], axis=0)


def put_side(pay_ref, channels, bias, first=None):
    half = pay_ref.shape[0] // 2
    pay_ref[:, channels:] = jnp.zeros((2 * half, SIDE), bf16)
    for start, part in zip((0, half // 2), split(bias)):
        pay_ref[start : start + bias.shape[0], channels:] = part
    if first is not None:
        pay_ref[half:, channels:] = jnp.concatenate(split(first), axis=1)


def get_side(pay, channels, lanes, hid_count):
    half = pay.shape[0] // 2
    side = pay[:, channels:].astype(f32)
    low = side[half:]
    return side[:lanes] + side[half // 2 : half // 2 + lanes], low[:, :hid_count] + low[:, hid_count:]


def near_kernel(
    rows, shards, blocks, width, rank_ref, pair_ref, other_ref, pair_in_ref, middle_in_ref, spec_ref, weight_ref,
    rate_ref, front_ref, back_ref, trans_ref, featt_ref, slope_ref, conv_ref, corr_ref, ahead_ref, sums_ref, first_ref,
    near_ref, fields, fast, high_ref, low_ref, acc_ref,
):
    rank = rank_ref[0]
    inner = jnp.logical_and(rank > 0, rank < shards - 1)
    count = shards - 1
    kinds = (None, None, None) + (ROWS,) * 4 + (CUBE, ROWS, ROWS)
    common = (
        rank_ref, front_ref, back_ref, pair_ref, other_ref, pair_in_ref, middle_in_ref, spec_ref, conv_ref, corr_ref,
        fields, fast,
    )

    @pl.when(jnp.logical_not(inner))
    def _():
        looped(functools.partial(edge_strip, rows, shards), kinds, blocks, width)(*common)

    @pl.when(inner)
    def _():
        acc_ref[...] = jnp.zeros_like(acc_ref)
        looped(
            functools.partial(inner_strip, rows, shards), kinds + (None,) * 3 + (ROWS,) * 5, blocks, width
        )(*common, trans_ref, weight_ref, rate_ref, ahead_ref, sums_ref, near_ref, high_ref, low_ref, acc_ref)
        first_ref[...] = exact_dot(
            featt_ref[:, : count * rows], acc_ref[...] * slope_ref[: count * rows, :]
        )


def edge_strip(
    rows, shards, block, blocks, rank_ref, front_ref, back_ref, pair_ref, other_ref, pair_in_ref, middle_in_ref,
    spec_ref, conv_ref, corr_ref, fields, fast,
):
    del middle_in_ref
    top = rank_ref[0] == shards - 1
    source, cotan = ordered(rank_ref[0] % 2 == 0, pair_ref[...], other_ref[...])
    for index, block_in in enumerate((source, cotan, pair_in_ref[...])):
        fields[index] = forward(front_ref, block_in)
    on_conv = jnp.where(top, 1.0, 0.0).astype(f32)
    on_corr = jnp.where(top, 0.0, 1.0).astype(f32)
    for re, im, sign in row_groups(rows):
        x0, c0, near = ((fields[i, re, :], fields[i, im, :]) for i in range(3))
        w0, w1 = ((spec_ref[i, re, :].astype(f32), spec_ref[i, im, :].astype(f32)) for i in range(2))
        values = (
            plus(times(w0, x0), scaled(times(w1, near), on_conv)),
            plus(conj_times(w0, c0), scaled(conj_times(w1, near), on_corr)),
        )
        for index, value in enumerate(values):
            fast[index, re, :] = value[0].astype(bf16)
            fast[index, im, :] = value[1].astype(bf16)
    conv_ref[...] = backward(back_ref, fast[0])
    corr_ref[...] = backward(back_ref, fast[1])


def inner_strip(
    rows, shards, block, blocks, rank_ref, front_ref, back_ref, pair_ref, other_ref, pair_in_ref, middle_in_ref,
    spec_ref, conv_ref, corr_ref, fields, fast, trans_ref, weight_ref, rate_ref, ahead_ref, sums_ref, near_ref, high_ref,
    low_ref, acc_ref,
):
    lower = rank_ref[0] == 1
    upper = jnp.where(lower, 0.0, 1.0).astype(f32)
    side = jnp.where(lower, -1.0, 1.0).astype(f32)
    count = shards - 1
    blocks_in = (
        *ordered(lower, other_ref[...], pair_ref[...]), *ordered(lower, pair_in_ref[...], middle_in_ref[...])
    )
    for index, block_in in enumerate(blocks_in):
        fields[index] = forward(front_ref, block_in)
    for re, im, sign in row_groups(rows):
        x0, c0, x1, c1 = ((fields[i, re, :], fields[i, im, :]) for i in range(4))
        w0, w1, w2 = ((spec_ref[i, re, :].astype(f32), spec_ref[i, im, :].astype(f32)) for i in range(3))
        values = (
            plus(times(w0, x0), times(w1, x1)),
            plus(conj_times(w0, c0), conj_times(w1, c1)),
            times((w2[0], w2[1] * side), choose(lower, c1, x1)),
        )
        for index, value in enumerate(values):
            fast[index, re, :] = value[0].astype(bf16)
            fast[index, im, :] = value[1].astype(bf16)
        near_ref[re, :], near_ref[im, :] = choose(lower, x1, c1)
        zero = conj_times(x0, c0)
        one = plus(conj_times(x1, c0), scaled(conj_times(x0, c1), upper))
        two = conj_times(x1, c1)
        for index, value in enumerate((plus(zero, turned(one, sign)), plus(one, turned(two, sign)), two)):
            for part, where in zip(value, (re, im)):
                high_ref[index, where, :], low_ref[index, where, :] = split(part)
    conv_ref[...] = backward(back_ref, fast[0])
    corr_ref[...] = backward(back_ref, fast[1])
    ahead_ref[...] = backward(back_ref, fast[2])
    rate = rate_ref[...]
    env = decay(rate, rows, float(rows * shards) ** -0.5)
    parts = []
    for lag in range(count):
        grad = backward(back_ref, high_ref[lag], low_ref[lag])
        parts.append(split(grad * (env * jnp.exp(rate * (-float(lag * rows))))))
    m_high = jnp.concatenate([p[0] for p in parts], axis=0)
    m_low = jnp.concatenate([p[1] for p in parts], axis=0)
    sums_ref[...] = weight_sums(trans_ref[:, : count * rows], m_high, m_low)
    acc_ref[...] += hidden_sums(m_high, m_low, *split(weight_ref[...]))


def only(inner, shards, rank_at, kernel):
    def run(*refs):
        rank = refs[rank_at][0]

        @pl.when(jnp.logical_and(rank > 0, rank < shards - 1) == inner)
        def _():
            kernel(*refs)

    return run


def far_kernel(
    rows, block, blocks, rank_ref, far_ref, spec_ref, front_ref, back_ref, ahead_ref, part_ref, far_spec_ref
):
    side = jnp.where(rank_ref[0] == 2, 1.0, -1.0).astype(f32)
    far = forward(front_ref, far_ref[...])
    far_spec_ref[...] = far
    w3 = (spec_ref[0, :rows, :].astype(f32), spec_ref[0, rows:, :].astype(f32) * side)
    ahead = jnp.concatenate(times(w3, (far[:rows], far[rows:])), axis=0).astype(bf16)
    part_ref[...] = (ahead_ref[...] + backward(back_ref, ahead)).astype(bf16)


def late_kernel(rows, block, blocks, rank_ref, far_ref, spec_ref, back_ref, late_ref):
    side = jnp.where(rank_ref[0] == 2, 1.0, -1.0).astype(f32)
    w2 = (spec_ref[0, :rows, :].astype(f32), spec_ref[0, rows:, :].astype(f32) * side)
    late = jnp.concatenate(times(w2, (far_ref[:rows, :], far_ref[rows:, :])), axis=0).astype(bf16)
    late_ref[...] = backward(back_ref, late)


def last_kernel(
    rows, shards, channels, block, blocks, after_ref, rank_ref, near_ref, far_ref, weight_ref, rate_ref, back_ref,
    trans_ref, featt_ref, slope_ref, sums_ref, first_ref, bias_ref, in_ref, pay_ref, total_ref, acc_ref,
):
    del after_ref
    hid_count, width = weight_ref.shape
    lower = rank_ref[0] == 1
    start = pl.multiple_of(block * width, width)
    here = sums_ref[...] + in_ref[:, pl.ds(start, width)].astype(f32)
    mine = (block < blocks // 2) == lower

    @pl.when(block == 0)
    def _():
        acc_ref[...] = jnp.zeros_like(acc_ref)

    @pl.when(mine)
    def _():
        sign = jnp.where(lower, 1.0, -1.0).astype(f32)
        three = conj_times((near_ref[:rows, :], near_ref[rows:, :]), (far_ref[:rows, :], far_ref[rows:, :]))
        three = (three[0], three[1] * sign)
        half = rows // 2
        two = jnp.concatenate([three[1][:half], -three[1][half:], -three[0][:half], three[0][half:]], axis=0)
        rate = rate_ref[...]
        env = decay(rate, rows, float(rows * shards) ** -0.5)
        parts = []
        for lag, value in ((shards - 2, two), (shards - 1, jnp.concatenate(three, axis=0))):
            grad = backward(back_ref, *split(value))
            parts.append(split(grad * (env * jnp.exp(rate * (-float(lag * rows))))))
        m_high = jnp.concatenate([p[0] for p in parts], axis=0)
        m_low = jnp.concatenate([p[1] for p in parts], axis=0)
        trans = trans_ref[:, (shards - 2) * rows :]
        pay_ref[:, pl.ds(start, width)] = (here + weight_sums(trans, m_high, m_low)).astype(bf16)
        w_high, w_low = split(weight_ref[...])
        acc_ref[...] += hidden_sums(m_high, m_low, w_high, w_low)

    @pl.when(jnp.logical_not(mine))
    def _():
        pay_ref[:, pl.ds(start, width)] = here.astype(bf16)

    @pl.when(block == blocks - 1)
    def _():
        first = exact_dot(
            featt_ref[:, (shards - 2) * rows :], acc_ref[...] * slope_ref[(shards - 2) * rows :, :]
        )
        lanes = channels // 128
        in_bias, in_first = get_side(in_ref[...], channels, lanes, hid_count)
        first = first + first_ref[...] + in_first
        put_side(pay_ref, channels, fold(bias_ref[...]) + in_bias)
        total_ref[...] = first


def total_kernel(channels, hid_count, part_ref, first_ref, late_ref, own_ref, come_ref, pay_ref):
    del part_ref, first_ref, late_ref
    lanes = channels // 128
    pay_ref[:, :channels] = (own_ref[:, :channels].astype(f32) + come_ref[:, :channels].astype(f32)).astype(bf16)
    own, come = (get_side(ref[...], channels, lanes, hid_count)[0] for ref in (own_ref, come_ref))
    put_side(pay_ref, channels, own + come)


def gates_kernel(inner, shards, blocks, width, before, *refs):
    refs = refs[before:]
    inputs, outs, held, sems = refs[:10], refs[10:13], refs[13:16], refs[16]

    def leaving(block, i):
        cols = pl.ds(pl.multiple_of(block * width, width), width)
        return pltpu.make_async_copy(held[i].at[:, cols], outs[i].at[:, cols], sems.at[block, i])

    def strip(block, blocks, *views):
        gates_strip(inner, shards, *views)
        for i in range(3):
            leaving(block, i).start()

    looped(strip, (None,) + (ROWS,) * 12, blocks, width)(*inputs, *held)
    for block in range(blocks):
        for i in range(3):
            leaving(block, i).wait()


def gates_strip(
    inner, shards, rank_ref, one_ref, two_ref, val_ref, out_ref, skip_ref, conv_ref, corr_ref, late_ref, part_ref,
    grad_one_ref, grad_two_ref, grad_value_ref,
):
    late = late_ref[...] if inner else part_ref[...].astype(f32)
    upper = rank_ref[0] >= shards // 2
    zero = jnp.zeros_like(late)
    one = one_ref[...].astype(f32)
    val = val_ref[...].astype(f32)
    out = out_ref[...].astype(f32)
    skip = skip_ref[...]
    conv = conv_ref[...] + jnp.where(upper, late, zero)
    corr = corr_ref[...] + jnp.where(upper, zero, late)
    grad_two_ref[...] = (out * (conv + skip * (one * val))).astype(bf16)
    mid = corr + skip * (out * two_ref[...].astype(f32))
    grad_one_ref[...] = (mid * val).astype(bf16)
    grad_value_ref[...] = (mid * one).astype(bf16)


def finish_kernel(
    channels, shards, rank_ref, own_ref, come_ref, first_ref, first_come_ref, second_out, first_out, bias_out, second,
    first, bias, sems,
):
    rank = rank_ref[0]
    inner = jnp.logical_and(rank > 0, rank < shards - 1)
    lanes = channels // 128
    copies = [
        pltpu.make_async_copy(held, out, sems.at[i])
        for i, (held, out) in enumerate(((second, second_out), (first, first_out), (bias, bias_out)))
    ]
    picked = jnp.where(inner, own_ref[...], come_ref[...])
    second[...] = picked[:, :channels].astype(f32)
    copies[0].start()
    first[...] = jnp.where(inner, first_ref[...], first_come_ref[...])
    copies[1].start()
    rows = get_side(picked, channels, lanes, first.shape[1])[0]
    for i in range(lanes):
        bias[:, i * 128 : (i + 1) * 128] = rows[i : i + 1]
    copies[2].start()
    for copy in copies:
        copy.wait()


def few_shards_body(
    x_one, x_two, values, grad_out, first_weight, second_weight, skip_bias, decay_rate
):
    rows, channels = x_one.shape
    shards = lax.axis_size("ctx")
    feat_count, hid_count = first_weight.shape
    seq_len = rows * shards
    double = 2 * rows
    width = min(512, channels)
    blocks = channels // width
    wide = 2 * width if blocks % 4 == 0 else width
    few = channels // wide
    rank = lax.axis_index("ctx").astype(jnp.int32).reshape(1)
    front, back = block_tables(rows)
    feats = feature_table(seq_len)
    featt = np.ascontiguousarray(feats.T)
    skip_row = skip_bias.reshape(1, channels)
    rate_row = decay_rate.reshape(1, channels)
    smem = pl.BlockSpec(memory_space=pltpu.SMEM)
    vmem = pl.BlockSpec(memory_space=pltpu.VMEM)
    anywhere = pl.BlockSpec(memory_space=pl.ANY)
    mebi = 1024 * 1024

    def shape(*dims, dtype=f32):
        return jax.ShapeDtypeStruct(dims, dtype)

    def call(kernel, name, units, out_shape, in_specs, out_specs=None, scratch=(), limit=16, aliases={}):
        return pl.pallas_call(
            kernel,
            in_specs=in_specs,
            out_specs=out_specs if out_specs is not None else [vmem] * len(out_shape),
            out_shape=out_shape,
            scratch_shapes=scratch,
            input_output_aliases=aliases,
            compiler_params=pltpu.CompilerParams(vmem_limit_bytes=limit * mebi),
            cost_estimate=pl.CostEstimate(
                flops=2 * units * double * double * channels, bytes_accessed=rows * channels, transcendentals=0
            ),
            name=name,
        )

    def move(array, pairs):
        return lax.ppermute(array, "ctx", pairs)

    inward = [(0, 1), (shards - 1, shards - 2)]
    outward = [(1, 0), (shards - 2, shards - 1)]
    across = [(1, 2), (2, 1)]
    alone = [(0, 0), (shards - 1, shards - 1)]
    pay_shape = (hid_count, channels + SIDE)
    block_bf16 = shape(rows, channels, dtype=bf16)
    block_f32 = shape(rows, channels)

    row_step = max(rows // 2, 16)
    gate_rows = pl.BlockSpec((row_step, channels), lambda i: (i, 0))
    pair, other, edge, bias = pl.pallas_call(
        products_kernel,
        grid=(rows // row_step,),
        in_specs=[smem] + [gate_rows] * 4,
        out_specs=[gate_rows] * 3 + [pl.BlockSpec((1, channels), lambda i: (0, 0))],
        out_shape=[block_bf16] * 3 + [shape(1, channels)],
        compiler_params=pltpu.CompilerParams(vmem_limit_bytes=64 * mebi),
        name="products",
    )(rank, x_one, x_two, values, grad_out)
    pair_in = move(pair, inward + outward)
    middle_in = move(other, across)

    own_shapes = [
        shape(rows, feat_count), shape(feat_count, hid_count), block_bf16, block_bf16, shape(hid_count, channels),
        shape(1, channels), shape(double, double, dtype=bf16), shape(double, double, dtype=bf16),
        shape(feat_count, seq_len), shape(1, channels), shape(*pay_shape, dtype=bf16),
    ]
    (send,) = call(
        only(False, shards, 0, functools.partial(own_kernel, rows, shards, channels, blocks, width)), "own_pair", 8,
        [shape(*pay_shape, dtype=bf16)],
        [smem] + [anywhere] * 10,
        out_specs=[anywhere],
        scratch=[pltpu.VMEM(s.shape, s.dtype) for s in own_shapes]
        + [
            pltpu.VMEM((2 * hid_count, rows), bf16), pltpu.VMEM((rows, hid_count), f32),
            pltpu.SemaphoreType.DMA((10,)), pltpu.SemaphoreType.DMA,
        ],
        limit=60,
    )(rank, feats[:rows], first_weight, pair, other, second_weight, rate_row, front, back, featt, bias)
    come = move(send, inward)
    late_feats, _ = lax.optimization_barrier((jnp.asarray(feats), send))
    spec, trans, slope = call(
        functools.partial(filters_kernel, rows, shards, blocks, width), "filters", 8,
        [
            shape(shards, double, channels, dtype=bf16), shape(2 * hid_count, seq_len, dtype=bf16),
            shape(seq_len, hid_count),
        ],
        [vmem] * 5,
        scratch=[pltpu.VMEM((seq_len, 3 * hid_count), bf16)],
    )(late_feats, first_weight, second_weight, rate_row, front)

    edge, _ = lax.optimization_barrier((edge, slope))
    far = move(edge, [(0, 2), (shards - 1, shards - 3)])
    pair_in, come = lax.optimization_barrier((pair_in, come))

    conv, corr, ahead, sums, first, near_spec = call(
        functools.partial(near_kernel, rows, shards, blocks, width), "near_blocks", 20,
        [block_f32] * 3
        + [shape(hid_count, channels), shape(feat_count, hid_count), shape(double, channels)],
        [smem] + [vmem] * 12,
        scratch=[
            pltpu.VMEM((4, double, width), f32),
            pltpu.VMEM((3, double, width), bf16),
            pltpu.VMEM((shards - 1, double, width), bf16),
            pltpu.VMEM((shards - 1, double, width), bf16),
            pltpu.VMEM(((shards - 1) * rows, hid_count), f32),
        ],
    )(rank, pair, other, pair_in, middle_in, spec, second_weight, rate_row, front, back, trans, featt, slope)

    part, far_spec = call(
        only(
            True, shards, 0,
            looped(
                functools.partial(far_kernel, rows),
                (None, ROWS, (slice(3, 4), slice(None)), None, None, ROWS, ROWS, ROWS),
                few, wide,
            ),
        ),
        "far_block", 1,
        [block_bf16, shape(double, channels)],
        [smem] + [vmem] * 5,
    )(rank, far, spec, front, back, ahead)
    (late,) = call(
        only(
            True, shards, 0,
            looped(
                functools.partial(late_kernel, rows),
                (None, ROWS, (slice(2, 3), slice(None)), None, ROWS),
                few, wide,
            ),
        ),
        "late_block", 1,
        [block_f32],
        [smem] + [vmem] * 3,
    )(rank, far_spec, spec, back)
    part_come = move(part, outward)

    pay, first = call(
        only(
            True, shards, 1,
            looped(
                functools.partial(last_kernel, rows, shards, channels),
                (None, None, ROWS, ROWS, ROWS, ROWS, None, None, None, None, ROWS),
                few, wide,
            ),
        ),
        "last_pair", 1,
        [shape(*pay_shape, dtype=bf16), shape(feat_count, hid_count)],
        [anywhere, smem] + [vmem] * 12,
        scratch=[pltpu.VMEM((2 * rows, hid_count), f32)],
    )(part, rank, near_spec, far_spec, second_weight, rate_row, back, trans, featt, slope, sums, first, bias, come)
    pay_come = move(pay, across + alone)
    group = lax.axis_size(("ch", "sub"))
    bit = 1
    while bit < group:
        first = first + lax.ppermute(first, ("ch", "sub"), [(i, i ^ bit) for i in range(group)])
        bit *= 2

    (total,) = call(
        functools.partial(total_kernel, channels, hid_count), "total", 0,
        [shape(*pay_shape, dtype=bf16)],
        [anywhere] * 3 + [vmem] * 2,
    )(part_come, first, late, pay, pay_come)
    total_come = move(total, inward + outward)

    def gates(inner, *before):
        return call(
            only(
                inner, shards, len(before),
                functools.partial(gates_kernel, inner, shards, blocks, width, len(before)),
            ),
            "gates", 0,
            [block_bf16] * 3,
            [anywhere] * len(before) + [smem] + [vmem] * 9,
            out_specs=[anywhere] * 3,
            scratch=[pltpu.VMEM((rows, channels), bf16)] * 3 + [pltpu.SemaphoreType.DMA((blocks, 3))],
            aliases={i: i for i in range(3)} if inner else {},
        )(*before, rank, x_one, x_two, values, grad_out, skip_row, conv, corr, late, part_come)

    grads = gates(False, total)
    first, _ = lax.optimization_barrier((first, grads[0]))
    first = first + move(first, across + alone)
    first_come = move(first, inward + outward)
    grad_one, grad_two, grad_value = gates(True, *grads)

    outs = [shape(hid_count, channels), shape(feat_count, hid_count), shape(1, channels)]
    grad_second, grad_first, grad_bias = call(
        functools.partial(finish_kernel, channels, shards), "finish", 0,
        outs,
        [smem] + [vmem] * 4,
        out_specs=[anywhere] * 3,
        scratch=[pltpu.VMEM(o.shape, f32) for o in outs] + [pltpu.SemaphoreType.DMA((3,))],
    )(rank, total, total_come, first, first_come)
    return (grad_one, grad_two, grad_value, grad_first, grad_second, grad_bias.reshape(channels))


def solution(mesh):
    in_specs = (
        P(("parts", "ctx"), ("ch", "sub")),
        P(("parts", "ctx"), ("ch", "sub")),
        P(("parts", "ctx"), ("ch", "sub")),
        P(("parts", "ctx"), ("ch", "sub")),
        P(),
        P(None, ("ch", "sub")),
        P(("ch", "sub")),
        P(("ch", "sub")),
    )
    out_specs = (
        P(("parts", "ctx"), ("ch", "sub")),
        P(("parts", "ctx"), ("ch", "sub")),
        P(("parts", "ctx"), ("ch", "sub")),
        P("parts", None),
        P("parts", ("ch", "sub")),
        P(("parts", "ch", "sub")),
    )
    body = few_shards_body if mesh.shape["ctx"] == 4 else many_shards_body
    return jax.shard_map(body, mesh=mesh, in_specs=in_specs, out_specs=out_specs, check_vma=False)
```

```python
import functools
import math

import jax
import jax.numpy as jnp
import numpy as np
from jax import lax
from jax.experimental import pallas as pl
from jax.experimental.pallas import tpu as pltpu
from jax.sharding import PartitionSpec as P

band_steps = (1763, 1201, 811, 547, 367, 251, 167, 113, 79, 53, 37, 23, 17, 11, 7, 3)
highest = lax.Precision.HIGHEST
f32 = jnp.float32
bf16 = jnp.bfloat16


def features(positions):
    multiplier = jnp.array(band_steps, dtype=jnp.int32)
    phase = positions[:, None] * multiplier[None, :] % 4096
    angle = phase.astype(jnp.float32) * (2.0 * math.pi / 4096.0)
    return jnp.concatenate([jnp.cos(angle), jnp.sin(angle)], axis=1)


def tables(out_count, in_count, modulus, sign_value):
    row_index = lax.broadcasted_iota(jnp.int32, (out_count, in_count), 0)
    col_index = lax.broadcasted_iota(jnp.int32, (out_count, in_count), 1)
    angle = (row_index * col_index % modulus).astype(jnp.float32) * (2.0 * math.pi / modulus)
    return (jnp.cos(angle), sign_value * jnp.sin(angle))


def twiddle(spec_re, spec_im, freq_count, span, modulus, sign_value):
    freq_index = lax.broadcasted_iota(jnp.int32, (freq_count, span), 0)
    pos_index = lax.broadcasted_iota(jnp.int32, (freq_count, span), 1)
    angle = (freq_index * pos_index % modulus).astype(jnp.float32) * (2.0 * math.pi / modulus)
    factor_re = jnp.cos(angle)[None, None, :, :]
    factor_im = (sign_value * jnp.sin(angle))[None, None, :, :]
    return (spec_re * factor_re - spec_im * factor_im, spec_re * factor_im + spec_im * factor_re)


def contract(kernel, array):
    return jnp.einsum(
        "lj,mckj->mckl", kernel, array, precision=highest, preferred_element_type=jnp.float32
    )


def along_positions(spec_re, spec_im, kernel_re, kernel_im):
    return (
        contract(kernel_re, spec_re) - contract(kernel_im, spec_im),
        contract(kernel_re, spec_im) + contract(kernel_im, spec_re),
    )


def many_shards_body(
    x_one, x_two, values, grad_out, first_weight, second_weight, skip_bias, decay_rate
):
    row_count, chan_count = x_one.shape
    shards = lax.axis_size("ctx")
    rank = lax.axis_index("ctx")
    seq_len = row_count * shards
    total = 2 * seq_len
    narrow = chan_count // shards
    chan_weight = lax.dynamic_slice_in_dim(second_weight, rank * narrow, narrow, 1)
    chan_rate = lax.dynamic_slice_in_dim(decay_rate, rank * narrow, narrow, 0)
    source = x_one.astype(jnp.float32) * values.astype(jnp.float32)
    cotan = grad_out.astype(jnp.float32) * x_two.astype(jnp.float32)
    spread = lax.all_to_all(
        jnp.stack([source.T, cotan.T])[:, :, None, :],
        "ctx",
        split_axis=1,
        concat_axis=2,
        tiled=True,
    )
    far_source = spread[0]
    far_cotan = spread[1]
    positions = jnp.arange(seq_len, dtype=jnp.int32)
    feats = features(positions)
    pre_act = jnp.dot(feats, first_weight, precision=highest, preferred_element_type=jnp.float32)
    hidden = jnp.sin(pre_act)
    envelope = jnp.exp(-chan_rate[:, None] * positions.astype(jnp.float32)[None, :]) * float(
        seq_len
    ) ** (-0.5)
    filt = (
        jnp.einsum(
            "th,hc->ct", hidden, chan_weight, precision=highest, preferred_element_type=jnp.float32
        )
        * envelope
    )
    filt_blocks = filt.reshape(narrow, shards, row_count)
    fields = jnp.stack([far_source, far_cotan])

    def first_section(kernel):
        field_part = jnp.einsum(
            "kn,mcnj->mckj", kernel, fields, precision=highest, preferred_element_type=jnp.float32
        )
        filter_part = jnp.einsum(
            "kn,cnj->ckj",
            kernel,
            filt_blocks,
            precision=highest,
            preferred_element_type=jnp.float32,
        )
        return jnp.concatenate([field_part, filter_part[None]], axis=0)

    first_re, first_im = tables(2 * shards, shards, 2 * shards, -1.0)
    spec_re, spec_im = (first_section(first_re), first_section(first_im))
    spec_re, spec_im = twiddle(spec_re, spec_im, 2 * shards, row_count, total, -1.0)
    fwd_re, fwd_im = tables(row_count, row_count, row_count, -1.0)
    spec_re, spec_im = along_positions(spec_re, spec_im, fwd_re, fwd_im)
    source_re, source_im = (spec_re[0], spec_im[0])
    cotan_re, cotan_im = (spec_re[1], spec_im[1])
    filter_re, filter_im = (spec_re[2], spec_im[2])
    prod_re = jnp.stack(
        [
            source_re * filter_re - source_im * filter_im,
            cotan_re * filter_re + cotan_im * filter_im,
            cotan_re * source_re + cotan_im * source_im,
        ]
    )
    prod_im = jnp.stack(
        [
            source_re * filter_im + source_im * filter_re,
            cotan_im * filter_re - cotan_re * filter_im,
            cotan_im * source_re - cotan_re * source_im,
        ]
    )
    back_re, back_im = tables(row_count, row_count, row_count, 1.0)
    prod_re, prod_im = along_positions(prod_re, prod_im, back_re, back_im)
    prod_re, prod_im = twiddle(prod_re, prod_im, 2 * shards, row_count, total, 1.0)
    last_re, last_im = tables(shards, 2 * shards, 2 * shards, 1.0)
    field_out = jnp.einsum(
        "nk,mckj->mcnj", last_re, prod_re[:2], precision=highest, preferred_element_type=jnp.float32
    ) - jnp.einsum(
        "nk,mckj->mcnj", last_im, prod_im[:2], precision=highest, preferred_element_type=jnp.float32
    )
    field_out = field_out * (1.0 / total)
    filt_grad = jnp.einsum(
        "nk,ckj->cnj", last_re, prod_re[2], precision=highest, preferred_element_type=jnp.float32
    ) - jnp.einsum(
        "nk,ckj->cnj", last_im, prod_im[2], precision=highest, preferred_element_type=jnp.float32
    )
    filt_grad = (filt_grad * (1.0 / total)).reshape(narrow, seq_len)
    modulated = filt_grad * envelope
    weight_part = jnp.einsum(
        "th,ct->hc", hidden, modulated, precision=highest, preferred_element_type=jnp.float32
    )
    hidden_grad = jnp.einsum(
        "ct,hc->th", modulated, chan_weight, precision=highest, preferred_element_type=jnp.float32
    )
    first_part = jnp.dot(
        feats.T,
        hidden_grad * jnp.cos(pre_act),
        precision=highest,
        preferred_element_type=jnp.float32,
    )
    grad_first = lax.psum(first_part, ("ctx", "ch", "sub"))
    returned = lax.all_to_all(
        field_out.astype(jnp.bfloat16), "ctx", split_axis=2, concat_axis=1, tiled=True
    ).astype(field_out.dtype)
    conv_part = returned[0, :, 0, :].T
    corr_part = returned[1, :, 0, :].T
    grad_two = (grad_out.astype(jnp.float32) * (conv_part + skip_bias[None, :] * source)).astype(
        jnp.bfloat16
    )
    grad_mid = corr_part + skip_bias[None, :] * cotan
    grad_one = (grad_mid * values.astype(jnp.float32)).astype(jnp.bfloat16)
    grad_value = (grad_mid * x_one.astype(jnp.float32)).astype(jnp.bfloat16)
    grad_bias = lax.psum(jnp.sum(source * cotan, axis=0), "ctx")
    grad_second = lax.all_gather(weight_part, "ctx", axis=1, tiled=True)
    return (grad_one, grad_two, grad_value, grad_first, grad_second, grad_bias)


STEP = 16
SIDE = 128


def halves(array):
    array = np.asarray(array, np.float32)
    high = array.astype(bf16)
    low = (array - high.astype(np.float32)).astype(bf16)
    return high, low


def block_tables(rows):
    freq = np.concatenate([np.arange(0, rows, 2), np.arange(1, rows, 2)])
    phase = (2 * freq + 1)[:, None] * np.arange(rows)[None, :] % (4 * rows)
    angle = phase * (2.0 * np.pi / (4 * rows))
    forward = np.concatenate([np.cos(angle), -np.sin(angle)], axis=0)
    front = np.ascontiguousarray(np.concatenate(halves(forward), axis=1))
    back = np.ascontiguousarray(np.concatenate(halves(forward.T / rows), axis=0))
    return front, back


def feature_table(seq_len):
    phase = np.arange(seq_len)[:, None] * np.array(band_steps)[None, :] % 4096
    angle = phase * (2.0 * np.pi / 4096.0)
    return np.concatenate([np.cos(angle), np.sin(angle)], axis=1).astype(np.float32)


def split(array):
    high = array.astype(bf16)
    return high, (array - high.astype(f32)).astype(bf16)


def dot(left, right):
    return jnp.dot(left, right, preferred_element_type=f32)


def exact_dot(left, right):
    return jnp.dot(left, right, precision=highest, preferred_element_type=f32)


def dot_across(left, right):
    return lax.dot_general(left, right, (((1,), (1,)), ((), ())), preferred_element_type=f32)


def decay(rate, rows, scale):
    place = lax.broadcasted_iota(jnp.int32, (rows, rate.shape[1]), 0)
    return jnp.exp(-place.astype(f32) * rate) * scale


def times(a, b):
    return a[0] * b[0] - a[1] * b[1], a[0] * b[1] + a[1] * b[0]


def conj_times(a, b):
    return a[0] * b[0] + a[1] * b[1], a[0] * b[1] - a[1] * b[0]


def plus(a, b):
    return a[0] + b[0], a[1] + b[1]


def scaled(a, factor):
    return a[0] * factor, a[1] * factor


def choose(condition, a, b):
    return jnp.where(condition, a[0], b[0]), jnp.where(condition, a[1], b[1])


def turned(a, sign):
    return (a[1], -a[0]) if sign > 0 else (-a[1], a[0])


def forward(front_ref, block):
    return dot(front_ref[...], jnp.concatenate([block, block], axis=0))


def backward(back_ref, high, low=None):
    both = dot(back_ref[...], high)
    rows = both.shape[0] // 2
    out = both[:rows] + both[rows:]
    return out if low is None else out + dot(back_ref[:rows], low)


def row_groups(rows):
    for step in range(rows // STEP):
        sign = 1 if step * STEP < rows // 2 else -1
        yield slice(step * STEP, (step + 1) * STEP), slice(rows + step * STEP, rows + (step + 1) * STEP), sign


def weight_sums(trans, m_high, m_low):
    both = dot(trans, m_high)
    count = both.shape[0] // 2
    return both[:count] + both[count:] + dot(trans[:count], m_low)


def hidden_sums(m_high, m_low, w_high, w_low):
    left = jnp.concatenate([m_high, m_high, m_low], axis=1)
    right = jnp.concatenate([w_high, w_low, w_high], axis=1)
    return dot_across(left, right)


def looped(kernel, kinds, blocks, width):
    def over_strips(*refs):
        def step(block, carry):
            cols = pl.ds(pl.multiple_of(block * width, width), width)
            views = [
                ref if kind is None else ref.at[(*kind, cols)]
                for ref, kind in zip(refs, kinds + (None,) * (len(refs) - len(kinds)))
            ]
            kernel(block, blocks, *views)
            return carry

        lax.fori_loop(0, blocks, step, 0)

    return over_strips


ROWS = (slice(None),)
CUBE = (slice(None), slice(None))


def products_kernel(rank_ref, one_ref, two_ref, val_ref, out_ref, pair_ref, other_ref, edge_ref, bias_ref):
    source = one_ref[...].astype(f32) * val_ref[...].astype(f32)
    cotan = out_ref[...].astype(f32) * two_ref[...].astype(f32)
    even = rank_ref[0] % 2 == 0
    pair_ref[...] = jnp.where(even, source, cotan).astype(bf16)
    edge_ref[...] = pair_ref[...]
    other_ref[...] = jnp.where(even, cotan, source).astype(bf16)
    part = jnp.sum(source * cotan, axis=0, keepdims=True)

    @pl.when(pl.program_id(0) == 0)
    def _():
        bias_ref[...] = part

    @pl.when(pl.program_id(0) > 0)
    def _():
        bias_ref[...] += part


def ordered(first, a, b):
    return (jnp.where(first, a, b), jnp.where(first, b, a))


def sin_cos(angle):
    turns = jnp.floor(angle * (2.0 / math.pi) + 0.5)
    rest = ((angle - turns * 1.5703125) - turns * 4.837512969970703e-4) - turns * 7.54978995489188e-8
    square = rest * rest
    sine = rest + rest * square * (
        -1.6666654611e-1 + square * (8.3321608736e-3 + square * -1.9515295891e-4)
    )
    cosine = 1.0 - 0.5 * square + square * square * (
        4.166664568298827e-2 + square * (-1.388731625493765e-3 + square * 2.443315711809948e-5)
    )
    quarter = turns.astype(jnp.int32)
    odd = (quarter & 1) == 1
    sin_sign = jnp.where((quarter & 2) == 2, -1.0, 1.0).astype(f32)
    cos_sign = jnp.where(((quarter + 1) & 2) == 2, -1.0, 1.0).astype(f32)
    return jnp.where(odd, cosine, sine) * sin_sign, jnp.where(odd, sine, cosine) * cos_sign


def turned_over(hidden, slope):
    both = jnp.concatenate([hidden, slope], axis=1).T
    return jnp.concatenate(split(both[: hidden.shape[1]]), axis=0)


def filters_kernel(
    rows, shards, blocks, width, feats_ref, first_ref, weight_ref, rate_ref, front_ref, spec_ref, trans_ref, slope_ref,
    hid_ref,
):
    hidden, slope = sin_cos(exact_dot(feats_ref[...], first_ref[...]))
    slope_ref[...] = slope
    high, low = split(hidden)
    hid_ref[...] = jnp.concatenate([high, high, low], axis=1)
    trans_ref[...] = turned_over(hidden, slope)
    strips = looped(
        functools.partial(filter_strip, rows, shards), (None, ROWS, ROWS, None, CUBE), blocks, width
    )
    strips(hid_ref, weight_ref, rate_ref, front_ref, spec_ref)


def filter_strip(rows, shards, block, blocks, hid_ref, weight_ref, rate_ref, front_ref, spec_ref):
    scale = float(rows * shards) ** -0.5
    w_high, w_low = split(weight_ref[...])
    stacked = jnp.concatenate([w_high, w_low, w_high], axis=0)
    rate = rate_ref[...]
    env = decay(rate, rows, scale)
    before = None
    for lag in range(shards):
        part = dot(hid_ref[lag * rows : (lag + 1) * rows, :], stacked)
        part = part * (env * jnp.exp(rate * (-float(lag * rows))))
        f_high, f_low = split(part)
        now = forward(front_ref, f_high) + dot(front_ref[:, :rows], f_low)
        for re, im, sign in row_groups(rows):
            here = (now[re], now[im])
            if before is not None:
                here = plus(here, turned((before[re], before[im]), -sign))
            spec_ref[lag, re, :] = here[0].astype(bf16)
            spec_ref[lag, im, :] = here[1].astype(bf16)
        before = now


def own_kernel(rows, shards, channels, blocks, width, rank_ref, *refs):
    inputs, send_out, held = refs[:10], refs[10], refs[11:21]
    send_ref, trans_ref, acc_ref, sems, out_sem = refs[21:]
    (
        feats_ref, first_ref, pair_ref, other_ref, weight_ref, rate_ref, front_ref, back_ref, featt_ref, bias_ref
    ) = held
    copies = [pltpu.make_async_copy(far, near, sems.at[i]) for i, (far, near) in enumerate(zip(inputs, held))]
    for copy in copies:
        copy.start()
    acc_ref[...] = jnp.zeros_like(acc_ref)
    copies[0].wait()
    copies[1].wait()
    hidden, slope = sin_cos(exact_dot(feats_ref[...], first_ref[...]))
    trans_ref[...] = turned_over(hidden, slope)
    for copy in copies[2:]:
        copy.wait()
    kinds = (None, ROWS, ROWS, ROWS, ROWS, None, None, None, ROWS, None)
    looped(functools.partial(own_strip, rows, shards), kinds, blocks, width)(
        rank_ref, pair_ref, other_ref, weight_ref, rate_ref, front_ref, back_ref, trans_ref, send_ref, acc_ref
    )
    first = exact_dot(featt_ref[:, :rows], acc_ref[...] * slope)
    put_side(send_ref, channels, fold(bias_ref[...]), first)
    last = pltpu.make_async_copy(send_ref, send_out, out_sem)
    last.start()
    last.wait()


def own_strip(
    rows, shards, block, blocks, rank_ref, pair_ref, other_ref, weight_ref, rate_ref, front_ref, back_ref, trans_ref,
    send_ref, acc_ref,
):
    source, cotan = ordered(rank_ref[0] % 2 == 0, pair_ref[...], other_ref[...])
    x0 = forward(front_ref, source)
    c0 = forward(front_ref, cotan)
    pair = conj_times((x0[:rows], x0[rows:]), (c0[:rows], c0[rows:]))
    high, low = split(jnp.concatenate(pair, axis=0))
    env = decay(rate_ref[...], rows, float(rows * shards) ** -0.5)
    m_high, m_low = split(backward(back_ref, high, low) * env)
    send_ref[...] = weight_sums(trans_ref[...], m_high, m_low).astype(bf16)
    acc_ref[...] += hidden_sums(m_high, m_low, *split(weight_ref[...]))


def fold(bias):
    return jnp.concatenate([bias[:, i * 128 : (i + 1) * 128] for i in range(bias.shape[1] // 128)], axis=0)


def put_side(pay_ref, channels, bias, first=None):
    half = pay_ref.shape[0] // 2
    pay_ref[:, channels:] = jnp.zeros((2 * half, SIDE), bf16)
    for start, part in zip((0, half // 2), split(bias)):
        pay_ref[start : start + bias.shape[0], channels:] = part
    if first is not None:
        pay_ref[half:, channels:] = jnp.concatenate(split(first), axis=1)


def get_side(pay, channels, lanes, hid_count):
    half = pay.shape[0] // 2
    side = pay[:, channels:].astype(f32)
    low = side[half:]
    return side[:lanes] + side[half // 2 : half // 2 + lanes], low[:, :hid_count] + low[:, hid_count:]


def near_kernel(
    rows, shards, blocks, width, rank_ref, pair_ref, other_ref, pair_in_ref, middle_in_ref, spec_ref, weight_ref,
    rate_ref, front_ref, back_ref, trans_ref, featt_ref, slope_ref, conv_ref, corr_ref, ahead_ref, sums_ref, first_ref,
    near_ref, fields, fast, high_ref, low_ref, acc_ref,
):
    rank = rank_ref[0]
    inner = jnp.logical_and(rank > 0, rank < shards - 1)
    count = shards - 1
    kinds = (None, None, None) + (ROWS,) * 4 + (CUBE, ROWS, ROWS)
    common = (
        rank_ref, front_ref, back_ref, pair_ref, other_ref, pair_in_ref, middle_in_ref, spec_ref, conv_ref, corr_ref,
        fields, fast,
    )

    @pl.when(jnp.logical_not(inner))
    def _():
        looped(functools.partial(edge_strip, rows, shards), kinds, blocks, width)(*common)

    @pl.when(inner)
    def _():
        acc_ref[...] = jnp.zeros_like(acc_ref)
        looped(
            functools.partial(inner_strip, rows, shards), kinds + (None,) * 3 + (ROWS,) * 5, blocks, width
        )(*common, trans_ref, weight_ref, rate_ref, ahead_ref, sums_ref, near_ref, high_ref, low_ref, acc_ref)
        first_ref[...] = exact_dot(
            featt_ref[:, : count * rows], acc_ref[...] * slope_ref[: count * rows, :]
        )


def edge_strip(
    rows, shards, block, blocks, rank_ref, front_ref, back_ref, pair_ref, other_ref, pair_in_ref, middle_in_ref,
    spec_ref, conv_ref, corr_ref, fields, fast,
):
    del middle_in_ref
    top = rank_ref[0] == shards - 1
    source, cotan = ordered(rank_ref[0] % 2 == 0, pair_ref[...], other_ref[...])
    for index, block_in in enumerate((source, cotan, pair_in_ref[...])):
        fields[index] = forward(front_ref, block_in)
    on_conv = jnp.where(top, 1.0, 0.0).astype(f32)
    on_corr = jnp.where(top, 0.0, 1.0).astype(f32)
    for re, im, sign in row_groups(rows):
        x0, c0, near = ((fields[i, re, :], fields[i, im, :]) for i in range(3))
        w0, w1 = ((spec_ref[i, re, :].astype(f32), spec_ref[i, im, :].astype(f32)) for i in range(2))
        values = (
            plus(times(w0, x0), scaled(times(w1, near), on_conv)),
            plus(conj_times(w0, c0), scaled(conj_times(w1, near), on_corr)),
        )
        for index, value in enumerate(values):
            fast[index, re, :] = value[0].astype(bf16)
            fast[index, im, :] = value[1].astype(bf16)
    conv_ref[...] = backward(back_ref, fast[0])
    corr_ref[...] = backward(back_ref, fast[1])


def inner_strip(
    rows, shards, block, blocks, rank_ref, front_ref, back_ref, pair_ref, other_ref, pair_in_ref, middle_in_ref,
    spec_ref, conv_ref, corr_ref, fields, fast, trans_ref, weight_ref, rate_ref, ahead_ref, sums_ref, near_ref, high_ref,
    low_ref, acc_ref,
):
    lower = rank_ref[0] == 1
    upper = jnp.where(lower, 0.0, 1.0).astype(f32)
    side = jnp.where(lower, -1.0, 1.0).astype(f32)
    count = shards - 1
    blocks_in = (
        *ordered(lower, other_ref[...], pair_ref[...]), *ordered(lower, pair_in_ref[...], middle_in_ref[...])
    )
    for index, block_in in enumerate(blocks_in):
        fields[index] = forward(front_ref, block_in)
    for re, im, sign in row_groups(rows):
        x0, c0, x1, c1 = ((fields[i, re, :], fields[i, im, :]) for i in range(4))
        w0, w1, w2 = ((spec_ref[i, re, :].astype(f32), spec_ref[i, im, :].astype(f32)) for i in range(3))
        values = (
            plus(times(w0, x0), times(w1, x1)),
            plus(conj_times(w0, c0), conj_times(w1, c1)),
            times((w2[0], w2[1] * side), choose(lower, c1, x1)),
        )
        for index, value in enumerate(values):
            fast[index, re, :] = value[0].astype(bf16)
            fast[index, im, :] = value[1].astype(bf16)
        near_ref[re, :], near_ref[im, :] = choose(lower, x1, c1)
        zero = conj_times(x0, c0)
        one = plus(conj_times(x1, c0), scaled(conj_times(x0, c1), upper))
        two = conj_times(x1, c1)
        for index, value in enumerate((plus(zero, turned(one, sign)), plus(one, turned(two, sign)), two)):
            for part, where in zip(value, (re, im)):
                high_ref[index, where, :], low_ref[index, where, :] = split(part)
    conv_ref[...] = backward(back_ref, fast[0])
    corr_ref[...] = backward(back_ref, fast[1])
    ahead_ref[...] = backward(back_ref, fast[2])
    rate = rate_ref[...]
    env = decay(rate, rows, float(rows * shards) ** -0.5)
    parts = []
    for lag in range(count):
        grad = backward(back_ref, high_ref[lag], low_ref[lag])
        parts.append(split(grad * (env * jnp.exp(rate * (-float(lag * rows))))))
    m_high = jnp.concatenate([p[0] for p in parts], axis=0)
    m_low = jnp.concatenate([p[1] for p in parts], axis=0)
    sums_ref[...] = weight_sums(trans_ref[:, : count * rows], m_high, m_low)
    acc_ref[...] += hidden_sums(m_high, m_low, *split(weight_ref[...]))


def only(inner, shards, rank_at, kernel):
    def run(*refs):
        rank = refs[rank_at][0]

        @pl.when(jnp.logical_and(rank > 0, rank < shards - 1) == inner)
        def _():
            kernel(*refs)

    return run


def far_kernel(
    rows, block, blocks, rank_ref, far_ref, spec_ref, front_ref, back_ref, ahead_ref, part_ref, far_spec_ref
):
    side = jnp.where(rank_ref[0] == 2, 1.0, -1.0).astype(f32)
    far = forward(front_ref, far_ref[...])
    far_spec_ref[...] = far
    w3 = (spec_ref[0, :rows, :].astype(f32), spec_ref[0, rows:, :].astype(f32) * side)
    ahead = jnp.concatenate(times(w3, (far[:rows], far[rows:])), axis=0).astype(bf16)
    part_ref[...] = (ahead_ref[...] + backward(back_ref, ahead)).astype(bf16)


def late_kernel(rows, block, blocks, rank_ref, far_ref, spec_ref, back_ref, late_ref):
    side = jnp.where(rank_ref[0] == 2, 1.0, -1.0).astype(f32)
    w2 = (spec_ref[0, :rows, :].astype(f32), spec_ref[0, rows:, :].astype(f32) * side)
    late = jnp.concatenate(times(w2, (far_ref[:rows, :], far_ref[rows:, :])), axis=0).astype(bf16)
    late_ref[...] = backward(back_ref, late)


def last_kernel(
    rows, shards, channels, block, blocks, after_ref, rank_ref, near_ref, far_ref, weight_ref, rate_ref, back_ref,
    trans_ref, featt_ref, slope_ref, sums_ref, first_ref, bias_ref, in_ref, pay_ref, total_ref, acc_ref,
):
    del after_ref
    hid_count, width = weight_ref.shape
    lower = rank_ref[0] == 1
    start = pl.multiple_of(block * width, width)
    here = sums_ref[...] + in_ref[:, pl.ds(start, width)].astype(f32)
    mine = (block < blocks // 2) == lower

    @pl.when(block == 0)
    def _():
        acc_ref[...] = jnp.zeros_like(acc_ref)

    @pl.when(mine)
    def _():
        sign = jnp.where(lower, 1.0, -1.0).astype(f32)
        three = conj_times((near_ref[:rows, :], near_ref[rows:, :]), (far_ref[:rows, :], far_ref[rows:, :]))
        three = (three[0], three[1] * sign)
        half = rows // 2
        two = jnp.concatenate([three[1][:half], -three[1][half:], -three[0][:half], three[0][half:]], axis=0)
        rate = rate_ref[...]
        env = decay(rate, rows, float(rows * shards) ** -0.5)
        parts = []
        for lag, value in ((shards - 2, two), (shards - 1, jnp.concatenate(three, axis=0))):
            grad = backward(back_ref, *split(value))
            parts.append(split(grad * (env * jnp.exp(rate * (-float(lag * rows))))))
        m_high = jnp.concatenate([p[0] for p in parts], axis=0)
        m_low = jnp.concatenate([p[1] for p in parts], axis=0)
        trans = trans_ref[:, (shards - 2) * rows :]
        pay_ref[:, pl.ds(start, width)] = (here + weight_sums(trans, m_high, m_low)).astype(bf16)
        w_high, w_low = split(weight_ref[...])
        acc_ref[...] += hidden_sums(m_high, m_low, w_high, w_low)

    @pl.when(jnp.logical_not(mine))
    def _():
        pay_ref[:, pl.ds(start, width)] = here.astype(bf16)

    @pl.when(block == blocks - 1)
    def _():
        first = exact_dot(
            featt_ref[:, (shards - 2) * rows :], acc_ref[...] * slope_ref[(shards - 2) * rows :, :]
        )
        lanes = channels // 128
        in_bias, in_first = get_side(in_ref[...], channels, lanes, hid_count)
        first = first + first_ref[...] + in_first
        put_side(pay_ref, channels, fold(bias_ref[...]) + in_bias)
        total_ref[...] = first


def total_kernel(channels, hid_count, part_ref, first_ref, late_ref, own_ref, come_ref, pay_ref):
    del part_ref, first_ref, late_ref
    lanes = channels // 128
    pay_ref[:, :channels] = (own_ref[:, :channels].astype(f32) + come_ref[:, :channels].astype(f32)).astype(bf16)
    own, come = (get_side(ref[...], channels, lanes, hid_count)[0] for ref in (own_ref, come_ref))
    put_side(pay_ref, channels, own + come)


def gates_kernel(inner, shards, blocks, width, before, *refs):
    refs = refs[before:]
    inputs, outs, held, sems = refs[:10], refs[10:13], refs[13:16], refs[16]

    def leaving(block, i):
        cols = pl.ds(pl.multiple_of(block * width, width), width)
        return pltpu.make_async_copy(held[i].at[:, cols], outs[i].at[:, cols], sems.at[block, i])

    def strip(block, blocks, *views):
        gates_strip(inner, shards, *views)
        for i in range(3):
            leaving(block, i).start()

    looped(strip, (None,) + (ROWS,) * 12, blocks, width)(*inputs, *held)
    for block in range(blocks):
        for i in range(3):
            leaving(block, i).wait()


def gates_strip(
    inner, shards, rank_ref, one_ref, two_ref, val_ref, out_ref, skip_ref, conv_ref, corr_ref, late_ref, part_ref,
    grad_one_ref, grad_two_ref, grad_value_ref,
):
    late = late_ref[...] if inner else part_ref[...].astype(f32)
    upper = rank_ref[0] >= shards // 2
    zero = jnp.zeros_like(late)
    one = one_ref[...].astype(f32)
    val = val_ref[...].astype(f32)
    out = out_ref[...].astype(f32)
    skip = skip_ref[...]
    conv = conv_ref[...] + jnp.where(upper, late, zero)
    corr = corr_ref[...] + jnp.where(upper, zero, late)
    grad_two_ref[...] = (out * (conv + skip * (one * val))).astype(bf16)
    mid = corr + skip * (out * two_ref[...].astype(f32))
    grad_one_ref[...] = (mid * val).astype(bf16)
    grad_value_ref[...] = (mid * one).astype(bf16)


def finish_kernel(
    channels, shards, rank_ref, own_ref, come_ref, first_ref, first_come_ref, second_out, first_out, bias_out, second,
    first, bias, sems,
):
    rank = rank_ref[0]
    inner = jnp.logical_and(rank > 0, rank < shards - 1)
    lanes = channels // 128
    copies = [
        pltpu.make_async_copy(held, out, sems.at[i])
        for i, (held, out) in enumerate(((second, second_out), (first, first_out), (bias, bias_out)))
    ]
    picked = jnp.where(inner, own_ref[...], come_ref[...])
    second[...] = picked[:, :channels].astype(f32)
    copies[0].start()
    first[...] = jnp.where(inner, first_ref[...], first_come_ref[...])
    copies[1].start()
    rows = get_side(picked, channels, lanes, first.shape[1])[0]
    for i in range(lanes):
        bias[:, i * 128 : (i + 1) * 128] = rows[i : i + 1]
    copies[2].start()
    for copy in copies:
        copy.wait()


def few_shards_body(
    x_one, x_two, values, grad_out, first_weight, second_weight, skip_bias, decay_rate
):
    rows, channels = x_one.shape
    shards = lax.axis_size("ctx")
    feat_count, hid_count = first_weight.shape
    seq_len = rows * shards
    double = 2 * rows
    width = min(512, channels)
    blocks = channels // width
    wide = 2 * width if blocks % 4 == 0 else width
    few = channels // wide
    rank = lax.axis_index("ctx").astype(jnp.int32).reshape(1)
    front, back = block_tables(rows)
    feats = feature_table(seq_len)
    featt = np.ascontiguousarray(feats.T)
    skip_row = skip_bias.reshape(1, channels)
    rate_row = decay_rate.reshape(1, channels)
    smem = pl.BlockSpec(memory_space=pltpu.SMEM)
    vmem = pl.BlockSpec(memory_space=pltpu.VMEM)
    anywhere = pl.BlockSpec(memory_space=pl.ANY)
    mebi = 1024 * 1024

    def shape(*dims, dtype=f32):
        return jax.ShapeDtypeStruct(dims, dtype)

    def call(kernel, name, units, out_shape, in_specs, out_specs=None, scratch=(), limit=16, aliases={}):
        return pl.pallas_call(
            kernel,
            in_specs=in_specs,
            out_specs=out_specs if out_specs is not None else [vmem] * len(out_shape),
            out_shape=out_shape,
            scratch_shapes=scratch,
            input_output_aliases=aliases,
            compiler_params=pltpu.CompilerParams(vmem_limit_bytes=limit * mebi),
            cost_estimate=pl.CostEstimate(
                flops=2 * units * double * double * channels, bytes_accessed=rows * channels, transcendentals=0
            ),
            name=name,
        )

    def move(array, pairs):
        return lax.ppermute(array, "ctx", pairs)

    inward = [(0, 1), (shards - 1, shards - 2)]
    outward = [(1, 0), (shards - 2, shards - 1)]
    across = [(1, 2), (2, 1)]
    alone = [(0, 0), (shards - 1, shards - 1)]
    pay_shape = (hid_count, channels + SIDE)
    block_bf16 = shape(rows, channels, dtype=bf16)
    block_f32 = shape(rows, channels)

    row_step = max(rows // 2, 16)
    gate_rows = pl.BlockSpec((row_step, channels), lambda i: (i, 0))
    pair, other, edge, bias = pl.pallas_call(
        products_kernel,
        grid=(rows // row_step,),
        in_specs=[smem] + [gate_rows] * 4,
        out_specs=[gate_rows] * 3 + [pl.BlockSpec((1, channels), lambda i: (0, 0))],
        out_shape=[block_bf16] * 3 + [shape(1, channels)],
        compiler_params=pltpu.CompilerParams(vmem_limit_bytes=64 * mebi),
        name="products",
    )(rank, x_one, x_two, values, grad_out)
    pair_in = move(pair, inward + outward)
    middle_in = move(other, across)

    own_shapes = [
        shape(rows, feat_count), shape(feat_count, hid_count), block_bf16, block_bf16, shape(hid_count, channels),
        shape(1, channels), shape(double, double, dtype=bf16), shape(double, double, dtype=bf16),
        shape(feat_count, seq_len), shape(1, channels), shape(*pay_shape, dtype=bf16),
    ]
    (send,) = call(
        only(False, shards, 0, functools.partial(own_kernel, rows, shards, channels, blocks, width)), "own_pair", 8,
        [shape(*pay_shape, dtype=bf16)],
        [smem] + [anywhere] * 10,
        out_specs=[anywhere],
        scratch=[pltpu.VMEM(s.shape, s.dtype) for s in own_shapes]
        + [
            pltpu.VMEM((2 * hid_count, rows), bf16), pltpu.VMEM((rows, hid_count), f32),
            pltpu.SemaphoreType.DMA((10,)), pltpu.SemaphoreType.DMA,
        ],
        limit=60,
    )(rank, feats[:rows], first_weight, pair, other, second_weight, rate_row, front, back, featt, bias)
    come = move(send, inward)
    late_feats, _ = lax.optimization_barrier((jnp.asarray(feats), send))
    spec, trans, slope = call(
        functools.partial(filters_kernel, rows, shards, blocks, width), "filters", 8,
        [
            shape(shards, double, channels, dtype=bf16), shape(2 * hid_count, seq_len, dtype=bf16),
            shape(seq_len, hid_count),
        ],
        [vmem] * 5,
        scratch=[pltpu.VMEM((seq_len, 3 * hid_count), bf16)],
    )(late_feats, first_weight, second_weight, rate_row, front)

    edge, _ = lax.optimization_barrier((edge, slope))
    far = move(edge, [(0, 2), (shards - 1, shards - 3)])
    conv, corr, ahead, sums, first, near_spec = call(
        functools.partial(near_kernel, rows, shards, blocks, width), "near_blocks", 20,
        [block_f32] * 3
        + [shape(hid_count, channels), shape(feat_count, hid_count), shape(double, channels)],
        [smem] + [vmem] * 12,
        scratch=[
            pltpu.VMEM((4, double, width), f32),
            pltpu.VMEM((3, double, width), bf16),
            pltpu.VMEM((shards - 1, double, width), bf16),
            pltpu.VMEM((shards - 1, double, width), bf16),
            pltpu.VMEM(((shards - 1) * rows, hid_count), f32),
        ],
    )(rank, pair, other, pair_in, middle_in, spec, second_weight, rate_row, front, back, trans, featt, slope)

    part, far_spec = call(
        only(
            True, shards, 0,
            looped(
                functools.partial(far_kernel, rows),
                (None, ROWS, (slice(3, 4), slice(None)), None, None, ROWS, ROWS, ROWS),
                few, wide,
            ),
        ),
        "far_block", 1,
        [block_bf16, shape(double, channels)],
        [smem] + [vmem] * 5,
    )(rank, far, spec, front, back, ahead)
    (late,) = call(
        only(
            True, shards, 0,
            looped(
                functools.partial(late_kernel, rows),
                (None, ROWS, (slice(2, 3), slice(None)), None, ROWS),
                few, wide,
            ),
        ),
        "late_block", 1,
        [block_f32],
        [smem] + [vmem] * 3,
    )(rank, far_spec, spec, back)
    part_come = move(part, outward)

    pay, first = call(
        only(
            True, shards, 1,
            looped(
                functools.partial(last_kernel, rows, shards, channels),
                (None, None, ROWS, ROWS, ROWS, ROWS, None, None, None, None, ROWS),
                few, wide,
            ),
        ),
        "last_pair", 1,
        [shape(*pay_shape, dtype=bf16), shape(feat_count, hid_count)],
        [anywhere, smem] + [vmem] * 12,
        scratch=[pltpu.VMEM((2 * rows, hid_count), f32)],
    )(part, rank, near_spec, far_spec, second_weight, rate_row, back, trans, featt, slope, sums, first, bias, come)
    pay_come = move(pay, across + alone)
    group = lax.axis_size(("ch", "sub"))

    def swapped(array, bits):
        for bit in bits:
            array = array + lax.ppermute(array, ("ch", "sub"), [(i, i ^ bit) for i in range(group)])
        return array

    bits = [1 << i for i in range(group.bit_length() - 1)]
    first = swapped(first, bits[:1])
    first = first + move(first, across + alone)

    (total,) = call(
        functools.partial(total_kernel, channels, hid_count), "total", 0,
        [shape(*pay_shape, dtype=bf16)],
        [anywhere] * 3 + [vmem] * 2,
    )(part_come, first, late, pay, pay_come)
    total_come = move(total, inward + outward)

    def gates(inner, *before):
        return call(
            only(
                inner, shards, len(before),
                functools.partial(gates_kernel, inner, shards, blocks, width, len(before)),
            ),
            "gates", 0,
            [block_bf16] * 3,
            [anywhere] * len(before) + [smem] + [vmem] * 9,
            out_specs=[anywhere] * 3,
            scratch=[pltpu.VMEM((rows, channels), bf16)] * 3 + [pltpu.SemaphoreType.DMA((blocks, 3))],
            aliases={i: i for i in range(3)} if inner else {},
        )(*before, rank, x_one, x_two, values, grad_out, skip_row, conv, corr, late, part_come)

    grads = gates(False, total)
    first, _ = lax.optimization_barrier((first, grads[0]))
    first = swapped(first, bits[1:])
    first_come = move(first, inward + outward)
    grad_one, grad_two, grad_value = gates(True, *grads)

    outs = [shape(hid_count, channels), shape(feat_count, hid_count), shape(1, channels)]
    grad_second, grad_first, grad_bias = call(
        functools.partial(finish_kernel, channels, shards), "finish", 0,
        outs,
        [smem] + [vmem] * 4,
        out_specs=[anywhere] * 3,
        scratch=[pltpu.VMEM(o.shape, f32) for o in outs] + [pltpu.SemaphoreType.DMA((3,))],
    )(rank, total, total_come, first, first_come)
    return (grad_one, grad_two, grad_value, grad_first, grad_second, grad_bias.reshape(channels))


def solution(mesh):
    in_specs = (
        P(("parts", "ctx"), ("ch", "sub")),
        P(("parts", "ctx"), ("ch", "sub")),
        P(("parts", "ctx"), ("ch", "sub")),
        P(("parts", "ctx"), ("ch", "sub")),
        P(),
        P(None, ("ch", "sub")),
        P(("ch", "sub")),
        P(("ch", "sub")),
    )
    out_specs = (
        P(("parts", "ctx"), ("ch", "sub")),
        P(("parts", "ctx"), ("ch", "sub")),
        P(("parts", "ctx"), ("ch", "sub")),
        P("parts", None),
        P("parts", ("ch", "sub")),
        P(("parts", "ch", "sub")),
    )
    body = few_shards_body if mesh.shape["ctx"] == 4 else many_shards_body
    return jax.shard_map(body, mesh=mesh, in_specs=in_specs, out_specs=out_specs, check_vma=False)
```

```python
import functools
import math

import jax
import jax.numpy as jnp
import numpy as np
from jax import lax
from jax.experimental import pallas as pl
from jax.experimental.pallas import tpu as pltpu
from jax.sharding import PartitionSpec as P

band_steps = (1763, 1201, 811, 547, 367, 251, 167, 113, 79, 53, 37, 23, 17, 11, 7, 3)
highest = lax.Precision.HIGHEST
f32 = jnp.float32
bf16 = jnp.bfloat16


def features(positions):
    multiplier = jnp.array(band_steps, dtype=jnp.int32)
    phase = positions[:, None] * multiplier[None, :] % 4096
    angle = phase.astype(jnp.float32) * (2.0 * math.pi / 4096.0)
    return jnp.concatenate([jnp.cos(angle), jnp.sin(angle)], axis=1)


def tables(out_count, in_count, modulus, sign_value):
    row_index = lax.broadcasted_iota(jnp.int32, (out_count, in_count), 0)
    col_index = lax.broadcasted_iota(jnp.int32, (out_count, in_count), 1)
    angle = (row_index * col_index % modulus).astype(jnp.float32) * (2.0 * math.pi / modulus)
    return (jnp.cos(angle), sign_value * jnp.sin(angle))


def twiddle(spec_re, spec_im, freq_count, span, modulus, sign_value):
    freq_index = lax.broadcasted_iota(jnp.int32, (freq_count, span), 0)
    pos_index = lax.broadcasted_iota(jnp.int32, (freq_count, span), 1)
    angle = (freq_index * pos_index % modulus).astype(jnp.float32) * (2.0 * math.pi / modulus)
    factor_re = jnp.cos(angle)[None, None, :, :]
    factor_im = (sign_value * jnp.sin(angle))[None, None, :, :]
    return (spec_re * factor_re - spec_im * factor_im, spec_re * factor_im + spec_im * factor_re)


def contract(kernel, array):
    return jnp.einsum(
        "lj,mckj->mckl", kernel, array, precision=highest, preferred_element_type=jnp.float32
    )


def along_positions(spec_re, spec_im, kernel_re, kernel_im):
    return (
        contract(kernel_re, spec_re) - contract(kernel_im, spec_im),
        contract(kernel_re, spec_im) + contract(kernel_im, spec_re),
    )


def many_shards_body(
    x_one, x_two, values, grad_out, first_weight, second_weight, skip_bias, decay_rate
):
    row_count, chan_count = x_one.shape
    shards = lax.axis_size("ctx")
    rank = lax.axis_index("ctx")
    seq_len = row_count * shards
    total = 2 * seq_len
    narrow = chan_count // shards
    chan_weight = lax.dynamic_slice_in_dim(second_weight, rank * narrow, narrow, 1)
    chan_rate = lax.dynamic_slice_in_dim(decay_rate, rank * narrow, narrow, 0)
    source = x_one.astype(jnp.float32) * values.astype(jnp.float32)
    cotan = grad_out.astype(jnp.float32) * x_two.astype(jnp.float32)
    spread = lax.all_to_all(
        jnp.stack([source.T, cotan.T])[:, :, None, :],
        "ctx",
        split_axis=1,
        concat_axis=2,
        tiled=True,
    )
    far_source = spread[0]
    far_cotan = spread[1]
    positions = jnp.arange(seq_len, dtype=jnp.int32)
    feats = features(positions)
    pre_act = jnp.dot(feats, first_weight, precision=highest, preferred_element_type=jnp.float32)
    hidden = jnp.sin(pre_act)
    envelope = jnp.exp(-chan_rate[:, None] * positions.astype(jnp.float32)[None, :]) * float(
        seq_len
    ) ** (-0.5)
    filt = (
        jnp.einsum(
            "th,hc->ct", hidden, chan_weight, precision=highest, preferred_element_type=jnp.float32
        )
        * envelope
    )
    filt_blocks = filt.reshape(narrow, shards, row_count)
    fields = jnp.stack([far_source, far_cotan])

    def first_section(kernel):
        field_part = jnp.einsum(
            "kn,mcnj->mckj", kernel, fields, precision=highest, preferred_element_type=jnp.float32
        )
        filter_part = jnp.einsum(
            "kn,cnj->ckj",
            kernel,
            filt_blocks,
            precision=highest,
            preferred_element_type=jnp.float32,
        )
        return jnp.concatenate([field_part, filter_part[None]], axis=0)

    first_re, first_im = tables(2 * shards, shards, 2 * shards, -1.0)
    spec_re, spec_im = (first_section(first_re), first_section(first_im))
    spec_re, spec_im = twiddle(spec_re, spec_im, 2 * shards, row_count, total, -1.0)
    fwd_re, fwd_im = tables(row_count, row_count, row_count, -1.0)
    spec_re, spec_im = along_positions(spec_re, spec_im, fwd_re, fwd_im)
    source_re, source_im = (spec_re[0], spec_im[0])
    cotan_re, cotan_im = (spec_re[1], spec_im[1])
    filter_re, filter_im = (spec_re[2], spec_im[2])
    prod_re = jnp.stack(
        [
            source_re * filter_re - source_im * filter_im,
            cotan_re * filter_re + cotan_im * filter_im,
            cotan_re * source_re + cotan_im * source_im,
        ]
    )
    prod_im = jnp.stack(
        [
            source_re * filter_im + source_im * filter_re,
            cotan_im * filter_re - cotan_re * filter_im,
            cotan_im * source_re - cotan_re * source_im,
        ]
    )
    back_re, back_im = tables(row_count, row_count, row_count, 1.0)
    prod_re, prod_im = along_positions(prod_re, prod_im, back_re, back_im)
    prod_re, prod_im = twiddle(prod_re, prod_im, 2 * shards, row_count, total, 1.0)
    last_re, last_im = tables(shards, 2 * shards, 2 * shards, 1.0)
    field_out = jnp.einsum(
        "nk,mckj->mcnj", last_re, prod_re[:2], precision=highest, preferred_element_type=jnp.float32
    ) - jnp.einsum(
        "nk,mckj->mcnj", last_im, prod_im[:2], precision=highest, preferred_element_type=jnp.float32
    )
    field_out = field_out * (1.0 / total)
    filt_grad = jnp.einsum(
        "nk,ckj->cnj", last_re, prod_re[2], precision=highest, preferred_element_type=jnp.float32
    ) - jnp.einsum(
        "nk,ckj->cnj", last_im, prod_im[2], precision=highest, preferred_element_type=jnp.float32
    )
    filt_grad = (filt_grad * (1.0 / total)).reshape(narrow, seq_len)
    modulated = filt_grad * envelope
    weight_part = jnp.einsum(
        "th,ct->hc", hidden, modulated, precision=highest, preferred_element_type=jnp.float32
    )
    hidden_grad = jnp.einsum(
        "ct,hc->th", modulated, chan_weight, precision=highest, preferred_element_type=jnp.float32
    )
    first_part = jnp.dot(
        feats.T,
        hidden_grad * jnp.cos(pre_act),
        precision=highest,
        preferred_element_type=jnp.float32,
    )
    grad_first = lax.psum(first_part, ("ctx", "ch", "sub"))
    returned = lax.all_to_all(
        field_out.astype(jnp.bfloat16), "ctx", split_axis=2, concat_axis=1, tiled=True
    ).astype(field_out.dtype)
    conv_part = returned[0, :, 0, :].T
    corr_part = returned[1, :, 0, :].T
    grad_two = (grad_out.astype(jnp.float32) * (conv_part + skip_bias[None, :] * source)).astype(
        jnp.bfloat16
    )
    grad_mid = corr_part + skip_bias[None, :] * cotan
    grad_one = (grad_mid * values.astype(jnp.float32)).astype(jnp.bfloat16)
    grad_value = (grad_mid * x_one.astype(jnp.float32)).astype(jnp.bfloat16)
    grad_bias = lax.psum(jnp.sum(source * cotan, axis=0), "ctx")
    grad_second = lax.all_gather(weight_part, "ctx", axis=1, tiled=True)
    return (grad_one, grad_two, grad_value, grad_first, grad_second, grad_bias)


STEP = 16
SIDE = 128


def halves(array):
    array = np.asarray(array, np.float32)
    high = array.astype(bf16)
    low = (array - high.astype(np.float32)).astype(bf16)
    return high, low


def block_tables(rows):
    freq = np.concatenate([np.arange(0, rows, 2), np.arange(1, rows, 2)])
    phase = (2 * freq + 1)[:, None] * np.arange(rows)[None, :] % (4 * rows)
    angle = phase * (2.0 * np.pi / (4 * rows))
    forward = np.concatenate([np.cos(angle), -np.sin(angle)], axis=0)
    front = np.ascontiguousarray(np.concatenate(halves(forward), axis=1))
    back = np.ascontiguousarray(np.concatenate(halves(forward.T / rows), axis=0))
    return front, back


def feature_table(seq_len):
    phase = np.arange(seq_len)[:, None] * np.array(band_steps)[None, :] % 4096
    angle = phase * (2.0 * np.pi / 4096.0)
    return np.concatenate([np.cos(angle), np.sin(angle)], axis=1).astype(np.float32)


def split(array):
    high = array.astype(bf16)
    return high, (array - high.astype(f32)).astype(bf16)


def dot(left, right):
    return jnp.dot(left, right, preferred_element_type=f32)


def exact_dot(left, right):
    return jnp.dot(left, right, precision=highest, preferred_element_type=f32)


def dot_across(left, right):
    return lax.dot_general(left, right, (((1,), (1,)), ((), ())), preferred_element_type=f32)


def decay(rate, rows, scale):
    place = lax.broadcasted_iota(jnp.int32, (rows, rate.shape[1]), 0)
    return jnp.exp(-place.astype(f32) * rate) * scale


def times(a, b):
    return a[0] * b[0] - a[1] * b[1], a[0] * b[1] + a[1] * b[0]


def conj_times(a, b):
    return a[0] * b[0] + a[1] * b[1], a[0] * b[1] - a[1] * b[0]


def plus(a, b):
    return a[0] + b[0], a[1] + b[1]


def scaled(a, factor):
    return a[0] * factor, a[1] * factor


def choose(condition, a, b):
    return jnp.where(condition, a[0], b[0]), jnp.where(condition, a[1], b[1])


def turned(a, sign):
    return (a[1], -a[0]) if sign > 0 else (-a[1], a[0])


def forward(front_ref, block):
    return dot(front_ref[...], jnp.concatenate([block, block], axis=0))


def backward(back_ref, high, low=None):
    both = dot(back_ref[...], high)
    rows = both.shape[0] // 2
    out = both[:rows] + both[rows:]
    return out if low is None else out + dot(back_ref[:rows], low)


def row_groups(rows):
    for step in range(rows // STEP):
        sign = 1 if step * STEP < rows // 2 else -1
        yield slice(step * STEP, (step + 1) * STEP), slice(rows + step * STEP, rows + (step + 1) * STEP), sign


def weight_sums(trans, m_high, m_low):
    both = dot(trans, m_high)
    count = both.shape[0] // 2
    return both[:count] + both[count:] + dot(trans[:count], m_low)


def hidden_sums(m_high, m_low, w_high, w_low):
    left = jnp.concatenate([m_high, m_high, m_low], axis=1)
    right = jnp.concatenate([w_high, w_low, w_high], axis=1)
    return dot_across(left, right)


def looped(kernel, kinds, blocks, width):
    def over_strips(*refs):
        def step(block, carry):
            cols = pl.ds(pl.multiple_of(block * width, width), width)
            views = [
                ref if kind is None else ref.at[(*kind, cols)]
                for ref, kind in zip(refs, kinds + (None,) * (len(refs) - len(kinds)))
            ]
            kernel(block, blocks, *views)
            return carry

        lax.fori_loop(0, blocks, step, 0)

    return over_strips


ROWS = (slice(None),)
CUBE = (slice(None), slice(None))


def products_kernel(rank_ref, one_ref, two_ref, val_ref, out_ref, pair_ref, other_ref, edge_ref, bias_ref):
    source = one_ref[...].astype(f32) * val_ref[...].astype(f32)
    cotan = out_ref[...].astype(f32) * two_ref[...].astype(f32)
    even = rank_ref[0] % 2 == 0
    pair_ref[...] = jnp.where(even, source, cotan).astype(bf16)
    edge_ref[...] = pair_ref[...]
    other_ref[...] = jnp.where(even, cotan, source).astype(bf16)
    part = jnp.sum(source * cotan, axis=0, keepdims=True)

    @pl.when(pl.program_id(0) == 0)
    def _():
        bias_ref[...] = part

    @pl.when(pl.program_id(0) > 0)
    def _():
        bias_ref[...] += part


def ordered(first, a, b):
    return (jnp.where(first, a, b), jnp.where(first, b, a))


def sin_cos(angle):
    turns = jnp.floor(angle * (2.0 / math.pi) + 0.5)
    rest = ((angle - turns * 1.5703125) - turns * 4.837512969970703e-4) - turns * 7.54978995489188e-8
    square = rest * rest
    sine = rest + rest * square * (
        -1.6666654611e-1 + square * (8.3321608736e-3 + square * -1.9515295891e-4)
    )
    cosine = 1.0 - 0.5 * square + square * square * (
        4.166664568298827e-2 + square * (-1.388731625493765e-3 + square * 2.443315711809948e-5)
    )
    quarter = turns.astype(jnp.int32)
    odd = (quarter & 1) == 1
    sin_sign = jnp.where((quarter & 2) == 2, -1.0, 1.0).astype(f32)
    cos_sign = jnp.where(((quarter + 1) & 2) == 2, -1.0, 1.0).astype(f32)
    return jnp.where(odd, cosine, sine) * sin_sign, jnp.where(odd, sine, cosine) * cos_sign


def turned_over(hidden, slope):
    both = jnp.concatenate([hidden, slope], axis=1).T
    return jnp.concatenate(split(both[: hidden.shape[1]]), axis=0)


def filters_kernel(
    rows, shards, blocks, width, feats_ref, first_ref, weight_ref, rate_ref, front_ref, spec_ref, trans_ref, slope_ref,
    hid_ref,
):
    hidden, slope = sin_cos(exact_dot(feats_ref[...], first_ref[...]))
    slope_ref[...] = slope
    high, low = split(hidden)
    hid_ref[...] = jnp.concatenate([high, high, low], axis=1)
    trans_ref[...] = turned_over(hidden, slope)
    strips = looped(
        functools.partial(filter_strip, rows, shards), (None, ROWS, ROWS, None, CUBE), blocks, width
    )
    strips(hid_ref, weight_ref, rate_ref, front_ref, spec_ref)


def filter_strip(rows, shards, block, blocks, hid_ref, weight_ref, rate_ref, front_ref, spec_ref):
    scale = float(rows * shards) ** -0.5
    w_high, w_low = split(weight_ref[...])
    stacked = jnp.concatenate([w_high, w_low, w_high], axis=0)
    rate = rate_ref[...]
    env = decay(rate, rows, scale)
    before = None
    for lag in range(shards):
        part = dot(hid_ref[lag * rows : (lag + 1) * rows, :], stacked)
        part = part * (env * jnp.exp(rate * (-float(lag * rows))))
        f_high, f_low = split(part)
        now = forward(front_ref, f_high) + dot(front_ref[:, :rows], f_low)
        for re, im, sign in row_groups(rows):
            here = (now[re], now[im])
            if before is not None:
                here = plus(here, turned((before[re], before[im]), -sign))
            spec_ref[lag, re, :] = here[0].astype(bf16)
            spec_ref[lag, im, :] = here[1].astype(bf16)
        before = now


def own_kernel(rows, shards, channels, blocks, width, rank_ref, *refs):
    inputs, send_out, held = refs[:10], refs[10], refs[11:21]
    send_ref, trans_ref, acc_ref, sems, out_sem = refs[21:]
    (
        feats_ref, first_ref, pair_ref, other_ref, weight_ref, rate_ref, front_ref, back_ref, featt_ref, bias_ref
    ) = held
    copies = [pltpu.make_async_copy(far, near, sems.at[i]) for i, (far, near) in enumerate(zip(inputs, held))]
    for copy in copies:
        copy.start()
    acc_ref[...] = jnp.zeros_like(acc_ref)
    copies[0].wait()
    copies[1].wait()
    hidden, slope = sin_cos(exact_dot(feats_ref[...], first_ref[...]))
    trans_ref[...] = turned_over(hidden, slope)
    for copy in copies[2:]:
        copy.wait()
    kinds = (None, ROWS, ROWS, ROWS, ROWS, None, None, None, ROWS, None)
    looped(functools.partial(own_strip, rows, shards), kinds, blocks, width)(
        rank_ref, pair_ref, other_ref, weight_ref, rate_ref, front_ref, back_ref, trans_ref, send_ref, acc_ref
    )
    first = exact_dot(featt_ref[:, :rows], acc_ref[...] * slope)
    put_side(send_ref, channels, fold(bias_ref[...]), first)
    last = pltpu.make_async_copy(send_ref, send_out, out_sem)
    last.start()
    last.wait()


def own_strip(
    rows, shards, block, blocks, rank_ref, pair_ref, other_ref, weight_ref, rate_ref, front_ref, back_ref, trans_ref,
    send_ref, acc_ref,
):
    source, cotan = ordered(rank_ref[0] % 2 == 0, pair_ref[...], other_ref[...])
    x0 = forward(front_ref, source)
    c0 = forward(front_ref, cotan)
    pair = conj_times((x0[:rows], x0[rows:]), (c0[:rows], c0[rows:]))
    high, low = split(jnp.concatenate(pair, axis=0))
    env = decay(rate_ref[...], rows, float(rows * shards) ** -0.5)
    m_high, m_low = split(backward(back_ref, high, low) * env)
    send_ref[...] = weight_sums(trans_ref[...], m_high, m_low).astype(bf16)
    acc_ref[...] += hidden_sums(m_high, m_low, *split(weight_ref[...]))


def fold(bias):
    return jnp.concatenate([bias[:, i * 128 : (i + 1) * 128] for i in range(bias.shape[1] // 128)], axis=0)


def put_side(pay_ref, channels, bias, first=None):
    half = pay_ref.shape[0] // 2
    pay_ref[:, channels:] = jnp.zeros((2 * half, SIDE), bf16)
    for start, part in zip((0, half // 2), split(bias)):
        pay_ref[start : start + bias.shape[0], channels:] = part
    if first is not None:
        pay_ref[half:, channels:] = jnp.concatenate(split(first), axis=1)


def get_side(pay, channels, lanes, hid_count):
    half = pay.shape[0] // 2
    side = pay[:, channels:].astype(f32)
    low = side[half:]
    return side[:lanes] + side[half // 2 : half // 2 + lanes], low[:, :hid_count] + low[:, hid_count:]


def near_kernel(
    rows, shards, blocks, width, rank_ref, pair_ref, other_ref, pair_in_ref, middle_in_ref, spec_ref, weight_ref,
    rate_ref, front_ref, back_ref, trans_ref, featt_ref, slope_ref, conv_ref, corr_ref, ahead_ref, sums_ref, first_ref,
    near_ref, fields, fast, high_ref, low_ref, acc_ref,
):
    rank = rank_ref[0]
    inner = jnp.logical_and(rank > 0, rank < shards - 1)
    count = shards - 1
    kinds = (None, None, None) + (ROWS,) * 4 + (CUBE, ROWS, ROWS)
    common = (
        rank_ref, front_ref, back_ref, pair_ref, other_ref, pair_in_ref, middle_in_ref, spec_ref, conv_ref, corr_ref,
        fields, fast,
    )

    @pl.when(jnp.logical_not(inner))
    def _():
        looped(functools.partial(edge_strip, rows, shards), kinds, blocks, width)(*common)

    @pl.when(inner)
    def _():
        acc_ref[...] = jnp.zeros_like(acc_ref)
        looped(
            functools.partial(inner_strip, rows, shards), kinds + (None,) * 3 + (ROWS,) * 5, blocks, width
        )(*common, trans_ref, weight_ref, rate_ref, ahead_ref, sums_ref, near_ref, high_ref, low_ref, acc_ref)
        first_ref[...] = exact_dot(
            featt_ref[:, : count * rows], acc_ref[...] * slope_ref[: count * rows, :]
        )


def edge_strip(
    rows, shards, block, blocks, rank_ref, front_ref, back_ref, pair_ref, other_ref, pair_in_ref, middle_in_ref,
    spec_ref, conv_ref, corr_ref, fields, fast,
):
    del middle_in_ref
    top = rank_ref[0] == shards - 1
    source, cotan = ordered(rank_ref[0] % 2 == 0, pair_ref[...], other_ref[...])
    for index, block_in in enumerate((source, cotan, pair_in_ref[...])):
        fields[index] = forward(front_ref, block_in)
    on_conv = jnp.where(top, 1.0, 0.0).astype(f32)
    on_corr = jnp.where(top, 0.0, 1.0).astype(f32)
    for re, im, sign in row_groups(rows):
        x0, c0, near = ((fields[i, re, :], fields[i, im, :]) for i in range(3))
        w0, w1 = ((spec_ref[i, re, :].astype(f32), spec_ref[i, im, :].astype(f32)) for i in range(2))
        values = (
            plus(times(w0, x0), scaled(times(w1, near), on_conv)),
            plus(conj_times(w0, c0), scaled(conj_times(w1, near), on_corr)),
        )
        for index, value in enumerate(values):
            fast[index, re, :] = value[0].astype(bf16)
            fast[index, im, :] = value[1].astype(bf16)
    conv_ref[...] = backward(back_ref, fast[0])
    corr_ref[...] = backward(back_ref, fast[1])


def inner_strip(
    rows, shards, block, blocks, rank_ref, front_ref, back_ref, pair_ref, other_ref, pair_in_ref, middle_in_ref,
    spec_ref, conv_ref, corr_ref, fields, fast, trans_ref, weight_ref, rate_ref, ahead_ref, sums_ref, near_ref, high_ref,
    low_ref, acc_ref,
):
    lower = rank_ref[0] == 1
    upper = jnp.where(lower, 0.0, 1.0).astype(f32)
    side = jnp.where(lower, -1.0, 1.0).astype(f32)
    count = shards - 1
    blocks_in = (
        *ordered(lower, other_ref[...], pair_ref[...]), *ordered(lower, pair_in_ref[...], middle_in_ref[...])
    )
    for index, block_in in enumerate(blocks_in):
        fields[index] = forward(front_ref, block_in)
    for re, im, sign in row_groups(rows):
        x0, c0, x1, c1 = ((fields[i, re, :], fields[i, im, :]) for i in range(4))
        w0, w1, w2 = ((spec_ref[i, re, :].astype(f32), spec_ref[i, im, :].astype(f32)) for i in range(3))
        values = (
            plus(times(w0, x0), times(w1, x1)),
            plus(conj_times(w0, c0), conj_times(w1, c1)),
            times((w2[0], w2[1] * side), choose(lower, c1, x1)),
        )
        for index, value in enumerate(values):
            fast[index, re, :] = value[0].astype(bf16)
            fast[index, im, :] = value[1].astype(bf16)
        near_ref[re, :], near_ref[im, :] = choose(lower, x1, c1)
        zero = conj_times(x0, c0)
        one = plus(conj_times(x1, c0), scaled(conj_times(x0, c1), upper))
        two = conj_times(x1, c1)
        for index, value in enumerate((plus(zero, turned(one, sign)), plus(one, turned(two, sign)), two)):
            for part, where in zip(value, (re, im)):
                high_ref[index, where, :], low_ref[index, where, :] = split(part)
    conv_ref[...] = backward(back_ref, fast[0])
    corr_ref[...] = backward(back_ref, fast[1])
    ahead_ref[...] = backward(back_ref, fast[2])
    rate = rate_ref[...]
    env = decay(rate, rows, float(rows * shards) ** -0.5)
    parts = []
    for lag in range(count):
        grad = backward(back_ref, high_ref[lag], low_ref[lag])
        parts.append(split(grad * (env * jnp.exp(rate * (-float(lag * rows))))))
    m_high = jnp.concatenate([p[0] for p in parts], axis=0)
    m_low = jnp.concatenate([p[1] for p in parts], axis=0)
    sums_ref[...] = weight_sums(trans_ref[:, : count * rows], m_high, m_low)
    acc_ref[...] += hidden_sums(m_high, m_low, *split(weight_ref[...]))


def only(inner, shards, rank_at, kernel):
    def run(*refs):
        rank = refs[rank_at][0]

        @pl.when(jnp.logical_and(rank > 0, rank < shards - 1) == inner)
        def _():
            kernel(*refs)

    return run


def far_kernel(
    rows, block, blocks, rank_ref, far_ref, spec_ref, front_ref, back_ref, ahead_ref, part_ref, far_spec_ref
):
    side = jnp.where(rank_ref[0] == 2, 1.0, -1.0).astype(f32)
    far = forward(front_ref, far_ref[...])
    far_spec_ref[...] = far
    w3 = (spec_ref[0, :rows, :].astype(f32), spec_ref[0, rows:, :].astype(f32) * side)
    ahead = jnp.concatenate(times(w3, (far[:rows], far[rows:])), axis=0).astype(bf16)
    part_ref[...] = (ahead_ref[...] + backward(back_ref, ahead)).astype(bf16)


def late_kernel(rows, block, blocks, rank_ref, far_ref, spec_ref, back_ref, late_ref):
    side = jnp.where(rank_ref[0] == 2, 1.0, -1.0).astype(f32)
    w2 = (spec_ref[0, :rows, :].astype(f32), spec_ref[0, rows:, :].astype(f32) * side)
    late = jnp.concatenate(times(w2, (far_ref[:rows, :], far_ref[rows:, :])), axis=0).astype(bf16)
    late_ref[...] = backward(back_ref, late)


def last_kernel(
    rows, shards, channels, block, blocks, after_ref, rank_ref, near_ref, far_ref, weight_ref, rate_ref, back_ref,
    trans_ref, featt_ref, slope_ref, sums_ref, first_ref, bias_ref, in_ref, pay_ref, total_ref, acc_ref,
):
    del after_ref
    hid_count, width = weight_ref.shape
    lower = rank_ref[0] == 1
    start = pl.multiple_of(block * width, width)
    here = sums_ref[...] + in_ref[:, pl.ds(start, width)].astype(f32)
    mine = (block < blocks // 2) == lower

    @pl.when(block == 0)
    def _():
        acc_ref[...] = jnp.zeros_like(acc_ref)

    @pl.when(mine)
    def _():
        sign = jnp.where(lower, 1.0, -1.0).astype(f32)
        three = conj_times((near_ref[:rows, :], near_ref[rows:, :]), (far_ref[:rows, :], far_ref[rows:, :]))
        three = (three[0], three[1] * sign)
        half = rows // 2
        two = jnp.concatenate([three[1][:half], -three[1][half:], -three[0][:half], three[0][half:]], axis=0)
        rate = rate_ref[...]
        env = decay(rate, rows, float(rows * shards) ** -0.5)
        parts = []
        for lag, value in ((shards - 2, two), (shards - 1, jnp.concatenate(three, axis=0))):
            grad = backward(back_ref, *split(value))
            parts.append(split(grad * (env * jnp.exp(rate * (-float(lag * rows))))))
        m_high = jnp.concatenate([p[0] for p in parts], axis=0)
        m_low = jnp.concatenate([p[1] for p in parts], axis=0)
        trans = trans_ref[:, (shards - 2) * rows :]
        pay_ref[:, pl.ds(start, width)] = (here + weight_sums(trans, m_high, m_low)).astype(bf16)
        w_high, w_low = split(weight_ref[...])
        acc_ref[...] += hidden_sums(m_high, m_low, w_high, w_low)

    @pl.when(jnp.logical_not(mine))
    def _():
        pay_ref[:, pl.ds(start, width)] = here.astype(bf16)

    @pl.when(block == blocks - 1)
    def _():
        first = exact_dot(
            featt_ref[:, (shards - 2) * rows :], acc_ref[...] * slope_ref[(shards - 2) * rows :, :]
        )
        lanes = channels // 128
        in_bias, in_first = get_side(in_ref[...], channels, lanes, hid_count)
        first = first + first_ref[...] + in_first
        put_side(pay_ref, channels, fold(bias_ref[...]) + in_bias)
        total_ref[...] = first


def total_kernel(channels, hid_count, part_ref, first_ref, late_ref, own_ref, come_ref, pay_ref):
    del part_ref, first_ref, late_ref
    lanes = channels // 128
    pay_ref[:, :channels] = (own_ref[:, :channels].astype(f32) + come_ref[:, :channels].astype(f32)).astype(bf16)
    own, come = (get_side(ref[...], channels, lanes, hid_count)[0] for ref in (own_ref, come_ref))
    put_side(pay_ref, channels, own + come)


def gates_kernel(inner, shards, blocks, width, before, *refs):
    refs = refs[before:]
    inputs, outs, held, sems = refs[:10], refs[10:13], refs[13:16], refs[16]

    def leaving(block, i):
        cols = pl.ds(pl.multiple_of(block * width, width), width)
        return pltpu.make_async_copy(held[i].at[:, cols], outs[i].at[:, cols], sems.at[block, i])

    def strip(block, blocks, *views):
        gates_strip(inner, shards, *views)
        for i in range(3):
            leaving(block, i).start()

    looped(strip, (None,) + (ROWS,) * 12, blocks, width)(*inputs, *held)
    for block in range(blocks):
        for i in range(3):
            leaving(block, i).wait()


def gates_strip(
    inner, shards, rank_ref, one_ref, two_ref, val_ref, out_ref, skip_ref, conv_ref, corr_ref, late_ref, part_ref,
    grad_one_ref, grad_two_ref, grad_value_ref,
):
    late = late_ref[...] if inner else part_ref[...].astype(f32)
    upper = rank_ref[0] >= shards // 2
    zero = jnp.zeros_like(late)
    one = one_ref[...].astype(f32)
    val = val_ref[...].astype(f32)
    out = out_ref[...].astype(f32)
    skip = skip_ref[...]
    conv = conv_ref[...] + jnp.where(upper, late, zero)
    corr = corr_ref[...] + jnp.where(upper, zero, late)
    grad_two_ref[...] = (out * (conv + skip * (one * val))).astype(bf16)
    mid = corr + skip * (out * two_ref[...].astype(f32))
    grad_one_ref[...] = (mid * val).astype(bf16)
    grad_value_ref[...] = (mid * one).astype(bf16)


def finish_kernel(
    channels, shards, rank_ref, own_ref, come_ref, first_ref, first_come_ref, second_out, first_out, bias_out, second,
    first, bias, sems,
):
    rank = rank_ref[0]
    inner = jnp.logical_and(rank > 0, rank < shards - 1)
    lanes = channels // 128
    copies = [
        pltpu.make_async_copy(held, out, sems.at[i])
        for i, (held, out) in enumerate(((second, second_out), (first, first_out), (bias, bias_out)))
    ]
    picked = jnp.where(inner, own_ref[...], come_ref[...])
    second[...] = picked[:, :channels].astype(f32)
    copies[0].start()
    first[...] = jnp.where(inner, first_ref[...], first_come_ref[...])
    copies[1].start()
    rows = get_side(picked, channels, lanes, first.shape[1])[0]
    for i in range(lanes):
        bias[:, i * 128 : (i + 1) * 128] = rows[i : i + 1]
    copies[2].start()
    for copy in copies:
        copy.wait()


def few_shards_body(
    x_one, x_two, values, grad_out, first_weight, second_weight, skip_bias, decay_rate
):
    rows, channels = x_one.shape
    shards = lax.axis_size("ctx")
    feat_count, hid_count = first_weight.shape
    seq_len = rows * shards
    double = 2 * rows
    width = min(512, channels)
    blocks = channels // width
    wide = 2 * width if blocks % 4 == 0 else width
    few = channels // wide
    rank = lax.axis_index("ctx").astype(jnp.int32).reshape(1)
    front, back = block_tables(rows)
    feats = feature_table(seq_len)
    featt = np.ascontiguousarray(feats.T)
    skip_row = skip_bias.reshape(1, channels)
    rate_row = decay_rate.reshape(1, channels)
    smem = pl.BlockSpec(memory_space=pltpu.SMEM)
    vmem = pl.BlockSpec(memory_space=pltpu.VMEM)
    anywhere = pl.BlockSpec(memory_space=pl.ANY)
    mebi = 1024 * 1024

    def shape(*dims, dtype=f32):
        return jax.ShapeDtypeStruct(dims, dtype)

    def call(kernel, name, units, out_shape, in_specs, out_specs=None, scratch=(), limit=16, aliases={}):
        return pl.pallas_call(
            kernel,
            in_specs=in_specs,
            out_specs=out_specs if out_specs is not None else [vmem] * len(out_shape),
            out_shape=out_shape,
            scratch_shapes=scratch,
            input_output_aliases=aliases,
            compiler_params=pltpu.CompilerParams(vmem_limit_bytes=limit * mebi),
            cost_estimate=pl.CostEstimate(
                flops=2 * units * double * double * channels, bytes_accessed=rows * channels, transcendentals=0
            ),
            name=name,
        )

    def move(array, pairs):
        return lax.ppermute(array, "ctx", pairs)

    inward = [(0, 1), (shards - 1, shards - 2)]
    outward = [(1, 0), (shards - 2, shards - 1)]
    across = [(1, 2), (2, 1)]
    alone = [(0, 0), (shards - 1, shards - 1)]
    pay_shape = (hid_count, channels + SIDE)
    block_bf16 = shape(rows, channels, dtype=bf16)
    block_f32 = shape(rows, channels)

    row_step = max(rows // 2, 16)
    gate_rows = pl.BlockSpec((row_step, channels), lambda i: (i, 0))
    pair, other, edge, bias = pl.pallas_call(
        products_kernel,
        grid=(rows // row_step,),
        in_specs=[smem] + [gate_rows] * 4,
        out_specs=[gate_rows] * 3 + [pl.BlockSpec((1, channels), lambda i: (0, 0))],
        out_shape=[block_bf16] * 3 + [shape(1, channels)],
        compiler_params=pltpu.CompilerParams(vmem_limit_bytes=64 * mebi),
        name="products",
    )(rank, x_one, x_two, values, grad_out)
    pair_in = move(pair, inward + outward)
    middle_in = move(other, across)

    own_shapes = [
        shape(rows, feat_count), shape(feat_count, hid_count), block_bf16, block_bf16, shape(hid_count, channels),
        shape(1, channels), shape(double, double, dtype=bf16), shape(double, double, dtype=bf16),
        shape(feat_count, seq_len), shape(1, channels), shape(*pay_shape, dtype=bf16),
    ]
    (send,) = call(
        only(False, shards, 0, functools.partial(own_kernel, rows, shards, channels, blocks, width)), "own_pair", 8,
        [shape(*pay_shape, dtype=bf16)],
        [smem] + [anywhere] * 10,
        out_specs=[anywhere],
        scratch=[pltpu.VMEM(s.shape, s.dtype) for s in own_shapes]
        + [
            pltpu.VMEM((2 * hid_count, rows), bf16), pltpu.VMEM((rows, hid_count), f32),
            pltpu.SemaphoreType.DMA((10,)), pltpu.SemaphoreType.DMA,
        ],
        limit=60,
    )(rank, feats[:rows], first_weight, pair, other, second_weight, rate_row, front, back, featt, bias)
    come = move(send, inward)
    late_feats, _ = lax.optimization_barrier((jnp.asarray(feats), send))
    spec, trans, slope = call(
        functools.partial(filters_kernel, rows, shards, blocks, width), "filters", 8,
        [
            shape(shards, double, channels, dtype=bf16), shape(2 * hid_count, seq_len, dtype=bf16),
            shape(seq_len, hid_count),
        ],
        [vmem] * 5,
        scratch=[pltpu.VMEM((seq_len, 3 * hid_count), bf16)],
    )(late_feats, first_weight, second_weight, rate_row, front)

    edge, _ = lax.optimization_barrier((edge, slope))
    far = move(edge, [(0, 2), (shards - 1, shards - 3)])
    conv, corr, ahead, sums, first, near_spec = call(
        functools.partial(near_kernel, rows, shards, blocks, width), "near_blocks", 20,
        [block_f32] * 3
        + [shape(hid_count, channels), shape(feat_count, hid_count), shape(double, channels)],
        [smem] + [vmem] * 12,
        scratch=[
            pltpu.VMEM((4, double, width), f32),
            pltpu.VMEM((3, double, width), bf16),
            pltpu.VMEM((shards - 1, double, width), bf16),
            pltpu.VMEM((shards - 1, double, width), bf16),
            pltpu.VMEM(((shards - 1) * rows, hid_count), f32),
        ],
    )(rank, pair, other, pair_in, middle_in, spec, second_weight, rate_row, front, back, trans, featt, slope)

    part, far_spec = call(
        only(
            True, shards, 0,
            looped(
                functools.partial(far_kernel, rows),
                (None, ROWS, (slice(3, 4), slice(None)), None, None, ROWS, ROWS, ROWS),
                few, wide,
            ),
        ),
        "far_block", 1,
        [block_bf16, shape(double, channels)],
        [smem] + [vmem] * 5,
    )(rank, far, spec, front, back, ahead)
    (late,) = call(
        only(
            True, shards, 0,
            looped(
                functools.partial(late_kernel, rows),
                (None, ROWS, (slice(2, 3), slice(None)), None, ROWS),
                few, wide,
            ),
        ),
        "late_block", 1,
        [block_f32],
        [smem] + [vmem] * 3,
    )(rank, far_spec, spec, back)
    part_come = move(part, outward)

    pay, first = call(
        only(
            True, shards, 1,
            looped(
                functools.partial(last_kernel, rows, shards, channels),
                (None, None, ROWS, ROWS, ROWS, ROWS, None, None, None, None, ROWS),
                few, wide,
            ),
        ),
        "last_pair", 1,
        [shape(*pay_shape, dtype=bf16), shape(feat_count, hid_count)],
        [anywhere, smem] + [vmem] * 12,
        scratch=[pltpu.VMEM((2 * rows, hid_count), f32)],
    )(part, rank, near_spec, far_spec, second_weight, rate_row, back, trans, featt, slope, sums, first, bias, come)
    pay_come = move(pay, across + alone)
    group = lax.axis_size(("ch", "sub"))

    def swapped(array, bits):
        for bit in bits:
            array = array + lax.ppermute(array, ("ch", "sub"), [(i, i ^ bit) for i in range(group)])
        return array

    bits = [1 << i for i in range(group.bit_length() - 1)]
    first = swapped(first, bits[:1])
    first = first + move(first, across + alone)

    (total,) = call(
        functools.partial(total_kernel, channels, hid_count), "total", 0,
        [shape(*pay_shape, dtype=bf16)],
        [anywhere] * 3 + [vmem] * 2,
    )(part_come, first, late, pay, pay_come)
    total_come = move(total, inward + outward)

    def gates(inner, *before):
        return call(
            only(
                inner, shards, len(before),
                functools.partial(gates_kernel, inner, shards, blocks, width, len(before)),
            ),
            "gates", 0,
            [block_bf16] * 3,
            [anywhere] * len(before) + [smem] + [vmem] * 9,
            out_specs=[anywhere] * 3,
            scratch=[pltpu.VMEM((rows, channels), bf16)] * 3 + [pltpu.SemaphoreType.DMA((blocks, 3))],
            aliases={i: i for i in range(3)} if inner else {},
        )(*before, rank, x_one, x_two, values, grad_out, skip_row, conv, corr, late, part_come)

    grads = gates(False, total)
    first = swapped(first, bits[1:])
    first_come = move(first, inward + outward)
    grad_one, grad_two, grad_value = gates(True, *grads)

    outs = [shape(hid_count, channels), shape(feat_count, hid_count), shape(1, channels)]
    grad_second, grad_first, grad_bias = call(
        functools.partial(finish_kernel, channels, shards), "finish", 0,
        outs,
        [smem] + [vmem] * 4,
        out_specs=[anywhere] * 3,
        scratch=[pltpu.VMEM(o.shape, f32) for o in outs] + [pltpu.SemaphoreType.DMA((3,))],
    )(rank, total, total_come, first, first_come)
    return (grad_one, grad_two, grad_value, grad_first, grad_second, grad_bias.reshape(channels))


def solution(mesh):
    in_specs = (
        P(("parts", "ctx"), ("ch", "sub")),
        P(("parts", "ctx"), ("ch", "sub")),
        P(("parts", "ctx"), ("ch", "sub")),
        P(("parts", "ctx"), ("ch", "sub")),
        P(),
        P(None, ("ch", "sub")),
        P(("ch", "sub")),
        P(("ch", "sub")),
    )
    out_specs = (
        P(("parts", "ctx"), ("ch", "sub")),
        P(("parts", "ctx"), ("ch", "sub")),
        P(("parts", "ctx"), ("ch", "sub")),
        P("parts", None),
        P("parts", ("ch", "sub")),
        P(("parts", "ch", "sub")),
    )
    body = few_shards_body if mesh.shape["ctx"] == 4 else many_shards_body
    return jax.shard_map(body, mesh=mesh, in_specs=in_specs, out_specs=out_specs, check_vma=False)
```

```python
import functools
import math

import jax
import jax.numpy as jnp
import numpy as np
from jax import lax
from jax.experimental import pallas as pl
from jax.experimental.pallas import tpu as pltpu
from jax.sharding import PartitionSpec as P

band_steps = (1763, 1201, 811, 547, 367, 251, 167, 113, 79, 53, 37, 23, 17, 11, 7, 3)
highest = lax.Precision.HIGHEST
f32 = jnp.float32
bf16 = jnp.bfloat16


def features(positions):
    multiplier = jnp.array(band_steps, dtype=jnp.int32)
    phase = positions[:, None] * multiplier[None, :] % 4096
    angle = phase.astype(jnp.float32) * (2.0 * math.pi / 4096.0)
    return jnp.concatenate([jnp.cos(angle), jnp.sin(angle)], axis=1)


def tables(out_count, in_count, modulus, sign_value):
    row_index = lax.broadcasted_iota(jnp.int32, (out_count, in_count), 0)
    col_index = lax.broadcasted_iota(jnp.int32, (out_count, in_count), 1)
    angle = (row_index * col_index % modulus).astype(jnp.float32) * (2.0 * math.pi / modulus)
    return (jnp.cos(angle), sign_value * jnp.sin(angle))


def twiddle(spec_re, spec_im, freq_count, span, modulus, sign_value):
    freq_index = lax.broadcasted_iota(jnp.int32, (freq_count, span), 0)
    pos_index = lax.broadcasted_iota(jnp.int32, (freq_count, span), 1)
    angle = (freq_index * pos_index % modulus).astype(jnp.float32) * (2.0 * math.pi / modulus)
    factor_re = jnp.cos(angle)[None, None, :, :]
    factor_im = (sign_value * jnp.sin(angle))[None, None, :, :]
    return (spec_re * factor_re - spec_im * factor_im, spec_re * factor_im + spec_im * factor_re)


def contract(kernel, array):
    return jnp.einsum(
        "lj,mckj->mckl", kernel, array, precision=highest, preferred_element_type=jnp.float32
    )


def along_positions(spec_re, spec_im, kernel_re, kernel_im):
    return (
        contract(kernel_re, spec_re) - contract(kernel_im, spec_im),
        contract(kernel_re, spec_im) + contract(kernel_im, spec_re),
    )


def many_shards_body(
    x_one, x_two, values, grad_out, first_weight, second_weight, skip_bias, decay_rate
):
    row_count, chan_count = x_one.shape
    shards = lax.axis_size("ctx")
    rank = lax.axis_index("ctx")
    seq_len = row_count * shards
    total = 2 * seq_len
    narrow = chan_count // shards
    chan_weight = lax.dynamic_slice_in_dim(second_weight, rank * narrow, narrow, 1)
    chan_rate = lax.dynamic_slice_in_dim(decay_rate, rank * narrow, narrow, 0)
    source = x_one.astype(jnp.float32) * values.astype(jnp.float32)
    cotan = grad_out.astype(jnp.float32) * x_two.astype(jnp.float32)
    spread = lax.all_to_all(
        jnp.stack([source.T, cotan.T])[:, :, None, :],
        "ctx",
        split_axis=1,
        concat_axis=2,
        tiled=True,
    )
    far_source = spread[0]
    far_cotan = spread[1]
    positions = jnp.arange(seq_len, dtype=jnp.int32)
    feats = features(positions)
    pre_act = jnp.dot(feats, first_weight, precision=highest, preferred_element_type=jnp.float32)
    hidden = jnp.sin(pre_act)
    envelope = jnp.exp(-chan_rate[:, None] * positions.astype(jnp.float32)[None, :]) * float(
        seq_len
    ) ** (-0.5)
    filt = (
        jnp.einsum(
            "th,hc->ct", hidden, chan_weight, precision=highest, preferred_element_type=jnp.float32
        )
        * envelope
    )
    filt_blocks = filt.reshape(narrow, shards, row_count)
    fields = jnp.stack([far_source, far_cotan])

    def first_section(kernel):
        field_part = jnp.einsum(
            "kn,mcnj->mckj", kernel, fields, precision=highest, preferred_element_type=jnp.float32
        )
        filter_part = jnp.einsum(
            "kn,cnj->ckj",
            kernel,
            filt_blocks,
            precision=highest,
            preferred_element_type=jnp.float32,
        )
        return jnp.concatenate([field_part, filter_part[None]], axis=0)

    first_re, first_im = tables(2 * shards, shards, 2 * shards, -1.0)
    spec_re, spec_im = (first_section(first_re), first_section(first_im))
    spec_re, spec_im = twiddle(spec_re, spec_im, 2 * shards, row_count, total, -1.0)
    fwd_re, fwd_im = tables(row_count, row_count, row_count, -1.0)
    spec_re, spec_im = along_positions(spec_re, spec_im, fwd_re, fwd_im)
    source_re, source_im = (spec_re[0], spec_im[0])
    cotan_re, cotan_im = (spec_re[1], spec_im[1])
    filter_re, filter_im = (spec_re[2], spec_im[2])
    prod_re = jnp.stack(
        [
            source_re * filter_re - source_im * filter_im,
            cotan_re * filter_re + cotan_im * filter_im,
            cotan_re * source_re + cotan_im * source_im,
        ]
    )
    prod_im = jnp.stack(
        [
            source_re * filter_im + source_im * filter_re,
            cotan_im * filter_re - cotan_re * filter_im,
            cotan_im * source_re - cotan_re * source_im,
        ]
    )
    back_re, back_im = tables(row_count, row_count, row_count, 1.0)
    prod_re, prod_im = along_positions(prod_re, prod_im, back_re, back_im)
    prod_re, prod_im = twiddle(prod_re, prod_im, 2 * shards, row_count, total, 1.0)
    last_re, last_im = tables(shards, 2 * shards, 2 * shards, 1.0)
    field_out = jnp.einsum(
        "nk,mckj->mcnj", last_re, prod_re[:2], precision=highest, preferred_element_type=jnp.float32
    ) - jnp.einsum(
        "nk,mckj->mcnj", last_im, prod_im[:2], precision=highest, preferred_element_type=jnp.float32
    )
    field_out = field_out * (1.0 / total)
    filt_grad = jnp.einsum(
        "nk,ckj->cnj", last_re, prod_re[2], precision=highest, preferred_element_type=jnp.float32
    ) - jnp.einsum(
        "nk,ckj->cnj", last_im, prod_im[2], precision=highest, preferred_element_type=jnp.float32
    )
    filt_grad = (filt_grad * (1.0 / total)).reshape(narrow, seq_len)
    modulated = filt_grad * envelope
    weight_part = jnp.einsum(
        "th,ct->hc", hidden, modulated, precision=highest, preferred_element_type=jnp.float32
    )
    hidden_grad = jnp.einsum(
        "ct,hc->th", modulated, chan_weight, precision=highest, preferred_element_type=jnp.float32
    )
    first_part = jnp.dot(
        feats.T,
        hidden_grad * jnp.cos(pre_act),
        precision=highest,
        preferred_element_type=jnp.float32,
    )
    grad_first = lax.psum(first_part, ("ctx", "ch", "sub"))
    returned = lax.all_to_all(
        field_out.astype(jnp.bfloat16), "ctx", split_axis=2, concat_axis=1, tiled=True
    ).astype(field_out.dtype)
    conv_part = returned[0, :, 0, :].T
    corr_part = returned[1, :, 0, :].T
    grad_two = (grad_out.astype(jnp.float32) * (conv_part + skip_bias[None, :] * source)).astype(
        jnp.bfloat16
    )
    grad_mid = corr_part + skip_bias[None, :] * cotan
    grad_one = (grad_mid * values.astype(jnp.float32)).astype(jnp.bfloat16)
    grad_value = (grad_mid * x_one.astype(jnp.float32)).astype(jnp.bfloat16)
    grad_bias = lax.psum(jnp.sum(source * cotan, axis=0), "ctx")
    grad_second = lax.all_gather(weight_part, "ctx", axis=1, tiled=True)
    return (grad_one, grad_two, grad_value, grad_first, grad_second, grad_bias)


STEP = 16
SIDE = 128


def halves(array):
    array = np.asarray(array, np.float32)
    high = array.astype(bf16)
    low = (array - high.astype(np.float32)).astype(bf16)
    return high, low


def block_tables(rows):
    freq = np.concatenate([np.arange(0, rows, 2), np.arange(1, rows, 2)])
    phase = (2 * freq + 1)[:, None] * np.arange(rows)[None, :] % (4 * rows)
    angle = phase * (2.0 * np.pi / (4 * rows))
    forward = np.concatenate([np.cos(angle), -np.sin(angle)], axis=0)
    front = np.ascontiguousarray(np.concatenate(halves(forward), axis=1))
    back = np.ascontiguousarray(np.concatenate(halves(forward.T / rows), axis=0))
    return front, back


def feature_table(seq_len):
    phase = np.arange(seq_len)[:, None] * np.array(band_steps)[None, :] % 4096
    angle = phase * (2.0 * np.pi / 4096.0)
    return np.concatenate([np.cos(angle), np.sin(angle)], axis=1).astype(np.float32)


def split(array):
    high = array.astype(bf16)
    return high, (array - high.astype(f32)).astype(bf16)


def dot(left, right):
    return jnp.dot(left, right, preferred_element_type=f32)


def exact_dot(left, right):
    return jnp.dot(left, right, precision=highest, preferred_element_type=f32)


def dot_across(left, right):
    return lax.dot_general(left, right, (((1,), (1,)), ((), ())), preferred_element_type=f32)


def decay(rate, rows, scale):
    place = lax.broadcasted_iota(jnp.int32, (rows, rate.shape[1]), 0)
    return jnp.exp(-place.astype(f32) * rate) * scale


def times(a, b):
    return a[0] * b[0] - a[1] * b[1], a[0] * b[1] + a[1] * b[0]


def conj_times(a, b):
    return a[0] * b[0] + a[1] * b[1], a[0] * b[1] - a[1] * b[0]


def plus(a, b):
    return a[0] + b[0], a[1] + b[1]


def scaled(a, factor):
    return a[0] * factor, a[1] * factor


def choose(condition, a, b):
    return jnp.where(condition, a[0], b[0]), jnp.where(condition, a[1], b[1])


def turned(a, sign):
    return (a[1], -a[0]) if sign > 0 else (-a[1], a[0])


def forward(front_ref, block):
    return dot(front_ref[...], jnp.concatenate([block, block], axis=0))


def backward(back_ref, high, low=None):
    both = dot(back_ref[...], high)
    rows = both.shape[0] // 2
    out = both[:rows] + both[rows:]
    return out if low is None else out + dot(back_ref[:rows], low)


def row_groups(rows):
    for step in range(rows // STEP):
        sign = 1 if step * STEP < rows // 2 else -1
        yield slice(step * STEP, (step + 1) * STEP), slice(rows + step * STEP, rows + (step + 1) * STEP), sign


def weight_sums(trans, m_high, m_low):
    both = dot(trans, m_high)
    count = both.shape[0] // 2
    return both[:count] + both[count:] + dot(trans[:count], m_low)


def hidden_sums(m_high, m_low, w_high, w_low):
    left = jnp.concatenate([m_high, m_high, m_low], axis=1)
    right = jnp.concatenate([w_high, w_low, w_high], axis=1)
    return dot_across(left, right)


def looped(kernel, kinds, blocks, width):
    def over_strips(*refs):
        def step(block, carry):
            cols = pl.ds(pl.multiple_of(block * width, width), width)
            views = [
                ref if kind is None else ref.at[(*kind, cols)]
                for ref, kind in zip(refs, kinds + (None,) * (len(refs) - len(kinds)))
            ]
            kernel(block, blocks, *views)
            return carry

        lax.fori_loop(0, blocks, step, 0)

    return over_strips


ROWS = (slice(None),)
CUBE = (slice(None), slice(None))


def products_kernel(rank_ref, one_ref, two_ref, val_ref, out_ref, pair_ref, other_ref, edge_ref, bias_ref):
    source = one_ref[...].astype(f32) * val_ref[...].astype(f32)
    cotan = out_ref[...].astype(f32) * two_ref[...].astype(f32)
    even = rank_ref[0] % 2 == 0
    pair_ref[...] = jnp.where(even, source, cotan).astype(bf16)
    edge_ref[...] = pair_ref[...]
    other_ref[...] = jnp.where(even, cotan, source).astype(bf16)
    part = jnp.sum(source * cotan, axis=0, keepdims=True)

    @pl.when(pl.program_id(0) == 0)
    def _():
        bias_ref[...] = part

    @pl.when(pl.program_id(0) > 0)
    def _():
        bias_ref[...] += part


def ordered(first, a, b):
    return (jnp.where(first, a, b), jnp.where(first, b, a))


def sin_cos(angle):
    turns = jnp.floor(angle * (2.0 / math.pi) + 0.5)
    rest = ((angle - turns * 1.5703125) - turns * 4.837512969970703e-4) - turns * 7.54978995489188e-8
    square = rest * rest
    sine = rest + rest * square * (
        -1.6666654611e-1 + square * (8.3321608736e-3 + square * -1.9515295891e-4)
    )
    cosine = 1.0 - 0.5 * square + square * square * (
        4.166664568298827e-2 + square * (-1.388731625493765e-3 + square * 2.443315711809948e-5)
    )
    quarter = turns.astype(jnp.int32)
    odd = (quarter & 1) == 1
    sin_sign = jnp.where((quarter & 2) == 2, -1.0, 1.0).astype(f32)
    cos_sign = jnp.where(((quarter + 1) & 2) == 2, -1.0, 1.0).astype(f32)
    return jnp.where(odd, cosine, sine) * sin_sign, jnp.where(odd, sine, cosine) * cos_sign


def turned_over(hidden, slope):
    both = jnp.concatenate([hidden, slope], axis=1).T
    return jnp.concatenate(split(both[: hidden.shape[1]]), axis=0)


def filters_kernel(
    rows, shards, blocks, width, feats_ref, first_ref, weight_ref, rate_ref, front_ref, spec_ref, trans_ref, slope_ref,
    hid_ref,
):
    hidden, slope = sin_cos(exact_dot(feats_ref[...], first_ref[...]))
    slope_ref[...] = slope
    high, low = split(hidden)
    hid_ref[...] = jnp.concatenate([high, high, low], axis=1)
    trans_ref[...] = turned_over(hidden, slope)
    strips = looped(
        functools.partial(filter_strip, rows, shards), (None, ROWS, ROWS, None, CUBE), blocks, width
    )
    strips(hid_ref, weight_ref, rate_ref, front_ref, spec_ref)


def filter_strip(rows, shards, block, blocks, hid_ref, weight_ref, rate_ref, front_ref, spec_ref):
    scale = float(rows * shards) ** -0.5
    w_high, w_low = split(weight_ref[...])
    stacked = jnp.concatenate([w_high, w_low, w_high], axis=0)
    rate = rate_ref[...]
    env = decay(rate, rows, scale)
    before = None
    for lag in range(shards):
        part = dot(hid_ref[lag * rows : (lag + 1) * rows, :], stacked)
        part = part * (env * jnp.exp(rate * (-float(lag * rows))))
        f_high, f_low = split(part)
        now = forward(front_ref, f_high) + dot(front_ref[:, :rows], f_low)
        for re, im, sign in row_groups(rows):
            here = (now[re], now[im])
            if before is not None:
                here = plus(here, turned((before[re], before[im]), -sign))
            spec_ref[lag, re, :] = here[0].astype(bf16)
            spec_ref[lag, im, :] = here[1].astype(bf16)
        before = now


def own_kernel(rows, shards, channels, blocks, width, rank_ref, *refs):
    inputs, send_out, held = refs[:10], refs[10], refs[11:21]
    send_ref, trans_ref, acc_ref, sems, out_sem = refs[21:]
    (
        feats_ref, first_ref, pair_ref, other_ref, weight_ref, rate_ref, front_ref, back_ref, featt_ref, bias_ref
    ) = held
    copies = [pltpu.make_async_copy(far, near, sems.at[i]) for i, (far, near) in enumerate(zip(inputs, held))]
    for copy in copies:
        copy.start()
    acc_ref[...] = jnp.zeros_like(acc_ref)
    copies[0].wait()
    copies[1].wait()
    hidden, slope = sin_cos(exact_dot(feats_ref[...], first_ref[...]))
    trans_ref[...] = turned_over(hidden, slope)
    for copy in copies[2:]:
        copy.wait()
    kinds = (None, ROWS, ROWS, ROWS, ROWS, None, None, None, ROWS, None)
    looped(functools.partial(own_strip, rows, shards), kinds, blocks, width)(
        rank_ref, pair_ref, other_ref, weight_ref, rate_ref, front_ref, back_ref, trans_ref, send_ref, acc_ref
    )
    first = exact_dot(featt_ref[:, :rows], acc_ref[...] * slope)
    put_side(send_ref, channels, fold(bias_ref[...]), first)
    last = pltpu.make_async_copy(send_ref, send_out, out_sem)
    last.start()
    last.wait()


def own_strip(
    rows, shards, block, blocks, rank_ref, pair_ref, other_ref, weight_ref, rate_ref, front_ref, back_ref, trans_ref,
    send_ref, acc_ref,
):
    source, cotan = ordered(rank_ref[0] % 2 == 0, pair_ref[...], other_ref[...])
    x0 = forward(front_ref, source)
    c0 = forward(front_ref, cotan)
    pair = conj_times((x0[:rows], x0[rows:]), (c0[:rows], c0[rows:]))
    high, low = split(jnp.concatenate(pair, axis=0))
    env = decay(rate_ref[...], rows, float(rows * shards) ** -0.5)
    m_high, m_low = split(backward(back_ref, high, low) * env)
    send_ref[...] = weight_sums(trans_ref[...], m_high, m_low).astype(bf16)
    acc_ref[...] += hidden_sums(m_high, m_low, *split(weight_ref[...]))


def fold(bias):
    return jnp.concatenate([bias[:, i * 128 : (i + 1) * 128] for i in range(bias.shape[1] // 128)], axis=0)


def put_side(pay_ref, channels, bias, first=None):
    half = pay_ref.shape[0] // 2
    pay_ref[:, channels:] = jnp.zeros((2 * half, SIDE), bf16)
    for start, part in zip((0, half // 2), split(bias)):
        pay_ref[start : start + bias.shape[0], channels:] = part
    if first is not None:
        pay_ref[half:, channels:] = jnp.concatenate(split(first), axis=1)


def get_side(pay, channels, lanes, hid_count):
    half = pay.shape[0] // 2
    side = pay[:, channels:].astype(f32)
    low = side[half:]
    return side[:lanes] + side[half // 2 : half // 2 + lanes], low[:, :hid_count] + low[:, hid_count:]


def near_kernel(
    rows, shards, blocks, width, rank_ref, pair_ref, other_ref, pair_in_ref, middle_in_ref, spec_ref, weight_ref,
    rate_ref, front_ref, back_ref, trans_ref, featt_ref, slope_ref, conv_ref, corr_ref, ahead_ref, sums_ref, first_ref,
    near_ref, fields, fast, high_ref, low_ref, acc_ref,
):
    rank = rank_ref[0]
    inner = jnp.logical_and(rank > 0, rank < shards - 1)
    count = shards - 1
    kinds = (None, None, None) + (ROWS,) * 4 + (CUBE, ROWS, ROWS)
    common = (
        rank_ref, front_ref, back_ref, pair_ref, other_ref, pair_in_ref, middle_in_ref, spec_ref, conv_ref, corr_ref,
        fields, fast,
    )

    @pl.when(jnp.logical_not(inner))
    def _():
        looped(functools.partial(edge_strip, rows, shards), kinds, blocks, width)(*common)

    @pl.when(inner)
    def _():
        acc_ref[...] = jnp.zeros_like(acc_ref)
        looped(
            functools.partial(inner_strip, rows, shards), kinds + (None,) * 3 + (ROWS,) * 5, blocks, width
        )(*common, trans_ref, weight_ref, rate_ref, ahead_ref, sums_ref, near_ref, high_ref, low_ref, acc_ref)
        first_ref[...] = exact_dot(
            featt_ref[:, : count * rows], acc_ref[...] * slope_ref[: count * rows, :]
        )


def edge_strip(
    rows, shards, block, blocks, rank_ref, front_ref, back_ref, pair_ref, other_ref, pair_in_ref, middle_in_ref,
    spec_ref, conv_ref, corr_ref, fields, fast,
):
    del middle_in_ref
    top = rank_ref[0] == shards - 1
    source, cotan = ordered(rank_ref[0] % 2 == 0, pair_ref[...], other_ref[...])
    for index, block_in in enumerate((source, cotan, pair_in_ref[...])):
        fields[index] = forward(front_ref, block_in)
    on_conv = jnp.where(top, 1.0, 0.0).astype(f32)
    on_corr = jnp.where(top, 0.0, 1.0).astype(f32)
    for re, im, sign in row_groups(rows):
        x0, c0, near = ((fields[i, re, :], fields[i, im, :]) for i in range(3))
        w0, w1 = ((spec_ref[i, re, :].astype(f32), spec_ref[i, im, :].astype(f32)) for i in range(2))
        values = (
            plus(times(w0, x0), scaled(times(w1, near), on_conv)),
            plus(conj_times(w0, c0), scaled(conj_times(w1, near), on_corr)),
        )
        for index, value in enumerate(values):
            fast[index, re, :] = value[0].astype(bf16)
            fast[index, im, :] = value[1].astype(bf16)
    conv_ref[...] = backward(back_ref, fast[0])
    corr_ref[...] = backward(back_ref, fast[1])


def inner_strip(
    rows, shards, block, blocks, rank_ref, front_ref, back_ref, pair_ref, other_ref, pair_in_ref, middle_in_ref,
    spec_ref, conv_ref, corr_ref, fields, fast, trans_ref, weight_ref, rate_ref, ahead_ref, sums_ref, near_ref, high_ref,
    low_ref, acc_ref,
):
    lower = rank_ref[0] == 1
    upper = jnp.where(lower, 0.0, 1.0).astype(f32)
    side = jnp.where(lower, -1.0, 1.0).astype(f32)
    count = shards - 1
    blocks_in = (
        *ordered(lower, other_ref[...], pair_ref[...]), *ordered(lower, pair_in_ref[...], middle_in_ref[...])
    )
    for index, block_in in enumerate(blocks_in):
        fields[index] = forward(front_ref, block_in)
    for re, im, sign in row_groups(rows):
        x0, c0, x1, c1 = ((fields[i, re, :], fields[i, im, :]) for i in range(4))
        w0, w1, w2 = ((spec_ref[i, re, :].astype(f32), spec_ref[i, im, :].astype(f32)) for i in range(3))
        values = (
            plus(times(w0, x0), times(w1, x1)),
            plus(conj_times(w0, c0), conj_times(w1, c1)),
            times((w2[0], w2[1] * side), choose(lower, c1, x1)),
        )
        for index, value in enumerate(values):
            fast[index, re, :] = value[0].astype(bf16)
            fast[index, im, :] = value[1].astype(bf16)
        near_ref[re, :], near_ref[im, :] = choose(lower, x1, c1)
        zero = conj_times(x0, c0)
        one = plus(conj_times(x1, c0), scaled(conj_times(x0, c1), upper))
        two = conj_times(x1, c1)
        for index, value in enumerate((plus(zero, turned(one, sign)), plus(one, turned(two, sign)), two)):
            for part, where in zip(value, (re, im)):
                high_ref[index, where, :], low_ref[index, where, :] = split(part)
    conv_ref[...] = backward(back_ref, fast[0])
    corr_ref[...] = backward(back_ref, fast[1])
    ahead_ref[...] = backward(back_ref, fast[2])
    rate = rate_ref[...]
    env = decay(rate, rows, float(rows * shards) ** -0.5)
    parts = []
    for lag in range(count):
        grad = backward(back_ref, high_ref[lag], low_ref[lag])
        parts.append(split(grad * (env * jnp.exp(rate * (-float(lag * rows))))))
    m_high = jnp.concatenate([p[0] for p in parts], axis=0)
    m_low = jnp.concatenate([p[1] for p in parts], axis=0)
    sums_ref[...] = weight_sums(trans_ref[:, : count * rows], m_high, m_low)
    acc_ref[...] += hidden_sums(m_high, m_low, *split(weight_ref[...]))


def only(inner, shards, rank_at, kernel):
    def run(*refs):
        rank = refs[rank_at][0]

        @pl.when(jnp.logical_and(rank > 0, rank < shards - 1) == inner)
        def _():
            kernel(*refs)

    return run


def far_kernel(
    rows, block, blocks, rank_ref, far_ref, spec_ref, front_ref, back_ref, ahead_ref, part_ref, far_spec_ref
):
    side = jnp.where(rank_ref[0] == 2, 1.0, -1.0).astype(f32)
    far = forward(front_ref, far_ref[...])
    far_spec_ref[...] = far
    w3 = (spec_ref[0, :rows, :].astype(f32), spec_ref[0, rows:, :].astype(f32) * side)
    ahead = jnp.concatenate(times(w3, (far[:rows], far[rows:])), axis=0).astype(bf16)
    part_ref[...] = (ahead_ref[...] + backward(back_ref, ahead)).astype(bf16)


def late_kernel(rows, block, blocks, rank_ref, far_ref, spec_ref, back_ref, late_ref):
    side = jnp.where(rank_ref[0] == 2, 1.0, -1.0).astype(f32)
    w2 = (spec_ref[0, :rows, :].astype(f32), spec_ref[0, rows:, :].astype(f32) * side)
    late = jnp.concatenate(times(w2, (far_ref[:rows, :], far_ref[rows:, :])), axis=0).astype(bf16)
    late_ref[...] = backward(back_ref, late)


def last_kernel(
    rows, shards, channels, block, blocks, after_ref, rank_ref, near_ref, far_ref, weight_ref, rate_ref, back_ref,
    trans_ref, featt_ref, slope_ref, sums_ref, first_ref, bias_ref, in_ref, pay_ref, total_ref, acc_ref,
):
    del after_ref
    hid_count, width = weight_ref.shape
    lower = rank_ref[0] == 1
    start = pl.multiple_of(block * width, width)
    here = sums_ref[...] + in_ref[:, pl.ds(start, width)].astype(f32)
    mine = (block < blocks // 2) == lower

    @pl.when(block == 0)
    def _():
        acc_ref[...] = jnp.zeros_like(acc_ref)

    @pl.when(mine)
    def _():
        sign = jnp.where(lower, 1.0, -1.0).astype(f32)
        three = conj_times((near_ref[:rows, :], near_ref[rows:, :]), (far_ref[:rows, :], far_ref[rows:, :]))
        three = (three[0], three[1] * sign)
        half = rows // 2
        two = jnp.concatenate([three[1][:half], -three[1][half:], -three[0][:half], three[0][half:]], axis=0)
        rate = rate_ref[...]
        env = decay(rate, rows, float(rows * shards) ** -0.5)
        parts = []
        for lag, value in ((shards - 2, two), (shards - 1, jnp.concatenate(three, axis=0))):
            grad = backward(back_ref, *split(value))
            parts.append(split(grad * (env * jnp.exp(rate * (-float(lag * rows))))))
        m_high = jnp.concatenate([p[0] for p in parts], axis=0)
        m_low = jnp.concatenate([p[1] for p in parts], axis=0)
        trans = trans_ref[:, (shards - 2) * rows :]
        pay_ref[:, pl.ds(start, width)] = (here + weight_sums(trans, m_high, m_low)).astype(bf16)
        w_high, w_low = split(weight_ref[...])
        acc_ref[...] += hidden_sums(m_high, m_low, w_high, w_low)

    @pl.when(jnp.logical_not(mine))
    def _():
        pay_ref[:, pl.ds(start, width)] = here.astype(bf16)

    @pl.when(block == blocks - 1)
    def _():
        first = exact_dot(
            featt_ref[:, (shards - 2) * rows :], acc_ref[...] * slope_ref[(shards - 2) * rows :, :]
        )
        lanes = channels // 128
        in_bias, in_first = get_side(in_ref[...], channels, lanes, hid_count)
        first = first + first_ref[...] + in_first
        put_side(pay_ref, channels, fold(bias_ref[...]) + in_bias)
        total_ref[...] = first


def total_kernel(channels, hid_count, part_ref, first_ref, late_ref, own_ref, come_ref, pay_ref):
    del part_ref, first_ref, late_ref
    lanes = channels // 128
    pay_ref[:, :channels] = (own_ref[:, :channels].astype(f32) + come_ref[:, :channels].astype(f32)).astype(bf16)
    own, come = (get_side(ref[...], channels, lanes, hid_count)[0] for ref in (own_ref, come_ref))
    put_side(pay_ref, channels, own + come)


def gates_kernel(inner, shards, blocks, width, before, *refs):
    refs = refs[before:]
    inputs, outs, held, sems = refs[:10], refs[10:13], refs[13:16], refs[16]

    def leaving(block, i):
        cols = pl.ds(pl.multiple_of(block * width, width), width)
        return pltpu.make_async_copy(held[i].at[:, cols], outs[i].at[:, cols], sems.at[block, i])

    def strip(block, blocks, *views):
        gates_strip(inner, shards, *views)
        for i in range(3):
            leaving(block, i).start()

    looped(strip, (None,) + (ROWS,) * 12, blocks, width)(*inputs, *held)
    for block in range(blocks):
        for i in range(3):
            leaving(block, i).wait()


def gates_strip(
    inner, shards, rank_ref, one_ref, two_ref, val_ref, out_ref, skip_ref, conv_ref, corr_ref, late_ref, part_ref,
    grad_one_ref, grad_two_ref, grad_value_ref,
):
    late = late_ref[...] if inner else part_ref[...].astype(f32)
    upper = rank_ref[0] >= shards // 2
    zero = jnp.zeros_like(late)
    one = one_ref[...].astype(f32)
    val = val_ref[...].astype(f32)
    out = out_ref[...].astype(f32)
    skip = skip_ref[...]
    conv = conv_ref[...] + jnp.where(upper, late, zero)
    corr = corr_ref[...] + jnp.where(upper, zero, late)
    grad_two_ref[...] = (out * (conv + skip * (one * val))).astype(bf16)
    mid = corr + skip * (out * two_ref[...].astype(f32))
    grad_one_ref[...] = (mid * val).astype(bf16)
    grad_value_ref[...] = (mid * one).astype(bf16)


def finish_kernel(
    channels, shards, rank_ref, own_ref, come_ref, first_ref, first_come_ref, second_out, first_out, bias_out, second,
    first, bias, sems,
):
    rank = rank_ref[0]
    inner = jnp.logical_and(rank > 0, rank < shards - 1)
    lanes = channels // 128
    copies = [
        pltpu.make_async_copy(held, out, sems.at[i])
        for i, (held, out) in enumerate(((second, second_out), (first, first_out), (bias, bias_out)))
    ]
    picked = jnp.where(inner, own_ref[...], come_ref[...])
    second[...] = picked[:, :channels].astype(f32)
    copies[0].start()
    first[...] = jnp.where(inner, first_ref[...], first_come_ref[...])
    copies[1].start()
    rows = get_side(picked, channels, lanes, first.shape[1])[0]
    for i in range(lanes):
        bias[:, i * 128 : (i + 1) * 128] = rows[i : i + 1]
    copies[2].start()
    for copy in copies:
        copy.wait()


def few_shards_body(
    x_one, x_two, values, grad_out, first_weight, second_weight, skip_bias, decay_rate
):
    rows, channels = x_one.shape
    shards = lax.axis_size("ctx")
    feat_count, hid_count = first_weight.shape
    seq_len = rows * shards
    double = 2 * rows
    width = min(512, channels)
    blocks = channels // width
    wide = 2 * width if blocks % 4 == 0 else width
    few = channels // wide
    rank = lax.axis_index("ctx").astype(jnp.int32).reshape(1)
    front, back = block_tables(rows)
    feats = feature_table(seq_len)
    featt = np.ascontiguousarray(feats.T)
    skip_row = skip_bias.reshape(1, channels)
    rate_row = decay_rate.reshape(1, channels)
    smem = pl.BlockSpec(memory_space=pltpu.SMEM)
    vmem = pl.BlockSpec(memory_space=pltpu.VMEM)
    anywhere = pl.BlockSpec(memory_space=pl.ANY)
    mebi = 1024 * 1024

    def shape(*dims, dtype=f32):
        return jax.ShapeDtypeStruct(dims, dtype)

    def call(kernel, name, units, out_shape, in_specs, out_specs=None, scratch=(), limit=16, aliases={}):
        return pl.pallas_call(
            kernel,
            in_specs=in_specs,
            out_specs=out_specs if out_specs is not None else [vmem] * len(out_shape),
            out_shape=out_shape,
            scratch_shapes=scratch,
            input_output_aliases=aliases,
            compiler_params=pltpu.CompilerParams(vmem_limit_bytes=limit * mebi),
            cost_estimate=pl.CostEstimate(
                flops=2 * units * double * double * channels, bytes_accessed=rows * channels, transcendentals=0
            ),
            name=name,
        )

    def move(array, pairs):
        return lax.ppermute(array, "ctx", pairs)

    inward = [(0, 1), (shards - 1, shards - 2)]
    outward = [(1, 0), (shards - 2, shards - 1)]
    across = [(1, 2), (2, 1)]
    alone = [(0, 0), (shards - 1, shards - 1)]
    pay_shape = (hid_count, channels + SIDE)
    block_bf16 = shape(rows, channels, dtype=bf16)
    block_f32 = shape(rows, channels)

    row_step = max(rows // 2, 16)
    gate_rows = pl.BlockSpec((row_step, channels), lambda i: (i, 0))
    pair, other, edge, bias = pl.pallas_call(
        products_kernel,
        grid=(rows // row_step,),
        in_specs=[smem] + [gate_rows] * 4,
        out_specs=[gate_rows] * 3 + [pl.BlockSpec((1, channels), lambda i: (0, 0))],
        out_shape=[block_bf16] * 3 + [shape(1, channels)],
        compiler_params=pltpu.CompilerParams(vmem_limit_bytes=64 * mebi),
        name="products",
    )(rank, x_one, x_two, values, grad_out)
    pair_in = move(pair, inward + outward)
    middle_in = move(other, across)

    own_shapes = [
        shape(rows, feat_count), shape(feat_count, hid_count), block_bf16, block_bf16, shape(hid_count, channels),
        shape(1, channels), shape(double, double, dtype=bf16), shape(double, double, dtype=bf16),
        shape(feat_count, seq_len), shape(1, channels), shape(*pay_shape, dtype=bf16),
    ]
    (send,) = call(
        only(False, shards, 0, functools.partial(own_kernel, rows, shards, channels, blocks, width)), "own_pair", 8,
        [shape(*pay_shape, dtype=bf16)],
        [smem] + [anywhere] * 10,
        out_specs=[anywhere],
        scratch=[pltpu.VMEM(s.shape, s.dtype) for s in own_shapes]
        + [
            pltpu.VMEM((2 * hid_count, rows), bf16), pltpu.VMEM((rows, hid_count), f32),
            pltpu.SemaphoreType.DMA((10,)), pltpu.SemaphoreType.DMA,
        ],
        limit=60,
    )(rank, feats[:rows], first_weight, pair, other, second_weight, rate_row, front, back, featt, bias)
    come = move(send, inward)
    late_feats, _ = lax.optimization_barrier((jnp.asarray(feats), send))
    spec, trans, slope = call(
        functools.partial(filters_kernel, rows, shards, blocks, width), "filters", 8,
        [
            shape(shards, double, channels, dtype=bf16), shape(2 * hid_count, seq_len, dtype=bf16),
            shape(seq_len, hid_count),
        ],
        [vmem] * 5,
        scratch=[pltpu.VMEM((seq_len, 3 * hid_count), bf16)],
    )(late_feats, first_weight, second_weight, rate_row, front)

    edge, _ = lax.optimization_barrier((edge, slope))
    far = move(edge, [(0, 2), (shards - 1, shards - 3)])
    conv, corr, ahead, sums, first, near_spec = call(
        functools.partial(near_kernel, rows, shards, blocks, width), "near_blocks", 20,
        [block_f32] * 3
        + [shape(hid_count, channels), shape(feat_count, hid_count), shape(double, channels)],
        [smem] + [vmem] * 12,
        scratch=[
            pltpu.VMEM((4, double, width), f32),
            pltpu.VMEM((3, double, width), bf16),
            pltpu.VMEM((shards - 1, double, width), bf16),
            pltpu.VMEM((shards - 1, double, width), bf16),
            pltpu.VMEM(((shards - 1) * rows, hid_count), f32),
        ],
    )(rank, pair, other, pair_in, middle_in, spec, second_weight, rate_row, front, back, trans, featt, slope)

    part, far_spec = call(
        only(
            True, shards, 0,
            looped(
                functools.partial(far_kernel, rows),
                (None, ROWS, (slice(3, 4), slice(None)), None, None, ROWS, ROWS, ROWS),
                few, wide,
            ),
        ),
        "far_block", 1,
        [block_bf16, shape(double, channels)],
        [smem] + [vmem] * 5,
    )(rank, far, spec, front, back, ahead)
    (late,) = call(
        only(
            True, shards, 0,
            looped(
                functools.partial(late_kernel, rows),
                (None, ROWS, (slice(2, 3), slice(None)), None, ROWS),
                few, wide,
            ),
        ),
        "late_block", 1,
        [block_f32],
        [smem] + [vmem] * 3,
    )(rank, far_spec, spec, back)
    part_come = move(part, outward)

    pay, first = call(
        only(
            True, shards, 1,
            looped(
                functools.partial(last_kernel, rows, shards, channels),
                (None, None, ROWS, ROWS, ROWS, ROWS, None, None, None, None, ROWS),
                few, wide,
            ),
        ),
        "last_pair", 1,
        [shape(*pay_shape, dtype=bf16), shape(feat_count, hid_count)],
        [anywhere, smem] + [vmem] * 12,
        scratch=[pltpu.VMEM((2 * rows, hid_count), f32)],
    )(part, rank, near_spec, far_spec, second_weight, rate_row, back, trans, featt, slope, sums, first, bias, come)
    pay_come = move(pay, across + alone)
    group = lax.axis_size(("ch", "sub"))

    def swapped(array, bits):
        for bit in bits:
            pairs = [
                (c * group + i, c * group + (i ^ bit if 0 < c < shards - 1 else i))
                for c in range(shards) for i in range(group)
            ]
            array = array + lax.ppermute(array, ("ctx", "ch", "sub"), pairs)
        return array

    bits = [1 << i for i in range(group.bit_length() - 1)]
    first = swapped(first, bits[:1])
    first = first + move(first, across + alone)

    (total,) = call(
        functools.partial(total_kernel, channels, hid_count), "total", 0,
        [shape(*pay_shape, dtype=bf16)],
        [anywhere] * 3 + [vmem] * 2,
    )(part_come, first, late, pay, pay_come)
    total_come = move(total, inward + outward)

    def gates(inner, *before):
        return call(
            only(
                inner, shards, len(before),
                functools.partial(gates_kernel, inner, shards, blocks, width, len(before)),
            ),
            "gates", 0,
            [block_bf16] * 3,
            [anywhere] * len(before) + [smem] + [vmem] * 9,
            out_specs=[anywhere] * 3,
            scratch=[pltpu.VMEM((rows, channels), bf16)] * 3 + [pltpu.SemaphoreType.DMA((blocks, 3))],
            aliases={i: i for i in range(3)} if inner else {},
        )(*before, rank, x_one, x_two, values, grad_out, skip_row, conv, corr, late, part_come)

    grads = gates(False, total)
    first = swapped(first, bits[1:])
    first_come = move(first, inward + outward)
    grad_one, grad_two, grad_value = gates(True, *grads)

    outs = [shape(hid_count, channels), shape(feat_count, hid_count), shape(1, channels)]
    grad_second, grad_first, grad_bias = call(
        functools.partial(finish_kernel, channels, shards), "finish", 0,
        outs,
        [smem] + [vmem] * 4,
        out_specs=[anywhere] * 3,
        scratch=[pltpu.VMEM(o.shape, f32) for o in outs] + [pltpu.SemaphoreType.DMA((3,))],
    )(rank, total, total_come, first, first_come)
    return (grad_one, grad_two, grad_value, grad_first, grad_second, grad_bias.reshape(channels))


def solution(mesh):
    in_specs = (
        P(("parts", "ctx"), ("ch", "sub")),
        P(("parts", "ctx"), ("ch", "sub")),
        P(("parts", "ctx"), ("ch", "sub")),
        P(("parts", "ctx"), ("ch", "sub")),
        P(),
        P(None, ("ch", "sub")),
        P(("ch", "sub")),
        P(("ch", "sub")),
    )
    out_specs = (
        P(("parts", "ctx"), ("ch", "sub")),
        P(("parts", "ctx"), ("ch", "sub")),
        P(("parts", "ctx"), ("ch", "sub")),
        P("parts", None),
        P("parts", ("ch", "sub")),
        P(("parts", "ch", "sub")),
    )
    body = few_shards_body if mesh.shape["ctx"] == 4 else many_shards_body
    return jax.shard_map(body, mesh=mesh, in_specs=in_specs, out_specs=out_specs, check_vma=False)
```

```python
import functools
import math

import jax
import jax.numpy as jnp
import numpy as np
from jax import lax
from jax.experimental import pallas as pl
from jax.experimental.pallas import tpu as pltpu
from jax.sharding import PartitionSpec as P

band_steps = (1763, 1201, 811, 547, 367, 251, 167, 113, 79, 53, 37, 23, 17, 11, 7, 3)
highest = lax.Precision.HIGHEST
f32 = jnp.float32
bf16 = jnp.bfloat16


def features(positions):
    multiplier = jnp.array(band_steps, dtype=jnp.int32)
    phase = positions[:, None] * multiplier[None, :] % 4096
    angle = phase.astype(jnp.float32) * (2.0 * math.pi / 4096.0)
    return jnp.concatenate([jnp.cos(angle), jnp.sin(angle)], axis=1)


def tables(out_count, in_count, modulus, sign_value):
    row_index = lax.broadcasted_iota(jnp.int32, (out_count, in_count), 0)
    col_index = lax.broadcasted_iota(jnp.int32, (out_count, in_count), 1)
    angle = (row_index * col_index % modulus).astype(jnp.float32) * (2.0 * math.pi / modulus)
    return (jnp.cos(angle), sign_value * jnp.sin(angle))


def twiddle(spec_re, spec_im, freq_count, span, modulus, sign_value):
    freq_index = lax.broadcasted_iota(jnp.int32, (freq_count, span), 0)
    pos_index = lax.broadcasted_iota(jnp.int32, (freq_count, span), 1)
    angle = (freq_index * pos_index % modulus).astype(jnp.float32) * (2.0 * math.pi / modulus)
    factor_re = jnp.cos(angle)[None, None, :, :]
    factor_im = (sign_value * jnp.sin(angle))[None, None, :, :]
    return (spec_re * factor_re - spec_im * factor_im, spec_re * factor_im + spec_im * factor_re)


def contract(kernel, array):
    return jnp.einsum(
        "lj,mckj->mckl", kernel, array, precision=highest, preferred_element_type=jnp.float32
    )


def along_positions(spec_re, spec_im, kernel_re, kernel_im):
    return (
        contract(kernel_re, spec_re) - contract(kernel_im, spec_im),
        contract(kernel_re, spec_im) + contract(kernel_im, spec_re),
    )


def many_shards_body(
    x_one, x_two, values, grad_out, first_weight, second_weight, skip_bias, decay_rate
):
    row_count, chan_count = x_one.shape
    shards = lax.axis_size("ctx")
    rank = lax.axis_index("ctx")
    seq_len = row_count * shards
    total = 2 * seq_len
    narrow = chan_count // shards
    chan_weight = lax.dynamic_slice_in_dim(second_weight, rank * narrow, narrow, 1)
    chan_rate = lax.dynamic_slice_in_dim(decay_rate, rank * narrow, narrow, 0)
    source = x_one.astype(jnp.float32) * values.astype(jnp.float32)
    cotan = grad_out.astype(jnp.float32) * x_two.astype(jnp.float32)
    spread = lax.all_to_all(
        jnp.stack([source.T, cotan.T])[:, :, None, :],
        "ctx",
        split_axis=1,
        concat_axis=2,
        tiled=True,
    )
    far_source = spread[0]
    far_cotan = spread[1]
    positions = jnp.arange(seq_len, dtype=jnp.int32)
    feats = features(positions)
    pre_act = jnp.dot(feats, first_weight, precision=highest, preferred_element_type=jnp.float32)
    hidden = jnp.sin(pre_act)
    envelope = jnp.exp(-chan_rate[:, None] * positions.astype(jnp.float32)[None, :]) * float(
        seq_len
    ) ** (-0.5)
    filt = (
        jnp.einsum(
            "th,hc->ct", hidden, chan_weight, precision=highest, preferred_element_type=jnp.float32
        )
        * envelope
    )
    filt_blocks = filt.reshape(narrow, shards, row_count)
    fields = jnp.stack([far_source, far_cotan])

    def first_section(kernel):
        field_part = jnp.einsum(
            "kn,mcnj->mckj", kernel, fields, precision=highest, preferred_element_type=jnp.float32
        )
        filter_part = jnp.einsum(
            "kn,cnj->ckj",
            kernel,
            filt_blocks,
            precision=highest,
            preferred_element_type=jnp.float32,
        )
        return jnp.concatenate([field_part, filter_part[None]], axis=0)

    first_re, first_im = tables(2 * shards, shards, 2 * shards, -1.0)
    spec_re, spec_im = (first_section(first_re), first_section(first_im))
    spec_re, spec_im = twiddle(spec_re, spec_im, 2 * shards, row_count, total, -1.0)
    fwd_re, fwd_im = tables(row_count, row_count, row_count, -1.0)
    spec_re, spec_im = along_positions(spec_re, spec_im, fwd_re, fwd_im)
    source_re, source_im = (spec_re[0], spec_im[0])
    cotan_re, cotan_im = (spec_re[1], spec_im[1])
    filter_re, filter_im = (spec_re[2], spec_im[2])
    prod_re = jnp.stack(
        [
            source_re * filter_re - source_im * filter_im,
            cotan_re * filter_re + cotan_im * filter_im,
            cotan_re * source_re + cotan_im * source_im,
        ]
    )
    prod_im = jnp.stack(
        [
            source_re * filter_im + source_im * filter_re,
            cotan_im * filter_re - cotan_re * filter_im,
            cotan_im * source_re - cotan_re * source_im,
        ]
    )
    back_re, back_im = tables(row_count, row_count, row_count, 1.0)
    prod_re, prod_im = along_positions(prod_re, prod_im, back_re, back_im)
    prod_re, prod_im = twiddle(prod_re, prod_im, 2 * shards, row_count, total, 1.0)
    last_re, last_im = tables(shards, 2 * shards, 2 * shards, 1.0)
    field_out = jnp.einsum(
        "nk,mckj->mcnj", last_re, prod_re[:2], precision=highest, preferred_element_type=jnp.float32
    ) - jnp.einsum(
        "nk,mckj->mcnj", last_im, prod_im[:2], precision=highest, preferred_element_type=jnp.float32
    )
    field_out = field_out * (1.0 / total)
    filt_grad = jnp.einsum(
        "nk,ckj->cnj", last_re, prod_re[2], precision=highest, preferred_element_type=jnp.float32
    ) - jnp.einsum(
        "nk,ckj->cnj", last_im, prod_im[2], precision=highest, preferred_element_type=jnp.float32
    )
    filt_grad = (filt_grad * (1.0 / total)).reshape(narrow, seq_len)
    modulated = filt_grad * envelope
    weight_part = jnp.einsum(
        "th,ct->hc", hidden, modulated, precision=highest, preferred_element_type=jnp.float32
    )
    hidden_grad = jnp.einsum(
        "ct,hc->th", modulated, chan_weight, precision=highest, preferred_element_type=jnp.float32
    )
    first_part = jnp.dot(
        feats.T,
        hidden_grad * jnp.cos(pre_act),
        precision=highest,
        preferred_element_type=jnp.float32,
    )
    grad_first = lax.psum(first_part, ("ctx", "ch", "sub"))
    returned = lax.all_to_all(
        field_out.astype(jnp.bfloat16), "ctx", split_axis=2, concat_axis=1, tiled=True
    ).astype(field_out.dtype)
    conv_part = returned[0, :, 0, :].T
    corr_part = returned[1, :, 0, :].T
    grad_two = (grad_out.astype(jnp.float32) * (conv_part + skip_bias[None, :] * source)).astype(
        jnp.bfloat16
    )
    grad_mid = corr_part + skip_bias[None, :] * cotan
    grad_one = (grad_mid * values.astype(jnp.float32)).astype(jnp.bfloat16)
    grad_value = (grad_mid * x_one.astype(jnp.float32)).astype(jnp.bfloat16)
    grad_bias = lax.psum(jnp.sum(source * cotan, axis=0), "ctx")
    grad_second = lax.all_gather(weight_part, "ctx", axis=1, tiled=True)
    return (grad_one, grad_two, grad_value, grad_first, grad_second, grad_bias)


STEP = 16
SIDE = 128


def halves(array):
    array = np.asarray(array, np.float32)
    high = array.astype(bf16)
    low = (array - high.astype(np.float32)).astype(bf16)
    return high, low


def block_tables(rows):
    freq = np.concatenate([np.arange(0, rows, 2), np.arange(1, rows, 2)])
    phase = (2 * freq + 1)[:, None] * np.arange(rows)[None, :] % (4 * rows)
    angle = phase * (2.0 * np.pi / (4 * rows))
    forward = np.concatenate([np.cos(angle), -np.sin(angle)], axis=0)
    front = np.ascontiguousarray(np.concatenate(halves(forward), axis=1))
    back = np.ascontiguousarray(np.concatenate(halves(forward.T / rows), axis=0))
    return front, back


def feature_table(seq_len):
    phase = np.arange(seq_len)[:, None] * np.array(band_steps)[None, :] % 4096
    angle = phase * (2.0 * np.pi / 4096.0)
    return np.concatenate([np.cos(angle), np.sin(angle)], axis=1).astype(np.float32)


def split(array):
    high = array.astype(bf16)
    return high, (array - high.astype(f32)).astype(bf16)


def dot(left, right):
    return jnp.dot(left, right, preferred_element_type=f32)


def exact_dot(left, right):
    return jnp.dot(left, right, precision=highest, preferred_element_type=f32)


def dot_across(left, right):
    return lax.dot_general(left, right, (((1,), (1,)), ((), ())), preferred_element_type=f32)


def decay(rate, rows, scale):
    place = lax.broadcasted_iota(jnp.int32, (rows, rate.shape[1]), 0)
    return jnp.exp(-place.astype(f32) * rate) * scale


def times(a, b):
    return a[0] * b[0] - a[1] * b[1], a[0] * b[1] + a[1] * b[0]


def conj_times(a, b):
    return a[0] * b[0] + a[1] * b[1], a[0] * b[1] - a[1] * b[0]


def plus(a, b):
    return a[0] + b[0], a[1] + b[1]


def scaled(a, factor):
    return a[0] * factor, a[1] * factor


def choose(condition, a, b):
    return jnp.where(condition, a[0], b[0]), jnp.where(condition, a[1], b[1])


def turned(a, sign):
    return (a[1], -a[0]) if sign > 0 else (-a[1], a[0])


def forward(front_ref, block):
    return dot(front_ref[...], jnp.concatenate([block, block], axis=0))


def backward(back_ref, high, low=None):
    both = dot(back_ref[...], high)
    rows = both.shape[0] // 2
    out = both[:rows] + both[rows:]
    return out if low is None else out + dot(back_ref[:rows], low)


def row_groups(rows):
    for step in range(rows // STEP):
        sign = 1 if step * STEP < rows // 2 else -1
        yield slice(step * STEP, (step + 1) * STEP), slice(rows + step * STEP, rows + (step + 1) * STEP), sign


def weight_sums(trans, m_high, m_low):
    both = dot(trans, m_high)
    count = both.shape[0] // 2
    return both[:count] + both[count:] + dot(trans[:count], m_low)


def hidden_sums(m_high, m_low, w_high, w_low):
    left = jnp.concatenate([m_high, m_high, m_low], axis=1)
    right = jnp.concatenate([w_high, w_low, w_high], axis=1)
    return dot_across(left, right)


def looped(kernel, kinds, blocks, width):
    def over_strips(*refs):
        def step(block, carry):
            cols = pl.ds(pl.multiple_of(block * width, width), width)
            views = [
                ref if kind is None else ref.at[(*kind, cols)]
                for ref, kind in zip(refs, kinds + (None,) * (len(refs) - len(kinds)))
            ]
            kernel(block, blocks, *views)
            return carry

        lax.fori_loop(0, blocks, step, 0)

    return over_strips


ROWS = (slice(None),)
CUBE = (slice(None), slice(None))


def products_kernel(rank_ref, one_ref, two_ref, val_ref, out_ref, pair_ref, other_ref, edge_ref, bias_ref):
    source = one_ref[...].astype(f32) * val_ref[...].astype(f32)
    cotan = out_ref[...].astype(f32) * two_ref[...].astype(f32)
    even = rank_ref[0] % 2 == 0
    pair_ref[...] = jnp.where(even, source, cotan).astype(bf16)
    edge_ref[...] = pair_ref[...]
    other_ref[...] = jnp.where(even, cotan, source).astype(bf16)
    part = jnp.sum(source * cotan, axis=0, keepdims=True)

    @pl.when(pl.program_id(0) == 0)
    def _():
        bias_ref[...] = part

    @pl.when(pl.program_id(0) > 0)
    def _():
        bias_ref[...] += part


def ordered(first, a, b):
    return (jnp.where(first, a, b), jnp.where(first, b, a))


def sin_cos(angle):
    turns = jnp.floor(angle * (2.0 / math.pi) + 0.5)
    rest = ((angle - turns * 1.5703125) - turns * 4.837512969970703e-4) - turns * 7.54978995489188e-8
    square = rest * rest
    sine = rest + rest * square * (
        -1.6666654611e-1 + square * (8.3321608736e-3 + square * -1.9515295891e-4)
    )
    cosine = 1.0 - 0.5 * square + square * square * (
        4.166664568298827e-2 + square * (-1.388731625493765e-3 + square * 2.443315711809948e-5)
    )
    quarter = turns.astype(jnp.int32)
    odd = (quarter & 1) == 1
    sin_sign = jnp.where((quarter & 2) == 2, -1.0, 1.0).astype(f32)
    cos_sign = jnp.where(((quarter + 1) & 2) == 2, -1.0, 1.0).astype(f32)
    return jnp.where(odd, cosine, sine) * sin_sign, jnp.where(odd, sine, cosine) * cos_sign


def turned_over(hidden, slope):
    both = jnp.concatenate([hidden, slope], axis=1).T
    return jnp.concatenate(split(both[: hidden.shape[1]]), axis=0)


def filters_kernel(
    rows, shards, blocks, width, feats_ref, first_ref, weight_ref, rate_ref, front_ref, spec_ref, trans_ref, slope_ref,
    hid_ref,
):
    hidden, slope = sin_cos(exact_dot(feats_ref[...], first_ref[...]))
    slope_ref[...] = slope
    high, low = split(hidden)
    hid_ref[...] = jnp.concatenate([high, high, low], axis=1)
    trans_ref[...] = turned_over(hidden, slope)
    strips = looped(
        functools.partial(filter_strip, rows, shards), (None, ROWS, ROWS, None, CUBE), blocks, width
    )
    strips(hid_ref, weight_ref, rate_ref, front_ref, spec_ref)


def filter_strip(rows, shards, block, blocks, hid_ref, weight_ref, rate_ref, front_ref, spec_ref):
    scale = float(rows * shards) ** -0.5
    w_high, w_low = split(weight_ref[...])
    stacked = jnp.concatenate([w_high, w_low, w_high], axis=0)
    rate = rate_ref[...]
    env = decay(rate, rows, scale)
    before = None
    for lag in range(shards):
        part = dot(hid_ref[lag * rows : (lag + 1) * rows, :], stacked)
        part = part * (env * jnp.exp(rate * (-float(lag * rows))))
        f_high, f_low = split(part)
        now = forward(front_ref, f_high) + dot(front_ref[:, :rows], f_low)
        for re, im, sign in row_groups(rows):
            here = (now[re], now[im])
            if before is not None:
                here = plus(here, turned((before[re], before[im]), -sign))
            spec_ref[lag, re, :] = here[0].astype(bf16)
            spec_ref[lag, im, :] = here[1].astype(bf16)
        before = now


def own_kernel(rows, shards, channels, blocks, width, rank_ref, *refs):
    inputs, send_out, held = refs[:10], refs[10], refs[11:21]
    send_ref, trans_ref, acc_ref, sems, out_sem = refs[21:]
    (
        feats_ref, first_ref, pair_ref, other_ref, weight_ref, rate_ref, front_ref, back_ref, featt_ref, bias_ref
    ) = held
    copies = [pltpu.make_async_copy(far, near, sems.at[i]) for i, (far, near) in enumerate(zip(inputs, held))]
    for copy in copies:
        copy.start()
    acc_ref[...] = jnp.zeros_like(acc_ref)
    copies[0].wait()
    copies[1].wait()
    hidden, slope = sin_cos(exact_dot(feats_ref[...], first_ref[...]))
    trans_ref[...] = turned_over(hidden, slope)
    for copy in copies[2:]:
        copy.wait()
    kinds = (None, ROWS, ROWS, ROWS, ROWS, None, None, None, ROWS, None)
    looped(functools.partial(own_strip, rows, shards), kinds, blocks, width)(
        rank_ref, pair_ref, other_ref, weight_ref, rate_ref, front_ref, back_ref, trans_ref, send_ref, acc_ref
    )
    first = exact_dot(featt_ref[:, :rows], acc_ref[...] * slope)
    put_side(send_ref, channels, fold(bias_ref[...]), first)
    last = pltpu.make_async_copy(send_ref, send_out, out_sem)
    last.start()
    last.wait()


def own_strip(
    rows, shards, block, blocks, rank_ref, pair_ref, other_ref, weight_ref, rate_ref, front_ref, back_ref, trans_ref,
    send_ref, acc_ref,
):
    source, cotan = ordered(rank_ref[0] % 2 == 0, pair_ref[...], other_ref[...])
    x0 = forward(front_ref, source)
    c0 = forward(front_ref, cotan)
    pair = conj_times((x0[:rows], x0[rows:]), (c0[:rows], c0[rows:]))
    high, low = split(jnp.concatenate(pair, axis=0))
    env = decay(rate_ref[...], rows, float(rows * shards) ** -0.5)
    m_high, m_low = split(backward(back_ref, high, low) * env)
    send_ref[...] = weight_sums(trans_ref[...], m_high, m_low).astype(bf16)
    acc_ref[...] += hidden_sums(m_high, m_low, *split(weight_ref[...]))


def fold(bias):
    return jnp.concatenate([bias[:, i * 128 : (i + 1) * 128] for i in range(bias.shape[1] // 128)], axis=0)


def put_side(pay_ref, channels, bias, first=None):
    half = pay_ref.shape[0] // 2
    pay_ref[:, channels:] = jnp.zeros((2 * half, SIDE), bf16)
    for start, part in zip((0, half // 2), split(bias)):
        pay_ref[start : start + bias.shape[0], channels:] = part
    if first is not None:
        pay_ref[half:, channels:] = jnp.concatenate(split(first), axis=1)


def get_side(pay, channels, lanes, hid_count):
    half = pay.shape[0] // 2
    side = pay[:, channels:].astype(f32)
    low = side[half:]
    return side[:lanes] + side[half // 2 : half // 2 + lanes], low[:, :hid_count] + low[:, hid_count:]


def near_kernel(
    rows, shards, blocks, width, rank_ref, pair_ref, other_ref, pair_in_ref, middle_in_ref, spec_ref, weight_ref,
    rate_ref, front_ref, back_ref, trans_ref, featt_ref, slope_ref, conv_ref, corr_ref, ahead_ref, sums_ref, first_ref,
    near_ref, fields, fast, high_ref, low_ref, acc_ref,
):
    rank = rank_ref[0]
    inner = jnp.logical_and(rank > 0, rank < shards - 1)
    count = shards - 1
    kinds = (None, None, None) + (ROWS,) * 4 + (CUBE, ROWS, ROWS)
    common = (
        rank_ref, front_ref, back_ref, pair_ref, other_ref, pair_in_ref, middle_in_ref, spec_ref, conv_ref, corr_ref,
        fields, fast,
    )

    @pl.when(jnp.logical_not(inner))
    def _():
        looped(functools.partial(edge_strip, rows, shards), kinds, blocks, width)(*common)

    @pl.when(inner)
    def _():
        acc_ref[...] = jnp.zeros_like(acc_ref)
        looped(
            functools.partial(inner_strip, rows, shards), kinds + (None,) * 3 + (ROWS,) * 5, blocks, width
        )(*common, trans_ref, weight_ref, rate_ref, ahead_ref, sums_ref, near_ref, high_ref, low_ref, acc_ref)
        first_ref[...] = exact_dot(
            featt_ref[:, : count * rows], acc_ref[...] * slope_ref[: count * rows, :]
        )


def edge_strip(
    rows, shards, block, blocks, rank_ref, front_ref, back_ref, pair_ref, other_ref, pair_in_ref, middle_in_ref,
    spec_ref, conv_ref, corr_ref, fields, fast,
):
    del middle_in_ref
    top = rank_ref[0] == shards - 1
    source, cotan = ordered(rank_ref[0] % 2 == 0, pair_ref[...], other_ref[...])
    for index, block_in in enumerate((source, cotan, pair_in_ref[...])):
        fields[index] = forward(front_ref, block_in)
    on_conv = jnp.where(top, 1.0, 0.0).astype(f32)
    on_corr = jnp.where(top, 0.0, 1.0).astype(f32)
    for re, im, sign in row_groups(rows):
        x0, c0, near = ((fields[i, re, :], fields[i, im, :]) for i in range(3))
        w0, w1 = ((spec_ref[i, re, :].astype(f32), spec_ref[i, im, :].astype(f32)) for i in range(2))
        values = (
            plus(times(w0, x0), scaled(times(w1, near), on_conv)),
            plus(conj_times(w0, c0), scaled(conj_times(w1, near), on_corr)),
        )
        for index, value in enumerate(values):
            fast[index, re, :] = value[0].astype(bf16)
            fast[index, im, :] = value[1].astype(bf16)
    conv_ref[...] = backward(back_ref, fast[0])
    corr_ref[...] = backward(back_ref, fast[1])


def inner_strip(
    rows, shards, block, blocks, rank_ref, front_ref, back_ref, pair_ref, other_ref, pair_in_ref, middle_in_ref,
    spec_ref, conv_ref, corr_ref, fields, fast, trans_ref, weight_ref, rate_ref, ahead_ref, sums_ref, near_ref, high_ref,
    low_ref, acc_ref,
):
    lower = rank_ref[0] == 1
    upper = jnp.where(lower, 0.0, 1.0).astype(f32)
    side = jnp.where(lower, -1.0, 1.0).astype(f32)
    count = shards - 1
    blocks_in = (
        *ordered(lower, other_ref[...], pair_ref[...]), *ordered(lower, pair_in_ref[...], middle_in_ref[...])
    )
    for index, block_in in enumerate(blocks_in):
        fields[index] = forward(front_ref, block_in)
    for re, im, sign in row_groups(rows):
        x0, c0, x1, c1 = ((fields[i, re, :], fields[i, im, :]) for i in range(4))
        w0, w1, w2 = ((spec_ref[i, re, :].astype(f32), spec_ref[i, im, :].astype(f32)) for i in range(3))
        values = (
            plus(times(w0, x0), times(w1, x1)),
            plus(conj_times(w0, c0), conj_times(w1, c1)),
            times((w2[0], w2[1] * side), choose(lower, c1, x1)),
        )
        for index, value in enumerate(values):
            fast[index, re, :] = value[0].astype(bf16)
            fast[index, im, :] = value[1].astype(bf16)
        near_ref[re, :], near_ref[im, :] = choose(lower, x1, c1)
        zero = conj_times(x0, c0)
        one = plus(conj_times(x1, c0), scaled(conj_times(x0, c1), upper))
        two = conj_times(x1, c1)
        for index, value in enumerate((plus(zero, turned(one, sign)), plus(one, turned(two, sign)), two)):
            for part, where in zip(value, (re, im)):
                high_ref[index, where, :], low_ref[index, where, :] = split(part)
    conv_ref[...] = backward(back_ref, fast[0])
    corr_ref[...] = backward(back_ref, fast[1])
    ahead_ref[...] = backward(back_ref, fast[2])
    rate = rate_ref[...]
    env = decay(rate, rows, float(rows * shards) ** -0.5)
    parts = []
    for lag in range(count):
        grad = backward(back_ref, high_ref[lag], low_ref[lag])
        parts.append(split(grad * (env * jnp.exp(rate * (-float(lag * rows))))))
    m_high = jnp.concatenate([p[0] for p in parts], axis=0)
    m_low = jnp.concatenate([p[1] for p in parts], axis=0)
    sums_ref[...] = weight_sums(trans_ref[:, : count * rows], m_high, m_low)
    acc_ref[...] += hidden_sums(m_high, m_low, *split(weight_ref[...]))


def only(inner, shards, rank_at, kernel):
    def run(*refs):
        rank = refs[rank_at][0]

        @pl.when(jnp.logical_and(rank > 0, rank < shards - 1) == inner)
        def _():
            kernel(*refs)

    return run


def far_kernel(
    rows, block, blocks, rank_ref, far_ref, spec_ref, front_ref, back_ref, ahead_ref, part_ref, far_spec_ref
):
    side = jnp.where(rank_ref[0] == 2, 1.0, -1.0).astype(f32)
    far = forward(front_ref, far_ref[...])
    far_spec_ref[...] = far
    w3 = (spec_ref[0, :rows, :].astype(f32), spec_ref[0, rows:, :].astype(f32) * side)
    ahead = jnp.concatenate(times(w3, (far[:rows], far[rows:])), axis=0).astype(bf16)
    part_ref[...] = (ahead_ref[...] + backward(back_ref, ahead)).astype(bf16)


def late_kernel(rows, block, blocks, rank_ref, far_ref, spec_ref, back_ref, late_ref):
    side = jnp.where(rank_ref[0] == 2, 1.0, -1.0).astype(f32)
    w2 = (spec_ref[0, :rows, :].astype(f32), spec_ref[0, rows:, :].astype(f32) * side)
    late = jnp.concatenate(times(w2, (far_ref[:rows, :], far_ref[rows:, :])), axis=0).astype(bf16)
    late_ref[...] = backward(back_ref, late)


def last_kernel(
    rows, shards, channels, block, blocks, after_ref, rank_ref, near_ref, far_ref, weight_ref, rate_ref, back_ref,
    trans_ref, featt_ref, slope_ref, sums_ref, first_ref, bias_ref, in_ref, pay_ref, total_ref, acc_ref,
):
    del after_ref
    hid_count, width = weight_ref.shape
    lower = rank_ref[0] == 1
    start = pl.multiple_of(block * width, width)
    here = sums_ref[...] + in_ref[:, pl.ds(start, width)].astype(f32)
    mine = (block < blocks // 2) == lower

    @pl.when(block == 0)
    def _():
        acc_ref[...] = jnp.zeros_like(acc_ref)

    @pl.when(mine)
    def _():
        sign = jnp.where(lower, 1.0, -1.0).astype(f32)
        three = conj_times((near_ref[:rows, :], near_ref[rows:, :]), (far_ref[:rows, :], far_ref[rows:, :]))
        three = (three[0], three[1] * sign)
        half = rows // 2
        two = jnp.concatenate([three[1][:half], -three[1][half:], -three[0][:half], three[0][half:]], axis=0)
        rate = rate_ref[...]
        env = decay(rate, rows, float(rows * shards) ** -0.5)
        parts = []
        for lag, value in ((shards - 2, two), (shards - 1, jnp.concatenate(three, axis=0))):
            grad = backward(back_ref, *split(value))
            parts.append(split(grad * (env * jnp.exp(rate * (-float(lag * rows))))))
        m_high = jnp.concatenate([p[0] for p in parts], axis=0)
        m_low = jnp.concatenate([p[1] for p in parts], axis=0)
        trans = trans_ref[:, (shards - 2) * rows :]
        pay_ref[:, pl.ds(start, width)] = (here + weight_sums(trans, m_high, m_low)).astype(bf16)
        w_high, w_low = split(weight_ref[...])
        acc_ref[...] += hidden_sums(m_high, m_low, w_high, w_low)

    @pl.when(jnp.logical_not(mine))
    def _():
        pay_ref[:, pl.ds(start, width)] = here.astype(bf16)

    @pl.when(block == blocks - 1)
    def _():
        first = exact_dot(
            featt_ref[:, (shards - 2) * rows :], acc_ref[...] * slope_ref[(shards - 2) * rows :, :]
        )
        lanes = channels // 128
        in_bias, in_first = get_side(in_ref[...], channels, lanes, hid_count)
        first = first + first_ref[...] + in_first
        put_side(pay_ref, channels, fold(bias_ref[...]) + in_bias)
        total_ref[...] = first


def total_kernel(channels, hid_count, part_ref, first_ref, late_ref, own_ref, come_ref, pay_ref):
    del part_ref, first_ref, late_ref
    lanes = channels // 128
    pay_ref[:, :channels] = (own_ref[:, :channels].astype(f32) + come_ref[:, :channels].astype(f32)).astype(bf16)
    own, come = (get_side(ref[...], channels, lanes, hid_count)[0] for ref in (own_ref, come_ref))
    put_side(pay_ref, channels, own + come)


def gates_kernel(inner, shards, blocks, width, before, *refs):
    refs = refs[before:]
    inputs, outs, held, sems = refs[:10], refs[10:13], refs[13:16], refs[16]

    def leaving(block, i):
        cols = pl.ds(pl.multiple_of(block * width, width), width)
        return pltpu.make_async_copy(held[i].at[:, cols], outs[i].at[:, cols], sems.at[block, i])

    def strip(block, blocks, *views):
        gates_strip(inner, shards, *views)
        for i in range(3):
            leaving(block, i).start()

    looped(strip, (None,) + (ROWS,) * 12, blocks, width)(*inputs, *held)
    for block in range(blocks):
        for i in range(3):
            leaving(block, i).wait()


def gates_strip(
    inner, shards, rank_ref, one_ref, two_ref, val_ref, out_ref, skip_ref, conv_ref, corr_ref, late_ref, part_ref,
    grad_one_ref, grad_two_ref, grad_value_ref,
):
    late = late_ref[...] if inner else part_ref[...].astype(f32)
    upper = rank_ref[0] >= shards // 2
    zero = jnp.zeros_like(late)
    one = one_ref[...].astype(f32)
    val = val_ref[...].astype(f32)
    out = out_ref[...].astype(f32)
    skip = skip_ref[...]
    conv = conv_ref[...] + jnp.where(upper, late, zero)
    corr = corr_ref[...] + jnp.where(upper, zero, late)
    grad_two_ref[...] = (out * (conv + skip * (one * val))).astype(bf16)
    mid = corr + skip * (out * two_ref[...].astype(f32))
    grad_one_ref[...] = (mid * val).astype(bf16)
    grad_value_ref[...] = (mid * one).astype(bf16)


def finish_kernel(
    channels, shards, rank_ref, own_ref, come_ref, first_ref, first_come_ref, second_out, first_out, bias_out, second,
    first, bias, sems,
):
    rank = rank_ref[0]
    inner = jnp.logical_and(rank > 0, rank < shards - 1)
    lanes = channels // 128
    copies = [
        pltpu.make_async_copy(held, out, sems.at[i])
        for i, (held, out) in enumerate(((second, second_out), (first, first_out), (bias, bias_out)))
    ]
    picked = jnp.where(inner, own_ref[...], come_ref[...])
    second[...] = picked[:, :channels].astype(f32)
    copies[0].start()
    first[...] = jnp.where(inner, first_ref[...], first_come_ref[...])
    copies[1].start()
    rows = get_side(picked, channels, lanes, first.shape[1])[0]
    for i in range(lanes):
        bias[:, i * 128 : (i + 1) * 128] = rows[i : i + 1]
    copies[2].start()
    for copy in copies:
        copy.wait()


def few_shards_body(
    x_one, x_two, values, grad_out, first_weight, second_weight, skip_bias, decay_rate
):
    rows, channels = x_one.shape
    shards = lax.axis_size("ctx")
    feat_count, hid_count = first_weight.shape
    seq_len = rows * shards
    double = 2 * rows
    width = min(512, channels)
    blocks = channels // width
    wide = 2 * width if blocks % 4 == 0 else width
    few = channels // wide
    rank = lax.axis_index("ctx").astype(jnp.int32).reshape(1)
    front, back = block_tables(rows)
    feats = feature_table(seq_len)
    featt = np.ascontiguousarray(feats.T)
    skip_row = skip_bias.reshape(1, channels)
    rate_row = decay_rate.reshape(1, channels)
    smem = pl.BlockSpec(memory_space=pltpu.SMEM)
    vmem = pl.BlockSpec(memory_space=pltpu.VMEM)
    anywhere = pl.BlockSpec(memory_space=pl.ANY)
    mebi = 1024 * 1024

    def shape(*dims, dtype=f32):
        return jax.ShapeDtypeStruct(dims, dtype)

    def call(kernel, name, units, out_shape, in_specs, out_specs=None, scratch=(), limit=16, aliases={}):
        return pl.pallas_call(
            kernel,
            in_specs=in_specs,
            out_specs=out_specs if out_specs is not None else [vmem] * len(out_shape),
            out_shape=out_shape,
            scratch_shapes=scratch,
            input_output_aliases=aliases,
            compiler_params=pltpu.CompilerParams(vmem_limit_bytes=limit * mebi),
            cost_estimate=pl.CostEstimate(
                flops=2 * units * double * double * channels, bytes_accessed=rows * channels, transcendentals=0
            ),
            name=name,
        )

    def move(array, pairs):
        return lax.ppermute(array, "ctx", pairs)

    inward = [(0, 1), (shards - 1, shards - 2)]
    outward = [(1, 0), (shards - 2, shards - 1)]
    across = [(1, 2), (2, 1)]
    alone = [(0, 0), (shards - 1, shards - 1)]
    pay_shape = (hid_count, channels + SIDE)
    block_bf16 = shape(rows, channels, dtype=bf16)
    block_f32 = shape(rows, channels)

    row_step = max(rows // 2, 16)
    gate_rows = pl.BlockSpec((row_step, channels), lambda i: (i, 0))
    pair, other, edge, bias = pl.pallas_call(
        products_kernel,
        grid=(rows // row_step,),
        in_specs=[smem] + [gate_rows] * 4,
        out_specs=[gate_rows] * 3 + [pl.BlockSpec((1, channels), lambda i: (0, 0))],
        out_shape=[block_bf16] * 3 + [shape(1, channels)],
        compiler_params=pltpu.CompilerParams(vmem_limit_bytes=64 * mebi),
        name="products",
    )(rank, x_one, x_two, values, grad_out)
    pair_in = move(pair, inward + outward)
    middle_in = move(other, across)

    own_shapes = [
        shape(rows, feat_count), shape(feat_count, hid_count), block_bf16, block_bf16, shape(hid_count, channels),
        shape(1, channels), shape(double, double, dtype=bf16), shape(double, double, dtype=bf16),
        shape(feat_count, seq_len), shape(1, channels), shape(*pay_shape, dtype=bf16),
    ]
    (send,) = call(
        only(False, shards, 0, functools.partial(own_kernel, rows, shards, channels, few, wide)), "own_pair", 8,
        [shape(*pay_shape, dtype=bf16)],
        [smem] + [anywhere] * 10,
        out_specs=[anywhere],
        scratch=[pltpu.VMEM(s.shape, s.dtype) for s in own_shapes]
        + [
            pltpu.VMEM((2 * hid_count, rows), bf16), pltpu.VMEM((rows, hid_count), f32),
            pltpu.SemaphoreType.DMA((10,)), pltpu.SemaphoreType.DMA,
        ],
        limit=60,
    )(rank, feats[:rows], first_weight, pair, other, second_weight, rate_row, front, back, featt, bias)
    come = move(send, inward)
    late_feats, _ = lax.optimization_barrier((jnp.asarray(feats), send))
    spec, trans, slope = call(
        functools.partial(filters_kernel, rows, shards, blocks, width), "filters", 8,
        [
            shape(shards, double, channels, dtype=bf16), shape(2 * hid_count, seq_len, dtype=bf16),
            shape(seq_len, hid_count),
        ],
        [vmem] * 5,
        scratch=[pltpu.VMEM((seq_len, 3 * hid_count), bf16)],
    )(late_feats, first_weight, second_weight, rate_row, front)

    edge, _ = lax.optimization_barrier((edge, slope))
    far = move(edge, [(0, 2), (shards - 1, shards - 3)])
    conv, corr, ahead, sums, first, near_spec = call(
        functools.partial(near_kernel, rows, shards, blocks, width), "near_blocks", 20,
        [block_f32] * 3
        + [shape(hid_count, channels), shape(feat_count, hid_count), shape(double, channels)],
        [smem] + [vmem] * 12,
        scratch=[
            pltpu.VMEM((4, double, width), f32),
            pltpu.VMEM((3, double, width), bf16),
            pltpu.VMEM((shards - 1, double, width), bf16),
            pltpu.VMEM((shards - 1, double, width), bf16),
            pltpu.VMEM(((shards - 1) * rows, hid_count), f32),
        ],
    )(rank, pair, other, pair_in, middle_in, spec, second_weight, rate_row, front, back, trans, featt, slope)

    part, far_spec = call(
        only(
            True, shards, 0,
            looped(
                functools.partial(far_kernel, rows),
                (None, ROWS, (slice(3, 4), slice(None)), None, None, ROWS, ROWS, ROWS),
                few, wide,
            ),
        ),
        "far_block", 1,
        [block_bf16, shape(double, channels)],
        [smem] + [vmem] * 5,
    )(rank, far, spec, front, back, ahead)
    (late,) = call(
        only(
            True, shards, 0,
            looped(
                functools.partial(late_kernel, rows),
                (None, ROWS, (slice(2, 3), slice(None)), None, ROWS),
                few, wide,
            ),
        ),
        "late_block", 1,
        [block_f32],
        [smem] + [vmem] * 3,
    )(rank, far_spec, spec, back)
    part_come = move(part, outward)

    pay, first = call(
        only(
            True, shards, 1,
            looped(
                functools.partial(last_kernel, rows, shards, channels),
                (None, None, ROWS, ROWS, ROWS, ROWS, None, None, None, None, ROWS),
                few, wide,
            ),
        ),
        "last_pair", 1,
        [shape(*pay_shape, dtype=bf16), shape(feat_count, hid_count)],
        [anywhere, smem] + [vmem] * 12,
        scratch=[pltpu.VMEM((2 * rows, hid_count), f32)],
    )(part, rank, near_spec, far_spec, second_weight, rate_row, back, trans, featt, slope, sums, first, bias, come)
    pay_come = move(pay, across + alone)
    group = lax.axis_size(("ch", "sub"))
    bit = 1
    while bit < group:
        first = first + lax.ppermute(first, ("ch", "sub"), [(i, i ^ bit) for i in range(group)])
        bit *= 2

    (total,) = call(
        functools.partial(total_kernel, channels, hid_count), "total", 0,
        [shape(*pay_shape, dtype=bf16)],
        [anywhere] * 3 + [vmem] * 2,
    )(part_come, first, late, pay, pay_come)
    total_come = move(total, inward + outward)

    def gates(inner, *before):
        return call(
            only(
                inner, shards, len(before),
                functools.partial(gates_kernel, inner, shards, blocks, width, len(before)),
            ),
            "gates", 0,
            [block_bf16] * 3,
            [anywhere] * len(before) + [smem] + [vmem] * 9,
            out_specs=[anywhere] * 3,
            scratch=[pltpu.VMEM((rows, channels), bf16)] * 3 + [pltpu.SemaphoreType.DMA((blocks, 3))],
            aliases={i: i for i in range(3)} if inner else {},
        )(*before, rank, x_one, x_two, values, grad_out, skip_row, conv, corr, late, part_come)

    grads = gates(False, total)
    first, _ = lax.optimization_barrier((first, grads[0]))
    first = first + move(first, across + alone)
    first_come = move(first, inward + outward)
    grad_one, grad_two, grad_value = gates(True, *grads)

    outs = [shape(hid_count, channels), shape(feat_count, hid_count), shape(1, channels)]
    grad_second, grad_first, grad_bias = call(
        functools.partial(finish_kernel, channels, shards), "finish", 0,
        outs,
        [smem] + [vmem] * 4,
        out_specs=[anywhere] * 3,
        scratch=[pltpu.VMEM(o.shape, f32) for o in outs] + [pltpu.SemaphoreType.DMA((3,))],
    )(rank, total, total_come, first, first_come)
    return (grad_one, grad_two, grad_value, grad_first, grad_second, grad_bias.reshape(channels))


def solution(mesh):
    in_specs = (
        P(("parts", "ctx"), ("ch", "sub")),
        P(("parts", "ctx"), ("ch", "sub")),
        P(("parts", "ctx"), ("ch", "sub")),
        P(("parts", "ctx"), ("ch", "sub")),
        P(),
        P(None, ("ch", "sub")),
        P(("ch", "sub")),
        P(("ch", "sub")),
    )
    out_specs = (
        P(("parts", "ctx"), ("ch", "sub")),
        P(("parts", "ctx"), ("ch", "sub")),
        P(("parts", "ctx"), ("ch", "sub")),
        P("parts", None),
        P("parts", ("ch", "sub")),
        P(("parts", "ch", "sub")),
    )
    body = few_shards_body if mesh.shape["ctx"] == 4 else many_shards_body
    return jax.shard_map(body, mesh=mesh, in_specs=in_specs, out_specs=out_specs, check_vma=False)
```
